32 devices in a mesh: gx: 4 (over y, x), gy: 8 (over z, core).
Axes of the slice: x: 2, y: 2, z: 4, core: 2. Of those that a mesh axis runs over, the one named last changes fastest.
Arguments:
- old_fields: float32 [4, 128, 128, 128], P(None, 'gx', 'gy'), may hold values from -12 to 12, as said below
- inverse_step: float32 [128, 128, 128], P('gx', 'gy'), may hold values from 8 to 64
- boundary: int32 [128, 128, 128], P('gx', 'gy'), may hold values from 0 to 1, as said below
Outputs:
- new_fields: float32 [4, 128, 128, 128], P(None, 'gx', 'gy')
- pressure: float32 [128, 128, 128], P('gx', 'gy')
The draws below stay inside these ranges and needn't reach their ends.
Inputs may be any that keep to these rules, and one draw needn't show every extreme that they name: `old_fields`: drawn with a random sign and a magnitude that may vary over the brick. `boundary`: all copies of one mesh node hold the same value; the lowest node layer of every column and the top node plane are 0, and a column may have up to three fixed bottom layers.
All inputs are finite; a program needn't handle non-finite values.
Results may differ from the reference program's by a relative error of at most 0.00012.
Values sent between devices are 32-bit elements; how exact they have to be, the bound alone decides.
No kernel may reach another device: no remote copies, remote signals or barrier semaphores. Data moves between devices by JAX's collectives and lax.ppermute only.
A program may use at most 64 MiB of HBM per device.

```python
import math
import jax
import jax.numpy as jnp
import numpy as np
from jax import lax

EZ = 16
ITERS = 6
CHEB = 6
NXP = 128
NYP = 128
NZP = 128


def draw_old_fields(key, part):
    key = jax.random.fold_in(key, 5)
    envelope = 1.0 + (jnp.arange(NXP, dtype=jnp.float32) / NXP).reshape(1, NXP, 1, 1) + (jnp.arange(NYP, dtype=jnp.float32) / NYP).reshape(1, 1, NYP, 1)
    sample = jnp.clip(jax.random.normal(key, (4, NXP, NYP, NZP), jnp.float32), -4.0, 4.0)
    return sample * envelope


def draw_boundary(key, part):
    key = jax.random.fold_in(key, 11)
    columns_x = NXP // 8 * 7
    columns_y = NYP // 8 * 7
    heights = jax.random.randint(key, (columns_x, columns_y), 1, 4)
    place_x = (jnp.arange(NXP) // 8 * 7 + jnp.arange(NXP) % 8) % columns_x
    place_y = (jnp.arange(NYP) // 8 * 7 + jnp.arange(NYP) % 8) % columns_y
    level_index = jnp.arange(NZP) // 8 * 7 + jnp.arange(NZP) % 8
    ground = heights[place_x[:, None], place_y[None, :]]
    pinned = (level_index[None, None, :] < ground[:, :, None]) | (level_index[None, None, :] == EZ * 7)
    return jnp.where(pinned, 0, 1).astype(jnp.int32)


def steps_of(stream_key, extent, shards, low, top_value):
    level = 1.0
    for dim, parts in shards:
        steps = jax.random.uniform(jax.random.fold_in(jax.random.fold_in(stream_key, 6), dim), (parts,), jnp.float32, low / len(shards), top_value / len(shards))
        level = level * jnp.repeat(jnp.exp(steps), extent[dim] // parts).reshape((-1,) + (1,) * (len(extent) - 1 - dim))
    return level


def setup_inputs(seed: int = 0) -> dict:
    arg_keys = jax.random.split(jax.random.key(seed), 4)
    return {
        "old_fields": draw_old_fields(jax.random.fold_in(arg_keys[3], 71), 0),
        "inverse_step": jnp.clip(jnp.exp(math.log(64.0) - 2.0794415 * jax.random.uniform(arg_keys[1], (NXP, NYP, NZP), jnp.float32) ** steps_of(arg_keys[1], (NXP, NYP, NZP), ((0, 4), (1, 8)), -0.2, 0.2)), 8.0, 64.0),
        "boundary": draw_boundary(jax.random.fold_in(arg_keys[3], 71), 0),
    }


SIGMA_SHIFT = 0.5
DIFFUSE = (1.0, 1.0, 1.0, 1.4)
COUPLING = 1.0
STRATIFY = 1.0
SPREAD = 20.0
HIGHEST_PRECISION = lax.Precision.HIGHEST
LOBATTO_POINTS = (-1.0, -0.8717401485096066, -0.5917001814331423, -0.2092992179024789, 0.2092992179024789, 0.5917001814331423, 0.8717401485096066, 1.0)


def legendre_value(points, degree):
    previous = points * 0.0 + 1.0
    current = points
    for order in range(1, degree):
        following = ((2 * order + 1) * points * current - order * previous) / (order + 1)
        previous = current
        current = following
    return current


def quadrature_tables():
    degree = 7
    points = np.array(LOBATTO_POINTS)
    values = legendre_value(points, degree)
    weights = 2.0 / (degree * (degree + 1) * values * values)
    derive = np.zeros((degree + 1, degree + 1))
    for row_index in range(degree + 1):
        for column_index in range(degree + 1):
            if row_index != column_index:
                derive[row_index, column_index] = values[row_index] / (values[column_index] * (points[row_index] - points[column_index]))
    derive[0, 0] = -degree * (degree + 1) / 4.0
    derive[degree, degree] = degree * (degree + 1) / 4.0
    stiffness_table = derive.T @ (weights[:, None] * derive)
    return weights, derive, stiffness_table


def node_lines(vector, extent_x, extent_y, extent_z):
    line_x = jnp.asarray(np.tile(vector, extent_x // 8), jnp.float32).reshape(extent_x, 1, 1)
    line_y = jnp.asarray(np.tile(vector, extent_y // 8), jnp.float32).reshape(extent_y, 1)
    line_z = jnp.asarray(np.tile(vector, extent_z // 8), jnp.float32)
    return line_x, line_y, line_z


def along_first(nodal, matrix):
    components, extent_x, extent_y, extent_z = nodal.shape
    blocks = nodal.reshape(components, extent_x // 8, 8, extent_y, extent_z)
    contracted = jnp.einsum("ab,pebyz->peayz", jnp.asarray(matrix, jnp.float32), blocks, precision=HIGHEST_PRECISION)
    return contracted.reshape(nodal.shape)


def along_second(nodal, matrix):
    components, extent_x, extent_y, extent_z = nodal.shape
    blocks = nodal.reshape(components, extent_x, extent_y // 8, 8, extent_z)
    contracted = jnp.einsum("ab,pxebz->pxeaz", jnp.asarray(matrix, jnp.float32), blocks, precision=HIGHEST_PRECISION)
    return contracted.reshape(nodal.shape)


def along_third(nodal, matrix):
    components, extent_x, extent_y, extent_z = nodal.shape
    blocks = nodal.reshape(components, extent_x, extent_y, extent_z // 8, 8)
    contracted = jnp.einsum("ab,pxyeb->pxyea", jnp.asarray(matrix, jnp.float32), blocks, precision=HIGHEST_PRECISION)
    return contracted.reshape(nodal.shape)


def stiffness(nodal):
    weights, derive, stiffness_table = quadrature_tables()
    weight_x, weight_y, weight_z = node_lines(weights, nodal.shape[1], nodal.shape[2], nodal.shape[3])
    total = along_first(nodal, stiffness_table) * weight_y * weight_z
    total = total + along_second(nodal, stiffness_table) * weight_x * weight_z
    return total + along_third(nodal, stiffness_table) * weight_x * weight_y


def pair_sum(nodal, dimension, preceding, following):
    length = nodal.shape[dimension]
    before = jnp.concatenate([preceding, lax.slice_in_dim(nodal, 0, length - 1, axis=dimension)], axis=dimension)
    after_plane = jnp.concatenate([lax.slice_in_dim(nodal, 1, length, axis=dimension), following], axis=dimension)
    layout = [1] * nodal.ndim
    layout[dimension] = length
    position = (jnp.arange(length) % 8).reshape(layout)
    return nodal + jnp.where(position == 0, before, 0.0) + jnp.where(position == 7, after_plane, 0.0)


def assemble(nodal):
    nodal = pair_sum(nodal, 1, nodal[:, -1:], nodal[:, :1])
    nodal = pair_sum(nodal, 2, nodal[:, :, -1:], nodal[:, :, :1])
    empty_plane = jnp.zeros_like(nodal[:, :, :, :1])
    return pair_sum(nodal, 3, empty_plane, empty_plane)


def multiplicity_weights(extent_x, extent_y, extent_z):
    along_x = jnp.where(jnp.arange(extent_x) % 8 % 7 == 0, 0.5, 1.0).astype(jnp.float32)
    along_y = jnp.where(jnp.arange(extent_y) % 8 % 7 == 0, 0.5, 1.0).astype(jnp.float32)
    index_z = jnp.arange(extent_z)
    shared_z = (index_z % 8 % 7 == 0) & (index_z > 0) & (index_z < extent_z - 1)
    along_z = jnp.where(shared_z, 0.5, 1.0).astype(jnp.float32)
    return along_x.reshape(extent_x, 1, 1) * along_y.reshape(extent_y, 1) * along_z


def products(left_field, right_field, multiplicity):
    return jnp.sum(left_field * right_field * multiplicity, axis=(1, 2, 3))


def chebyshev_bounds():
    weights, derive, stiffness_table = quadrature_tables()
    weight_matrix = np.eye(8) * weights
    element_matrix = np.kron(np.kron(stiffness_table, weight_matrix), weight_matrix)
    element_matrix = element_matrix + np.kron(np.kron(weight_matrix, stiffness_table), weight_matrix)
    element_matrix = element_matrix + np.kron(np.kron(weight_matrix, weight_matrix), stiffness_table)
    element_matrix = element_matrix + SIGMA_SHIFT * np.kron(np.kron(weight_matrix, weight_matrix), weight_matrix)
    diagonal_index = np.arange(element_matrix.shape[0])
    bounds_ratio = np.sum(np.abs(element_matrix), axis=1) / element_matrix[diagonal_index, diagonal_index]
    upper_bound = float(np.max(bounds_ratio))
    lower_bound = upper_bound / SPREAD
    return (upper_bound + lower_bound) / 2.0, (upper_bound - lower_bound) / 2.0


def reference(old_fields, inverse_step, boundary):
    weights, derive, stiffness_table = quadrature_tables()
    free_nodes = boundary.astype(jnp.float32)
    extent_x, extent_y, extent_z = inverse_step.shape
    weight_x, weight_y, weight_z = node_lines(weights, extent_x, extent_y, extent_z)
    mass_weights = weight_x * weight_y * weight_z
    multiplicity = multiplicity_weights(extent_x, extent_y, extent_z)
    diffuse = jnp.asarray(np.array(DIFFUSE), jnp.float32).reshape(4, 1, 1, 1)
    nothing = jnp.zeros_like(old_fields[0])
    buoyancy = jnp.stack([nothing, nothing, COUPLING * old_fields[3], -STRATIFY * old_fields[2]])
    residual = free_nodes * assemble(mass_weights * (inverse_step * old_fields + buoyancy))
    solution = jnp.zeros_like(old_fields)
    direction = residual
    norm_now = products(residual, residual, multiplicity)
    for iteration in range(ITERS):
        applied = free_nodes * assemble(diffuse * stiffness(direction) + inverse_step * mass_weights * direction)
        step_size = (norm_now / products(direction, applied, multiplicity)).reshape(4, 1, 1, 1)
        solution = solution + step_size * direction
        residual = residual - step_size * applied
        norm_next = products(residual, residual, multiplicity)
        direction = residual + (norm_next / norm_now).reshape(4, 1, 1, 1) * direction
        norm_now = norm_next
    spread = along_first(solution[0:1], derive) + along_second(solution[1:2], derive) + along_third(solution[2:3], derive)
    source_term = -free_nodes * assemble(mass_weights * spread)
    table_index = np.arange(8)
    diag_x, diag_y, diag_z = node_lines(stiffness_table[table_index, table_index], extent_x, extent_y, extent_z)
    local_diagonal = diag_x * weight_y * weight_z + weight_x * diag_y * weight_z + weight_x * weight_y * diag_z + SIGMA_SHIFT * mass_weights
    diagonal = assemble(local_diagonal[None])
    inverse = 1.0 / diagonal
    centre_value, half_width = chebyshev_bounds()
    factor = centre_value / half_width
    pressure = jnp.zeros_like(source_term)
    remainder = source_term
    update = inverse * remainder / centre_value
    damping = 1.0 / factor
    for iteration in range(CHEB):
        pressure = pressure + update
        if iteration < CHEB - 1:
            remainder = remainder - free_nodes * assemble(stiffness(update) + SIGMA_SHIFT * mass_weights * update)
            damping_next = 1.0 / (2.0 * factor - damping)
            update = damping_next * damping * update + (2.0 * damping_next / half_width) * inverse * remainder
            damping = damping_next
    return solution, pressure[0]
```

```python
import jax
import jax.numpy as jnp
import numpy as np
from jax import lax
from jax.sharding import PartitionSpec as P

ITERS = 6
CHEB = 6

SIGMA_SHIFT = 0.5
DIFFUSE = (1.0, 1.0, 1.0, 1.4)
COUPLING = 1.0
STRATIFY = 1.0
SPREAD = 20.0
STEP_MAX = 64.0
HIGHEST_PRECISION = lax.Precision.HIGHEST
LOBATTO_POINTS = (
    -1.0,
    -0.8717401485096066,
    -0.5917001814331423,
    -0.2092992179024789,
    0.2092992179024789,
    0.5917001814331423,
    0.8717401485096066,
    1.0,
)


def legendre_value(points, degree):
    previous = points * 0.0 + 1.0
    current = points
    for order in range(1, degree):
        following = ((2 * order + 1) * points * current - order * previous) / (order + 1)
        previous = current
        current = following
    return current


def quadrature_tables():
    degree = 7
    points = np.array(LOBATTO_POINTS)
    values = legendre_value(points, degree)
    weights = 2.0 / (degree * (degree + 1) * values * values)
    derive = np.zeros((degree + 1, degree + 1))
    for row_index in range(degree + 1):
        for column_index in range(degree + 1):
            if row_index != column_index:
                derive[row_index, column_index] = values[row_index] / (
                    values[column_index] * (points[row_index] - points[column_index])
                )
    derive[0, 0] = -degree * (degree + 1) / 4.0
    derive[degree, degree] = degree * (degree + 1) / 4.0
    stiffness_table = derive.T @ (weights[:, None] * derive)
    return (weights, derive, stiffness_table)


WEIGHTS, DERIVE, STIFF = quadrature_tables()
COPIES = np.where(np.arange(8) % 7 == 0, 2.0, 1.0)


def chebyshev_bounds():
    weight_matrix = np.eye(8) * WEIGHTS

    def kron3(a, b, c):
        return np.kron(np.kron(a, b), c)

    element_matrix = (
        kron3(STIFF, weight_matrix, weight_matrix)
        + kron3(weight_matrix, STIFF, weight_matrix)
        + kron3(weight_matrix, weight_matrix, STIFF)
        + SIGMA_SHIFT * kron3(weight_matrix, weight_matrix, weight_matrix)
    )
    bounds_ratio = np.sum(np.abs(element_matrix), axis=1) / np.diagonal(element_matrix)
    upper_bound = float(np.max(bounds_ratio))
    lower_bound = upper_bound / SPREAD
    return ((upper_bound + lower_bound) / 2.0, (upper_bound - lower_bound) / 2.0)


def spectrum_top(diffuse):
    root = np.sqrt(COPIES)
    stiff = root[:, None] * STIFF * root[None, :]
    weight = np.diag(WEIGHTS * COPIES)

    def kron3(a, b, c):
        return np.kron(np.kron(a, b), c)

    element = diffuse * (
        kron3(stiff, weight, weight) + kron3(weight, stiff, weight) + kron3(weight, weight, stiff)
    ) + STEP_MAX * kron3(weight, weight, weight)
    return float(np.linalg.eigvalsh(element)[-1])


def line_sums(table, length):
    matrix = np.kron(np.eye(length // 8), table)
    total = matrix.copy()
    for start in range(8, length, 8):
        total[start] += matrix[start - 1]
        total[start - 1] += matrix[start]
    return jnp.asarray(total, jnp.float32)


def summed_line(vector, length, closed):
    line = np.tile(vector * COPIES, length // 8)
    if closed:
        line[0] = vector[0]
        line[-1] = vector[-1]
    return line


def neighbours(axis):
    size = lax.axis_size(axis)
    up = [(i, (i + 1) % size) for i in range(size)]
    return up, [(j, i) for i, j in up]


def exchange_faces(axis, dim, field):
    length = field.shape[dim]
    up, down = neighbours(axis)
    before = lax.ppermute(lax.slice_in_dim(field, length - 1, length, axis=dim), axis, up)
    after = lax.ppermute(lax.slice_in_dim(field, 0, 1, axis=dim), axis, down)
    return before, after


def add_faces(field, dim, faces):
    before, after = faces
    layout = [1] * field.ndim
    length = field.shape[dim]
    layout[dim] = length
    place = jnp.arange(length).reshape(layout)
    return field + jnp.where(place == 0, before, 0.0) + jnp.where(place == length - 1, after, 0.0)


def inner_sums(nodal, dim):
    length = nodal.shape[dim]
    layout = [1] * nodal.ndim
    layout[dim] = length
    place = jnp.arange(length).reshape(layout)
    before = jnp.roll(nodal, 1, axis=dim)
    after = jnp.roll(nodal, -1, axis=dim)
    return (
        nodal
        + jnp.where((place % 8 == 0) & (place > 0), before, 0.0)
        + jnp.where((place % 8 == 7) & (place < length - 1), after, 0.0)
    )


def all_sum(values, axis):
    size = lax.axis_size(axis)
    if size & (size - 1):
        return lax.psum(values, axis)
    bit = 1

    def swapped(mask):
        return lax.ppermute(values, axis, [(i, i ^ mask) for i in range(size)])

    while bit < size:
        if 2 * bit < size:
            one, two, three = swapped(bit), swapped(2 * bit), swapped(3 * bit)
            values = (values + one) + (two + three)
            bit *= 4
        else:
            values = values + swapped(bit)
            bit *= 2
    return values


def conjugate_coefficients(moments, centre, half):
    remaining, towards = list(moments), list(moments)
    one, zero = jnp.ones_like(moments[0]), jnp.zeros_like(moments[0])
    direction = [one] + [zero] * ITERS
    residual = list(direction)
    total = [zero] * ITERS
    for step in range(ITERS):
        count = len(towards) - 1
        image = []
        for level in range(count):
            side = (
                half * towards[1] if level == 0 else 0.5 * half * (towards[level + 1] + towards[level - 1])
            )
            image.append(centre * towards[level] + side)
        alpha = remaining[step] / image[step]
        total = [total[i] + alpha * direction[i] for i in range(ITERS)]
        if step == ITERS - 1:
            break
        applied = []
        for i in range(ITERS + 1):
            term = centre * direction[i]
            if i >= 1:
                term = term + (half if i == 1 else 0.5 * half) * direction[i - 1]
            if i < ITERS:
                term = term + 0.5 * half * direction[i + 1]
            applied.append(term)
        residual = [residual[i] - alpha * applied[i] for i in range(ITERS + 1)]
        following = [remaining[i] - alpha * image[i] for i in range(count)]
        beta = -alpha * (half if step == 0 else 0.5 * half) * following[step + 1] / remaining[step]
        towards = [following[i] + beta * towards[i] for i in range(count)]
        direction = [residual[i] + beta * direction[i] for i in range(ITERS + 1)]
        remaining = following
    return total


def on_device(old_fields, inverse_step, boundary):
    free = boundary.astype(jnp.float32)
    extent = inverse_step.shape
    tiles = [jnp.asarray(np.tile(WEIGHTS, n // 8), jnp.float32) for n in extent]
    mass = tiles[0][:, None, None] * tiles[1][:, None] * tiles[2]
    lines = [summed_line(WEIGHTS, n, d == 2) for d, n in enumerate(extent)]
    wx = jnp.asarray(lines[0], jnp.float32)[:, None, None]
    wy = jnp.asarray(lines[1], jnp.float32)[:, None]
    wz = jnp.asarray(lines[2], jnp.float32)
    count_x = np.tile(1.0 / COPIES, extent[0] // 8)
    count_y = np.tile(1.0 / COPIES, extent[1] // 8)
    count_z = np.tile(1.0 / COPIES, extent[2] // 8)
    count_z[0] = count_z[-1] = 1.0
    open_x, open_y = count_x.copy(), count_y.copy()
    open_x[0] = open_x[-1] = open_y[0] = open_y[-1] = 1.0

    def outer(a, b, c):
        return jnp.asarray(a[:, None, None] * b[:, None] * c, jnp.float32)

    share = outer(count_x, count_y, count_z)
    stiff = [line_sums(STIFF, n) for n in extent]
    slope = [line_sums(WEIGHTS[:, None] * DERIVE, n) for n in extent]

    def along(field, matrices, dims=(0, 1, 2)):
        forms = ("ab,pbyz->payz", "ab,pxbz->pxaz", "ab,pxyb->pxya")
        return [
            jnp.einsum(forms[d], matrices[d], field, precision=HIGHEST_PRECISION) for d in dims
        ]

    nothing = jnp.zeros_like(old_fields[0])
    forcing = jnp.stack([nothing, nothing, COUPLING * old_fields[3], -STRATIFY * old_fields[2]])
    local = mass * (inverse_step * old_fields + forcing)
    local = jnp.concatenate([local, (mass * inverse_step)[None]])
    local = inner_sums(inner_sums(inner_sums(local, 3), 2), 1)
    local = add_faces(local, 1, exchange_faces("gx", 1, local))
    local = add_faces(local, 2, exchange_faces("gy", 2, local))
    right = free * local[:4]
    reaction = local[4]

    top = np.array([spectrum_top(c) for c in DIFFUSE])
    half = jnp.asarray(0.5 * top, jnp.float32)
    half4 = half.reshape(4, 1, 1, 1)
    scale = jnp.asarray(np.array(DIFFUSE) / (0.5 * top), jnp.float32).reshape(4, 1, 1, 1)
    shifted = reaction / half4 - 1.0

    def helmholtz(field):
        kx, ky, kz = along(field, stiff)
        near_x = exchange_faces("gx", 1, kx)
        near_y = exchange_faces("gy", 2, ky)
        kx = add_faces(kx, 1, near_x)
        ky = add_faces(ky, 2, near_y)
        return free * (scale * (kx * wy * wz + ky * wx * wz + kz * wx * wy) + shifted * field)

    def dot(a, b):
        return jnp.sum(a * b * share, axis=(1, 2, 3))

    basis = [right, helmholtz(right)]
    for _ in range(2, ITERS):
        basis.append(2.0 * helmholtz(basis[-1]) - basis[-2])
    sums = [dot(basis[0], basis[0]), dot(basis[1], basis[0])]
    for level in range(1, ITERS):
        sums.append(dot(basis[level], basis[level]))
        if level < ITERS - 1:
            sums.append(dot(basis[level + 1], basis[level]))
    last = basis[-1]
    kx, ky, kz = along(last, stiff)
    energy = scale * (
        kx * wy * wz * outer(open_x, count_y, count_z)
        + ky * wx * wz * outer(count_x, open_y, count_z)
        + kz * wx * wy * share
    ) + shifted * last * share
    sums.append(2.0 * jnp.sum(energy * last, axis=(1, 2, 3)) - dot(basis[-2], last))
    sums = all_sum(all_sum(jnp.stack(sums), "gx"), "gy")
    moments = [sums[0], sums[1]]
    for level in range(2, 2 * ITERS):
        moments.append(2.0 * sums[level] - sums[level % 2])
    weights = conjugate_coefficients(moments, half, half)
    fields = sum(w.reshape(4, 1, 1, 1) * v for w, v in zip(weights, basis))

    (sx,) = along(fields[0:1], slope, (0,))
    (sy,) = along(fields[1:2], slope, (1,))
    (sz,) = along(fields[2:3], slope, (2,))
    near_x = exchange_faces("gx", 1, sx)
    near_y = exchange_faces("gy", 2, sy)
    sx = add_faces(sx, 1, near_x)
    sy = add_faces(sy, 2, near_y)
    remainder = -free * (sx * wy * wz + sy * wx * wz + sz * wx * wy)
    table = np.diagonal(STIFF)
    diag = [summed_line(table, n, d == 2) for d, n in enumerate(extent)]
    diagonal = (
        outer(diag[0], lines[1], lines[2])
        + outer(lines[0], diag[1], lines[2])
        + outer(lines[0], lines[1], diag[2])
        + SIGMA_SHIFT * outer(*lines)
    )
    inverse = 1.0 / diagonal
    centre_value, half_width = chebyshev_bounds()
    factor = centre_value / half_width
    pressure = jnp.zeros_like(remainder)
    update = inverse * remainder / centre_value
    damping = 1.0 / factor
    for iteration in range(CHEB):
        pressure = pressure + update
        if iteration < CHEB - 1:
            kx, ky, kz = along(update, stiff)
            near_x = exchange_faces("gx", 1, kx)
            near_y = exchange_faces("gy", 2, ky)
            kx = add_faces(kx, 1, near_x)
            ky = add_faces(ky, 2, near_y)
            remainder = remainder - free * (
                kx * wy * wz + ky * wx * wz + kz * wx * wy + SIGMA_SHIFT * wx * wy * wz * update
            )
            damping_next = 1.0 / (2.0 * factor - damping)
            update = (
                damping_next * damping * update
                + 2.0 * damping_next / half_width * inverse * remainder
            )
            damping = damping_next
    return (fields, pressure[0])


def solution(mesh):
    return jax.shard_map(
        on_device,
        mesh=mesh,
        in_specs=(P(None, "gx", "gy", None), P("gx", "gy", None), P("gx", "gy", None)),
        out_specs=(P(None, "gx", "gy", None), P("gx", "gy", None)),
        check_vma=False,
    )
```

```python
import functools

import jax
import jax.numpy as jnp
import numpy as np
from jax import lax
from jax.experimental import pallas as pl
from jax.experimental.pallas import tpu as pltpu
from jax.sharding import PartitionSpec as P

ITERS = 6
CHEB = 6

SIGMA_SHIFT = 0.5
DIFFUSE = (1.0, 1.0, 1.0, 1.4)
COUPLING = 1.0
STRATIFY = 1.0
SPREAD = 20.0
STEP_MAX = 64.0
HIGHEST_PRECISION = lax.Precision.HIGHEST
LOBATTO_POINTS = (
    -1.0,
    -0.8717401485096066,
    -0.5917001814331423,
    -0.2092992179024789,
    0.2092992179024789,
    0.5917001814331423,
    0.8717401485096066,
    1.0,
)


def legendre_value(points, degree):
    previous = points * 0.0 + 1.0
    current = points
    for order in range(1, degree):
        following = ((2 * order + 1) * points * current - order * previous) / (order + 1)
        previous = current
        current = following
    return current


def quadrature_tables():
    degree = 7
    points = np.array(LOBATTO_POINTS)
    values = legendre_value(points, degree)
    weights = 2.0 / (degree * (degree + 1) * values * values)
    derive = np.zeros((degree + 1, degree + 1))
    for row_index in range(degree + 1):
        for column_index in range(degree + 1):
            if row_index != column_index:
                derive[row_index, column_index] = values[row_index] / (
                    values[column_index] * (points[row_index] - points[column_index])
                )
    derive[0, 0] = -degree * (degree + 1) / 4.0
    derive[degree, degree] = degree * (degree + 1) / 4.0
    stiffness_table = derive.T @ (weights[:, None] * derive)
    return (weights, derive, stiffness_table)


WEIGHTS, DERIVE, STIFF = quadrature_tables()
COPIES = np.where(np.arange(8) % 7 == 0, 2.0, 1.0)


def chebyshev_bounds():
    weight_matrix = np.eye(8) * WEIGHTS

    def kron3(a, b, c):
        return np.kron(np.kron(a, b), c)

    element_matrix = (
        kron3(STIFF, weight_matrix, weight_matrix)
        + kron3(weight_matrix, STIFF, weight_matrix)
        + kron3(weight_matrix, weight_matrix, STIFF)
        + SIGMA_SHIFT * kron3(weight_matrix, weight_matrix, weight_matrix)
    )
    bounds_ratio = np.sum(np.abs(element_matrix), axis=1) / np.diagonal(element_matrix)
    upper_bound = float(np.max(bounds_ratio))
    lower_bound = upper_bound / SPREAD
    return ((upper_bound + lower_bound) / 2.0, (upper_bound - lower_bound) / 2.0)


def spectrum_top(diffuse):
    root = np.sqrt(COPIES)
    stiff = root[:, None] * STIFF * root[None, :]
    weight = np.diag(WEIGHTS * COPIES)

    def kron3(a, b, c):
        return np.kron(np.kron(a, b), c)

    element = diffuse * (
        kron3(stiff, weight, weight) + kron3(weight, stiff, weight) + kron3(weight, weight, stiff)
    ) + STEP_MAX * kron3(weight, weight, weight)
    return float(np.linalg.eigvalsh(element)[-1])


def line_sums(table, length):
    matrix = np.kron(np.eye(length // 8), table)
    total = matrix.copy()
    for start in range(8, length, 8):
        total[start] += matrix[start - 1]
        total[start - 1] += matrix[start]
    return total


def depth_line(vector, length):
    line = np.tile(vector * COPIES, length // 8)
    line[0] = vector[0]
    line[-1] = vector[-1]
    return line


def f32(array):
    return np.ascontiguousarray(array, np.float32)


def rolled_rows(table):
    out = np.zeros((8, 8, 128))
    for shift in range(8):
        for row in range(8):
            out[shift, row] = table[row, (row - shift) % 8]
    return out


def block(a, b, c):
    return a[:, None, None] * b[:, None] * c


class Tables:
    def __init__(self, depth):
        ones8, ones = np.ones(8), np.ones(depth)
        wide = WEIGHTS * COPIES
        deep = depth_line(WEIGHTS, depth)
        flat = np.tile(WEIGHTS, depth // 8)
        stiff = np.diagonal(STIFF)
        wide_s, deep_s = stiff * COPIES, depth_line(stiff, depth)
        share = 1.0 / COPIES
        share_z = np.tile(share, depth // 8)
        share_z[0] = share_z[-1] = 1.0
        self.summed = f32(
            np.stack([block(ones8, wide, deep), block(wide, ones8, deep), block(wide, wide, ones)])
        )
        self.local = f32(
            np.stack(
                [block(ones8, WEIGHTS, flat), block(WEIGHTS, ones8, flat), block(WEIGHTS, WEIGHTS, ones)]
            )
        )
        self.mass = f32(block(WEIGHTS, WEIGHTS, flat))
        self.share = f32(block(share, share, share_z))
        diagonal = (
            block(wide_s, wide, deep)
            + block(wide, wide_s, deep)
            + block(wide, wide, deep_s)
            + SIGMA_SHIFT * block(wide, wide, deep)
        )
        self.inverse = f32(1.0 / diagonal)
        self.shift = f32(SIGMA_SHIFT * block(wide, wide, deep))
        self.stiff_y = f32(rolled_rows(STIFF))
        self.slope_y = f32(rolled_rows(WEIGHTS[:, None] * DERIVE))
        self.stiff_z = f32(line_sums(STIFF, depth).T)
        self.plain_z = f32(np.kron(np.eye(depth // 8), STIFF).T)
        self.slope_z = f32(line_sums(WEIGHTS[:, None] * DERIVE, depth).T)
        low, high = np.zeros((8, 128)), np.zeros((8, 128))
        low[0], high[7] = 1.0, 1.0
        place = np.arange(depth)
        after = ((place % 8 == 0) & (place > 0)).astype(float)
        before = ((place % 8 == 7) & (place < depth - 1)).astype(float)
        rows = np.ones((8, 1))
        self.edges = f32(np.stack([low, high, rows * after, rows * before]))


def along_x(rows, table):
    if np.allclose(table, table[::-1, ::-1]):
        even = 0.5 * (table[:4, :4] + table[:4, :3:-1])
        odd = 0.5 * (table[:4, :4] - table[:4, :3:-1])
        plus = [rows[i] + rows[7 - i] for i in range(4)]
        minus = [rows[i] - rows[7 - i] for i in range(4)]
        out = [None] * 8
        for a in range(4):
            p = sum(float(even[a, b]) * plus[b] for b in range(4))
            m = sum(float(odd[a, b]) * minus[b] for b in range(4))
            out[a], out[7 - a] = p + m, p - m
        return out
    return [sum(float(table[a, b]) * rows[b] for b in range(8)) for a in range(8)]


def along_y(tiles, factors):
    total = factors[0] * tiles
    for shift in range(1, 8):
        total = total + factors[shift] * pltpu.roll(tiles, shift, axis=1)
    return total


def along_z(tiles, matrix):
    x, y, z = tiles.shape
    out = jnp.dot(
        tiles.reshape(x * y, z), matrix, precision=HIGHEST_PRECISION, preferred_element_type=jnp.float32
    )
    return out.reshape(x, y, z)


def join_y(parts, low, high):
    out = list(parts)
    for e in range(1, len(parts)):
        out[e - 1] = out[e - 1] + high * pltpu.roll(parts[e], 7, axis=1)
        out[e] = out[e] + low * pltpu.roll(parts[e - 1], 1, axis=1)
    return out


def spread_rows(rows):
    return jnp.broadcast_to(rows[:, None, :], (rows.shape[0], 8, rows.shape[1]))


def column_sums(x_rows, y_parts, z_parts, summed, edges):
    y_parts = join_y(y_parts, edges[0], edges[1])
    return [
        jnp.stack(kx) * summed[0, 0] + ky * summed[1] + kz * summed[2]
        for kx, ky, kz in zip(x_rows, y_parts, z_parts)
    ]


def emit_column(ex, x_rows, y_parts, z_parts, extra, summed, edges, raw, faces, state):
    count = len(x_rows)
    fx_lo, fx_hi, fy_lo, fy_hi = faces
    columns = raw.shape[0] // 8
    rows = pl.ds(8 * ex, 8)
    parts = column_sums(x_rows, y_parts, z_parts, summed, edges)
    fy_lo[rows] = y_parts[0][:, 0]
    fy_hi[rows] = y_parts[-1][:, 7]
    for e in range(count):
        ys = pl.ds(8 * e, 8)
        part = parts[e] if extra is None else parts[e] + extra[e]
        raw[rows, ys] = part
        if ex:
            raw[8 * ex, ys] += state[e] * summed[0, 0]
            raw[8 * ex - 1, ys] += x_rows[e][0] * summed[0, 0]
        else:
            fx_lo[ys] = x_rows[e][0]
        if ex == columns - 1:
            fx_hi[ys] = x_rows[e][7]
    return [r[7] for r in x_rows]


def with_faces(tile, ex, e, columns, count, received, summed, edges):
    bx, ax, by, ay = received
    rows, ys = pl.ds(8 * ex, 8), pl.ds(8 * e, 8)
    if e == 0:
        tile = tile + spread_rows(by[rows]) * (edges[0] * summed[1])
    if e == count - 1:
        tile = tile + spread_rows(ay[rows]) * (edges[1] * summed[1])
    if ex == 0:
        first = tile[0:1] + (bx[ys] * summed[0, 0])[None]
        tile = jnp.concatenate([first, tile[1:]], axis=0)
    if ex == columns - 1:
        last = tile[7:8] + (ax[ys] * summed[0, 0])[None]
        tile = jnp.concatenate([tile[:7], last], axis=0)
    return tile


def split_rows(block_rows):
    return [block_rows[i] for i in range(8)]


def load_local(old, step, boundary, mass, edges, out, fx_lo, fx_hi, fy_lo, fy_hi):
    columns, count = out.shape[1] // 8, out.shape[2] // 8
    for field in range(5):
        before = [None] * count
        for ex in range(columns):
            rows = pl.ds(8 * ex, 8)
            parts = []
            for e in range(count):
                ys = pl.ds(8 * e, 8)
                value = step[rows, ys]
                if field < 4:
                    value = value * old[field, rows, ys]
                if field == 2:
                    value = value + COUPLING * old[3, rows, ys]
                if field == 3:
                    value = value - STRATIFY * old[2, rows, ys]
                value = value * mass[...]
                flat = value.reshape(64, 128)
                flat = flat.reshape(8, 8, 128)
                value = (
                    flat
                    + edges[2] * pltpu.roll(flat, 1, axis=2)
                    + edges[3] * pltpu.roll(flat, 127, axis=2)
                )
                parts.append(value)
            parts = join_y(parts, edges[0], edges[1])
            for e in range(count):
                ys = pl.ds(8 * e, 8)
                out[field, rows, ys] = parts[e]
                if ex:
                    out[field, 8 * ex, ys] += before[e]
                    out[field, 8 * ex - 1, ys] += parts[e][0]
                before[e] = parts[e][7]
        for e in range(count):
            ys = pl.ds(8 * e, 8)
            fx_lo[field, ys] = out[field, 0, ys]
            fx_hi[field, ys] = out[field, 8 * columns - 1, ys]
        for ex in range(columns):
            rows = pl.ds(8 * ex, 8)
            fy_lo[field, rows] = out[field, rows, pl.ds(0, 8)][:, 0]
            fy_hi[field, rows] = out[field, rows, pl.ds(8 * count - 8, 8)][:, 7]


def fix_corners(fy_lo, fy_hi, bx, ax, lo, hi):
    length = fy_lo.shape[1]
    last = bx.shape[1] - 1
    lo[...] = fy_lo[...]
    hi[...] = fy_hi[...]
    for field in range(5):
        lo[field, 0:1] += bx[field, 0:1]
        lo[field, length - 1 : length] += ax[field, 0:1]
        hi[field, 0:1] += bx[field, last : last + 1]
        hi[field, length - 1 : length] += ax[field, last : last + 1]


def rows_of(first, second):
    return jnp.sum(first, axis=0, keepdims=True), jnp.sum(second, axis=0, keepdims=True)


def start_basis(local, boundary, bx, ax, by, ay, summed, edges, share, stiff_y, stiff_z,
                right, reaction, free, raw, fx_lo, fx_hi, fy_lo, fy_hi, dots):
    columns, count = raw.shape[1] // 8, raw.shape[2] // 8
    dots[...] = jnp.zeros_like(dots)

    def complete(field, ex, e):
        rows, ys = pl.ds(8 * ex, 8), pl.ds(8 * e, 8)
        tile = local[field, rows, ys]
        if e == 0:
            tile = tile + spread_rows(by[field, rows]) * edges[0]
        if e == count - 1:
            tile = tile + spread_rows(ay[field, rows]) * edges[1]
        if ex == 0:
            tile = jnp.concatenate([tile[0:1] + bx[field, ys][None], tile[1:]], axis=0)
        if ex == columns - 1:
            tile = jnp.concatenate([tile[:7], tile[7:8] + ax[field, ys][None]], axis=0)
        return tile

    for ex in range(columns):
        for e in range(count):
            rows, ys = pl.ds(8 * ex, 8), pl.ds(8 * e, 8)
            reaction[rows, ys] = complete(4, ex, e)
            free[rows, ys] = boundary[rows, ys].astype(jnp.float32)

    def component(c, carry):
        total = jnp.zeros((8, 128), jnp.float32)
        state = None
        for ex in range(columns):
            rows = pl.ds(8 * ex, 8)
            tiles = []
            for e in range(count):
                ys = pl.ds(8 * e, 8)
                tile = complete(c, ex, e) * free[rows, ys]
                right[c, rows, ys] = tile
                total = total + jnp.sum(tile * tile * share[...], axis=0)
                tiles.append(tile)
            state = stiff_column(ex, tiles, c, summed, edges, stiff_y, stiff_z, raw,
                                 (fx_lo, fx_hi, fy_lo, fy_hi), state)
        dots[pl.ds(c, 1)] = jnp.sum(total, axis=0, keepdims=True)
        return carry

    lax.fori_loop(0, 4, component, 0)


def stiff_terms(tiles, stiff_y, stiff_z):
    x_rows = [along_x(split_rows(t), STIFF) for t in tiles]
    y_parts = [along_y(t, stiff_y) for t in tiles]
    z_all = along_z(jnp.concatenate(tiles, axis=0), stiff_z[...])
    z_parts = [z_all[8 * e : 8 * e + 8] for e in range(len(tiles))]
    return x_rows, y_parts, z_parts


def stiff_column(ex, tiles, c, summed, edges, stiff_y, stiff_z, raw, faces, state):
    x_rows, y_parts, z_parts = stiff_terms(tiles, stiff_y, stiff_z)
    return emit_column(ex, x_rows, y_parts, z_parts, None, summed, edges, raw.at[c],
                       [f.at[c] for f in faces], state)


def next_field(k, c, ex, e, raw, newest, older, reaction, free, received, summed, edges, scale, rate, columns, count):
    rows, ys = pl.ds(8 * ex, 8), pl.ds(8 * e, 8)
    tile = with_faces(raw[c, rows, ys], ex, e, columns, count, [r.at[c] for r in received], summed, edges)
    now = newest[c, rows, ys]
    tile = (scale * tile + (rate * reaction[rows, ys] - 1.0) * now) * free[rows, ys]
    if k > 1:
        tile = 2.0 * tile - older[c, rows, ys]
    return tile, now


def pick(c, values):
    out = jnp.float32(values[0])
    for i in range(1, 4):
        out = jnp.where(c == i, jnp.float32(values[i]), out)
    return out


def grow_basis(k, scales, rates, last, *refs):
    refs = list(refs)
    raw_in, newest = refs[:2]
    older = refs[2] if k > 1 else None
    refs = refs[3:] if k > 1 else refs[2:]
    reaction, free, bx, ax, by, ay, summed, edges, share, stiff_y, stiff_z = refs[:11]
    refs = refs[11:]
    if last:
        local, out, dots, energy = refs
    else:
        out, raw, fx_lo, fx_hi, fy_lo, fy_hi, dots = refs
    columns, count = raw_in.shape[1] // 8, raw_in.shape[2] // 8
    received = (bx, ax, by, ay)
    if last:
        energy[...] = jnp.zeros_like(energy)

    def component(c, carry):
        scale, rate = pick(c, scales), pick(c, rates)
        same = jnp.zeros((8, 128), jnp.float32)
        cross = jnp.zeros((8, 128), jnp.float32)
        work = jnp.zeros((8, 128), jnp.float32)
        state = None
        for ex in range(columns):
            rows = pl.ds(8 * ex, 8)
            tiles = []
            for e in range(count):
                ys = pl.ds(8 * e, 8)
                tile, now = next_field(k, c, ex, e, raw_in, newest, older, reaction, free, received,
                                       summed, edges, scale, rate, columns, count)
                out[c, rows, ys] = tile
                weighted = tile * share[...]
                same = same + jnp.sum(weighted * tile, axis=0)
                cross = cross + jnp.sum(weighted * now, axis=0)
                if last:
                    extra = (rate * reaction[rows, ys] - 1.0) * tile
                    work = work + jnp.sum(weighted * extra, axis=0)
                tiles.append(tile)
            if last:
                x_rows, y_parts, z_parts = stiff_terms(tiles, stiff_y, stiff_z)
                for e in range(count):
                    term = (
                        jnp.stack(x_rows[e]) * local[0] + y_parts[e] * local[1] + z_parts[e] * local[2]
                    )
                    work = work + scale * jnp.sum(term * tiles[e], axis=0)
            else:
                state = stiff_column(ex, tiles, c, summed, edges, stiff_y, stiff_z, raw,
                                     (fx_lo, fx_hi, fy_lo, fy_hi), state)
        dots[pl.ds(c, 1)] = jnp.sum(same, axis=0, keepdims=True)
        dots[pl.ds(c + 4, 1)] = jnp.sum(cross, axis=0, keepdims=True)
        if last:
            energy[pl.ds(c + 4, 1)] = jnp.sum(work, axis=0, keepdims=True)
        return carry

    lax.fori_loop(0, 4, component, 0)


def finish_fields(halves, sums, b0, b1, b2, b3, b4, b5, summed, edges, slope_y, slope_z,
                  fields, raw, fx_lo, fx_hi, fy_lo, fy_hi, weights):
    basis = (b0, b1, b2, b3, b4, b5)
    columns, count = raw.shape[0] // 8, raw.shape[1] // 8
    total = [jnp.broadcast_to(jnp.sum(sums[i], axis=1, keepdims=True), (8, 128)) for i in range(ITERS)]
    other = [pltpu.roll(t, 4, axis=0) for t in total]
    row = lax.broadcasted_iota(jnp.int32, (8, 128), 0)
    half = jnp.full((8, 128), halves[0], jnp.float32)
    for i in range(1, 4):
        half = jnp.where(row == i, halves[i], half)
    moments = [total[0], other[1]]
    for level in range(2, 2 * ITERS - 1):
        inner = total[level // 2] if level % 2 == 0 else other[level // 2 + 1]
        moments.append(2.0 * inner - moments[level % 2])
    top = 2.0 * other[0] - other[5]
    moments.append(2.0 * top - moments[1])
    for i, value in enumerate(conjugate_coefficients(moments, half, half)):
        weights[i] = value

    def combine(c, carry):
        factor = [weights[i, pl.ds(c, 1)] for i in range(ITERS)]
        for x in range(0, 8 * columns, 8):
            rows = pl.ds(x, 8)
            value = basis[0][c, rows] * factor[0][None]
            for i in range(1, ITERS):
                value = value + basis[i][c, rows] * factor[i][None]
            fields[c, rows] = value
        return carry

    lax.fori_loop(0, 4, combine, 0)
    state = None
    for ex in range(columns):
        rows = pl.ds(8 * ex, 8)
        x_rows, y_parts, z_tiles = [], [], []
        for e in range(count):
            ys = pl.ds(8 * e, 8)
            x_rows.append(along_x(split_rows(fields[0, rows, ys]), WEIGHTS[:, None] * DERIVE))
            y_parts.append(along_y(fields[1, rows, ys], slope_y))
            z_tiles.append(fields[2, rows, ys])
        z_all = along_z(jnp.concatenate(z_tiles, axis=0), slope_z[...])
        z_parts = [z_all[8 * e : 8 * e + 8] for e in range(count)]
        state = emit_column(ex, x_rows, y_parts, z_parts, None, summed, edges, raw,
                            (fx_lo, fx_hi, fy_lo, fy_hi), state)


def pressure_step(first, last, keep, gain, *refs):
    refs = list(refs)
    raw_in, free, bx, ax, by, ay, summed, edges, inverse, shift, stiff_y, stiff_z = refs[:12]
    refs = refs[12:]
    if not first:
        remainder_in, update_in, pressure_in = refs[:3]
        refs = refs[3:]
    if last:
        (pressure,) = refs
    else:
        pressure, remainder, update, raw, fx_lo, fx_hi, fy_lo, fy_hi = refs
    columns, count = raw_in.shape[0] // 8, raw_in.shape[1] // 8
    state = None
    for ex in range(columns):
        rows = pl.ds(8 * ex, 8)
        tiles = []
        for e in range(count):
            ys = pl.ds(8 * e, 8)
            tile = with_faces(raw_in[rows, ys], ex, e, columns, count, (bx, ax, by, ay), summed, edges)
            tile = tile * free[rows, ys]
            left = -tile if first else remainder_in[rows, ys] - tile
            change = gain * inverse[...] * left
            if first:
                total = change
            else:
                change = change + keep * update_in[rows, ys]
                total = pressure_in[rows, ys] + change
            pressure[rows, ys] = total
            if not last:
                remainder[rows, ys] = left
                update[rows, ys] = change
            tiles.append(change)
        if not last:
            x_rows, y_parts, z_parts = stiff_terms(tiles, stiff_y, stiff_z)
            extra = [shift[...] * t for t in tiles]
            state = emit_column(ex, x_rows, y_parts, z_parts, extra, summed, edges, raw,
                                (fx_lo, fx_hi, fy_lo, fy_hi), state)


VMEM_BYTES = 24 * 1024 * 1024


def call(kernel, name, outs, *args, scratch=()):
    held = pl.BlockSpec(memory_space=pltpu.VMEM)
    return pl.pallas_call(
        kernel,
        name=name,
        out_shape=[OUT(s) for s in outs],
        in_specs=[held] * len(args),
        out_specs=[held] * len(outs),
        scratch_shapes=list(scratch),
        compiler_params=pltpu.CompilerParams(vmem_limit_bytes=VMEM_BYTES),
    )(*[IN(a) for a in args])


def OUT(shape):
    return jax.ShapeDtypeStruct(shape, jnp.float32)


def IN(a):
    return a


def neighbours(axis):
    size = lax.axis_size(axis)
    up = [(i, (i + 1) % size) for i in range(size)]
    return up, [(j, i) for i, j in up]


def swap_faces(axis, low, high):
    up, down = neighbours(axis)
    return lax.ppermute(high, axis, up), lax.ppermute(low, axis, down)


def swap_all(fx_lo, fx_hi, fy_lo, fy_hi):
    by, ay = swap_faces("gy", fy_lo, fy_hi)
    bx, ax = swap_faces("gx", fx_lo, fx_hi)
    return bx, ax, by, ay


def all_sum(values, axis):
    size = lax.axis_size(axis)
    if size & (size - 1):
        return lax.psum(values, axis)
    bit = 1

    def swapped(mask):
        return lax.ppermute(values, axis, [(i, i ^ mask) for i in range(size)])

    while bit < size:
        if 2 * bit < size:
            one, two, three = swapped(bit), swapped(2 * bit), swapped(3 * bit)
            values = (values + one) + (two + three)
            bit *= 4
        else:
            values = values + swapped(bit)
            bit *= 2
    return values


def conjugate_coefficients(moments, centre, half):
    remaining, towards = list(moments), list(moments)
    one, zero = jnp.ones_like(moments[0]), jnp.zeros_like(moments[0])
    direction = [one] + [zero] * ITERS
    residual = list(direction)
    total = [zero] * ITERS
    for step in range(ITERS):
        count = len(towards) - 1
        image = []
        for level in range(count):
            side = (
                half * towards[1] if level == 0 else 0.5 * half * (towards[level + 1] + towards[level - 1])
            )
            image.append(centre * towards[level] + side)
        alpha = remaining[step] / image[step]
        total = [total[i] + alpha * direction[i] for i in range(ITERS)]
        if step == ITERS - 1:
            break
        applied = []
        for i in range(ITERS + 1):
            term = centre * direction[i]
            if i >= 1:
                term = term + (half if i == 1 else 0.5 * half) * direction[i - 1]
            if i < ITERS:
                term = term + 0.5 * half * direction[i + 1]
            applied.append(term)
        residual = [residual[i] - alpha * applied[i] for i in range(ITERS + 1)]
        following = [remaining[i] - alpha * image[i] for i in range(count)]
        beta = -alpha * (half if step == 0 else 0.5 * half) * following[step + 1] / remaining[step]
        towards = [following[i] + beta * towards[i] for i in range(count)]
        direction = [residual[i] + beta * direction[i] for i in range(ITERS + 1)]
        remaining = following
    return total


def on_device(old_fields, inverse_step, boundary):
    x, y, z = inverse_step.shape
    t = Tables(z)
    brick, four = (x, y, z), (4, x, y, z)
    faces = [(y, z)] * 2 + [(x, z)] * 2
    faces4 = [(4,) + f for f in faces]
    faces5 = [(5,) + f for f in faces]

    local, fx_lo, fx_hi, fy_lo, fy_hi = call(
        load_local, "local_right", [(5,) + brick] + faces5, old_fields, inverse_step, boundary, t.mass, t.edges
    )
    bx, ax = swap_faces("gx", fx_lo, fx_hi)
    fy_lo, fy_hi = call(fix_corners, "corners", faces5[2:], fy_lo, fy_hi, bx, ax)
    by, ay = swap_faces("gy", fy_lo, fy_hi)

    top = np.array([spectrum_top(c) for c in DIFFUSE])
    halves = [float(v) for v in 0.5 * top]
    scales = [float(v) for v in np.array(DIFFUSE) / (0.5 * top)]
    rates = [float(v) for v in 1.0 / (0.5 * top)]

    right, reaction, free, raw, *sent, dots = call(
        start_basis, "basis_start", [four, brick, brick, four] + faces4 + [(8, 128)],
        local, boundary, bx, ax, by, ay, t.summed, t.edges, t.share, t.stiff_y, t.stiff_z,
    )
    basis, sums = [right], [dots]
    for k in range(1, ITERS):
        last = k == ITERS - 1
        received = swap_all(*sent)
        args = [raw, basis[-1]] + ([basis[-2]] if k > 1 else [])
        args += [reaction, free, *received, t.summed, t.edges, t.share, t.stiff_y]
        kernel = functools.partial(grow_basis, k, scales, rates, last)
        if last:
            field, dots, energy = call(
                kernel, "basis_last", [four, (8, 128), (8, 128)], *args, t.plain_z, t.local
            )
            sums[0] = sums[0] + energy
        else:
            field, raw, *sent, dots = call(
                kernel, "basis_grow", [four, four] + faces4 + [(8, 128)], *args, t.stiff_z
            )
        basis.append(field)
        sums.append(dots)
    sums = all_sum(all_sum(jnp.stack(sums), "gx"), "gy")

    fields, raw, *sent = call(
        functools.partial(finish_fields, halves), "fields", [four, brick] + faces,
        sums, *basis, t.summed, t.edges, t.slope_y, t.slope_z,
        scratch=[pltpu.VMEM((ITERS, 8, 128), jnp.float32)],
    )

    centre, half = chebyshev_bounds()
    factor = centre / half
    damping = 1.0 / factor
    keep, gain = 0.0, 1.0 / centre
    state = []
    for step in range(CHEB):
        first, last = step == 0, step == CHEB - 1
        received = swap_all(*sent)
        args = [raw, free, *received, t.summed, t.edges, t.inverse, t.shift, t.stiff_y, t.stiff_z] + state
        kernel = functools.partial(pressure_step, first, last, keep, gain)
        if last:
            (pressure,) = call(kernel, "pressure_last", [brick], *args)
            break
        pressure, remainder, update, raw, *sent = call(
            kernel, "pressure_step", [brick] * 4 + faces, *args
        )
        state = [remainder, update, pressure]
        following = 1.0 / (2.0 * factor - damping)
        keep, gain = following * damping, 2.0 * following / half
        damping = following
    return (fields, pressure)


def solution(mesh):
    return jax.shard_map(
        on_device,
        mesh=mesh,
        in_specs=(P(None, "gx", "gy", None), P("gx", "gy", None), P("gx", "gy", None)),
        out_specs=(P(None, "gx", "gy", None), P("gx", "gy", None)),
        check_vma=False,
    )
```

```python
import functools

import jax
import jax.numpy as jnp
import numpy as np
from jax import lax
from jax.experimental import pallas as pl
from jax.experimental.pallas import tpu as pltpu
from jax.sharding import PartitionSpec as P

ITERS = 6
CHEB = 6

SIGMA_SHIFT = 0.5
DIFFUSE = (1.0, 1.0, 1.0, 1.4)
COUPLING = 1.0
STRATIFY = 1.0
SPREAD = 20.0
STEP_MAX = 64.0
INTERVAL_SHARE = 0.82
HIGHEST_PRECISION = lax.Precision.HIGHEST
LOBATTO_POINTS = (
    -1.0,
    -0.8717401485096066,
    -0.5917001814331423,
    -0.2092992179024789,
    0.2092992179024789,
    0.5917001814331423,
    0.8717401485096066,
    1.0,
)


def legendre_value(points, degree):
    previous = points * 0.0 + 1.0
    current = points
    for order in range(1, degree):
        following = ((2 * order + 1) * points * current - order * previous) / (order + 1)
        previous = current
        current = following
    return current


def quadrature_tables():
    degree = 7
    points = np.array(LOBATTO_POINTS)
    values = legendre_value(points, degree)
    weights = 2.0 / (degree * (degree + 1) * values * values)
    derive = np.zeros((degree + 1, degree + 1))
    for row_index in range(degree + 1):
        for column_index in range(degree + 1):
            if row_index != column_index:
                derive[row_index, column_index] = values[row_index] / (
                    values[column_index] * (points[row_index] - points[column_index])
                )
    derive[0, 0] = -degree * (degree + 1) / 4.0
    derive[degree, degree] = degree * (degree + 1) / 4.0
    stiffness_table = derive.T @ (weights[:, None] * derive)
    return (weights, derive, stiffness_table)


WEIGHTS, DERIVE, STIFF = quadrature_tables()
COPIES = np.where(np.arange(8) % 7 == 0, 2.0, 1.0)


def chebyshev_bounds():
    weight_matrix = np.eye(8) * WEIGHTS

    def kron3(a, b, c):
        return np.kron(np.kron(a, b), c)

    element_matrix = (
        kron3(STIFF, weight_matrix, weight_matrix)
        + kron3(weight_matrix, STIFF, weight_matrix)
        + kron3(weight_matrix, weight_matrix, STIFF)
        + SIGMA_SHIFT * kron3(weight_matrix, weight_matrix, weight_matrix)
    )
    bounds_ratio = np.sum(np.abs(element_matrix), axis=1) / np.diagonal(element_matrix)
    upper_bound = float(np.max(bounds_ratio))
    lower_bound = upper_bound / SPREAD
    return ((upper_bound + lower_bound) / 2.0, (upper_bound - lower_bound) / 2.0)


def spectrum_top(diffuse):
    root = np.sqrt(COPIES)
    stiff = root[:, None] * STIFF * root[None, :]
    weight = np.diag(WEIGHTS * COPIES)

    def kron3(a, b, c):
        return np.kron(np.kron(a, b), c)

    element = diffuse * (
        kron3(stiff, weight, weight) + kron3(weight, stiff, weight) + kron3(weight, weight, stiff)
    ) + STEP_MAX * kron3(weight, weight, weight)
    return float(np.linalg.eigvalsh(element)[-1])


def line_sums(table, length):
    matrix = np.kron(np.eye(length // 8), table)
    total = matrix.copy()
    for start in range(8, length, 8):
        total[start] += matrix[start - 1]
        total[start - 1] += matrix[start]
    return total


def depth_line(vector, length):
    line = np.tile(vector * COPIES, length // 8)
    line[0] = vector[0]
    line[-1] = vector[-1]
    return line


def f32(array):
    return np.ascontiguousarray(array, np.float32)


def rolled_rows(table):
    out = np.zeros((8, 8, 128))
    for shift in range(8):
        for row in range(8):
            out[shift, row] = table[row, (row - shift) % 8]
    return out


def block(a, b, c):
    return a[:, None, None] * b[:, None] * c


class Tables:
    def __init__(self, depth):
        ones8, ones = np.ones(8), np.ones(depth)
        wide = WEIGHTS * COPIES
        deep = depth_line(WEIGHTS, depth)
        flat = np.tile(WEIGHTS, depth // 8)
        stiff = np.diagonal(STIFF)
        wide_s, deep_s = stiff * COPIES, depth_line(stiff, depth)
        share = 1.0 / COPIES
        share_z = np.tile(share, depth // 8)
        share_z[0] = share_z[-1] = 1.0
        self.summed = f32(
            np.stack([block(ones8, wide, deep), block(wide, ones8, deep), block(wide, wide, ones)])
        )
        self.local = f32(
            np.stack(
                [block(ones8, WEIGHTS, flat), block(WEIGHTS, ones8, flat), block(WEIGHTS, WEIGHTS, ones)]
            )
        )
        self.share = f32(block(share, share, share_z))
        diagonal = (
            block(wide_s, wide, deep)
            + block(wide, wide_s, deep)
            + block(wide, wide, deep_s)
            + SIGMA_SHIFT * block(wide, wide, deep)
        )
        self.inverse = f32(1.0 / diagonal)
        self.shift = f32(SIGMA_SHIFT * block(wide, wide, deep))
        self.stiff_y = f32(rolled_rows(STIFF))
        self.slope_y = f32(rolled_rows(WEIGHTS[:, None] * DERIVE))
        self.stiff_z = f32(line_sums(STIFF, depth).T)
        self.plain_z = f32(np.kron(np.eye(depth // 8), STIFF).T)
        self.slope_z = f32(line_sums(WEIGHTS[:, None] * DERIVE, depth).T)


def row_marks():
    row = lax.broadcasted_iota(jnp.int32, (8, 128), 0)
    return jnp.where(row == 0, 1.0, 0.0), jnp.where(row == 7, 1.0, 0.0)


def by_place(vector, place):
    out = jnp.full(place.shape, float(vector[0]), jnp.float32)
    for i in range(1, 8):
        out = jnp.where(place == i, float(vector[i]), out)
    return out


def along_x(rows, table):
    if np.allclose(table, table[::-1, ::-1]):
        even = 0.5 * (table[:4, :4] + table[:4, :3:-1])
        odd = 0.5 * (table[:4, :4] - table[:4, :3:-1])
        plus = [rows[i] + rows[7 - i] for i in range(4)]
        minus = [rows[i] - rows[7 - i] for i in range(4)]
        out = [None] * 8
        for a in range(4):
            p = sum(float(even[a, b]) * plus[b] for b in range(4))
            m = sum(float(odd[a, b]) * minus[b] for b in range(4))
            out[a], out[7 - a] = p + m, p - m
        return out
    return [sum(float(table[a, b]) * rows[b] for b in range(8)) for a in range(8)]


def along_y(tiles, factors):
    total = factors[0] * tiles
    for shift in range(1, 8):
        total = total + factors[shift] * pltpu.roll(tiles, shift, axis=1)
    return total


def along_z(tiles, matrix):
    x, y, z = tiles.shape
    out = jnp.dot(
        tiles.reshape(x * y, z), matrix, precision=HIGHEST_PRECISION, preferred_element_type=jnp.float32
    )
    return out.reshape(x, y, z)


def join_y(parts, low, high):
    out = list(parts)
    for e in range(1, len(parts)):
        out[e - 1] = out[e - 1] + high * pltpu.roll(parts[e], 7, axis=1)
        out[e] = out[e] + low * pltpu.roll(parts[e - 1], 1, axis=1)
    return out


def spread_rows(rows):
    return jnp.broadcast_to(rows[:, None, :], (rows.shape[0], 8, rows.shape[1]))


def column_sums(x_rows, y_parts, z_parts, summed, edges):
    y_parts = join_y(y_parts, edges[0], edges[1])
    return [
        jnp.stack(kx) * summed[0, 0] + ky * summed[1] + kz * summed[2]
        for kx, ky, kz in zip(x_rows, y_parts, z_parts)
    ]


def emit_column(ex, x_rows, y_parts, z_parts, extra, summed, edges, even, raw, faces, state):
    count = len(x_rows)
    x_near, x_far, y_near, y_far = faces
    columns = raw.shape[0] // 8
    rows = pl.ds(8 * ex, 8)
    parts = column_sums(x_rows, y_parts, z_parts, summed, edges)
    low, high = y_parts[0][:, 0], y_parts[-1][:, 7]
    y_near[rows] = jnp.where(even[1], high, low)
    y_far[rows] = jnp.where(even[1], low, high)
    for e in range(count):
        ys = pl.ds(8 * e, 8)
        part = parts[e] if extra is None else parts[e] + extra[e]
        raw[rows, ys] = part
        if ex:
            raw[8 * ex, ys] += state[e] * summed[0, 0]
            raw[8 * ex - 1, ys] += x_rows[e][0] * summed[0, 0]
        else:
            x_near[ys] = x_rows[e][0]
            x_far[ys] = x_rows[e][0]
        if ex == columns - 1:
            x_near[ys] = jnp.where(even[0], x_rows[e][7], x_near[ys])
            x_far[ys] = jnp.where(even[0], x_far[ys], x_rows[e][7])
    return [r[7] for r in x_rows]


def parity(even_ref):
    return even_ref[0] > 0.5, even_ref[1] > 0.5


def before_of(even, near, far):
    return jnp.where(even, far, near)


def after_of(even, near, far):
    return jnp.where(even, near, far)


def with_faces(tile, ex, e, columns, count, received, even, edges, weight_x=None, weight_y=None):
    x_near, x_far, y_near, y_far = received
    rows, ys = pl.ds(8 * ex, 8), pl.ds(8 * e, 8)

    def weighted(face, weight):
        return face if weight is None else face * weight

    if e == 0:
        face = before_of(even[1], y_near[rows], y_far[rows])
        tile = tile + spread_rows(face) * weighted(edges[0], weight_y)
    if e == count - 1:
        face = after_of(even[1], y_near[rows], y_far[rows])
        tile = tile + spread_rows(face) * weighted(edges[1], weight_y)
    if ex == 0:
        face = before_of(even[0], x_near[ys], x_far[ys])
        tile = jnp.concatenate([tile[0:1] + weighted(face, weight_x)[None], tile[1:]], axis=0)
    if ex == columns - 1:
        face = after_of(even[0], x_near[ys], x_far[ys])
        tile = jnp.concatenate([tile[:7], tile[7:8] + weighted(face, weight_x)[None]], axis=0)
    return tile


def split_rows(block_rows):
    return [block_rows[i] for i in range(8)]


def load_local(old, step, even_ref, out, x_near, x_far, y_near, y_far):
    columns, count, depth = out.shape[1] // 8, out.shape[2] // 8, out.shape[3]
    even, edges = parity(even_ref), row_marks()
    row = lax.broadcasted_iota(jnp.int32, (8, depth), 0)
    lane = lax.broadcasted_iota(jnp.int32, (8, depth), 1)
    place = lane & 7
    after = jnp.where((place == 0) & (lane > 0), 1.0, 0.0)
    before_z = jnp.where((place == 7) & (lane < depth - 1), 1.0, 0.0)
    plane = by_place(WEIGHTS, row) * by_place(WEIGHTS, place)
    mass = jnp.stack([float(w) * plane for w in WEIGHTS])
    for field in range(5):
        before = [None] * count
        for ex in range(columns):
            rows = pl.ds(8 * ex, 8)
            parts = []
            for e in range(count):
                ys = pl.ds(8 * e, 8)
                value = step[rows, ys]
                if field < 4:
                    value = value * old[field, rows, ys]
                if field == 2:
                    value = value + COUPLING * old[3, rows, ys]
                if field == 3:
                    value = value - STRATIFY * old[2, rows, ys]
                value = value * mass
                value = (
                    value
                    + after * pltpu.roll(value, 1, axis=2)
                    + before_z * pltpu.roll(value, depth - 1, axis=2)
                )
                parts.append(value)
            parts = join_y(parts, edges[0], edges[1])
            for e in range(count):
                ys = pl.ds(8 * e, 8)
                out[field, rows, ys] = parts[e]
                if ex:
                    out[field, 8 * ex, ys] += before[e]
                    out[field, 8 * ex - 1, ys] += parts[e][0]
                before[e] = parts[e][7]
        for e in range(count):
            ys = pl.ds(8 * e, 8)
            low, high = out[field, 0, ys], out[field, 8 * columns - 1, ys]
            x_near[field, ys] = jnp.where(even[0], high, low)
            x_far[field, ys] = jnp.where(even[0], low, high)
        for ex in range(columns):
            rows = pl.ds(8 * ex, 8)
            low = out[field, rows, pl.ds(0, 8)][:, 0]
            high = out[field, rows, pl.ds(8 * count - 8, 8)][:, 7]
            y_near[field, rows] = jnp.where(even[1], high, low)
            y_far[field, rows] = jnp.where(even[1], low, high)


def fix_corners(y_near, y_far, x_near, x_far, even_ref, near, far):
    length = y_near.shape[1]
    last = x_near.shape[1] - 1
    even = [even_ref[0, 0:1] > 0.5, even_ref[1, 0:1] > 0.5]
    near[...] = y_near[...]
    far[...] = y_far[...]
    for field in range(5):
        for end, place in ((before_of, 0), (after_of, length - 1)):
            first = end(even[0], x_near[field, 0:1], x_far[field, 0:1])
            final = end(even[0], x_near[field, last : last + 1], x_far[field, last : last + 1])
            near[field, place : place + 1] += jnp.where(even[1], final, first)
            far[field, place : place + 1] += jnp.where(even[1], first, final)


def start_basis(local, boundary, x_near, x_far, y_near, y_far, even_ref, summed, share, stiff_y, stiff_z,
                right, reaction, free, raw, fx_near, fx_far, fy_near, fy_far, dots):
    columns, count = raw.shape[1] // 8, raw.shape[2] // 8
    dots[...] = jnp.zeros_like(dots)

    even, edges = parity(even_ref), row_marks()
    received = (x_near, x_far, y_near, y_far)

    def complete(field, ex, e):
        rows, ys = pl.ds(8 * ex, 8), pl.ds(8 * e, 8)
        return with_faces(local[field, rows, ys], ex, e, columns, count, [r.at[field] for r in received],
                          even, edges)

    for ex in range(columns):
        for e in range(count):
            rows, ys = pl.ds(8 * ex, 8), pl.ds(8 * e, 8)
            reaction[rows, ys] = complete(4, ex, e)
            free[rows, ys] = boundary[rows, ys].astype(jnp.float32)

    def component(c, carry):
        total = jnp.zeros((8, 128), jnp.float32)
        state = None
        for ex in range(columns):
            rows = pl.ds(8 * ex, 8)
            tiles = []
            for e in range(count):
                ys = pl.ds(8 * e, 8)
                tile = complete(c, ex, e) * free[rows, ys]
                right[c, rows, ys] = tile
                total = total + jnp.sum(tile * tile * share[...], axis=0)
                tiles.append(tile)
            state = stiff_column(ex, tiles, c, summed, edges, even, stiff_y, stiff_z, raw,
                                 (fx_near, fx_far, fy_near, fy_far), state)
        dots[pl.ds(c, 1)] = jnp.sum(total, axis=0, keepdims=True)
        return carry

    lax.fori_loop(0, 4, component, 0)


def stiff_terms(tiles, stiff_y, stiff_z):
    x_rows = [along_x(split_rows(t), STIFF) for t in tiles]
    y_parts = [along_y(t, stiff_y) for t in tiles]
    z_all = along_z(jnp.concatenate(tiles, axis=0), stiff_z[...])
    z_parts = [z_all[8 * e : 8 * e + 8] for e in range(len(tiles))]
    return x_rows, y_parts, z_parts


def stiff_column(ex, tiles, c, summed, edges, even, stiff_y, stiff_z, raw, faces, state):
    x_rows, y_parts, z_parts = stiff_terms(tiles, stiff_y, stiff_z)
    return emit_column(ex, x_rows, y_parts, z_parts, None, summed, edges, even, raw.at[c],
                       [f.at[c] for f in faces], state)


def next_field(k, c, ex, e, raw, newest, older, reaction, free, received, summed, edges, even, scale, rate, columns, count):
    rows, ys = pl.ds(8 * ex, 8), pl.ds(8 * e, 8)
    tile = with_faces(raw[c, rows, ys], ex, e, columns, count, [r.at[c] for r in received],
                      even, edges, summed[0, 0], summed[1])
    now = newest[c, rows, ys]
    tile = (scale * tile + (rate * reaction[rows, ys] - 1.0) * now) * free[rows, ys]
    if k > 1:
        tile = 2.0 * tile - older[c, rows, ys]
    return tile, now


def pick(c, values):
    out = jnp.float32(values[0])
    for i in range(1, 4):
        out = jnp.where(c == i, jnp.float32(values[i]), out)
    return out


def grow_basis(k, scales, rates, last, *refs):
    refs = list(refs)
    raw_in, newest = refs[:2]
    older = refs[2] if k > 1 else None
    refs = refs[3:] if k > 1 else refs[2:]
    reaction, free, *received, even_ref, summed, share, stiff_y, stiff_z = refs[:11]
    refs = refs[11:]
    even, edges = parity(even_ref), row_marks()
    if last:
        local, out, dots, energy = refs
    else:
        out, raw, *faces, dots = refs
    columns, count = raw_in.shape[1] // 8, raw_in.shape[2] // 8
    if last:
        energy[...] = jnp.zeros_like(energy)

    def component(c, carry):
        scale, rate = pick(c, scales), pick(c, rates)
        same = jnp.zeros((8, 128), jnp.float32)
        cross = jnp.zeros((8, 128), jnp.float32)
        work = jnp.zeros((8, 128), jnp.float32)
        state = None
        for ex in range(columns):
            rows = pl.ds(8 * ex, 8)
            tiles = []
            for e in range(count):
                ys = pl.ds(8 * e, 8)
                tile, now = next_field(k, c, ex, e, raw_in, newest, older, reaction, free, received,
                                       summed, edges, even, scale, rate, columns, count)
                out[c, rows, ys] = tile
                weighted = tile * share[...]
                same = same + jnp.sum(weighted * tile, axis=0)
                cross = cross + jnp.sum(weighted * now, axis=0)
                if last:
                    extra = (rate * reaction[rows, ys] - 1.0) * tile
                    work = work + jnp.sum(weighted * extra, axis=0)
                tiles.append(tile)
            if last:
                x_rows, y_parts, z_parts = stiff_terms(tiles, stiff_y, stiff_z)
                for e in range(count):
                    term = (
                        jnp.stack(x_rows[e]) * local[0] + y_parts[e] * local[1] + z_parts[e] * local[2]
                    )
                    work = work + scale * jnp.sum(term * tiles[e], axis=0)
            else:
                state = stiff_column(ex, tiles, c, summed, edges, even, stiff_y, stiff_z, raw, faces, state)
        dots[pl.ds(c, 1)] = jnp.sum(same, axis=0, keepdims=True)
        dots[pl.ds(c + 4, 1)] = jnp.sum(cross, axis=0, keepdims=True)
        if last:
            energy[pl.ds(c + 4, 1)] = jnp.sum(work, axis=0, keepdims=True)
        return carry

    lax.fori_loop(0, 4, component, 0)


def finish_fields(halves, sums, b0, b1, b2, b3, b4, b5, even_ref, summed, slope_y, slope_z,
                  fields, raw, x_near, x_far, y_near, y_far, weights):
    basis = (b0, b1, b2, b3, b4, b5)
    even, edges = parity(even_ref), row_marks()
    columns, count = raw.shape[0] // 8, raw.shape[1] // 8
    total = [jnp.broadcast_to(jnp.sum(sums[i], axis=1, keepdims=True), (8, 128)) for i in range(ITERS)]
    other = [pltpu.roll(t, 4, axis=0) for t in total]
    row = lax.broadcasted_iota(jnp.int32, (8, 128), 0)
    half = jnp.full((8, 128), halves[0], jnp.float32)
    for i in range(1, 4):
        half = jnp.where(row == i, halves[i], half)
    moments = [total[0], other[1]]
    for level in range(2, 2 * ITERS - 1):
        inner = total[level // 2] if level % 2 == 0 else other[level // 2 + 1]
        moments.append(2.0 * inner - moments[level % 2])
    top = 2.0 * other[0] - other[5]
    moments.append(2.0 * top - moments[1])
    for i, value in enumerate(conjugate_coefficients(moments, half, half)):
        weights[i] = value

    def combine(c, carry):
        factor = [weights[i, pl.ds(c, 1)] for i in range(ITERS)]
        for x in range(0, 8 * columns, 8):
            rows = pl.ds(x, 8)
            value = basis[0][c, rows] * factor[0][None]
            for i in range(1, ITERS):
                value = value + basis[i][c, rows] * factor[i][None]
            fields[c, rows] = value
        return carry

    lax.fori_loop(0, 4, combine, 0)
    state = None
    for ex in range(columns):
        rows = pl.ds(8 * ex, 8)
        x_rows, y_parts, z_tiles = [], [], []
        for e in range(count):
            ys = pl.ds(8 * e, 8)
            x_rows.append(along_x(split_rows(fields[0, rows, ys]), WEIGHTS[:, None] * DERIVE))
            y_parts.append(along_y(fields[1, rows, ys], slope_y))
            z_tiles.append(fields[2, rows, ys])
        z_all = along_z(jnp.concatenate(z_tiles, axis=0), slope_z[...])
        z_parts = [z_all[8 * e : 8 * e + 8] for e in range(count)]
        state = emit_column(ex, x_rows, y_parts, z_parts, None, summed, edges, even, raw,
                            (x_near, x_far, y_near, y_far), state)


def pressure_step(first, last, keep, gain, *refs):
    refs = list(refs)
    raw_in, free, *received, even_ref, summed, inverse, shift, stiff_y, stiff_z = refs[:12]
    refs = refs[12:]
    even, edges = parity(even_ref), row_marks()
    if not first:
        remainder_in, update_in, pressure_in = refs[:3]
        refs = refs[3:]
    if last:
        (pressure,) = refs
    else:
        pressure, remainder, update, raw, *faces = refs
    columns, count = raw_in.shape[0] // 8, raw_in.shape[1] // 8
    state = None
    for ex in range(columns):
        rows = pl.ds(8 * ex, 8)
        tiles = []
        for e in range(count):
            ys = pl.ds(8 * e, 8)
            tile = with_faces(raw_in[rows, ys], ex, e, columns, count, received, even, edges,
                              summed[0, 0], summed[1])
            tile = tile * free[rows, ys]
            left = -tile if first else remainder_in[rows, ys] - tile
            change = gain * inverse[...] * left
            if first:
                total = change
            else:
                change = change + keep * update_in[rows, ys]
                total = pressure_in[rows, ys] + change
            pressure[rows, ys] = total
            if not last:
                remainder[rows, ys] = left
                update[rows, ys] = change
            tiles.append(change)
        if not last:
            x_rows, y_parts, z_parts = stiff_terms(tiles, stiff_y, stiff_z)
            extra = [shift[...] * t for t in tiles]
            state = emit_column(ex, x_rows, y_parts, z_parts, extra, summed, edges, even, raw, faces, state)


VMEM_BYTES = 24 * 1024 * 1024


def call(kernel, name, outs, *args, scratch=()):
    held = pl.BlockSpec(memory_space=pltpu.VMEM)
    return pl.pallas_call(
        kernel,
        name=name,
        out_shape=[OUT(s) for s in outs],
        in_specs=[held] * len(args),
        out_specs=[held] * len(outs),
        scratch_shapes=list(scratch),
        compiler_params=pltpu.CompilerParams(vmem_limit_bytes=VMEM_BYTES),
    )(*[IN(a) for a in args])


def OUT(shape):
    return jax.ShapeDtypeStruct(shape, jnp.float32)


def IN(a):
    return a


def swap_near(axis, face):
    return lax.ppermute(face, axis, [(i, i ^ 1) for i in range(lax.axis_size(axis))])


def swap_far(axis, face):
    size = lax.axis_size(axis)
    return lax.ppermute(face, axis, [(i, (i + 1 if i % 2 else i - 1) % size) for i in range(size)])


def swap_all(x_near, x_far, y_near, y_far):
    y_far = swap_far("gy", y_far)
    x_far = swap_far("gx", x_far)
    x_near = swap_near("gx", x_near)
    y_near = swap_near("gy", y_near)
    return x_near, x_far, y_near, y_far


def all_sum(values, axis):
    size = lax.axis_size(axis)
    if size & (size - 1):
        return lax.psum(values, axis)
    bit = 1
    while bit < size:
        values = values + lax.ppermute(values, axis, [(i, i ^ bit) for i in range(size)])
        bit *= 2
    return values


def conjugate_coefficients(moments, centre, half):
    remaining, towards = list(moments), list(moments)
    one, zero = jnp.ones_like(moments[0]), jnp.zeros_like(moments[0])
    direction = [one] + [zero] * ITERS
    residual = list(direction)
    total = [zero] * ITERS
    for step in range(ITERS):
        count = len(towards) - 1
        image = []
        for level in range(count):
            side = (
                half * towards[1] if level == 0 else 0.5 * half * (towards[level + 1] + towards[level - 1])
            )
            image.append(centre * towards[level] + side)
        alpha = remaining[step] / image[step]
        total = [total[i] + alpha * direction[i] for i in range(ITERS)]
        if step == ITERS - 1:
            break
        applied = []
        for i in range(ITERS + 1):
            term = centre * direction[i]
            if i >= 1:
                term = term + (half if i == 1 else 0.5 * half) * direction[i - 1]
            if i < ITERS:
                term = term + 0.5 * half * direction[i + 1]
            applied.append(term)
        residual = [residual[i] - alpha * applied[i] for i in range(ITERS + 1)]
        following = [remaining[i] - alpha * image[i] for i in range(count)]
        beta = -alpha * (half if step == 0 else 0.5 * half) * following[step + 1] / remaining[step]
        towards = [following[i] + beta * towards[i] for i in range(count)]
        direction = [residual[i] + beta * direction[i] for i in range(ITERS + 1)]
        remaining = following
    return total


def on_device(old_fields, inverse_step, boundary):
    x, y, z = inverse_step.shape
    t = Tables(z)
    brick, four = (x, y, z), (4, x, y, z)
    faces = [(y, z)] * 2 + [(x, z)] * 2
    faces4 = [(4,) + f for f in faces]
    faces5 = [(5,) + f for f in faces]

    place = [lax.axis_index(a) % 2 == 0 for a in ("gx", "gy")]
    even = jnp.stack([jnp.full((8, 128), p, jnp.float32) for p in place])

    local, x_near, x_far, y_near, y_far = call(
        load_local, "local_right", [(5,) + brick] + faces5, old_fields, inverse_step, even
    )
    x_far = swap_far("gx", x_far)
    x_near = swap_near("gx", x_near)
    y_near, y_far = call(fix_corners, "corners", faces5[2:], y_near, y_far, x_near, x_far, even)
    y_far = swap_far("gy", y_far)
    y_near = swap_near("gy", y_near)

    top = INTERVAL_SHARE * np.array([spectrum_top(c) for c in DIFFUSE])
    halves = [float(v) for v in 0.5 * top]
    scales = [float(v) for v in np.array(DIFFUSE) / (0.5 * top)]
    rates = [float(v) for v in 1.0 / (0.5 * top)]

    right, reaction, free, raw, *sent, dots = call(
        start_basis, "basis_start", [four, brick, brick, four] + faces4 + [(8, 128)],
        local, boundary, x_near, x_far, y_near, y_far, even, t.summed, t.share, t.stiff_y, t.stiff_z,
    )
    basis, sums = [right], [dots]
    for k in range(1, ITERS):
        last = k == ITERS - 1
        received = swap_all(*sent)
        args = [raw, basis[-1]] + ([basis[-2]] if k > 1 else [])
        args += [reaction, free, *received, even, t.summed, t.share, t.stiff_y]
        kernel = functools.partial(grow_basis, k, scales, rates, last)
        if last:
            field, dots, energy = call(
                kernel, "basis_last", [four, (8, 128), (8, 128)], *args, t.plain_z, t.local
            )
            sums[0] = sums[0] + energy
        else:
            field, raw, *sent, dots = call(
                kernel, "basis_grow", [four, four] + faces4 + [(8, 128)], *args, t.stiff_z
            )
        basis.append(field)
        sums.append(dots)
    sums = all_sum(all_sum(jnp.stack(sums), "gx"), "gy")

    fields, raw, *sent = call(
        functools.partial(finish_fields, halves), "fields", [four, brick] + faces,
        sums, *basis, even, t.summed, t.slope_y, t.slope_z,
        scratch=[pltpu.VMEM((ITERS, 8, 128), jnp.float32)],
    )

    centre, half = chebyshev_bounds()
    factor = centre / half
    damping = 1.0 / factor
    keep, gain = 0.0, 1.0 / centre
    state = []
    for step in range(CHEB):
        first, last = step == 0, step == CHEB - 1
        received = swap_all(*sent)
        args = [raw, free, *received, even, t.summed, t.inverse, t.shift, t.stiff_y, t.stiff_z] + state
        kernel = functools.partial(pressure_step, first, last, keep, gain)
        if last:
            (pressure,) = call(kernel, "pressure_last", [brick], *args)
            break
        pressure, remainder, update, raw, *sent = call(
            kernel, "pressure_step", [brick] * 4 + faces, *args
        )
        state = [remainder, update, pressure]
        following = 1.0 / (2.0 * factor - damping)
        keep, gain = following * damping, 2.0 * following / half
        damping = following
    return (fields, pressure)


def solution(mesh):
    return jax.shard_map(
        on_device,
        mesh=mesh,
        in_specs=(P(None, "gx", "gy", None), P("gx", "gy", None), P("gx", "gy", None)),
        out_specs=(P(None, "gx", "gy", None), P("gx", "gy", None)),
        check_vma=False,
    )
```

```python
import functools

import jax
import jax.numpy as jnp
import numpy as np
from jax import lax
from jax.experimental import pallas as pl
from jax.experimental.pallas import tpu as pltpu
from jax.sharding import PartitionSpec as P

ITERS = 6
CHEB = 6

SIGMA_SHIFT = 0.5
DIFFUSE = (1.0, 1.0, 1.0, 1.4)
COUPLING = 1.0
STRATIFY = 1.0
SPREAD = 20.0
STEP_MAX = 64.0
INTERVAL_SHARE = 0.82
HIGHEST_PRECISION = lax.Precision.HIGHEST
LOBATTO_POINTS = (
    -1.0,
    -0.8717401485096066,
    -0.5917001814331423,
    -0.2092992179024789,
    0.2092992179024789,
    0.5917001814331423,
    0.8717401485096066,
    1.0,
)


def legendre_value(points, degree):
    previous = points * 0.0 + 1.0
    current = points
    for order in range(1, degree):
        following = ((2 * order + 1) * points * current - order * previous) / (order + 1)
        previous = current
        current = following
    return current


def quadrature_tables():
    degree = 7
    points = np.array(LOBATTO_POINTS)
    values = legendre_value(points, degree)
    weights = 2.0 / (degree * (degree + 1) * values * values)
    derive = np.zeros((degree + 1, degree + 1))
    for row_index in range(degree + 1):
        for column_index in range(degree + 1):
            if row_index != column_index:
                derive[row_index, column_index] = values[row_index] / (
                    values[column_index] * (points[row_index] - points[column_index])
                )
    derive[0, 0] = -degree * (degree + 1) / 4.0
    derive[degree, degree] = degree * (degree + 1) / 4.0
    stiffness_table = derive.T @ (weights[:, None] * derive)
    return (weights, derive, stiffness_table)


WEIGHTS, DERIVE, STIFF = quadrature_tables()
SLOPE = WEIGHTS[:, None] * DERIVE
COPIES = np.where(np.arange(8) % 7 == 0, 2.0, 1.0)


def chebyshev_bounds():
    weight_matrix = np.eye(8) * WEIGHTS

    def kron3(a, b, c):
        return np.kron(np.kron(a, b), c)

    element_matrix = (
        kron3(STIFF, weight_matrix, weight_matrix)
        + kron3(weight_matrix, STIFF, weight_matrix)
        + kron3(weight_matrix, weight_matrix, STIFF)
        + SIGMA_SHIFT * kron3(weight_matrix, weight_matrix, weight_matrix)
    )
    bounds_ratio = np.sum(np.abs(element_matrix), axis=1) / np.diagonal(element_matrix)
    upper_bound = float(np.max(bounds_ratio))
    lower_bound = upper_bound / SPREAD
    return ((upper_bound + lower_bound) / 2.0, (upper_bound - lower_bound) / 2.0)


def spectrum_top(diffuse):
    root = np.sqrt(COPIES)
    stiff = root[:, None] * STIFF * root[None, :]
    weight = np.diag(WEIGHTS * COPIES)

    def kron3(a, b, c):
        return np.kron(np.kron(a, b), c)

    element = diffuse * (
        kron3(stiff, weight, weight) + kron3(weight, stiff, weight) + kron3(weight, weight, stiff)
    ) + STEP_MAX * kron3(weight, weight, weight)
    return float(np.linalg.eigvalsh(element)[-1])


def line_sums(table, length):
    matrix = np.kron(np.eye(length // 8), table)
    total = matrix.copy()
    for start in range(8, length, 8):
        total[start] += matrix[start - 1]
        total[start - 1] += matrix[start]
    return total


def depth_line(vector, length):
    line = np.tile(vector * COPIES, length // 8)
    line[0] = vector[0]
    line[-1] = vector[-1]
    return line


def f32(array):
    return np.ascontiguousarray(array, np.float32)


def rolled_rows(table):
    out = np.zeros((8, 8, 128))
    for shift in range(8):
        for row in range(8):
            out[shift, row] = table[row, (row - shift) % 8]
    return out


def block(a, b, c):
    return a[:, None, None] * b[:, None] * c


class Tables:
    def __init__(self, depth):
        ones8, ones = np.ones(8), np.ones(depth)
        wide = WEIGHTS * COPIES
        deep = depth_line(WEIGHTS, depth)
        flat = np.tile(WEIGHTS, depth // 8)
        stiff = np.diagonal(STIFF)
        wide_s, deep_s = stiff * COPIES, depth_line(stiff, depth)
        share = 1.0 / COPIES
        share_z = np.tile(share, depth // 8)
        share_z[0] = share_z[-1] = 1.0
        self.summed = f32(
            np.stack([block(ones8, wide, deep), block(wide, ones8, deep), block(wide, wide, ones)])
        )
        self.local = f32(
            np.stack(
                [block(ones8, WEIGHTS, flat), block(WEIGHTS, ones8, flat), block(WEIGHTS, WEIGHTS, ones)]
            )
        )
        self.share = f32(block(share, share, share_z))
        diagonal = (
            block(wide_s, wide, deep)
            + block(wide, wide_s, deep)
            + block(wide, wide, deep_s)
            + SIGMA_SHIFT * block(wide, wide, deep)
        )
        self.inverse = f32(1.0 / diagonal)
        self.shift = f32(SIGMA_SHIFT * block(wide, wide, deep))
        self.stiff_y = f32(rolled_rows(STIFF))
        self.slope_y = f32(rolled_rows(SLOPE))
        self.stiff_z = f32(line_sums(STIFF, depth).T)
        self.plain_z = f32(np.kron(np.eye(depth // 8), STIFF).T)
        self.slope_z = f32(line_sums(SLOPE, depth).T)


def row_marks():
    row = lax.broadcasted_iota(jnp.int32, (8, 128), 0)
    return jnp.where(row == 0, 1.0, 0.0), jnp.where(row == 7, 1.0, 0.0)


def by_place(vector, place):
    out = jnp.full(place.shape, float(vector[0]), jnp.float32)
    for i in range(1, 8):
        out = jnp.where(place == i, float(vector[i]), out)
    return out


def along_x(rows, table):
    if np.allclose(table, table[::-1, ::-1]):
        even = 0.5 * (table[:4, :4] + table[:4, :3:-1])
        odd = 0.5 * (table[:4, :4] - table[:4, :3:-1])
        plus = [rows[i] + rows[7 - i] for i in range(4)]
        minus = [rows[i] - rows[7 - i] for i in range(4)]
        out = [None] * 8
        for a in range(4):
            p = sum(float(even[a, b]) * plus[b] for b in range(4))
            m = sum(float(odd[a, b]) * minus[b] for b in range(4))
            out[a], out[7 - a] = p + m, p - m
        return out
    return [sum(float(table[a, b]) * rows[b] for b in range(8)) for a in range(8)]


def along_y(tiles, factors):
    total = factors[0] * tiles
    for shift in range(1, 8):
        total = total + factors[shift] * pltpu.roll(tiles, shift, axis=1)
    return total


def along_z(tiles, matrix):
    x, y, z = tiles.shape
    out = jnp.dot(
        tiles.reshape(x * y, z), matrix, precision=HIGHEST_PRECISION, preferred_element_type=jnp.float32
    )
    return out.reshape(x, y, z)


def join_y(parts, low, high):
    out = list(parts)
    for e in range(1, len(parts)):
        out[e - 1] = out[e - 1] + high * pltpu.roll(parts[e], 7, axis=1)
        out[e] = out[e] + low * pltpu.roll(parts[e - 1], 1, axis=1)
    return out


def spread_rows(rows):
    return jnp.broadcast_to(rows[:, None, :], (rows.shape[0], 8, rows.shape[1]))


def column_sums(x_rows, y_parts, z_parts, summed, edges):
    y_parts = join_y(y_parts, edges[0], edges[1])
    return [
        jnp.stack(kx) * summed[0, 0] + ky * summed[1] + kz * summed[2]
        for kx, ky, kz in zip(x_rows, y_parts, z_parts)
    ]


def emit_column(ex, x_rows, y_parts, z_parts, extra, summed, edges, raw, state):
    rows = pl.ds(8 * ex, 8)
    parts = column_sums(x_rows, y_parts, z_parts, summed, edges)
    for e, part in enumerate(parts):
        ys = pl.ds(8 * e, 8)
        raw[rows, ys] = part if extra is None else part + extra[e]
        if ex:
            raw[8 * ex, ys] += state[e] * summed[0, 0]
            raw[8 * ex - 1, ys] += x_rows[e][0] * summed[0, 0]
    return [r[7] for r in x_rows]


def end_rows(table):
    row = lax.broadcasted_iota(jnp.int32, (8, 128), 0)
    return (table[0], table[7]), (by_place(table[0], row), by_place(table[7], row))


def store_faces(ex, e, columns, count, tile, even, ends, faces, x=True, y=True):
    x_near, x_far, y_near, y_far = faces
    (x_low, x_high), (y_low, y_high) = ends
    rows, ys = pl.ds(8 * ex, 8), pl.ds(8 * e, 8)
    if x and ex == 0:
        low = sum(float(x_low[i]) * tile[i] for i in range(8))
        x_near[ys] = low
        x_far[ys] = low
    if x and ex == columns - 1:
        high = sum(float(x_high[i]) * tile[i] for i in range(8))
        x_near[ys] = jnp.where(even[0], high, x_near[ys])
        x_far[ys] = jnp.where(even[0], x_far[ys], high)
    if y and e == 0:
        low = jnp.sum(tile * y_low, axis=1)
        y_near[rows] = low
        y_far[rows] = low
    if y and e == count - 1:
        high = jnp.sum(tile * y_high, axis=1)
        y_near[rows] = jnp.where(even[1], high, y_near[rows])
        y_far[rows] = jnp.where(even[1], y_far[rows], high)


def parity(even_ref):
    return even_ref[0] > 0.5, even_ref[1] > 0.5


def before_of(even, near, far):
    return jnp.where(even, far, near)


def after_of(even, near, far):
    return jnp.where(even, near, far)


def with_faces(tile, ex, e, columns, count, received, even, edges, weight_x=None, weight_y=None):
    x_far, x_near, y_far, y_near = received
    rows, ys = pl.ds(8 * ex, 8), pl.ds(8 * e, 8)

    def weighted(face, weight):
        return face if weight is None else face * weight

    if e == 0:
        face = before_of(even[1], y_near[rows], y_far[rows])
        tile = tile + spread_rows(face) * weighted(edges[0], weight_y)
    if e == count - 1:
        face = after_of(even[1], y_near[rows], y_far[rows])
        tile = tile + spread_rows(face) * weighted(edges[1], weight_y)
    if ex == 0:
        face = before_of(even[0], x_near[ys], x_far[ys])
        tile = jnp.concatenate([tile[0:1] + weighted(face, weight_x)[None], tile[1:]], axis=0)
    if ex == columns - 1:
        face = after_of(even[0], x_near[ys], x_far[ys])
        tile = jnp.concatenate([tile[:7], tile[7:8] + weighted(face, weight_x)[None]], axis=0)
    return tile


def split_rows(block_rows):
    return [block_rows[i] for i in range(8)]


def load_local(old, step, even_ref, out, x_near, x_far, y_near, y_far):
    columns, count, depth = out.shape[1] // 8, out.shape[2] // 8, out.shape[3]
    even, edges = parity(even_ref), row_marks()
    row = lax.broadcasted_iota(jnp.int32, (8, depth), 0)
    lane = lax.broadcasted_iota(jnp.int32, (8, depth), 1)
    place = lane & 7
    after = jnp.where((place == 0) & (lane > 0), 1.0, 0.0)
    before_z = jnp.where((place == 7) & (lane < depth - 1), 1.0, 0.0)
    plane = by_place(WEIGHTS, row) * by_place(WEIGHTS, place)
    mass = jnp.stack([float(w) * plane for w in WEIGHTS])
    for field in range(5):
        before = [None] * count
        for ex in range(columns):
            rows = pl.ds(8 * ex, 8)
            parts = []
            for e in range(count):
                ys = pl.ds(8 * e, 8)
                value = step[rows, ys]
                if field < 4:
                    value = value * old[field, rows, ys]
                if field == 2:
                    value = value + COUPLING * old[3, rows, ys]
                if field == 3:
                    value = value - STRATIFY * old[2, rows, ys]
                value = value * mass
                value = (
                    value
                    + after * pltpu.roll(value, 1, axis=2)
                    + before_z * pltpu.roll(value, depth - 1, axis=2)
                )
                parts.append(value)
            parts = join_y(parts, edges[0], edges[1])
            for e in range(count):
                ys = pl.ds(8 * e, 8)
                out[field, rows, ys] = parts[e]
                if ex:
                    out[field, 8 * ex, ys] += before[e]
                    out[field, 8 * ex - 1, ys] += parts[e][0]
                before[e] = parts[e][7]
        for e in range(count):
            ys = pl.ds(8 * e, 8)
            low, high = out[field, 0, ys], out[field, 8 * columns - 1, ys]
            x_near[field, ys] = jnp.where(even[0], high, low)
            x_far[field, ys] = jnp.where(even[0], low, high)
        for ex in range(columns):
            rows = pl.ds(8 * ex, 8)
            low = out[field, rows, pl.ds(0, 8)][:, 0]
            high = out[field, rows, pl.ds(8 * count - 8, 8)][:, 7]
            y_near[field, rows] = jnp.where(even[1], high, low)
            y_far[field, rows] = jnp.where(even[1], low, high)


def fix_corners(y_near, y_far, x_near, x_far, even_ref, near, far):
    length = y_near.shape[1]
    last = x_near.shape[1] - 1
    even = [even_ref[0, 0:1] > 0.5, even_ref[1, 0:1] > 0.5]
    near[...] = y_near[...]
    far[...] = y_far[...]
    for field in range(5):
        for end, place in ((before_of, 0), (after_of, length - 1)):
            first = end(even[0], x_near[field, 0:1], x_far[field, 0:1])
            final = end(even[0], x_near[field, last : last + 1], x_far[field, last : last + 1])
            near[field, place : place + 1] += jnp.where(even[1], final, first)
            far[field, place : place + 1] += jnp.where(even[1], first, final)


def stiff_terms(tiles, stiff_y, stiff_z):
    x_rows = [along_x(split_rows(t), STIFF) for t in tiles]
    y_parts = [along_y(t, stiff_y) for t in tiles]
    z_all = along_z(jnp.concatenate(tiles, axis=0), stiff_z[...])
    z_parts = [z_all[8 * e : 8 * e + 8] for e in range(len(tiles))]
    return x_rows, y_parts, z_parts


def field_faces(c, ex, e, columns, count, tile, even, ends, slope_ends, faces):
    store_faces(ex, e, columns, count, tile, even, ends, [f.at[c] for f in faces])
    slopes = [f.at[4] for f in faces]
    if isinstance(c, int):
        store_faces(ex, e, columns, count, tile, even, slope_ends, slopes, c == 0, c == 1)
        return

    @pl.when(c == 0)
    def _():
        store_faces(ex, e, columns, count, tile, even, slope_ends, slopes, True, False)

    @pl.when(c == 1)
    def _():
        store_faces(ex, e, columns, count, tile, even, slope_ends, slopes, False, True)


def start_field(local, boundary, x_far, x_near, y_far, y_near, even_ref, right, *faces):
    columns, count = right.shape[1] // 8, right.shape[2] // 8
    even, edges = parity(even_ref), row_marks()
    received = (x_far, x_near, y_far, y_near)
    ends, slope_ends = end_rows(STIFF), end_rows(SLOPE)
    for c in range(4):
        for ex in range(columns):
            for e in range(count):
                rows, ys = pl.ds(8 * ex, 8), pl.ds(8 * e, 8)
                tile = with_faces(local[c, rows, ys], ex, e, columns, count, [r.at[c] for r in received],
                                  even, edges)
                tile = tile * boundary[rows, ys].astype(jnp.float32)
                right[c, rows, ys] = tile
                field_faces(c, ex, e, columns, count, tile, even, ends, slope_ends, faces)


def start_sums(local, boundary, x_far, x_near, y_far, y_near, even_ref, right, summed, share, stiff_y, stiff_z,
               reaction, free, raw, dots):
    columns, count = raw.shape[1] // 8, raw.shape[2] // 8
    even, edges = parity(even_ref), row_marks()
    received = [r.at[4] for r in (x_far, x_near, y_far, y_near)]
    for ex in range(columns):
        for e in range(count):
            rows, ys = pl.ds(8 * ex, 8), pl.ds(8 * e, 8)
            reaction[rows, ys] = with_faces(local[4, rows, ys], ex, e, columns, count, received, even, edges)
            free[rows, ys] = boundary[rows, ys].astype(jnp.float32)
    dots[...] = jnp.zeros_like(dots)
    basis_sums(right, None, summed, share, stiff_y, stiff_z, raw, dots)


def grow_sums(newest, older, summed, share, stiff_y, stiff_z, raw, dots):
    basis_sums(newest, older, summed, share, stiff_y, stiff_z, raw, dots)


def basis_sums(newest, older, summed, share, stiff_y, stiff_z, raw, dots):
    columns, count = raw.shape[1] // 8, raw.shape[2] // 8
    edges = row_marks()

    def component(c, carry):
        same = jnp.zeros((8, 128), jnp.float32)
        cross = jnp.zeros((8, 128), jnp.float32)
        state = None
        for ex in range(columns):
            rows = pl.ds(8 * ex, 8)
            tiles = []
            for e in range(count):
                ys = pl.ds(8 * e, 8)
                tile = newest[c, rows, ys]
                weighted = tile * share[...]
                same = same + jnp.sum(weighted * tile, axis=0)
                if older is not None:
                    cross = cross + jnp.sum(weighted * older[c, rows, ys], axis=0)
                tiles.append(tile)
            x_rows, y_parts, z_parts = stiff_terms(tiles, stiff_y, stiff_z)
            state = emit_column(ex, x_rows, y_parts, z_parts, None, summed, edges, raw.at[c], state)
        dots[pl.ds(c, 1)] = jnp.sum(same, axis=0, keepdims=True)
        if older is not None:
            dots[pl.ds(c + 4, 1)] = jnp.sum(cross, axis=0, keepdims=True)
        return carry

    lax.fori_loop(0, 4, component, 0)


def next_field(k, c, ex, e, raw, newest, older, reaction, free, received, summed, edges, even, scale, rate, columns, count):
    rows, ys = pl.ds(8 * ex, 8), pl.ds(8 * e, 8)
    tile = with_faces(raw[c, rows, ys], ex, e, columns, count, [r.at[c] for r in received],
                      even, edges, summed[0, 0], summed[1])
    now = newest[c, rows, ys]
    tile = (scale * tile + (rate * reaction[rows, ys] - 1.0) * now) * free[rows, ys]
    if k > 1:
        tile = 2.0 * tile - older[c, rows, ys]
    return tile, now


def grow_field(k, scales, rates, *refs):
    refs = list(refs)
    raw, newest = refs[:2]
    older = refs[2] if k > 1 else None
    refs = refs[3:] if k > 1 else refs[2:]
    reaction, free, *received, even_ref, summed = refs[:8]
    out, *faces = refs[8:]
    columns, count = raw.shape[1] // 8, raw.shape[2] // 8
    even, edges = parity(even_ref), row_marks()
    ends, slope_ends = end_rows(STIFF), end_rows(SLOPE)
    for c in range(4):
        for ex in range(columns):
            for e in range(count):
                tile, _ = next_field(k, c, ex, e, raw, newest, older, reaction, free, received, summed, edges, even,
                                     scales[c], rates[c], columns, count)
                out[c, pl.ds(8 * ex, 8), pl.ds(8 * e, 8)] = tile
                field_faces(c, ex, e, columns, count, tile, even, ends, slope_ends, faces)


def last_field(scales, rates, *refs):
    refs = list(refs)
    raw, newest, older, reaction, free, *received, even_ref, summed, share, stiff_y, stiff_z, local = refs[:15]
    dots, (out, sums, *slopes) = refs[15:20], refs[20:]
    columns, count = raw.shape[1] // 8, raw.shape[2] // 8
    even, edges = parity(even_ref), row_marks()
    slope_ends = end_rows(SLOPE)
    for i in range(1, ITERS - 1):
        sums[i] = dots[i][...]
    for c in range(4):
        scale, rate = scales[c], rates[c]
        same = jnp.zeros((8, 128), jnp.float32)
        cross = jnp.zeros((8, 128), jnp.float32)
        work = jnp.zeros((8, 128), jnp.float32)
        for ex in range(columns):
            rows = pl.ds(8 * ex, 8)
            tiles = []
            for e in range(count):
                ys = pl.ds(8 * e, 8)
                tile, now = next_field(ITERS - 1, c, ex, e, raw, newest, older, reaction, free, received, summed,
                                       edges, even, scale, rate, columns, count)
                out[c, rows, ys] = tile
                store_faces(ex, e, columns, count, tile, even, slope_ends, slopes, c == 0, c == 1)
                weighted = tile * share[...]
                same = same + jnp.sum(weighted * tile, axis=0)
                cross = cross + jnp.sum(weighted * now, axis=0)
                extra = (rate * reaction[rows, ys] - 1.0) * tile
                work = work + jnp.sum(weighted * extra, axis=0)
                tiles.append(tile)
            x_rows, y_parts, z_parts = stiff_terms(tiles, stiff_y, stiff_z)
            for e in range(count):
                term = jnp.stack(x_rows[e]) * local[0] + y_parts[e] * local[1] + z_parts[e] * local[2]
                work = work + scale * jnp.sum(term * tiles[e], axis=0)
        sums[ITERS - 1, c : c + 1] = jnp.sum(same, axis=0, keepdims=True)
        sums[ITERS - 1, c + 4 : c + 5] = jnp.sum(cross, axis=0, keepdims=True)
        sums[0, c : c + 1] = dots[0][c : c + 1]
        sums[0, c + 4 : c + 5] = jnp.sum(work, axis=0, keepdims=True)


def finish_fields(halves, gain, *refs):
    sums, *basis = refs[: ITERS + 1]
    refs = refs[ITERS + 1 :]
    slopes = [[r.at[4] for r in refs[4 * k : 4 * k + 4]] for k in range(ITERS - 1)]
    refs = refs[4 * ITERS - 4 :]
    slopes.append(refs[:4])
    even_ref, free, summed, slope_y, slope_z, inverse = refs[4:10]
    fields, remainder, update, *faces = refs[10:17]
    weights, raw, *joined = refs[17:]
    columns, count = raw.shape[0] // 8, raw.shape[1] // 8
    even, edges = parity(even_ref), row_marks()
    ends = end_rows(STIFF)
    total = [jnp.broadcast_to(jnp.sum(sums[i], axis=1, keepdims=True), (8, 128)) for i in range(ITERS)]
    other = [pltpu.roll(t, 4, axis=0) for t in total]
    row = lax.broadcasted_iota(jnp.int32, (8, 128), 0)
    half = jnp.full((8, 128), halves[0], jnp.float32)
    for i in range(1, 4):
        half = jnp.where(row == i, halves[i], half)
    moments = [total[0], other[1]]
    for level in range(2, 2 * ITERS - 1):
        inner = total[level // 2] if level % 2 == 0 else other[level // 2 + 1]
        moments.append(2.0 * inner - moments[level % 2])
    top = 2.0 * other[0] - other[5]
    moments.append(2.0 * top - moments[1])
    for i, value in enumerate(conjugate_coefficients(moments, half, half)):
        weights[i] = value

    def combine(c, carry):
        factor = [weights[i, pl.ds(c, 1)] for i in range(ITERS)]
        for x in range(0, 8 * columns, 8):
            rows = pl.ds(x, 8)
            value = basis[0][c, rows] * factor[0][None]
            for i in range(1, ITERS):
                value = value + basis[i][c, rows] * factor[i][None]
            fields[c, rows] = value
        return carry

    lax.fori_loop(0, 4, combine, 0)
    for n in range(4):
        c = n // 2
        joined[n][...] = sum(slopes[i][n][...] * weights[i, c : c + 1] for i in range(ITERS))
    state = None
    for ex in range(columns):
        rows = pl.ds(8 * ex, 8)
        x_rows, y_parts, z_tiles = [], [], []
        for e in range(count):
            ys = pl.ds(8 * e, 8)
            x_rows.append(along_x(split_rows(fields[0, rows, ys]), SLOPE))
            y_parts.append(along_y(fields[1, rows, ys], slope_y))
            z_tiles.append(fields[2, rows, ys])
        z_all = along_z(jnp.concatenate(z_tiles, axis=0), slope_z[...])
        z_parts = [z_all[8 * e : 8 * e + 8] for e in range(count)]
        state = emit_column(ex, x_rows, y_parts, z_parts, None, summed, edges, raw, state)
    for ex in range(columns):
        for e in range(count):
            rows, ys = pl.ds(8 * ex, 8), pl.ds(8 * e, 8)
            tile = with_faces(raw[rows, ys], ex, e, columns, count, joined, even, edges, summed[0, 0], summed[1])
            left = -tile * free[rows, ys]
            change = gain * inverse[...] * left
            remainder[rows, ys] = left
            update[rows, ys] = change
            store_faces(ex, e, columns, count, change, even, ends, faces)


def pressure_sums(update, summed, shift, stiff_y, stiff_z, raw):
    columns, count = raw.shape[0] // 8, raw.shape[1] // 8
    edges = row_marks()
    state = None
    for ex in range(columns):
        rows = pl.ds(8 * ex, 8)
        tiles = [update[rows, pl.ds(8 * e, 8)] for e in range(count)]
        x_rows, y_parts, z_parts = stiff_terms(tiles, stiff_y, stiff_z)
        extra = [shift[...] * t for t in tiles]
        state = emit_column(ex, x_rows, y_parts, z_parts, extra, summed, edges, raw, state)


def pressure_step(last, keep, gain, *refs):
    raw, free, *received, even_ref, summed, inverse, remainder_in, update_in, pressure_in = refs[:12]
    if last:
        (pressure,) = refs[12:]
    else:
        pressure, remainder, update, *faces = refs[12:]
    columns, count = raw.shape[0] // 8, raw.shape[1] // 8
    even, edges = parity(even_ref), row_marks()
    ends = end_rows(STIFF)
    for ex in range(columns):
        for e in range(count):
            rows, ys = pl.ds(8 * ex, 8), pl.ds(8 * e, 8)
            tile = with_faces(raw[rows, ys], ex, e, columns, count, received, even, edges,
                              summed[0, 0], summed[1])
            left = remainder_in[rows, ys] - tile * free[rows, ys]
            change = gain * inverse[...] * left + keep * update_in[rows, ys]
            pressure[rows, ys] = pressure_in[rows, ys] + change
            if not last:
                remainder[rows, ys] = left
                update[rows, ys] = change
                store_faces(ex, e, columns, count, change, even, ends, faces)


VMEM_BYTES = 24 * 1024 * 1024


def call(kernel, name, outs, *args, scratch=(), cost=None):
    held = pl.BlockSpec(memory_space=pltpu.VMEM)
    return pl.pallas_call(
        kernel,
        name=name,
        out_shape=[jax.ShapeDtypeStruct(s, jnp.float32) for s in outs],
        in_specs=[held] * len(args),
        out_specs=[held] * len(outs),
        scratch_shapes=[pltpu.VMEM(s, jnp.float32) for s in scratch],
        cost_estimate=cost,
        compiler_params=pltpu.CompilerParams(vmem_limit_bytes=VMEM_BYTES),
    )(*args)


def busy(bytes_accessed):
    return pl.CostEstimate(flops=0, bytes_accessed=bytes_accessed, transcendentals=0)


def swap_near(axis, face):
    return lax.ppermute(face, axis, [(i, i ^ 1) for i in range(lax.axis_size(axis))])


def swap_far(axis, face):
    size = lax.axis_size(axis)
    return lax.ppermute(face, axis, [(i, (i + 1 if i % 2 else i - 1) % size) for i in range(size)])


def swap_all(x_near, x_far, y_near, y_far):
    y_far = swap_far("gy", y_far)
    x_far = swap_far("gx", x_far)
    x_near = swap_near("gx", x_near)
    y_near = swap_near("gy", y_near)
    return x_far, x_near, y_far, y_near


def group_sum(values, axis, masks):
    def swapped(mask):
        return lax.ppermute(values, axis, [(i, i ^ mask) for i in range(lax.axis_size(axis))])

    if len(masks) == 1:
        return values + swapped(masks[0])
    one, two, three = [swapped(m) for m in (masks[0], masks[1], masks[0] ^ masks[1])]
    return (values + one) + (two + three)


def all_sum(values, axis, first=1):
    bits, size = [], lax.axis_size(axis)
    while first < size:
        bits.append(first)
        first *= 2
    while bits:
        values = group_sum(values, axis, bits[:2])
        bits = bits[2:]
    return values


def conjugate_coefficients(moments, centre, half):
    remaining, towards = list(moments), list(moments)
    one, zero = jnp.ones_like(moments[0]), jnp.zeros_like(moments[0])
    direction = [one] + [zero] * ITERS
    residual = list(direction)
    total = [zero] * ITERS
    for step in range(ITERS):
        count = len(towards) - 1
        image = []
        for level in range(count):
            side = (
                half * towards[1] if level == 0 else 0.5 * half * (towards[level + 1] + towards[level - 1])
            )
            image.append(centre * towards[level] + side)
        alpha = remaining[step] / image[step]
        total = [total[i] + alpha * direction[i] for i in range(ITERS)]
        if step == ITERS - 1:
            break
        applied = []
        for i in range(ITERS + 1):
            term = centre * direction[i]
            if i >= 1:
                term = term + (half if i == 1 else 0.5 * half) * direction[i - 1]
            if i < ITERS:
                term = term + 0.5 * half * direction[i + 1]
            applied.append(term)
        residual = [residual[i] - alpha * applied[i] for i in range(ITERS + 1)]
        following = [remaining[i] - alpha * image[i] for i in range(count)]
        beta = -alpha * (half if step == 0 else 0.5 * half) * following[step + 1] / remaining[step]
        towards = [following[i] + beta * towards[i] for i in range(count)]
        direction = [residual[i] + beta * direction[i] for i in range(ITERS + 1)]
        remaining = following
    return total


def on_device(old_fields, inverse_step, boundary):
    x, y, z = inverse_step.shape
    t = Tables(z)
    brick, four = (x, y, z), (4, x, y, z)
    faces = [(y, z)] * 2 + [(x, z)] * 2
    faces5 = [(5,) + f for f in faces]

    place = [lax.axis_index(a) % 2 == 0 for a in ("gx", "gy")]
    even = jnp.stack([jnp.full((8, 128), p, jnp.float32) for p in place])

    local, x_near, x_far, y_near, y_far = call(
        load_local, "local_right", [(5,) + brick] + faces5, old_fields, inverse_step, even
    )
    x_far = swap_far("gx", x_far)
    x_near = swap_near("gx", x_near)
    y_near, y_far = call(fix_corners, "corners", faces5[2:], y_near, y_far, x_near, x_far, even)
    y_far = swap_far("gy", y_far)
    y_near = swap_near("gy", y_near)

    top = INTERVAL_SHARE * np.array([spectrum_top(c) for c in DIFFUSE])
    halves = [float(v) for v in 0.5 * top]
    scales = [float(v) for v in np.array(DIFFUSE) / (0.5 * top)]
    rates = [float(v) for v in 1.0 / (0.5 * top)]

    received = (x_far, x_near, y_far, y_near)
    right, *sent = call(start_field, "right_field", [four] + faces5, local, boundary, *received, even)
    heard = [swap_all(*sent)]
    reaction, free, raw, dots = call(
        start_sums, "right_sums", [brick, brick, four, (8, 128)],
        local, boundary, *received, even, right, t.summed, t.share, t.stiff_y, t.stiff_z, cost=busy(8 << 20),
    )
    basis, sums = [right], [dots]
    for k in range(1, ITERS):
        args = [raw] + basis[: -3 : -1] + [reaction, free, *heard[-1], even, t.summed]
        if k == ITERS - 1:
            field, sums, *slopes = call(
                functools.partial(last_field, scales, rates), "last_field", [four, (ITERS, 8, 128)] + faces,
                *args, t.share, t.stiff_y, t.plain_z, t.local, *sums,
            )
            basis.append(field)
            break
        field, *sent = call(
            functools.partial(grow_field, k, scales, rates), "basis_field", [four] + faces5, *args
        )
        heard.append(swap_all(*sent))
        raw, dots = call(
            grow_sums, "basis_sums", [four, (8, 128)],
            field, basis[-1], t.summed, t.share, t.stiff_y, t.stiff_z, cost=busy(8 << 20),
        )
        basis.append(field)
        sums.append(dots)
    slopes = swap_all(*slopes)
    sums = all_sum(sums, "gx")
    sums = all_sum(sums, "gy", 2)
    sums = group_sum(sums, "gy", [1])

    centre, half = chebyshev_bounds()
    factor = centre / half
    damping = 1.0 / factor
    fields, remainder, update, *sent = call(
        functools.partial(finish_fields, halves, 1.0 / centre), "fields", [four, brick, brick] + faces,
        sums, *basis, *[a for h in heard for a in h], *slopes, even, free, t.summed, t.slope_y, t.slope_z, t.inverse,
        scratch=[(ITERS, 8, 128), brick] + faces,
    )
    pressure = update
    for step in range(1, CHEB):
        last = step == CHEB - 1
        received = swap_all(*sent)
        (raw,) = call(
            pressure_sums, "pressure_sums", [brick],
            update, t.summed, t.shift, t.stiff_y, t.stiff_z, cost=busy(2 << 20),
        )
        following = 1.0 / (2.0 * factor - damping)
        keep, gain = following * damping, 2.0 * following / half
        damping = following
        kernel = functools.partial(pressure_step, last, keep, gain)
        args = [raw, free, *received, even, t.summed, t.inverse, remainder, update, pressure]
        if last:
            (pressure,) = call(kernel, "pressure_last", [brick], *args)
            break
        pressure, remainder, update, *sent = call(kernel, "pressure_step", [brick] * 3 + faces, *args)
    return (fields, pressure)


def solution(mesh):
    return jax.shard_map(
        on_device,
        mesh=mesh,
        in_specs=(P(None, "gx", "gy", None), P("gx", "gy", None), P("gx", "gy", None)),
        out_specs=(P(None, "gx", "gy", None), P("gx", "gy", None)),
        check_vma=False,
    )
```

```python
import functools

import jax
import jax.numpy as jnp
import numpy as np
from jax import lax
from jax.experimental import pallas as pl
from jax.experimental.pallas import tpu as pltpu
from jax.sharding import PartitionSpec as P

ITERS = 6
CHEB = 6

SIGMA_SHIFT = 0.5
DIFFUSE = (1.0, 1.0, 1.0, 1.4)
COUPLING = 1.0
STRATIFY = 1.0
SPREAD = 20.0
STEP_MAX = 64.0
INTERVAL_SHARE = 0.82
HIGHEST_PRECISION = lax.Precision.HIGHEST
LOBATTO_POINTS = (
    -1.0,
    -0.8717401485096066,
    -0.5917001814331423,
    -0.2092992179024789,
    0.2092992179024789,
    0.5917001814331423,
    0.8717401485096066,
    1.0,
)


def legendre_value(points, degree):
    previous = points * 0.0 + 1.0
    current = points
    for order in range(1, degree):
        following = ((2 * order + 1) * points * current - order * previous) / (order + 1)
        previous = current
        current = following
    return current


def quadrature_tables():
    degree = 7
    points = np.array(LOBATTO_POINTS)
    values = legendre_value(points, degree)
    weights = 2.0 / (degree * (degree + 1) * values * values)
    derive = np.zeros((degree + 1, degree + 1))
    for row_index in range(degree + 1):
        for column_index in range(degree + 1):
            if row_index != column_index:
                derive[row_index, column_index] = values[row_index] / (
                    values[column_index] * (points[row_index] - points[column_index])
                )
    derive[0, 0] = -degree * (degree + 1) / 4.0
    derive[degree, degree] = degree * (degree + 1) / 4.0
    stiffness_table = derive.T @ (weights[:, None] * derive)
    return (weights, derive, stiffness_table)


WEIGHTS, DERIVE, STIFF = quadrature_tables()
SLOPE = WEIGHTS[:, None] * DERIVE
COPIES = np.where(np.arange(8) % 7 == 0, 2.0, 1.0)


def chebyshev_bounds():
    weight_matrix = np.eye(8) * WEIGHTS

    def kron3(a, b, c):
        return np.kron(np.kron(a, b), c)

    element_matrix = (
        kron3(STIFF, weight_matrix, weight_matrix)
        + kron3(weight_matrix, STIFF, weight_matrix)
        + kron3(weight_matrix, weight_matrix, STIFF)
        + SIGMA_SHIFT * kron3(weight_matrix, weight_matrix, weight_matrix)
    )
    bounds_ratio = np.sum(np.abs(element_matrix), axis=1) / np.diagonal(element_matrix)
    upper_bound = float(np.max(bounds_ratio))
    lower_bound = upper_bound / SPREAD
    return ((upper_bound + lower_bound) / 2.0, (upper_bound - lower_bound) / 2.0)


def spectrum_top(diffuse):
    root = np.sqrt(COPIES)
    stiff = root[:, None] * STIFF * root[None, :]
    weight = np.diag(WEIGHTS * COPIES)

    def kron3(a, b, c):
        return np.kron(np.kron(a, b), c)

    element = diffuse * (
        kron3(stiff, weight, weight) + kron3(weight, stiff, weight) + kron3(weight, weight, stiff)
    ) + STEP_MAX * kron3(weight, weight, weight)
    return float(np.linalg.eigvalsh(element)[-1])


def line_sums(table, length):
    matrix = np.kron(np.eye(length // 8), table)
    total = matrix.copy()
    for start in range(8, length, 8):
        total[start] += matrix[start - 1]
        total[start - 1] += matrix[start]
    return total


def depth_line(vector, length):
    line = np.tile(vector * COPIES, length // 8)
    line[0] = vector[0]
    line[-1] = vector[-1]
    return line


def f32(array):
    return np.ascontiguousarray(array, np.float32)


def rolled_rows(table):
    out = np.zeros((8, 8, 128))
    for shift in range(8):
        for row in range(8):
            out[shift, row] = table[row, (row - shift) % 8]
    return out


def block(a, b, c):
    return a[:, None, None] * b[:, None] * c


class Tables:
    def __init__(self, depth):
        ones8, ones = np.ones(8), np.ones(depth)
        wide = WEIGHTS * COPIES
        deep = depth_line(WEIGHTS, depth)
        flat = np.tile(WEIGHTS, depth // 8)
        stiff = np.diagonal(STIFF)
        wide_s, deep_s = stiff * COPIES, depth_line(stiff, depth)
        share = 1.0 / COPIES
        share_z = np.tile(share, depth // 8)
        share_z[0] = share_z[-1] = 1.0
        self.summed = f32(
            np.stack([block(ones8, wide, deep), block(wide, ones8, deep), block(wide, wide, ones)])
        )
        self.local = f32(
            np.stack(
                [block(ones8, WEIGHTS, flat), block(WEIGHTS, ones8, flat), block(WEIGHTS, WEIGHTS, ones)]
            )
        )
        self.share = f32(block(share, share, share_z))
        diagonal = (
            block(wide_s, wide, deep)
            + block(wide, wide_s, deep)
            + block(wide, wide, deep_s)
            + SIGMA_SHIFT * block(wide, wide, deep)
        )
        self.inverse = f32(1.0 / diagonal)
        self.shift = f32(SIGMA_SHIFT * block(wide, wide, deep))
        self.stiff_y = f32(rolled_rows(STIFF))
        self.slope_y = f32(rolled_rows(SLOPE))
        self.stiff_z = f32(line_sums(STIFF, depth).T)
        self.plain_z = f32(np.kron(np.eye(depth // 8), STIFF).T)
        self.slope_z = f32(line_sums(SLOPE, depth).T)


def row_marks():
    row = lax.broadcasted_iota(jnp.int32, (8, 128), 0)
    return jnp.where(row == 0, 1.0, 0.0), jnp.where(row == 7, 1.0, 0.0)


def by_place(vector, place):
    out = jnp.full(place.shape, float(vector[0]), jnp.float32)
    for i in range(1, 8):
        out = jnp.where(place == i, float(vector[i]), out)
    return out


def along_x(rows, table):
    if np.allclose(table, table[::-1, ::-1]):
        even = 0.5 * (table[:4, :4] + table[:4, :3:-1])
        odd = 0.5 * (table[:4, :4] - table[:4, :3:-1])
        plus = [rows[i] + rows[7 - i] for i in range(4)]
        minus = [rows[i] - rows[7 - i] for i in range(4)]
        out = [None] * 8
        for a in range(4):
            p = sum(float(even[a, b]) * plus[b] for b in range(4))
            m = sum(float(odd[a, b]) * minus[b] for b in range(4))
            out[a], out[7 - a] = p + m, p - m
        return out
    return [sum(float(table[a, b]) * rows[b] for b in range(8)) for a in range(8)]


def along_y(tiles, factors):
    total = factors[0] * tiles
    for shift in range(1, 8):
        total = total + factors[shift] * pltpu.roll(tiles, shift, axis=1)
    return total


def along_z(tiles, matrix):
    x, y, z = tiles.shape
    out = jnp.dot(
        tiles.reshape(x * y, z), matrix, precision=HIGHEST_PRECISION, preferred_element_type=jnp.float32
    )
    return out.reshape(x, y, z)


def join_y(parts, low, high):
    out = list(parts)
    for e in range(1, len(parts)):
        out[e - 1] = out[e - 1] + high * pltpu.roll(parts[e], 7, axis=1)
        out[e] = out[e] + low * pltpu.roll(parts[e - 1], 1, axis=1)
    return out


def spread_rows(rows):
    return jnp.broadcast_to(rows[:, None, :], (rows.shape[0], 8, rows.shape[1]))


def column_sums(x_rows, y_parts, z_parts, summed, edges):
    y_parts = join_y(y_parts, edges[0], edges[1])
    return [
        jnp.stack(kx) * summed[0, 0] + ky * summed[1] + kz * summed[2]
        for kx, ky, kz in zip(x_rows, y_parts, z_parts)
    ]


def emit_column(ex, x_rows, y_parts, z_parts, summed, edges, out, state, finish=None, factor=None):
    rows = pl.ds(8 * ex, 8)
    parts = column_sums(x_rows, y_parts, z_parts, summed, edges)
    for e, part in enumerate(parts):
        ys = pl.ds(8 * e, 8)
        out[rows, ys] = part if finish is None else finish(e, part)
        if ex:
            for row, face in ((8 * ex, state[e]), (8 * ex - 1, x_rows[e][0])):
                face = face * summed[0, 0]
                out[row, ys] += face if factor is None else face * factor(row, ys)
    return [r[7] for r in x_rows]


def end_rows(table):
    row = lax.broadcasted_iota(jnp.int32, (8, 128), 0)
    return (table[0], table[7]), (by_place(table[0], row), by_place(table[7], row))


def store_faces(ex, e, columns, count, tile, even, ends, faces, x=True, y=True):
    x_near, x_far, y_near, y_far = faces
    (x_low, x_high), (y_low, y_high) = ends
    rows, ys = pl.ds(8 * ex, 8), pl.ds(8 * e, 8)
    if x and ex == 0:
        low = sum(float(x_low[i]) * tile[i] for i in range(8))
        x_near[ys] = low
        x_far[ys] = low
    if x and ex == columns - 1:
        high = sum(float(x_high[i]) * tile[i] for i in range(8))
        x_near[ys] = jnp.where(even[0], high, x_near[ys])
        x_far[ys] = jnp.where(even[0], x_far[ys], high)
    if y and e == 0:
        low = jnp.sum(tile * y_low, axis=1)
        y_near[rows] = low
        y_far[rows] = low
    if y and e == count - 1:
        high = jnp.sum(tile * y_high, axis=1)
        y_near[rows] = jnp.where(even[1], high, y_near[rows])
        y_far[rows] = jnp.where(even[1], y_far[rows], high)


def parity(even_ref):
    return even_ref[0] > 0.5, even_ref[1] > 0.5


def before_of(even, near, far):
    return jnp.where(even, far, near)


def after_of(even, near, far):
    return jnp.where(even, near, far)


def with_faces(tile, ex, e, columns, count, received, even, edges, weight_x=None, weight_y=None, mask=None):
    x_far, x_near, y_far, y_near = received
    rows, ys = pl.ds(8 * ex, 8), pl.ds(8 * e, 8)

    def weighted(face, weight):
        return face if weight is None else face * weight

    if e == 0:
        face = before_of(even[1], y_near[rows], y_far[rows])
        face = spread_rows(face) * weighted(edges[0], weight_y)
        tile = tile + weighted(face, mask)
    if e == count - 1:
        face = after_of(even[1], y_near[rows], y_far[rows])
        face = spread_rows(face) * weighted(edges[1], weight_y)
        tile = tile + weighted(face, mask)
    if ex == 0:
        face = before_of(even[0], x_near[ys], x_far[ys])
        face = weighted(face, weight_x) if mask is None else weighted(face, weight_x) * mask[0]
        tile = jnp.concatenate([tile[0:1] + face[None], tile[1:]], axis=0)
    if ex == columns - 1:
        face = after_of(even[0], x_near[ys], x_far[ys])
        face = weighted(face, weight_x) if mask is None else weighted(face, weight_x) * mask[7]
        tile = jnp.concatenate([tile[:7], tile[7:8] + face[None]], axis=0)
    return tile


def split_rows(block_rows):
    return [block_rows[i] for i in range(8)]


def load_local(old_far, step_far, even_ref, out, x_near, x_far, y_near, y_far, old, step, arrived):
    columns, count, depth = out.shape[1] // 8, out.shape[2] // 8, out.shape[3]
    copies = [pltpu.make_async_copy(step_far, step, arrived.at[4])]
    copies += [pltpu.make_async_copy(old_far.at[i], old.at[i], arrived.at[i]) for i in range(4)]
    for copy in copies:
        copy.start()
    even, edges = parity(even_ref), row_marks()
    row = lax.broadcasted_iota(jnp.int32, (8, depth), 0)
    lane = lax.broadcasted_iota(jnp.int32, (8, depth), 1)
    place = lane & 7
    after = jnp.where((place == 0) & (lane > 0), 1.0, 0.0)
    before_z = jnp.where((place == 7) & (lane < depth - 1), 1.0, 0.0)
    plane = by_place(WEIGHTS, row) * by_place(WEIGHTS, place)
    mass = jnp.stack([float(w) * plane for w in WEIGHTS])
    for field in (4, 0, 1, 2, 3):
        if field != 3:
            copies[0 if field == 4 else field + 1].wait()
        if field == 2:
            copies[4].wait()
        before = [None] * count
        for ex in range(columns):
            rows = pl.ds(8 * ex, 8)
            parts = []
            for e in range(count):
                ys = pl.ds(8 * e, 8)
                value = step[rows, ys]
                if field < 4:
                    value = value * old[field, rows, ys]
                if field == 2:
                    value = value + COUPLING * old[3, rows, ys]
                if field == 3:
                    value = value - STRATIFY * old[2, rows, ys]
                value = value * mass
                value = (
                    value
                    + after * pltpu.roll(value, 1, axis=2)
                    + before_z * pltpu.roll(value, depth - 1, axis=2)
                )
                parts.append(value)
            parts = join_y(parts, edges[0], edges[1])
            for e in range(count):
                ys = pl.ds(8 * e, 8)
                out[field, rows, ys] = parts[e]
                if ex:
                    out[field, 8 * ex, ys] += before[e]
                    out[field, 8 * ex - 1, ys] += parts[e][0]
                before[e] = parts[e][7]
        for e in range(count):
            ys = pl.ds(8 * e, 8)
            low, high = out[field, 0, ys], out[field, 8 * columns - 1, ys]
            x_near[field, ys] = jnp.where(even[0], high, low)
            x_far[field, ys] = jnp.where(even[0], low, high)
        for ex in range(columns):
            rows = pl.ds(8 * ex, 8)
            low = out[field, rows, pl.ds(0, 8)][:, 0]
            high = out[field, rows, pl.ds(8 * count - 8, 8)][:, 7]
            y_near[field, rows] = jnp.where(even[1], high, low)
            y_far[field, rows] = jnp.where(even[1], low, high)


def fix_corners(y_near, y_far, x_near, x_far, even_ref, near, far):
    length = y_near.shape[1]
    last = x_near.shape[1] - 1
    even = [even_ref[0, 0:1] > 0.5, even_ref[1, 0:1] > 0.5]
    near[...] = y_near[...]
    far[...] = y_far[...]
    for field in range(5):
        for end, place in ((before_of, 0), (after_of, length - 1)):
            first = end(even[0], x_near[field, 0:1], x_far[field, 0:1])
            final = end(even[0], x_near[field, last : last + 1], x_far[field, last : last + 1])
            near[field, place : place + 1] += jnp.where(even[1], final, first)
            far[field, place : place + 1] += jnp.where(even[1], first, final)


def stiff_terms(tiles, stiff_y, stiff_z):
    x_rows = [along_x(split_rows(t), STIFF) for t in tiles]
    y_parts = [along_y(t, stiff_y) for t in tiles]
    z_all = along_z(jnp.concatenate(tiles, axis=0), stiff_z[...])
    z_parts = [z_all[8 * e : 8 * e + 8] for e in range(len(tiles))]
    return x_rows, y_parts, z_parts


def field_faces(c, ex, e, columns, count, tile, even, ends, slope_ends, faces):
    store_faces(ex, e, columns, count, tile, even, ends, [f.at[c] for f in faces])
    slopes = [f.at[4] for f in faces]
    if isinstance(c, int):
        store_faces(ex, e, columns, count, tile, even, slope_ends, slopes, c == 0, c == 1)
        return

    @pl.when(c == 0)
    def _():
        store_faces(ex, e, columns, count, tile, even, slope_ends, slopes, True, False)

    @pl.when(c == 1)
    def _():
        store_faces(ex, e, columns, count, tile, even, slope_ends, slopes, False, True)


def start_field(local, boundary, x_far, x_near, y_far, y_near, even_ref, right, *faces):
    columns, count = right.shape[1] // 8, right.shape[2] // 8
    even, edges = parity(even_ref), row_marks()
    received = (x_far, x_near, y_far, y_near)
    ends, slope_ends = end_rows(STIFF), end_rows(SLOPE)
    for c in range(4):
        for ex in range(columns):
            for e in range(count):
                rows, ys = pl.ds(8 * ex, 8), pl.ds(8 * e, 8)
                tile = with_faces(local[c, rows, ys], ex, e, columns, count, [r.at[c] for r in received],
                                  even, edges)
                tile = tile * boundary[rows, ys].astype(jnp.float32)
                right[c, rows, ys] = tile
                field_faces(c, ex, e, columns, count, tile, even, ends, slope_ends, faces)


def pick(c, values):
    out = jnp.float32(values[0])
    for i in range(1, 4):
        out = jnp.where(c == i, jnp.float32(values[i]), out)
    return out


def start_sums(scales, rates, local, boundary, x_far, x_near, y_far, y_near, even_ref, right, summed, share, stiff_y,
               stiff_z, reaction, free, ahead, dots):
    columns, count = ahead.shape[1] // 8, ahead.shape[2] // 8
    even, edges = parity(even_ref), row_marks()
    received = [r.at[4] for r in (x_far, x_near, y_far, y_near)]
    for ex in range(columns):
        for e in range(count):
            rows, ys = pl.ds(8 * ex, 8), pl.ds(8 * e, 8)
            reaction[rows, ys] = with_faces(local[4, rows, ys], ex, e, columns, count, received, even, edges)
            free[rows, ys] = boundary[rows, ys].astype(jnp.float32)
    dots[...] = jnp.zeros_like(dots)
    basis_sums(scales, rates, right, None, reaction, free, summed, share, stiff_y, stiff_z, ahead, dots)


def basis_sums(scales, rates, newest, older, reaction, free, summed, share, stiff_y, stiff_z, ahead, dots):
    columns, count = ahead.shape[1] // 8, ahead.shape[2] // 8
    edges = row_marks()
    double = 1.0 if older is None else 2.0

    def component(c, carry):
        scale, rate = pick(c, [double * v for v in scales]), pick(c, [double * v for v in rates])
        same = jnp.zeros((8, 128), jnp.float32)
        cross = jnp.zeros((8, 128), jnp.float32)
        state = None
        for ex in range(columns):
            rows = pl.ds(8 * ex, 8)
            tiles = []
            for e in range(count):
                ys = pl.ds(8 * e, 8)
                tile = newest[c, rows, ys]
                weighted = tile * share[...]
                same = same + jnp.sum(weighted * tile, axis=0)
                if older is not None:
                    cross = cross + jnp.sum(weighted * older[c, rows, ys], axis=0)
                tiles.append(tile)
            x_rows, y_parts, z_parts = stiff_terms(tiles, stiff_y, stiff_z)

            def finish(e, part):
                ys = pl.ds(8 * e, 8)
                value = scale * part + (rate * reaction[rows, ys] - double) * tiles[e]
                value = value * free[rows, ys]
                return value if older is None else value - older[c, rows, ys]

            state = emit_column(ex, x_rows, y_parts, z_parts, summed, edges, ahead.at[c], state, finish,
                                lambda row, ys: scale * free[row, ys])
        dots[pl.ds(c, 1)] = jnp.sum(same, axis=0, keepdims=True)
        if older is not None:
            dots[pl.ds(c + 4, 1)] = jnp.sum(cross, axis=0, keepdims=True)
        return carry

    lax.fori_loop(0, 4, component, 0)


def next_field(c, ex, e, ahead, free, received, scale, summed, edges, even, columns, count):
    rows, ys = pl.ds(8 * ex, 8), pl.ds(8 * e, 8)
    return with_faces(ahead[c, rows, ys], ex, e, columns, count, [r.at[c] for r in received], even, edges,
                      summed[0, 0], summed[1], scale * free[rows, ys])


def grow_field(scales, ahead, free, x_far, x_near, y_far, y_near, even_ref, summed, out, *faces):
    received = (x_far, x_near, y_far, y_near)
    columns, count = out.shape[1] // 8, out.shape[2] // 8
    even, edges = parity(even_ref), row_marks()
    ends, slope_ends = end_rows(STIFF), end_rows(SLOPE)
    for c in range(4):
        for ex in range(columns):
            for e in range(count):
                tile = next_field(c, ex, e, ahead, free, received, scales[c], summed, edges, even, columns, count)
                out[c, pl.ds(8 * ex, 8), pl.ds(8 * e, 8)] = tile
                field_faces(c, ex, e, columns, count, tile, even, ends, slope_ends, faces)


def last_field(scales, rates, *refs):
    refs = list(refs)
    ahead, newest, reaction, free, *received, even_ref, summed, share, stiff_y, stiff_z, local = refs[:14]
    dots, (out, sums, *slopes) = refs[14:19], refs[19:]
    columns, count = out.shape[1] // 8, out.shape[2] // 8
    even, edges = parity(even_ref), row_marks()
    slope_ends = end_rows(SLOPE)
    for i in range(1, ITERS - 1):
        sums[i] = dots[i][...]
    for c in range(4):
        scale, rate = scales[c], rates[c]
        same = jnp.zeros((8, 128), jnp.float32)
        cross = jnp.zeros((8, 128), jnp.float32)
        work = jnp.zeros((8, 128), jnp.float32)
        for ex in range(columns):
            rows = pl.ds(8 * ex, 8)
            tiles = []
            for e in range(count):
                ys = pl.ds(8 * e, 8)
                tile = next_field(c, ex, e, ahead, free, received, 2.0 * scale, summed, edges, even, columns, count)
                now = newest[c, rows, ys]
                out[c, rows, ys] = tile
                store_faces(ex, e, columns, count, tile, even, slope_ends, slopes, c == 0, c == 1)
                weighted = tile * share[...]
                same = same + jnp.sum(weighted * tile, axis=0)
                cross = cross + jnp.sum(weighted * now, axis=0)
                extra = (rate * reaction[rows, ys] - 1.0) * tile
                work = work + jnp.sum(weighted * extra, axis=0)
                tiles.append(tile)
            x_rows, y_parts, z_parts = stiff_terms(tiles, stiff_y, stiff_z)
            for e in range(count):
                term = jnp.stack(x_rows[e]) * local[0] + y_parts[e] * local[1] + z_parts[e] * local[2]
                work = work + scale * jnp.sum(term * tiles[e], axis=0)
        sums[ITERS - 1, c : c + 1] = jnp.sum(same, axis=0, keepdims=True)
        sums[ITERS - 1, c + 4 : c + 5] = jnp.sum(cross, axis=0, keepdims=True)
        sums[0, c : c + 1] = dots[0][c : c + 1]
        sums[0, c + 4 : c + 5] = jnp.sum(work, axis=0, keepdims=True)


def finish_fields(halves, gain, *refs):
    sums, *basis = refs[: ITERS + 1]
    refs = refs[ITERS + 1 :]
    slopes = [[r.at[4] for r in refs[4 * k : 4 * k + 4]] for k in range(ITERS - 1)]
    refs = refs[4 * ITERS - 4 :]
    slopes.append(refs[:4])
    even_ref, free, summed, slope_y, slope_z, inverse = refs[4:10]
    fields, remainder, update, *faces = refs[10:17]
    weights, raw, *joined = refs[17:]
    columns, count = raw.shape[0] // 8, raw.shape[1] // 8
    even, edges = parity(even_ref), row_marks()
    ends = end_rows(STIFF)
    total = [jnp.broadcast_to(jnp.sum(sums[i], axis=1, keepdims=True), (8, 128)) for i in range(ITERS)]
    other = [pltpu.roll(t, 4, axis=0) for t in total]
    row = lax.broadcasted_iota(jnp.int32, (8, 128), 0)
    half = jnp.full((8, 128), halves[0], jnp.float32)
    for i in range(1, 4):
        half = jnp.where(row == i, halves[i], half)
    moments = [total[0], other[1]]
    for level in range(2, 2 * ITERS - 1):
        inner = total[level // 2] if level % 2 == 0 else other[level // 2 + 1]
        moments.append(2.0 * inner - moments[level % 2])
    top = 2.0 * other[0] - other[5]
    moments.append(2.0 * top - moments[1])
    for i, value in enumerate(conjugate_coefficients(moments, half, half)):
        weights[i] = value

    def combine(c, carry):
        factor = [weights[i, pl.ds(c, 1)] for i in range(ITERS)]
        for x in range(0, 8 * columns, 8):
            rows = pl.ds(x, 8)
            value = basis[0][c, rows] * factor[0][None]
            for i in range(1, ITERS):
                value = value + basis[i][c, rows] * factor[i][None]
            fields[c, rows] = value
        return carry

    lax.fori_loop(0, 4, combine, 0)
    for n in range(4):
        c = n // 2
        joined[n][...] = sum(slopes[i][n][...] * weights[i, c : c + 1] for i in range(ITERS))
    state = None
    for ex in range(columns):
        rows = pl.ds(8 * ex, 8)
        x_rows, y_parts, z_tiles = [], [], []
        for e in range(count):
            ys = pl.ds(8 * e, 8)
            x_rows.append(along_x(split_rows(fields[0, rows, ys]), SLOPE))
            y_parts.append(along_y(fields[1, rows, ys], slope_y))
            z_tiles.append(fields[2, rows, ys])
        z_all = along_z(jnp.concatenate(z_tiles, axis=0), slope_z[...])
        z_parts = [z_all[8 * e : 8 * e + 8] for e in range(count)]
        state = emit_column(ex, x_rows, y_parts, z_parts, summed, edges, raw, state)
    for ex in range(columns):
        for e in range(count):
            rows, ys = pl.ds(8 * ex, 8), pl.ds(8 * e, 8)
            tile = with_faces(raw[rows, ys], ex, e, columns, count, joined, even, edges, summed[0, 0], summed[1])
            left = -tile * free[rows, ys]
            change = gain * inverse[...] * left
            remainder[rows, ys] = left
            update[rows, ys] = change
            store_faces(ex, e, columns, count, change, even, ends, faces)


def pressure_sums(update, summed, shift, stiff_y, stiff_z, raw):
    columns, count = raw.shape[0] // 8, raw.shape[1] // 8
    edges = row_marks()
    state = None
    for ex in range(columns):
        rows = pl.ds(8 * ex, 8)
        tiles = [update[rows, pl.ds(8 * e, 8)] for e in range(count)]
        x_rows, y_parts, z_parts = stiff_terms(tiles, stiff_y, stiff_z)
        state = emit_column(ex, x_rows, y_parts, z_parts, summed, edges, raw, state,
                            lambda e, part: part + shift[...] * tiles[e])


def pressure_step(last, keep, gain, *refs):
    raw, free, *received, even_ref, summed, inverse, remainder_in, update_in, pressure_in = refs[:12]
    if last:
        pressure_far, pressure, left_here = refs[12:]
    else:
        pressure, remainder, update, *faces = refs[12:]
    columns, count = raw.shape[0] // 8, raw.shape[1] // 8
    copies = []
    even, edges = parity(even_ref), row_marks()
    ends = end_rows(STIFF)
    for ex in range(columns):
        for e in range(count):
            rows, ys = pl.ds(8 * ex, 8), pl.ds(8 * e, 8)
            tile = with_faces(raw[rows, ys], ex, e, columns, count, received, even, edges,
                              summed[0, 0], summed[1])
            left = remainder_in[rows, ys] - tile * free[rows, ys]
            change = gain * inverse[...] * left + keep * update_in[rows, ys]
            pressure[rows, ys] = pressure_in[rows, ys] + change
            if not last:
                remainder[rows, ys] = left
                update[rows, ys] = change
                store_faces(ex, e, columns, count, change, even, ends, faces)
        if last:
            rows = pl.ds(8 * ex, 8)
            copies.append(pltpu.make_async_copy(pressure.at[rows], pressure_far.at[rows], left_here.at[ex]))
            copies[-1].start()
    for copy in copies:
        copy.wait()


VMEM_BYTES = 24 * 1024 * 1024


def call(kernel, name, outs, *args, scratch=(), cost=None, far_in=0, far_out=0, copies=0):
    held, far = pl.BlockSpec(memory_space=pltpu.VMEM), pl.BlockSpec(memory_space=pltpu.HBM)
    scratch_shapes = [pltpu.VMEM(s, jnp.float32) for s in scratch]
    if copies:
        scratch_shapes.append(pltpu.SemaphoreType.DMA((copies,)))
    return pl.pallas_call(
        kernel,
        name=name,
        out_shape=[jax.ShapeDtypeStruct(s, jnp.float32) for s in outs],
        in_specs=[far] * far_in + [held] * (len(args) - far_in),
        out_specs=[far] * far_out + [held] * (len(outs) - far_out),
        scratch_shapes=scratch_shapes,
        cost_estimate=cost,
        compiler_params=pltpu.CompilerParams(vmem_limit_bytes=VMEM_BYTES),
    )(*[pltpu.with_memory_space_constraint(a, pltpu.HBM) for a in args[:far_in]], *args[far_in:])


def busy(bytes_accessed):
    return pl.CostEstimate(flops=0, bytes_accessed=bytes_accessed, transcendentals=0)


def swap_near(axis, face):
    return lax.ppermute(face, axis, [(i, i ^ 1) for i in range(lax.axis_size(axis))])


def swap_far(axis, face):
    size = lax.axis_size(axis)
    return lax.ppermute(face, axis, [(i, far_partner(i, size)) for i in range(size)])


def swap_all(x_near, x_far, y_near, y_far):
    y_far = swap_far("gy", y_far)
    x_far = swap_far("gx", x_far)
    x_near = swap_near("gx", x_near)
    y_near = swap_near("gy", y_near)
    return x_far, x_near, y_far, y_near


def far_partner(i, size):
    return (i + 1 if i % 2 else i - 1) % size


def partner_sum(values, axis, partners, riders):
    size, count = lax.axis_size(axis), values.shape[0]
    heard, faces = [], []
    for partner, rider in zip(partners, riders):
        load = values if rider is None else jnp.concatenate([values, rider])
        load = lax.ppermute(load, axis, [(i, partner(i)) for i in range(size)])
        heard.append(load[:count])
        if rider is not None:
            faces.append(load[count:])
    if len(heard) == 1:
        return values + heard[0], faces
    return (values + heard[0]) + (heard[1] + heard[2]), faces


def all_sum(values, axis, near, far):
    size = lax.axis_size(axis)
    half = size // 2

    def to_near(i):
        return i ^ 1

    def to_far(i):
        return far_partner(i, size)

    def across(i):
        return (i + half) % size

    def far_across(i):
        return across(to_far(i))

    if size == 4:
        values, (far, near) = partner_sum(values, axis, (to_far, to_near, across), (far, near, None))
        return values, near, far
    if size == 2:
        values, (far,) = partner_sum(values, axis, (to_far,), (far,))
        return values, lax.ppermute(near, axis, [(i, to_near(i)) for i in range(size)]), far
    values, (far,) = partner_sum(values, axis, (to_far, across, far_across), (far, None, None))
    values, (near,) = partner_sum(values, axis, (to_near,), (near,))
    bit = 4
    while bit < half:
        values, _ = partner_sum(values, axis, (lambda i, bit=bit: i ^ bit,), (None,))
        bit *= 2
    return values, near, far


def conjugate_coefficients(moments, centre, half):
    remaining, towards = list(moments), list(moments)
    one, zero = jnp.ones_like(moments[0]), jnp.zeros_like(moments[0])
    direction = [one] + [zero] * ITERS
    residual = list(direction)
    total = [zero] * ITERS
    for step in range(ITERS):
        count = len(towards) - 1
        image = []
        for level in range(count):
            side = (
                half * towards[1] if level == 0 else 0.5 * half * (towards[level + 1] + towards[level - 1])
            )
            image.append(centre * towards[level] + side)
        alpha = remaining[step] / image[step]
        total = [total[i] + alpha * direction[i] for i in range(ITERS)]
        if step == ITERS - 1:
            break
        applied = []
        for i in range(ITERS + 1):
            term = centre * direction[i]
            if i >= 1:
                term = term + (half if i == 1 else 0.5 * half) * direction[i - 1]
            if i < ITERS:
                term = term + 0.5 * half * direction[i + 1]
            applied.append(term)
        residual = [residual[i] - alpha * applied[i] for i in range(ITERS + 1)]
        following = [remaining[i] - alpha * image[i] for i in range(count)]
        beta = -alpha * (half if step == 0 else 0.5 * half) * following[step + 1] / remaining[step]
        towards = [following[i] + beta * towards[i] for i in range(count)]
        direction = [residual[i] + beta * direction[i] for i in range(ITERS + 1)]
        remaining = following
    return total


def on_device(old_fields, inverse_step, boundary):
    x, y, z = inverse_step.shape
    t = Tables(z)
    brick, four = (x, y, z), (4, x, y, z)
    faces = [(y, z)] * 2 + [(x, z)] * 2
    faces5 = [(5,) + f for f in faces]

    place = [lax.axis_index(a) % 2 == 0 for a in ("gx", "gy")]
    even = jnp.stack([jnp.full((8, 128), p, jnp.float32) for p in place])

    local, x_near, x_far, y_near, y_far = call(
        load_local, "local_right", [(5,) + brick] + faces5, old_fields, inverse_step, even,
        scratch=[four, brick], far_in=2, copies=5,
    )
    x_far = swap_far("gx", x_far)
    x_near = swap_near("gx", x_near)
    y_near, y_far = call(fix_corners, "corners", faces5[2:], y_near, y_far, x_near, x_far, even)
    y_far = swap_far("gy", y_far)
    y_near = swap_near("gy", y_near)

    top = INTERVAL_SHARE * np.array([spectrum_top(c) for c in DIFFUSE])
    halves = [float(v) for v in 0.5 * top]
    scales = [float(v) for v in np.array(DIFFUSE) / (0.5 * top)]
    rates = [float(v) for v in 1.0 / (0.5 * top)]

    received = (x_far, x_near, y_far, y_near)
    right, *sent = call(start_field, "right_field", [four] + faces5, local, boundary, *received, even)
    heard = [swap_all(*sent)]
    reaction, free, ahead, dots = call(
        functools.partial(start_sums, scales, rates), "right_sums", [brick, brick, four, (8, 128)],
        local, boundary, *received, even, right, t.summed, t.share, t.stiff_y, t.stiff_z, cost=busy(8 << 20),
    )
    basis, sums = [right], [dots]
    for k in range(1, ITERS - 1):
        here = scales if k == 1 else [2.0 * v for v in scales]
        field, *sent = call(
            functools.partial(grow_field, here), "basis_field", [four] + faces5,
            ahead, free, *heard[-1], even, t.summed,
        )
        heard.append(swap_all(*sent))
        ahead, dots = call(
            functools.partial(basis_sums, scales, rates), "basis_sums", [four, (8, 128)],
            field, basis[-1], reaction, free, t.summed, t.share, t.stiff_y, t.stiff_z, cost=busy(8 << 20),
        )
        basis.append(field)
        sums.append(dots)
    field, sums, x_near, x_far, y_near, y_far = call(
        functools.partial(last_field, scales, rates), "last_field", [four, (ITERS, 8, 128)] + faces,
        ahead, basis[-1], reaction, free, *heard[-1], even, t.summed, t.share, t.stiff_y, t.plain_z, t.local, *sums,
    )
    basis.append(field)
    sums = sums.reshape(ITERS * 8, z)
    sums, x_near, x_far = all_sum(sums, "gx", x_near, x_far)
    sums, y_near, y_far = all_sum(sums, "gy", y_near, y_far)
    sums = sums.reshape(ITERS, 8, z)
    slopes = (x_far, x_near, y_far, y_near)

    centre, half = chebyshev_bounds()
    factor = centre / half
    damping = 1.0 / factor
    fields, remainder, update, *sent = call(
        functools.partial(finish_fields, halves, 1.0 / centre), "fields", [four, brick, brick] + faces,
        sums, *basis, *[a for h in heard for a in h], *slopes, even, free, t.summed, t.slope_y, t.slope_z, t.inverse,
        scratch=[(ITERS, 8, 128), brick] + faces,
    )
    pressure = update
    for step in range(1, CHEB):
        last = step == CHEB - 1
        received = swap_all(*sent)
        (raw,) = call(
            pressure_sums, "pressure_sums", [brick],
            update, t.summed, t.shift, t.stiff_y, t.stiff_z, cost=busy(2 << 20),
        )
        following = 1.0 / (2.0 * factor - damping)
        keep, gain = following * damping, 2.0 * following / half
        damping = following
        kernel = functools.partial(pressure_step, last, keep, gain)
        args = [raw, free, *received, even, t.summed, t.inverse, remainder, update, pressure]
        if last:
            (pressure,) = call(
                kernel, "pressure_last", [brick], *args, scratch=[brick], far_out=1, copies=x // 8
            )
            break
        pressure, remainder, update, *sent = call(kernel, "pressure_step", [brick] * 3 + faces, *args)
    return (fields, pressure)


def solution(mesh):
    return jax.shard_map(
        on_device,
        mesh=mesh,
        in_specs=(P(None, "gx", "gy", None), P("gx", "gy", None), P("gx", "gy", None)),
        out_specs=(P(None, "gx", "gy", None), P("gx", "gy", None)),
        check_vma=False,
    )
```

```python
import functools

import jax
import jax.numpy as jnp
import numpy as np
from jax import lax
from jax.experimental import pallas as pl
from jax.experimental.pallas import tpu as pltpu
from jax.sharding import PartitionSpec as P

ITERS = 6
CHEB = 6

SIGMA_SHIFT = 0.5
DIFFUSE = (1.0, 1.0, 1.0, 1.4)
COUPLING = 1.0
STRATIFY = 1.0
SPREAD = 20.0
STEP_MAX = 64.0
INTERVAL_SHARE = 0.82
HIGHEST_PRECISION = lax.Precision.HIGHEST
LOBATTO_POINTS = (
    -1.0,
    -0.8717401485096066,
    -0.5917001814331423,
    -0.2092992179024789,
    0.2092992179024789,
    0.5917001814331423,
    0.8717401485096066,
    1.0,
)


def legendre_value(points, degree):
    previous = points * 0.0 + 1.0
    current = points
    for order in range(1, degree):
        following = ((2 * order + 1) * points * current - order * previous) / (order + 1)
        previous = current
        current = following
    return current


def quadrature_tables():
    degree = 7
    points = np.array(LOBATTO_POINTS)
    values = legendre_value(points, degree)
    weights = 2.0 / (degree * (degree + 1) * values * values)
    derive = np.zeros((degree + 1, degree + 1))
    for row_index in range(degree + 1):
        for column_index in range(degree + 1):
            if row_index != column_index:
                derive[row_index, column_index] = values[row_index] / (
                    values[column_index] * (points[row_index] - points[column_index])
                )
    derive[0, 0] = -degree * (degree + 1) / 4.0
    derive[degree, degree] = degree * (degree + 1) / 4.0
    stiffness_table = derive.T @ (weights[:, None] * derive)
    return (weights, derive, stiffness_table)


WEIGHTS, DERIVE, STIFF = quadrature_tables()
SLOPE = WEIGHTS[:, None] * DERIVE
COPIES = np.where(np.arange(8) % 7 == 0, 2.0, 1.0)


def chebyshev_bounds():
    weight_matrix = np.eye(8) * WEIGHTS

    def kron3(a, b, c):
        return np.kron(np.kron(a, b), c)

    element_matrix = (
        kron3(STIFF, weight_matrix, weight_matrix)
        + kron3(weight_matrix, STIFF, weight_matrix)
        + kron3(weight_matrix, weight_matrix, STIFF)
        + SIGMA_SHIFT * kron3(weight_matrix, weight_matrix, weight_matrix)
    )
    bounds_ratio = np.sum(np.abs(element_matrix), axis=1) / np.diagonal(element_matrix)
    upper_bound = float(np.max(bounds_ratio))
    lower_bound = upper_bound / SPREAD
    return ((upper_bound + lower_bound) / 2.0, (upper_bound - lower_bound) / 2.0)


def spectrum_top(diffuse):
    root = np.sqrt(COPIES)
    stiff = root[:, None] * STIFF * root[None, :]
    weight = np.diag(WEIGHTS * COPIES)

    def kron3(a, b, c):
        return np.kron(np.kron(a, b), c)

    element = diffuse * (
        kron3(stiff, weight, weight) + kron3(weight, stiff, weight) + kron3(weight, weight, stiff)
    ) + STEP_MAX * kron3(weight, weight, weight)
    return float(np.linalg.eigvalsh(element)[-1])


def line_sums(table, length):
    matrix = np.kron(np.eye(length // 8), table)
    total = matrix.copy()
    for start in range(8, length, 8):
        total[start] += matrix[start - 1]
        total[start - 1] += matrix[start]
    return total


def depth_line(vector, length):
    line = np.tile(vector * COPIES, length // 8)
    line[0] = vector[0]
    line[-1] = vector[-1]
    return line


def f32(array):
    return np.ascontiguousarray(array, np.float32)


def rolled_rows(table):
    out = np.zeros((8, 8, 128))
    for shift in range(8):
        for row in range(8):
            out[shift, row] = table[row, (row - shift) % 8]
    return out


def block(a, b, c):
    return a[:, None, None] * b[:, None] * c


class Tables:
    def __init__(self, depth):
        ones8, ones = np.ones(8), np.ones(depth)
        wide = WEIGHTS * COPIES
        deep = depth_line(WEIGHTS, depth)
        flat = np.tile(WEIGHTS, depth // 8)
        stiff = np.diagonal(STIFF)
        wide_s, deep_s = stiff * COPIES, depth_line(stiff, depth)
        share = 1.0 / COPIES
        share_z = np.tile(share, depth // 8)
        share_z[0] = share_z[-1] = 1.0
        self.summed = f32(
            np.stack([block(ones8, wide, deep), block(wide, ones8, deep), block(wide, wide, ones)])
        )
        self.local = f32(
            np.stack(
                [block(ones8, WEIGHTS, flat), block(WEIGHTS, ones8, flat), block(WEIGHTS, WEIGHTS, ones)]
            )
        )
        self.share = f32(block(share, share, share_z))
        diagonal = (
            block(wide_s, wide, deep)
            + block(wide, wide_s, deep)
            + block(wide, wide, deep_s)
            + SIGMA_SHIFT * block(wide, wide, deep)
        )
        self.inverse = f32(1.0 / diagonal)
        self.shift = f32(SIGMA_SHIFT * block(wide, wide, deep))
        self.stiff_y = f32(rolled_rows(STIFF))
        self.slope_y = f32(rolled_rows(SLOPE))
        self.stiff_z = f32(line_sums(STIFF, depth).T)
        self.plain_z = f32(np.kron(np.eye(depth // 8), STIFF).T)
        self.slope_z = f32(line_sums(SLOPE, depth).T)


def row_marks():
    row = lax.broadcasted_iota(jnp.int32, (8, 128), 0)
    return jnp.where(row == 0, 1.0, 0.0), jnp.where(row == 7, 1.0, 0.0)


def by_place(vector, place):
    out = jnp.full(place.shape, float(vector[0]), jnp.float32)
    for i in range(1, 8):
        out = jnp.where(place == i, float(vector[i]), out)
    return out


def along_x(rows, table):
    if np.allclose(table, table[::-1, ::-1]):
        even = 0.5 * (table[:4, :4] + table[:4, :3:-1])
        odd = 0.5 * (table[:4, :4] - table[:4, :3:-1])
        plus = [rows[i] + rows[7 - i] for i in range(4)]
        minus = [rows[i] - rows[7 - i] for i in range(4)]
        out = [None] * 8
        for a in range(4):
            p = sum(float(even[a, b]) * plus[b] for b in range(4))
            m = sum(float(odd[a, b]) * minus[b] for b in range(4))
            out[a], out[7 - a] = p + m, p - m
        return out
    return [sum(float(table[a, b]) * rows[b] for b in range(8)) for a in range(8)]


def along_y(tiles, factors):
    total = factors[0] * tiles
    for shift in range(1, 8):
        total = total + factors[shift] * pltpu.roll(tiles, shift, axis=1)
    return total


def along_z(tiles, matrix):
    x, y, z = tiles.shape
    out = jnp.dot(
        tiles.reshape(x * y, z), matrix, precision=HIGHEST_PRECISION, preferred_element_type=jnp.float32
    )
    return out.reshape(x, y, z)


def join_y(parts, low, high):
    out = list(parts)
    for e in range(1, len(parts)):
        out[e - 1] = out[e - 1] + high * pltpu.roll(parts[e], 7, axis=1)
        out[e] = out[e] + low * pltpu.roll(parts[e - 1], 1, axis=1)
    return out


def spread_rows(rows):
    return jnp.broadcast_to(rows[:, None, :], (rows.shape[0], 8, rows.shape[1]))


def column_sums(x_rows, y_parts, z_parts, summed, edges):
    y_parts = join_y(y_parts, edges[0], edges[1])
    return [
        jnp.stack(kx) * summed[0, 0] + ky * summed[1] + kz * summed[2]
        for kx, ky, kz in zip(x_rows, y_parts, z_parts)
    ]


def emit_column(ex, x_rows, y_parts, z_parts, summed, edges, out, state, finish=None, factor=None):
    rows = pl.ds(8 * ex, 8)
    parts = column_sums(x_rows, y_parts, z_parts, summed, edges)
    for e, part in enumerate(parts):
        ys = pl.ds(8 * e, 8)
        out[rows, ys] = part if finish is None else finish(e, part)
        if ex:
            for row, face in ((8 * ex, state[e]), (8 * ex - 1, x_rows[e][0])):
                face = face * summed[0, 0]
                out[row, ys] += face if factor is None else face * factor(row, ys)
    return [r[7] for r in x_rows]


def end_rows(table):
    row = lax.broadcasted_iota(jnp.int32, (8, 128), 0)
    return (table[0], table[7]), (by_place(table[0], row), by_place(table[7], row))


def store_faces(ex, e, columns, count, tile, even, ends, faces, x=True, y=True):
    x_near, x_far, y_near, y_far = faces
    (x_low, x_high), (y_low, y_high) = ends
    rows, ys = pl.ds(8 * ex, 8), pl.ds(8 * e, 8)
    if x and ex == 0:
        low = sum(float(x_low[i]) * tile[i] for i in range(8))
        x_near[ys] = low
        x_far[ys] = low
    if x and ex == columns - 1:
        high = sum(float(x_high[i]) * tile[i] for i in range(8))
        x_near[ys] = jnp.where(even[0], high, x_near[ys])
        x_far[ys] = jnp.where(even[0], x_far[ys], high)
    if y and e == 0:
        low = jnp.sum(tile * y_low, axis=1)
        y_near[rows] = low
        y_far[rows] = low
    if y and e == count - 1:
        high = jnp.sum(tile * y_high, axis=1)
        y_near[rows] = jnp.where(even[1], high, y_near[rows])
        y_far[rows] = jnp.where(even[1], y_far[rows], high)


def parity(even_ref):
    return even_ref[0] > 0.5, even_ref[1] > 0.5


def before_of(even, near, far):
    return jnp.where(even, far, near)


def after_of(even, near, far):
    return jnp.where(even, near, far)


def with_faces(tile, ex, e, columns, count, received, even, edges, weight_x=None, weight_y=None, mask=None):
    x_far, x_near, y_far, y_near = received
    rows, ys = pl.ds(8 * ex, 8), pl.ds(8 * e, 8)

    def weighted(face, weight):
        return face if weight is None else face * weight

    if e == 0:
        face = before_of(even[1], y_near[rows], y_far[rows])
        face = spread_rows(face) * weighted(edges[0], weight_y)
        tile = tile + weighted(face, mask)
    if e == count - 1:
        face = after_of(even[1], y_near[rows], y_far[rows])
        face = spread_rows(face) * weighted(edges[1], weight_y)
        tile = tile + weighted(face, mask)
    if ex == 0:
        face = before_of(even[0], x_near[ys], x_far[ys])
        face = weighted(face, weight_x) if mask is None else weighted(face, weight_x) * mask[0]
        tile = jnp.concatenate([tile[0:1] + face[None], tile[1:]], axis=0)
    if ex == columns - 1:
        face = after_of(even[0], x_near[ys], x_far[ys])
        face = weighted(face, weight_x) if mask is None else weighted(face, weight_x) * mask[7]
        tile = jnp.concatenate([tile[:7], tile[7:8] + face[None]], axis=0)
    return tile


def split_rows(block_rows):
    return [block_rows[i] for i in range(8)]


def load_local(old_far, step_far, even_ref, out, x_near, x_far, y_near, y_far, old, step, arrived):
    columns, count, depth = out.shape[1] // 8, out.shape[2] // 8, out.shape[3]
    copies = [pltpu.make_async_copy(step_far, step, arrived.at[4])]
    copies += [pltpu.make_async_copy(old_far.at[i], old.at[i], arrived.at[i]) for i in range(4)]
    for copy in copies:
        copy.start()
    even, edges = parity(even_ref), row_marks()
    row = lax.broadcasted_iota(jnp.int32, (8, depth), 0)
    lane = lax.broadcasted_iota(jnp.int32, (8, depth), 1)
    place = lane & 7
    after = jnp.where((place == 0) & (lane > 0), 1.0, 0.0)
    before_z = jnp.where((place == 7) & (lane < depth - 1), 1.0, 0.0)
    plane = by_place(WEIGHTS, row) * by_place(WEIGHTS, place)
    mass = jnp.stack([float(w) * plane for w in WEIGHTS])
    for field in (4, 0, 1, 2, 3):
        if field != 3:
            copies[0 if field == 4 else field + 1].wait()
        if field == 2:
            copies[4].wait()
        before = [None] * count
        for ex in range(columns):
            rows = pl.ds(8 * ex, 8)
            parts = []
            for e in range(count):
                ys = pl.ds(8 * e, 8)
                value = step[rows, ys]
                if field < 4:
                    value = value * old[field, rows, ys]
                if field == 2:
                    value = value + COUPLING * old[3, rows, ys]
                if field == 3:
                    value = value - STRATIFY * old[2, rows, ys]
                value = value * mass
                value = (
                    value
                    + after * pltpu.roll(value, 1, axis=2)
                    + before_z * pltpu.roll(value, depth - 1, axis=2)
                )
                parts.append(value)
            parts = join_y(parts, edges[0], edges[1])
            for e in range(count):
                ys = pl.ds(8 * e, 8)
                out[field, rows, ys] = parts[e]
                if ex:
                    out[field, 8 * ex, ys] += before[e]
                    out[field, 8 * ex - 1, ys] += parts[e][0]
                before[e] = parts[e][7]
        for e in range(count):
            ys = pl.ds(8 * e, 8)
            low, high = out[field, 0, ys], out[field, 8 * columns - 1, ys]
            x_near[field, ys] = jnp.where(even[0], high, low)
            x_far[field, ys] = jnp.where(even[0], low, high)
        for ex in range(columns):
            rows = pl.ds(8 * ex, 8)
            low = out[field, rows, pl.ds(0, 8)][:, 0]
            high = out[field, rows, pl.ds(8 * count - 8, 8)][:, 7]
            y_near[field, rows] = jnp.where(even[1], high, low)
            y_far[field, rows] = jnp.where(even[1], low, high)


def fix_corners(y_near, y_far, x_near, x_far, even_ref, near, far):
    length = y_near.shape[1]
    last = x_near.shape[1] - 1
    even = [even_ref[0, 0:1] > 0.5, even_ref[1, 0:1] > 0.5]
    near[...] = y_near[...]
    far[...] = y_far[...]
    for field in range(5):
        for end, place in ((before_of, 0), (after_of, length - 1)):
            first = end(even[0], x_near[field, 0:1], x_far[field, 0:1])
            final = end(even[0], x_near[field, last : last + 1], x_far[field, last : last + 1])
            near[field, place : place + 1] += jnp.where(even[1], final, first)
            far[field, place : place + 1] += jnp.where(even[1], first, final)


def stiff_terms(tiles, stiff_y, stiff_z):
    x_rows = [along_x(split_rows(t), STIFF) for t in tiles]
    y_parts = [along_y(t, stiff_y) for t in tiles]
    z_all = along_z(jnp.concatenate(tiles, axis=0), stiff_z[...])
    z_parts = [z_all[8 * e : 8 * e + 8] for e in range(len(tiles))]
    return x_rows, y_parts, z_parts


def field_faces(c, ex, e, columns, count, tile, even, ends, slope_ends, faces):
    store_faces(ex, e, columns, count, tile, even, ends, [f.at[c] for f in faces])
    slopes = [f.at[4] for f in faces]
    if isinstance(c, int):
        store_faces(ex, e, columns, count, tile, even, slope_ends, slopes, c == 0, c == 1)
        return

    @pl.when(c == 0)
    def _():
        store_faces(ex, e, columns, count, tile, even, slope_ends, slopes, True, False)

    @pl.when(c == 1)
    def _():
        store_faces(ex, e, columns, count, tile, even, slope_ends, slopes, False, True)


def start_field(local, boundary, x_far, x_near, y_far, y_near, even_ref, right, *faces):
    columns, count = right.shape[1] // 8, right.shape[2] // 8
    even, edges = parity(even_ref), row_marks()
    received = (x_far, x_near, y_far, y_near)
    ends, slope_ends = end_rows(STIFF), end_rows(SLOPE)
    for c in range(4):
        for ex in range(columns):
            for e in range(count):
                rows, ys = pl.ds(8 * ex, 8), pl.ds(8 * e, 8)
                tile = with_faces(local[c, rows, ys], ex, e, columns, count, [r.at[c] for r in received],
                                  even, edges)
                tile = tile * boundary[rows, ys].astype(jnp.float32)
                right[c, rows, ys] = tile
                field_faces(c, ex, e, columns, count, tile, even, ends, slope_ends, faces)


def pick(c, values):
    out = jnp.float32(values[0])
    for i in range(1, 4):
        out = jnp.where(c == i, jnp.float32(values[i]), out)
    return out


def start_sums(scales, rates, local, boundary, x_far, x_near, y_far, y_near, even_ref, right, summed, share, stiff_y,
               stiff_z, reaction, free, ahead, dots):
    columns, count = ahead.shape[1] // 8, ahead.shape[2] // 8
    even, edges = parity(even_ref), row_marks()
    received = [r.at[4] for r in (x_far, x_near, y_far, y_near)]
    for ex in range(columns):
        for e in range(count):
            rows, ys = pl.ds(8 * ex, 8), pl.ds(8 * e, 8)
            reaction[rows, ys] = with_faces(local[4, rows, ys], ex, e, columns, count, received, even, edges)
            free[rows, ys] = boundary[rows, ys].astype(jnp.float32)
    dots[...] = jnp.zeros_like(dots)
    basis_sums(scales, rates, right, None, reaction, free, summed, share, stiff_y, stiff_z, ahead, dots)


def basis_sums(scales, rates, newest, older, reaction, free, summed, share, stiff_y, stiff_z, ahead, dots):
    columns, count = ahead.shape[1] // 8, ahead.shape[2] // 8
    edges = row_marks()
    double = 1.0 if older is None else 2.0

    def component(c, carry):
        scale, rate = pick(c, [double * v for v in scales]), pick(c, [double * v for v in rates])
        same = jnp.zeros((8, 128), jnp.float32)
        cross = jnp.zeros((8, 128), jnp.float32)
        state = None
        for ex in range(columns):
            rows = pl.ds(8 * ex, 8)
            tiles = []
            for e in range(count):
                ys = pl.ds(8 * e, 8)
                tile = newest[c, rows, ys]
                weighted = tile * share[...]
                same = same + jnp.sum(weighted * tile, axis=0)
                if older is not None:
                    cross = cross + jnp.sum(weighted * older[c, rows, ys], axis=0)
                tiles.append(tile)
            x_rows, y_parts, z_parts = stiff_terms(tiles, stiff_y, stiff_z)

            def finish(e, part):
                ys = pl.ds(8 * e, 8)
                value = scale * part + (rate * reaction[rows, ys] - double) * tiles[e]
                value = value * free[rows, ys]
                return value if older is None else value - older[c, rows, ys]

            state = emit_column(ex, x_rows, y_parts, z_parts, summed, edges, ahead.at[c], state, finish,
                                lambda row, ys: scale * free[row, ys])
        dots[pl.ds(c, 1)] = jnp.sum(same, axis=0, keepdims=True)
        if older is not None:
            dots[pl.ds(c + 4, 1)] = jnp.sum(cross, axis=0, keepdims=True)
        return carry

    lax.fori_loop(0, 4, component, 0)


def next_field(c, ex, e, ahead, free, received, scale, summed, edges, even, columns, count):
    rows, ys = pl.ds(8 * ex, 8), pl.ds(8 * e, 8)
    return with_faces(ahead[c, rows, ys], ex, e, columns, count, [r.at[c] for r in received], even, edges,
                      summed[0, 0], summed[1], scale * free[rows, ys])


def grow_field(scales, ahead, free, x_far, x_near, y_far, y_near, even_ref, summed, out, *faces):
    received = (x_far, x_near, y_far, y_near)
    columns, count = out.shape[1] // 8, out.shape[2] // 8
    even, edges = parity(even_ref), row_marks()
    ends, slope_ends = end_rows(STIFF), end_rows(SLOPE)
    for c in range(4):
        for ex in range(columns):
            for e in range(count):
                tile = next_field(c, ex, e, ahead, free, received, scales[c], summed, edges, even, columns, count)
                out[c, pl.ds(8 * ex, 8), pl.ds(8 * e, 8)] = tile
                field_faces(c, ex, e, columns, count, tile, even, ends, slope_ends, faces)


def last_field(scales, rates, *refs):
    refs = list(refs)
    ahead, newest, reaction, free, *received, even_ref, summed, share, stiff_y, stiff_z, local = refs[:14]
    dots, (out, sums, *slopes) = refs[14:19], refs[19:]
    columns, count = out.shape[1] // 8, out.shape[2] // 8
    even, edges = parity(even_ref), row_marks()
    slope_ends = end_rows(SLOPE)
    for i in range(1, ITERS - 1):
        sums[i] = dots[i][...]
    for c in range(4):
        scale, rate = scales[c], rates[c]
        same = jnp.zeros((8, 128), jnp.float32)
        cross = jnp.zeros((8, 128), jnp.float32)
        work = jnp.zeros((8, 128), jnp.float32)
        for ex in range(columns):
            rows = pl.ds(8 * ex, 8)
            tiles = []
            for e in range(count):
                ys = pl.ds(8 * e, 8)
                tile = next_field(c, ex, e, ahead, free, received, 2.0 * scale, summed, edges, even, columns, count)
                now = newest[c, rows, ys]
                out[c, rows, ys] = tile
                store_faces(ex, e, columns, count, tile, even, slope_ends, slopes, c == 0, c == 1)
                weighted = tile * share[...]
                same = same + jnp.sum(weighted * tile, axis=0)
                cross = cross + jnp.sum(weighted * now, axis=0)
                extra = (rate * reaction[rows, ys] - 1.0) * tile
                work = work + jnp.sum(weighted * extra, axis=0)
                tiles.append(tile)
            x_rows, y_parts, z_parts = stiff_terms(tiles, stiff_y, stiff_z)
            for e in range(count):
                term = jnp.stack(x_rows[e]) * local[0] + y_parts[e] * local[1] + z_parts[e] * local[2]
                work = work + scale * jnp.sum(term * tiles[e], axis=0)
        sums[ITERS - 1, c : c + 1] = jnp.sum(same, axis=0, keepdims=True)
        sums[ITERS - 1, c + 4 : c + 5] = jnp.sum(cross, axis=0, keepdims=True)
        sums[0, c : c + 1] = dots[0][c : c + 1]
        sums[0, c + 4 : c + 5] = jnp.sum(work, axis=0, keepdims=True)


def finish_fields(halves, gain, *refs):
    sums, *basis = refs[: ITERS + 1]
    refs = refs[ITERS + 1 :]
    slopes = [[r.at[4] for r in refs[4 * k : 4 * k + 4]] for k in range(ITERS - 1)]
    refs = refs[4 * ITERS - 4 :]
    slopes.append(refs[:4])
    even_ref, free, summed, slope_y, slope_z, inverse = refs[4:10]
    fields, remainder, update, *faces = refs[10:17]
    weights, raw, *joined = refs[17:]
    columns, count = raw.shape[0] // 8, raw.shape[1] // 8
    even, edges = parity(even_ref), row_marks()
    ends = end_rows(STIFF)
    total = [jnp.broadcast_to(jnp.sum(sums[i], axis=1, keepdims=True), (8, 128)) for i in range(ITERS)]
    other = [pltpu.roll(t, 4, axis=0) for t in total]
    row = lax.broadcasted_iota(jnp.int32, (8, 128), 0)
    half = jnp.full((8, 128), halves[0], jnp.float32)
    for i in range(1, 4):
        half = jnp.where(row == i, halves[i], half)
    moments = [total[0], other[1]]
    for level in range(2, 2 * ITERS - 1):
        inner = total[level // 2] if level % 2 == 0 else other[level // 2 + 1]
        moments.append(2.0 * inner - moments[level % 2])
    top = 2.0 * other[0] - other[5]
    moments.append(2.0 * top - moments[1])
    for i, value in enumerate(conjugate_coefficients(moments, half, half)):
        weights[i] = value

    def combine(c, carry):
        factor = [weights[i, pl.ds(c, 1)] for i in range(ITERS)]
        for x in range(0, 8 * columns, 8):
            rows = pl.ds(x, 8)
            value = basis[0][c, rows] * factor[0][None]
            for i in range(1, ITERS):
                value = value + basis[i][c, rows] * factor[i][None]
            fields[c, rows] = value
        return carry

    lax.fori_loop(0, 4, combine, 0)
    for n in range(4):
        c = n // 2
        joined[n][...] = sum(slopes[i][n][...] * weights[i, c : c + 1] for i in range(ITERS))
    state = None
    for ex in range(columns):
        rows = pl.ds(8 * ex, 8)
        x_rows, y_parts, z_tiles = [], [], []
        for e in range(count):
            ys = pl.ds(8 * e, 8)
            x_rows.append(along_x(split_rows(fields[0, rows, ys]), SLOPE))
            y_parts.append(along_y(fields[1, rows, ys], slope_y))
            z_tiles.append(fields[2, rows, ys])
        z_all = along_z(jnp.concatenate(z_tiles, axis=0), slope_z[...])
        z_parts = [z_all[8 * e : 8 * e + 8] for e in range(count)]
        state = emit_column(ex, x_rows, y_parts, z_parts, summed, edges, raw, state)
    for ex in range(columns):
        for e in range(count):
            rows, ys = pl.ds(8 * ex, 8), pl.ds(8 * e, 8)
            tile = with_faces(raw[rows, ys], ex, e, columns, count, joined, even, edges, summed[0, 0], summed[1])
            left = -tile * free[rows, ys]
            change = gain * inverse[...] * left
            remainder[rows, ys] = left
            update[rows, ys] = change
            store_faces(ex, e, columns, count, change, even, ends, faces)


def pressure_sums(update, summed, shift, stiff_y, stiff_z, raw):
    columns, count = raw.shape[0] // 8, raw.shape[1] // 8
    edges = row_marks()
    state = None
    for ex in range(columns):
        rows = pl.ds(8 * ex, 8)
        tiles = [update[rows, pl.ds(8 * e, 8)] for e in range(count)]
        x_rows, y_parts, z_parts = stiff_terms(tiles, stiff_y, stiff_z)
        state = emit_column(ex, x_rows, y_parts, z_parts, summed, edges, raw, state,
                            lambda e, part: part + shift[...] * tiles[e])


def pressure_step(last, keep, gain, *refs):
    raw, free, *received, even_ref, summed, inverse, remainder_in, update_in, pressure_in = refs[:12]
    if last:
        pressure_far, pressure, left_here = refs[12:]
    else:
        pressure, remainder, update, *faces = refs[12:]
    columns, count = raw.shape[0] // 8, raw.shape[1] // 8
    copies = []
    even, edges = parity(even_ref), row_marks()
    ends = end_rows(STIFF)
    for ex in range(columns):
        for e in range(count):
            rows, ys = pl.ds(8 * ex, 8), pl.ds(8 * e, 8)
            tile = with_faces(raw[rows, ys], ex, e, columns, count, received, even, edges,
                              summed[0, 0], summed[1])
            left = remainder_in[rows, ys] - tile * free[rows, ys]
            change = gain * inverse[...] * left + keep * update_in[rows, ys]
            pressure[rows, ys] = pressure_in[rows, ys] + change
            if not last:
                remainder[rows, ys] = left
                update[rows, ys] = change
                store_faces(ex, e, columns, count, change, even, ends, faces)
        if last:
            rows = pl.ds(8 * ex, 8)
            copies.append(pltpu.make_async_copy(pressure.at[rows], pressure_far.at[rows], left_here.at[ex]))
            copies[-1].start()
    for copy in copies:
        copy.wait()


VMEM_BYTES = 24 * 1024 * 1024


def call(kernel, name, outs, *args, scratch=(), cost=None, far_in=0, far_out=0, copies=0):
    held, far = pl.BlockSpec(memory_space=pltpu.VMEM), pl.BlockSpec(memory_space=pltpu.HBM)
    scratch_shapes = [pltpu.VMEM(s, jnp.float32) for s in scratch]
    if copies:
        scratch_shapes.append(pltpu.SemaphoreType.DMA((copies,)))
    return pl.pallas_call(
        kernel,
        name=name,
        out_shape=[jax.ShapeDtypeStruct(s, jnp.float32) for s in outs],
        in_specs=[far] * far_in + [held] * (len(args) - far_in),
        out_specs=[far] * far_out + [held] * (len(outs) - far_out),
        scratch_shapes=scratch_shapes,
        cost_estimate=cost,
        compiler_params=pltpu.CompilerParams(vmem_limit_bytes=VMEM_BYTES),
    )(*[pltpu.with_memory_space_constraint(a, pltpu.HBM) for a in args[:far_in]], *args[far_in:])


def busy(bytes_accessed):
    return pl.CostEstimate(flops=0, bytes_accessed=bytes_accessed, transcendentals=0)


def swap_near(axis, face):
    return lax.ppermute(face, axis, [(i, i ^ 1) for i in range(lax.axis_size(axis))])


def swap_far(axis, face):
    size = lax.axis_size(axis)
    return lax.ppermute(face, axis, [(i, far_partner(i, size)) for i in range(size)])


def swap_all(x_near, x_far, y_near, y_far):
    y_far = swap_far("gy", y_far)
    x_far = swap_far("gx", x_far)
    x_near = swap_near("gx", x_near)
    y_near = swap_near("gy", y_near)
    return x_far, x_near, y_far, y_near


def swap_together(x_near, x_far, y_near, y_far):
    size, me = lax.axis_size("gx"), lax.axis_index("gx")
    place = jnp.arange(size)
    near = (place == me ^ 1)[:, None, None]
    far = (place == jnp.where(me % 2 == 1, me + 1, me - 1) % size)[:, None, None]
    load = jnp.where(near, x_near[None], jnp.where(far, x_far[None], 0.0))
    y_far = swap_far("gy", y_far)
    y_near = swap_near("gy", y_near)
    load = lax.all_to_all(load, "gx", 0, 0)
    x_near = jnp.sum(jnp.where(near, load, 0.0), axis=0)
    x_far = jnp.sum(jnp.where(far, load, 0.0), axis=0)
    return x_far, x_near, y_far, y_near


def far_partner(i, size):
    return (i + 1 if i % 2 else i - 1) % size


def partner_sum(values, axis, partners, riders):
    size, count = lax.axis_size(axis), values.shape[0]
    heard, faces = [], []
    for partner, rider in zip(partners, riders):
        load = values if rider is None else jnp.concatenate([values, rider])
        load = lax.ppermute(load, axis, [(i, partner(i)) for i in range(size)])
        heard.append(load[:count])
        if rider is not None:
            faces.append(load[count:])
    if len(heard) == 1:
        return values + heard[0], faces
    return (values + heard[0]) + (heard[1] + heard[2]), faces


def all_sum(values, axis, near, far):
    size = lax.axis_size(axis)
    half = size // 2

    def to_near(i):
        return i ^ 1

    def to_far(i):
        return far_partner(i, size)

    def across(i):
        return (i + half) % size

    def far_across(i):
        return across(to_far(i))

    if size == 4:
        values, (far, near) = partner_sum(values, axis, (to_far, to_near, across), (far, near, None))
        return values, near, far
    if size == 2:
        values, (far,) = partner_sum(values, axis, (to_far,), (far,))
        return values, lax.ppermute(near, axis, [(i, to_near(i)) for i in range(size)]), far
    values, (far,) = partner_sum(values, axis, (to_far, across, far_across), (far, None, None))
    values, (near,) = partner_sum(values, axis, (to_near,), (near,))
    bit = 4
    while bit < half:
        values, _ = partner_sum(values, axis, (lambda i, bit=bit: i ^ bit,), (None,))
        bit *= 2
    return values, near, far


def conjugate_coefficients(moments, centre, half):
    remaining, towards = list(moments), list(moments)
    one, zero = jnp.ones_like(moments[0]), jnp.zeros_like(moments[0])
    direction = [one] + [zero] * ITERS
    residual = list(direction)
    total = [zero] * ITERS
    for step in range(ITERS):
        count = len(towards) - 1
        image = []
        for level in range(count):
            side = (
                half * towards[1] if level == 0 else 0.5 * half * (towards[level + 1] + towards[level - 1])
            )
            image.append(centre * towards[level] + side)
        alpha = remaining[step] / image[step]
        total = [total[i] + alpha * direction[i] for i in range(ITERS)]
        if step == ITERS - 1:
            break
        applied = []
        for i in range(ITERS + 1):
            term = centre * direction[i]
            if i >= 1:
                term = term + (half if i == 1 else 0.5 * half) * direction[i - 1]
            if i < ITERS:
                term = term + 0.5 * half * direction[i + 1]
            applied.append(term)
        residual = [residual[i] - alpha * applied[i] for i in range(ITERS + 1)]
        following = [remaining[i] - alpha * image[i] for i in range(count)]
        beta = -alpha * (half if step == 0 else 0.5 * half) * following[step + 1] / remaining[step]
        towards = [following[i] + beta * towards[i] for i in range(count)]
        direction = [residual[i] + beta * direction[i] for i in range(ITERS + 1)]
        remaining = following
    return total


def on_device(old_fields, inverse_step, boundary):
    x, y, z = inverse_step.shape
    t = Tables(z)
    brick, four = (x, y, z), (4, x, y, z)
    faces = [(y, z)] * 2 + [(x, z)] * 2
    faces5 = [(5,) + f for f in faces]

    place = [lax.axis_index(a) % 2 == 0 for a in ("gx", "gy")]
    even = jnp.stack([jnp.full((8, 128), p, jnp.float32) for p in place])

    local, x_near, x_far, y_near, y_far = call(
        load_local, "local_right", [(5,) + brick] + faces5, old_fields, inverse_step, even,
        scratch=[four, brick], far_in=2, copies=5,
    )
    x_far = swap_far("gx", x_far)
    x_near = swap_near("gx", x_near)
    y_near, y_far = call(fix_corners, "corners", faces5[2:], y_near, y_far, x_near, x_far, even)
    y_far = swap_far("gy", y_far)
    y_near = swap_near("gy", y_near)

    top = INTERVAL_SHARE * np.array([spectrum_top(c) for c in DIFFUSE])
    halves = [float(v) for v in 0.5 * top]
    scales = [float(v) for v in np.array(DIFFUSE) / (0.5 * top)]
    rates = [float(v) for v in 1.0 / (0.5 * top)]

    received = (x_far, x_near, y_far, y_near)
    right, *sent = call(start_field, "right_field", [four] + faces5, local, boundary, *received, even)
    heard = [swap_all(*sent)]
    reaction, free, ahead, dots = call(
        functools.partial(start_sums, scales, rates), "right_sums", [brick, brick, four, (8, 128)],
        local, boundary, *received, even, right, t.summed, t.share, t.stiff_y, t.stiff_z, cost=busy(8 << 20),
    )
    basis, sums = [right], [dots]
    for k in range(1, ITERS - 1):
        here = scales if k == 1 else [2.0 * v for v in scales]
        field, *sent = call(
            functools.partial(grow_field, here), "basis_field", [four] + faces5,
            ahead, free, *heard[-1], even, t.summed,
        )
        heard.append(swap_all(*sent))
        ahead, dots = call(
            functools.partial(basis_sums, scales, rates), "basis_sums", [four, (8, 128)],
            field, basis[-1], reaction, free, t.summed, t.share, t.stiff_y, t.stiff_z, cost=busy(8 << 20),
        )
        basis.append(field)
        sums.append(dots)
    field, sums, x_near, x_far, y_near, y_far = call(
        functools.partial(last_field, scales, rates), "last_field", [four, (ITERS, 8, 128)] + faces,
        ahead, basis[-1], reaction, free, *heard[-1], even, t.summed, t.share, t.stiff_y, t.plain_z, t.local, *sums,
    )
    basis.append(field)
    sums = sums.reshape(ITERS * 8, z)
    sums, x_near, x_far = all_sum(sums, "gx", x_near, x_far)
    sums, y_near, y_far = all_sum(sums, "gy", y_near, y_far)
    sums = sums.reshape(ITERS, 8, z)
    slopes = (x_far, x_near, y_far, y_near)

    centre, half = chebyshev_bounds()
    factor = centre / half
    damping = 1.0 / factor
    fields, remainder, update, *sent = call(
        functools.partial(finish_fields, halves, 1.0 / centre), "fields", [four, brick, brick] + faces,
        sums, *basis, *[a for h in heard for a in h], *slopes, even, free, t.summed, t.slope_y, t.slope_z, t.inverse,
        scratch=[(ITERS, 8, 128), brick] + faces,
    )
    pressure = update
    for step in range(1, CHEB):
        last = step == CHEB - 1
        received = swap_together(*sent)
        (raw,) = call(
            pressure_sums, "pressure_sums", [brick],
            update, t.summed, t.shift, t.stiff_y, t.stiff_z, cost=busy(2 << 20),
        )
        following = 1.0 / (2.0 * factor - damping)
        keep, gain = following * damping, 2.0 * following / half
        damping = following
        kernel = functools.partial(pressure_step, last, keep, gain)
        args = [raw, free, *received, even, t.summed, t.inverse, remainder, update, pressure]
        if last:
            (pressure,) = call(
                kernel, "pressure_last", [brick], *args, scratch=[brick], far_out=1, copies=x // 8
            )
            break
        pressure, remainder, update, *sent = call(kernel, "pressure_step", [brick] * 3 + faces, *args)
    return (fields, pressure)


def solution(mesh):
    return jax.shard_map(
        on_device,
        mesh=mesh,
        in_specs=(P(None, "gx", "gy", None), P("gx", "gy", None), P("gx", "gy", None)),
        out_specs=(P(None, "gx", "gy", None), P("gx", "gy", None)),
        check_vma=False,
    )
```

```python
import functools

import jax
import jax.numpy as jnp
import numpy as np
from jax import lax
from jax.experimental import pallas as pl
from jax.experimental.pallas import tpu as pltpu
from jax.sharding import PartitionSpec as P

ITERS = 6
CHEB = 6

SIGMA_SHIFT = 0.5
DIFFUSE = (1.0, 1.0, 1.0, 1.4)
COUPLING = 1.0
STRATIFY = 1.0
SPREAD = 20.0
STEP_MAX = 64.0
INTERVAL_SHARE = 0.82
HIGHEST_PRECISION = lax.Precision.HIGHEST
LOBATTO_POINTS = (
    -1.0,
    -0.8717401485096066,
    -0.5917001814331423,
    -0.2092992179024789,
    0.2092992179024789,
    0.5917001814331423,
    0.8717401485096066,
    1.0,
)


def legendre_value(points, degree):
    previous = points * 0.0 + 1.0
    current = points
    for order in range(1, degree):
        following = ((2 * order + 1) * points * current - order * previous) / (order + 1)
        previous = current
        current = following
    return current


def quadrature_tables():
    degree = 7
    points = np.array(LOBATTO_POINTS)
    values = legendre_value(points, degree)
    weights = 2.0 / (degree * (degree + 1) * values * values)
    derive = np.zeros((degree + 1, degree + 1))
    for row_index in range(degree + 1):
        for column_index in range(degree + 1):
            if row_index != column_index:
                derive[row_index, column_index] = values[row_index] / (
                    values[column_index] * (points[row_index] - points[column_index])
                )
    derive[0, 0] = -degree * (degree + 1) / 4.0
    derive[degree, degree] = degree * (degree + 1) / 4.0
    stiffness_table = derive.T @ (weights[:, None] * derive)
    return (weights, derive, stiffness_table)


WEIGHTS, DERIVE, STIFF = quadrature_tables()
SLOPE = WEIGHTS[:, None] * DERIVE
COPIES = np.where(np.arange(8) % 7 == 0, 2.0, 1.0)


def chebyshev_bounds():
    weight_matrix = np.eye(8) * WEIGHTS

    def kron3(a, b, c):
        return np.kron(np.kron(a, b), c)

    element_matrix = (
        kron3(STIFF, weight_matrix, weight_matrix)
        + kron3(weight_matrix, STIFF, weight_matrix)
        + kron3(weight_matrix, weight_matrix, STIFF)
        + SIGMA_SHIFT * kron3(weight_matrix, weight_matrix, weight_matrix)
    )
    bounds_ratio = np.sum(np.abs(element_matrix), axis=1) / np.diagonal(element_matrix)
    upper_bound = float(np.max(bounds_ratio))
    lower_bound = upper_bound / SPREAD
    return ((upper_bound + lower_bound) / 2.0, (upper_bound - lower_bound) / 2.0)


def spectrum_top(diffuse):
    root = np.sqrt(COPIES)
    stiff = root[:, None] * STIFF * root[None, :]
    weight = np.diag(WEIGHTS * COPIES)

    def kron3(a, b, c):
        return np.kron(np.kron(a, b), c)

    element = diffuse * (
        kron3(stiff, weight, weight) + kron3(weight, stiff, weight) + kron3(weight, weight, stiff)
    ) + STEP_MAX * kron3(weight, weight, weight)
    return float(np.linalg.eigvalsh(element)[-1])


def line_sums(table, length):
    matrix = np.kron(np.eye(length // 8), table)
    total = matrix.copy()
    for start in range(8, length, 8):
        total[start] += matrix[start - 1]
        total[start - 1] += matrix[start]
    return total


def depth_line(vector, length):
    line = np.tile(vector * COPIES, length // 8)
    line[0] = vector[0]
    line[-1] = vector[-1]
    return line


def f32(array):
    return np.ascontiguousarray(array, np.float32)


def rolled_rows(table):
    out = np.zeros((8, 8, 128))
    for shift in range(8):
        for row in range(8):
            out[shift, row] = table[row, (row - shift) % 8]
    return out


def block(a, b, c):
    return a[:, None, None] * b[:, None] * c


class Tables:
    def __init__(self, depth):
        ones8, ones = np.ones(8), np.ones(depth)
        wide = WEIGHTS * COPIES
        deep = depth_line(WEIGHTS, depth)
        flat = np.tile(WEIGHTS, depth // 8)
        stiff = np.diagonal(STIFF)
        wide_s, deep_s = stiff * COPIES, depth_line(stiff, depth)
        share = 1.0 / COPIES
        share_z = np.tile(share, depth // 8)
        share_z[0] = share_z[-1] = 1.0
        self.summed = f32(
            np.stack([block(ones8, wide, deep), block(wide, ones8, deep), block(wide, wide, ones)])
        )
        self.local = f32(
            np.stack(
                [block(ones8, WEIGHTS, flat), block(WEIGHTS, ones8, flat), block(WEIGHTS, WEIGHTS, ones)]
            )
        )
        self.share = f32(block(share, share, share_z))
        diagonal = (
            block(wide_s, wide, deep)
            + block(wide, wide_s, deep)
            + block(wide, wide, deep_s)
            + SIGMA_SHIFT * block(wide, wide, deep)
        )
        self.inverse = f32(1.0 / diagonal)
        self.shift = f32(SIGMA_SHIFT * block(wide, wide, deep))
        self.stiff_y = f32(rolled_rows(STIFF))
        self.slope_y = f32(rolled_rows(SLOPE))
        self.stiff_z = f32(line_sums(STIFF, depth).T)
        self.plain_z = f32(np.kron(np.eye(depth // 8), STIFF).T)
        self.slope_z = f32(line_sums(SLOPE, depth).T)


def row_marks():
    row = lax.broadcasted_iota(jnp.int32, (8, 128), 0)
    return jnp.where(row == 0, 1.0, 0.0), jnp.where(row == 7, 1.0, 0.0)


def by_place(vector, place):
    out = jnp.full(place.shape, float(vector[0]), jnp.float32)
    for i in range(1, 8):
        out = jnp.where(place == i, float(vector[i]), out)
    return out


def along_x(rows, table):
    if np.allclose(table, table[::-1, ::-1]):
        even = 0.5 * (table[:4, :4] + table[:4, :3:-1])
        odd = 0.5 * (table[:4, :4] - table[:4, :3:-1])
        plus = [rows[i] + rows[7 - i] for i in range(4)]
        minus = [rows[i] - rows[7 - i] for i in range(4)]
        out = [None] * 8
        for a in range(4):
            p = sum(float(even[a, b]) * plus[b] for b in range(4))
            m = sum(float(odd[a, b]) * minus[b] for b in range(4))
            out[a], out[7 - a] = p + m, p - m
        return out
    return [sum(float(table[a, b]) * rows[b] for b in range(8)) for a in range(8)]


def along_y(tiles, factors):
    total = factors[0] * tiles
    for shift in range(1, 8):
        total = total + factors[shift] * pltpu.roll(tiles, shift, axis=1)
    return total


def along_z(tiles, matrix):
    x, y, z = tiles.shape
    out = jnp.dot(
        tiles.reshape(x * y, z), matrix, precision=HIGHEST_PRECISION, preferred_element_type=jnp.float32
    )
    return out.reshape(x, y, z)


def join_y(parts, low, high):
    out = list(parts)
    for e in range(1, len(parts)):
        out[e - 1] = out[e - 1] + high * pltpu.roll(parts[e], 7, axis=1)
        out[e] = out[e] + low * pltpu.roll(parts[e - 1], 1, axis=1)
    return out


def spread_rows(rows):
    return jnp.broadcast_to(rows[:, None, :], (rows.shape[0], 8, rows.shape[1]))


def column_sums(x_rows, y_parts, z_parts, summed, edges):
    y_parts = join_y(y_parts, edges[0], edges[1])
    return [
        jnp.stack(kx) * summed[0, 0] + ky * summed[1] + kz * summed[2]
        for kx, ky, kz in zip(x_rows, y_parts, z_parts)
    ]


def emit_column(ex, x_rows, y_parts, z_parts, summed, edges, out, state, finish=None, factor=None):
    rows = pl.ds(8 * ex, 8)
    parts = column_sums(x_rows, y_parts, z_parts, summed, edges)
    for e, part in enumerate(parts):
        ys = pl.ds(8 * e, 8)
        out[rows, ys] = part if finish is None else finish(e, part)
        if ex:
            for row, face in ((8 * ex, state[e]), (8 * ex - 1, x_rows[e][0])):
                face = face * summed[0, 0]
                out[row, ys] += face if factor is None else face * factor(row, ys)
    return [r[7] for r in x_rows]


def end_rows(table):
    row = lax.broadcasted_iota(jnp.int32, (8, 128), 0)
    return (table[0], table[7]), (by_place(table[0], row), by_place(table[7], row))


def store_faces(ex, e, columns, count, tile, even, ends, faces, x=True, y=True):
    x_near, x_far, y_near, y_far = faces
    (x_low, x_high), (y_low, y_high) = ends
    rows, ys = pl.ds(8 * ex, 8), pl.ds(8 * e, 8)
    if x and ex == 0:
        low = sum(float(x_low[i]) * tile[i] for i in range(8))
        x_near[ys] = low
        x_far[ys] = low
    if x and ex == columns - 1:
        high = sum(float(x_high[i]) * tile[i] for i in range(8))
        x_near[ys] = jnp.where(even[0], high, x_near[ys])
        x_far[ys] = jnp.where(even[0], x_far[ys], high)
    if y and e == 0:
        low = jnp.sum(tile * y_low, axis=1)
        y_near[rows] = low
        y_far[rows] = low
    if y and e == count - 1:
        high = jnp.sum(tile * y_high, axis=1)
        y_near[rows] = jnp.where(even[1], high, y_near[rows])
        y_far[rows] = jnp.where(even[1], y_far[rows], high)


def parity(even_ref):
    return even_ref[0] > 0.5, even_ref[1] > 0.5


def even_rows(even_ref):
    return even_ref[0, 0:1] > 0.5, even_ref[1, 0:1] > 0.5


def before_of(even, near, far):
    return jnp.where(even, far, near)


def after_of(even, near, far):
    return jnp.where(even, near, far)


def with_faces(tile, ex, e, columns, count, received, even, edges, weight_x=None, weight_y=None, mask=None):
    x_far, x_near, y_far, y_near = received
    rows, ys = pl.ds(8 * ex, 8), pl.ds(8 * e, 8)

    def weighted(face, weight):
        return face if weight is None else face * weight

    if e == 0:
        face = before_of(even[1], y_near[rows], y_far[rows])
        face = spread_rows(face) * weighted(edges[0], weight_y)
        tile = tile + weighted(face, mask)
    if e == count - 1:
        face = after_of(even[1], y_near[rows], y_far[rows])
        face = spread_rows(face) * weighted(edges[1], weight_y)
        tile = tile + weighted(face, mask)
    if ex == 0:
        face = before_of(even[0], x_near[ys], x_far[ys])
        face = weighted(face, weight_x) if mask is None else weighted(face, weight_x) * mask[0]
        tile = jnp.concatenate([tile[0:1] + face[None], tile[1:]], axis=0)
    if ex == columns - 1:
        face = after_of(even[0], x_near[ys], x_far[ys])
        face = weighted(face, weight_x) if mask is None else weighted(face, weight_x) * mask[7]
        tile = jnp.concatenate([tile[:7], tile[7:8] + face[None]], axis=0)
    return tile


def split_rows(block_rows):
    return [block_rows[i] for i in range(8)]


def load_local(old_far, step_far, even_ref, out, x_near, x_far, y_near, y_far, old, step, arrived):
    columns, count, depth = out.shape[1] // 8, out.shape[2] // 8, out.shape[3]
    copies = [pltpu.make_async_copy(step_far, step, arrived.at[4])]
    copies += [pltpu.make_async_copy(old_far.at[i], old.at[i], arrived.at[i]) for i in range(4)]
    for copy in copies:
        copy.start()
    even, edges = parity(even_ref), row_marks()
    row = lax.broadcasted_iota(jnp.int32, (8, depth), 0)
    lane = lax.broadcasted_iota(jnp.int32, (8, depth), 1)
    place = lane & 7
    after = jnp.where((place == 0) & (lane > 0), 1.0, 0.0)
    before_z = jnp.where((place == 7) & (lane < depth - 1), 1.0, 0.0)
    plane = by_place(WEIGHTS, row) * by_place(WEIGHTS, place)
    mass = jnp.stack([float(w) * plane for w in WEIGHTS])
    for field in (4, 0, 1, 2, 3):
        if field != 3:
            copies[0 if field == 4 else field + 1].wait()
        if field == 2:
            copies[4].wait()
        before = [None] * count
        for ex in range(columns):
            rows = pl.ds(8 * ex, 8)
            parts = []
            for e in range(count):
                ys = pl.ds(8 * e, 8)
                value = step[rows, ys]
                if field < 4:
                    value = value * old[field, rows, ys]
                if field == 2:
                    value = value + COUPLING * old[3, rows, ys]
                if field == 3:
                    value = value - STRATIFY * old[2, rows, ys]
                value = value * mass
                value = (
                    value
                    + after * pltpu.roll(value, 1, axis=2)
                    + before_z * pltpu.roll(value, depth - 1, axis=2)
                )
                parts.append(value)
            parts = join_y(parts, edges[0], edges[1])
            for e in range(count):
                ys = pl.ds(8 * e, 8)
                out[field, rows, ys] = parts[e]
                if ex:
                    out[field, 8 * ex, ys] += before[e]
                    out[field, 8 * ex - 1, ys] += parts[e][0]
                before[e] = parts[e][7]
        for e in range(count):
            ys = pl.ds(8 * e, 8)
            low, high = out[field, 0, ys], out[field, 8 * columns - 1, ys]
            x_near[field, ys] = jnp.where(even[0], high, low)
            x_far[field, ys] = jnp.where(even[0], low, high)
        for ex in range(columns):
            rows = pl.ds(8 * ex, 8)
            low = out[field, rows, pl.ds(0, 8)][:, 0]
            high = out[field, rows, pl.ds(8 * count - 8, 8)][:, 7]
            y_near[field, rows] = jnp.where(even[1], high, low)
            y_far[field, rows] = jnp.where(even[1], low, high)


def stiff_terms(tiles, stiff_y, stiff_z):
    x_rows = [along_x(split_rows(t), STIFF) for t in tiles]
    y_parts = [along_y(t, stiff_y) for t in tiles]
    z_all = along_z(jnp.concatenate(tiles, axis=0), stiff_z[...])
    z_parts = [z_all[8 * e : 8 * e + 8] for e in range(len(tiles))]
    return x_rows, y_parts, z_parts


def field_faces(c, ex, e, columns, count, tile, even, ends, slope_ends, faces):
    store_faces(ex, e, columns, count, tile, even, ends, [f.at[c] for f in faces])
    slopes = [f.at[4] for f in faces]
    if isinstance(c, int):
        store_faces(ex, e, columns, count, tile, even, slope_ends, slopes, c == 0, c == 1)
        return

    @pl.when(c == 0)
    def _():
        store_faces(ex, e, columns, count, tile, even, slope_ends, slopes, True, False)

    @pl.when(c == 1)
    def _():
        store_faces(ex, e, columns, count, tile, even, slope_ends, slopes, False, True)


def start_field(local, boundary, x_far, x_near, y_far, y_near, even_ref, right, *faces):
    columns, count = right.shape[1] // 8, right.shape[2] // 8
    even, edges = parity(even_ref), row_marks()
    received = (x_far, x_near, y_far, y_near)
    ends, slope_ends = end_rows(STIFF), end_rows(SLOPE)
    for c in range(4):
        for ex in range(columns):
            for e in range(count):
                rows, ys = pl.ds(8 * ex, 8), pl.ds(8 * e, 8)
                tile = with_faces(local[c, rows, ys], ex, e, columns, count, [r.at[c] for r in received],
                                  even, edges)
                tile = tile * boundary[rows, ys].astype(jnp.float32)
                right[c, rows, ys] = tile
                field_faces(c, ex, e, columns, count, tile, even, ends, slope_ends, faces)
    even = even_rows(even_ref)
    near, far = faces[2:]
    near[5] = jnp.zeros(near.shape[1:], jnp.float32)
    far[5] = jnp.zeros(far.shape[1:], jnp.float32)
    for xi, side in enumerate((before_of, after_of)):
        for field in range(5):
            low, high = [
                side(even[0], x_near[field, y : y + 1], x_far[field, y : y + 1]) for y in (0, 8 * count - 1)
            ]
            row = 8 * xi + field
            near[5, row : row + 1] = jnp.where(even[1], high, low)
            far[5, row : row + 1] = jnp.where(even[1], low, high)


def pick(c, values):
    out = jnp.float32(values[0])
    for i in range(1, 4):
        out = jnp.where(c == i, jnp.float32(values[i]), out)
    return out


def start_sums(scales, rates, local, boundary, x_far, x_near, y_far, y_near, even_ref, right, summed, share, stiff_y,
               stiff_z, reaction, free, ahead):
    columns, count = ahead.shape[1] // 8, ahead.shape[2] // 8
    even, edges = parity(even_ref), row_marks()
    received = [r.at[4] for r in (x_far, x_near, y_far, y_near)]
    for ex in range(columns):
        for e in range(count):
            rows, ys = pl.ds(8 * ex, 8), pl.ds(8 * e, 8)
            reaction[rows, ys] = with_faces(local[4, rows, ys], ex, e, columns, count, received, even, edges)
            free[rows, ys] = boundary[rows, ys].astype(jnp.float32)
    basis_sums(scales, rates, right, None, reaction, free, summed, share, stiff_y, stiff_z, ahead)


def basis_sums(scales, rates, newest, older, reaction, free, summed, share, stiff_y, stiff_z, ahead, dots=None, first=None):
    columns, count = ahead.shape[1] // 8, ahead.shape[2] // 8
    edges = row_marks()
    double = 1.0 if older is None else 2.0

    def component(c, carry):
        scale, rate = pick(c, [double * v for v in scales]), pick(c, [double * v for v in rates])
        same = jnp.zeros((8, 128), jnp.float32)
        cross = jnp.zeros((8, 128), jnp.float32)
        start = jnp.zeros((8, 128), jnp.float32)
        state = None
        for ex in range(columns):
            rows = pl.ds(8 * ex, 8)
            tiles = []
            for e in range(count):
                ys = pl.ds(8 * e, 8)
                tile = newest[c, rows, ys]
                if older is not None:
                    weighted = tile * share[...]
                    same = same + jnp.sum(weighted * tile, axis=0)
                    cross = cross + jnp.sum(weighted * older[c, rows, ys], axis=0)
                if first is not None:
                    start = start + jnp.sum(older[c, rows, ys] * older[c, rows, ys] * share[...], axis=0)
                tiles.append(tile)
            x_rows, y_parts, z_parts = stiff_terms(tiles, stiff_y, stiff_z)

            def finish(e, part):
                ys = pl.ds(8 * e, 8)
                value = scale * part + (rate * reaction[rows, ys] - double) * tiles[e]
                value = value * free[rows, ys]
                return value if older is None else value - older[c, rows, ys]

            state = emit_column(ex, x_rows, y_parts, z_parts, summed, edges, ahead.at[c], state, finish,
                                lambda row, ys: scale * free[row, ys])
        if older is not None:
            dots[pl.ds(c, 1)] = jnp.sum(same, axis=0, keepdims=True)
            dots[pl.ds(c + 4, 1)] = jnp.sum(cross, axis=0, keepdims=True)
        if first is not None:
            first[pl.ds(c, 1)] = jnp.sum(start, axis=0, keepdims=True)
            first[pl.ds(c + 4, 1)] = jnp.zeros((1, 128), jnp.float32)
        return carry

    lax.fori_loop(0, 4, component, 0)


def next_field(c, ex, e, ahead, free, received, scale, summed, edges, even, columns, count):
    rows, ys = pl.ds(8 * ex, 8), pl.ds(8 * e, 8)
    return with_faces(ahead[c, rows, ys], ex, e, columns, count, [r.at[c] for r in received], even, edges,
                      summed[0, 0], summed[1], scale * free[rows, ys])


def grow_field(scales, ahead, free, x_far, x_near, y_far, y_near, even_ref, summed, out, *faces):
    received = (x_far, x_near, y_far, y_near)
    columns, count = out.shape[1] // 8, out.shape[2] // 8
    even, edges = parity(even_ref), row_marks()
    ends, slope_ends = end_rows(STIFF), end_rows(SLOPE)
    for c in range(4):
        for ex in range(columns):
            for e in range(count):
                tile = next_field(c, ex, e, ahead, free, received, scales[c], summed, edges, even, columns, count)
                out[c, pl.ds(8 * ex, 8), pl.ds(8 * e, 8)] = tile
                field_faces(c, ex, e, columns, count, tile, even, ends, slope_ends, faces)


def second_field(scales, rates, ahead, free, x_far0, x_near0, y_far0, y_near0, x_far, x_near, y_far, y_near, even_ref,
                 summed, stiff_z, right_in, reaction_in, out, right, reaction, sx_far, sx_near, sy_far, sy_near,
                 x_near_out, x_far_out, y_near_out, y_far_out, lines, depth_lines):
    columns, count = out.shape[1] // 8, out.shape[2] // 8
    even, edges, even_row = parity(even_ref), row_marks(), even_rows(even_ref)
    received = (x_far, x_near, y_far, y_near)
    faces = (x_near_out, x_far_out, y_near_out, y_far_out)
    ends, slope_ends = end_rows(STIFF), end_rows(SLOPE)
    end_x, end_y = (0, 8 * columns - 1), (0, 8 * count - 1)
    sides = (before_of, after_of)
    corners = [(xi, yi) for xi in (0, 1) for yi in (0, 1)]

    def at(array, xi, yi):
        return array[end_x[xi], end_y[yi] : end_y[yi] + 1]

    def diagonal(field, xi, yi):
        row = 8 * xi + field
        return sides[yi](even_row[1], y_near[5, row : row + 1], y_far[5, row : row + 1])

    def beside(field, xi, yi):
        row = end_y[yi]
        return sides[xi](even_row[0], x_near0[field, row : row + 1], x_far0[field, row : row + 1])

    def beyond(field, xi, yi):
        row = end_x[xi]
        return sides[yi](even_row[1], y_near0[field, row : row + 1], y_far0[field, row : row + 1])

    for c in range(4):
        for n, (xi, yi) in enumerate(corners):
            lines[4 * c + n : 4 * c + n + 1] = diagonal(c, xi, yi) * at(free, xi, yi)
    depth_lines[...] = jnp.dot(
        lines[...], stiff_z[...], precision=HIGHEST_PRECISION, preferred_element_type=jnp.float32
    )

    def missed(c, ex, e):
        found = []
        for n, (xi, yi) in enumerate(corners):
            cx, ce, sx, sy = (columns - 1) * xi, (count - 1) * yi, 7 * xi, 7 * yi
            line = lines[4 * c + n : 4 * c + n + 1]
            weight_x, weight_y = summed[0, 0, sy : sy + 1], summed[1, sx, 0:1]
            along = scales[c] * line * weight_x
            across = scales[c] * line * weight_y
            if ex == cx and e == ce:
                for i in range(8):
                    found.append((i, float(STIFF[i, sx]) * along * edges[yi]))
                found.append((sx, across * ends[1][yi]))
                side = beyond(c, xi, yi) * weight_x + beside(c, xi, yi) * weight_y
                side = float(STIFF[0, 0]) * side
                depth = depth_lines[4 * c + n : 4 * c + n + 1] * summed[2, sx, sy : sy + 1]
                gained = diagonal(4, xi, yi)
                node = scales[c] * (side + depth)
                node = node + (rates[c] * (at(reaction_in, xi, yi) + gained) - 1.0) * line
                node = node + rates[c] * gained * at(right_in.at[c], xi, yi)
                found.append((sx, node * edges[yi]))
            elif e == ce and ex == cx + 1 - 2 * xi:
                found.append((sx, float(STIFF[7 - sx, sx]) * along * edges[yi]))
            elif ex == cx and e == ce + 1 - 2 * yi:
                found.append((sx, float(STIFF[7 - sy, sy]) * across * edges[yi]))
        return found

    for c in range(4):
        for ex in range(columns):
            for e in range(count):
                rows, ys = pl.ds(8 * ex, 8), pl.ds(8 * e, 8)
                tile = next_field(c, ex, e, ahead, free, received, scales[c], summed, edges, even, columns, count)
                found = missed(c, ex, e)
                if found:
                    parts = []
                    for i in range(8):
                        extra = [t for row, t in found if row == i]
                        parts.append(tile[i] + sum(extra) * free[8 * ex + i, ys] if extra else tile[i])
                    tile = jnp.stack(parts)
                out[c, rows, ys] = tile
                field_faces(c, ex, e, columns, count, tile, even, ends, slope_ends, faces)

    sx_far[...], sx_near[...], sy_far[...], sy_near[...] = x_far[4], x_near[4], y_far[4], y_near[4]
    low, high = float(SLOPE[7, 7]), float(SLOPE[0, 0])
    for i in (0, 1):
        y, x = end_y[i], end_x[i]
        before = low * beyond(0, 0, i) * at(free, 0, i)
        after = high * beyond(0, 1, i) * at(free, 1, i)
        sx_near[y : y + 1] += jnp.where(even_row[0], after, before)
        sx_far[y : y + 1] += jnp.where(even_row[0], before, after)
        before = low * beside(1, i, 0) * at(free, i, 0)
        after = high * beside(1, i, 1) * at(free, i, 1)
        sy_near[x : x + 1] += jnp.where(even_row[1], after, before)
        sy_far[x : x + 1] += jnp.where(even_row[1], before, after)
    for n, (xi, yi) in enumerate(corners):
        x, y = end_x[xi], end_y[yi]
        reaction[x, y : y + 1] = at(reaction_in, xi, yi) + diagonal(4, xi, yi)
        for c in range(4):
            right[c, x, y : y + 1] = at(right_in.at[c], xi, yi) + lines[4 * c + n : 4 * c + n + 1]


def last_field(scales, rates, *refs):
    refs = list(refs)
    ahead, newest, reaction, free, *received, even_ref, summed, share, stiff_y, stiff_z, local = refs[:14]
    dots, (out, sums, *slopes) = refs[14:19], refs[19:]
    columns, count = out.shape[1] // 8, out.shape[2] // 8
    even, edges = parity(even_ref), row_marks()
    slope_ends = end_rows(SLOPE)
    for i in range(1, ITERS - 1):
        sums[i] = dots[i][...]
    for c in range(4):
        scale, rate = scales[c], rates[c]
        same = jnp.zeros((8, 128), jnp.float32)
        cross = jnp.zeros((8, 128), jnp.float32)
        work = jnp.zeros((8, 128), jnp.float32)
        for ex in range(columns):
            rows = pl.ds(8 * ex, 8)
            tiles = []
            for e in range(count):
                ys = pl.ds(8 * e, 8)
                tile = next_field(c, ex, e, ahead, free, received, 2.0 * scale, summed, edges, even, columns, count)
                now = newest[c, rows, ys]
                out[c, rows, ys] = tile
                store_faces(ex, e, columns, count, tile, even, slope_ends, slopes, c == 0, c == 1)
                weighted = tile * share[...]
                same = same + jnp.sum(weighted * tile, axis=0)
                cross = cross + jnp.sum(weighted * now, axis=0)
                extra = (rate * reaction[rows, ys] - 1.0) * tile
                work = work + jnp.sum(weighted * extra, axis=0)
                tiles.append(tile)
            x_rows, y_parts, z_parts = stiff_terms(tiles, stiff_y, stiff_z)
            for e in range(count):
                term = jnp.stack(x_rows[e]) * local[0] + y_parts[e] * local[1] + z_parts[e] * local[2]
                work = work + scale * jnp.sum(term * tiles[e], axis=0)
        sums[ITERS - 1, c : c + 1] = jnp.sum(same, axis=0, keepdims=True)
        sums[ITERS - 1, c + 4 : c + 5] = jnp.sum(cross, axis=0, keepdims=True)
        sums[0, c : c + 1] = dots[0][c : c + 1]
        sums[0, c + 4 : c + 5] = jnp.sum(work, axis=0, keepdims=True)


def finish_fields(halves, gain, *refs):
    sums, *basis = refs[: ITERS + 1]
    refs = refs[ITERS + 1 :]
    slopes = [refs[:4]]
    slopes += [[r.at[4] for r in refs[4 * k : 4 * k + 4]] for k in range(1, ITERS - 1)]
    refs = refs[4 * ITERS - 4 :]
    slopes.append(refs[:4])
    even_ref, free, summed, slope_y, slope_z, inverse = refs[4:10]
    fields, remainder, update, *faces = refs[10:17]
    weights, raw, *joined = refs[17:]
    columns, count = raw.shape[0] // 8, raw.shape[1] // 8
    even, edges = parity(even_ref), row_marks()
    ends = end_rows(STIFF)
    total = [jnp.broadcast_to(jnp.sum(sums[i], axis=1, keepdims=True), (8, 128)) for i in range(ITERS)]
    other = [pltpu.roll(t, 4, axis=0) for t in total]
    row = lax.broadcasted_iota(jnp.int32, (8, 128), 0)
    half = jnp.full((8, 128), halves[0], jnp.float32)
    for i in range(1, 4):
        half = jnp.where(row == i, halves[i], half)
    moments = [total[0], other[1]]
    for level in range(2, 2 * ITERS - 1):
        inner = total[level // 2] if level % 2 == 0 else other[level // 2 + 1]
        moments.append(2.0 * inner - moments[level % 2])
    top = 2.0 * other[0] - other[5]
    moments.append(2.0 * top - moments[1])
    for i, value in enumerate(conjugate_coefficients(moments, half, half)):
        weights[i] = value

    def combine(c, carry):
        factor = [weights[i, pl.ds(c, 1)] for i in range(ITERS)]
        for x in range(0, 8 * columns, 8):
            rows = pl.ds(x, 8)
            value = basis[0][c, rows] * factor[0][None]
            for i in range(1, ITERS):
                value = value + basis[i][c, rows] * factor[i][None]
            fields[c, rows] = value
        return carry

    lax.fori_loop(0, 4, combine, 0)
    for n in range(4):
        c = n // 2
        joined[n][...] = sum(slopes[i][n][...] * weights[i, c : c + 1] for i in range(ITERS))
    state = None
    for ex in range(columns):
        rows = pl.ds(8 * ex, 8)
        x_rows, y_parts, z_tiles = [], [], []
        for e in range(count):
            ys = pl.ds(8 * e, 8)
            x_rows.append(along_x(split_rows(fields[0, rows, ys]), SLOPE))
            y_parts.append(along_y(fields[1, rows, ys], slope_y))
            z_tiles.append(fields[2, rows, ys])
        z_all = along_z(jnp.concatenate(z_tiles, axis=0), slope_z[...])
        z_parts = [z_all[8 * e : 8 * e + 8] for e in range(count)]
        state = emit_column(ex, x_rows, y_parts, z_parts, summed, edges, raw, state)
    for ex in range(columns):
        for e in range(count):
            rows, ys = pl.ds(8 * ex, 8), pl.ds(8 * e, 8)
            tile = with_faces(raw[rows, ys], ex, e, columns, count, joined, even, edges, summed[0, 0], summed[1])
            left = -tile * free[rows, ys]
            change = gain * inverse[...] * left
            remainder[rows, ys] = left
            update[rows, ys] = change
            store_faces(ex, e, columns, count, change, even, ends, faces)


def pressure_sums(update, summed, shift, stiff_y, stiff_z, raw):
    columns, count = raw.shape[0] // 8, raw.shape[1] // 8
    edges = row_marks()
    state = None
    for ex in range(columns):
        rows = pl.ds(8 * ex, 8)
        tiles = [update[rows, pl.ds(8 * e, 8)] for e in range(count)]
        x_rows, y_parts, z_parts = stiff_terms(tiles, stiff_y, stiff_z)
        state = emit_column(ex, x_rows, y_parts, z_parts, summed, edges, raw, state,
                            lambda e, part: part + shift[...] * tiles[e])


def pressure_step(last, keep, gain, *refs):
    raw, free, *received, even_ref, summed, inverse, remainder_in, update_in, pressure_in = refs[:12]
    if last:
        pressure_far, pressure, left_here = refs[12:]
    else:
        pressure, remainder, update, *faces = refs[12:]
    columns, count = raw.shape[0] // 8, raw.shape[1] // 8
    copies = []
    even, edges = parity(even_ref), row_marks()
    ends = end_rows(STIFF)
    for ex in range(columns):
        for e in range(count):
            rows, ys = pl.ds(8 * ex, 8), pl.ds(8 * e, 8)
            tile = with_faces(raw[rows, ys], ex, e, columns, count, received, even, edges,
                              summed[0, 0], summed[1])
            left = remainder_in[rows, ys] - tile * free[rows, ys]
            change = gain * inverse[...] * left + keep * update_in[rows, ys]
            pressure[rows, ys] = pressure_in[rows, ys] + change
            if not last:
                remainder[rows, ys] = left
                update[rows, ys] = change
                store_faces(ex, e, columns, count, change, even, ends, faces)
        if last:
            rows = pl.ds(8 * ex, 8)
            copies.append(pltpu.make_async_copy(pressure.at[rows], pressure_far.at[rows], left_here.at[ex]))
            copies[-1].start()
    for copy in copies:
        copy.wait()


VMEM_BYTES = 24 * 1024 * 1024


def call(kernel, name, outs, *args, scratch=(), cost=None, far_in=0, far_out=0, copies=0, aliases=()):
    held, far = pl.BlockSpec(memory_space=pltpu.VMEM), pl.BlockSpec(memory_space=pltpu.HBM)
    scratch_shapes = [pltpu.VMEM(s, jnp.float32) for s in scratch]
    if copies:
        scratch_shapes.append(pltpu.SemaphoreType.DMA((copies,)))
    return pl.pallas_call(
        kernel,
        name=name,
        out_shape=[jax.ShapeDtypeStruct(s, jnp.float32) for s in outs],
        in_specs=[far] * far_in + [held] * (len(args) - far_in),
        out_specs=[far] * far_out + [held] * (len(outs) - far_out),
        scratch_shapes=scratch_shapes,
        cost_estimate=cost,
        input_output_aliases=dict(aliases),
        compiler_params=pltpu.CompilerParams(vmem_limit_bytes=VMEM_BYTES),
    )(*[pltpu.with_memory_space_constraint(a, pltpu.HBM) for a in args[:far_in]], *args[far_in:])


def busy(bytes_accessed):
    return pl.CostEstimate(flops=0, bytes_accessed=bytes_accessed, transcendentals=0)


def swap_near(axis, face):
    return lax.ppermute(face, axis, [(i, i ^ 1) for i in range(lax.axis_size(axis))])


def swap_far(axis, face):
    size = lax.axis_size(axis)
    return lax.ppermute(face, axis, [(i, far_partner(i, size)) for i in range(size)])


def swap_all(x_near, x_far, y_near, y_far):
    y_far = swap_far("gy", y_far)
    x_far = swap_far("gx", x_far)
    x_near = swap_near("gx", x_near)
    y_near = swap_near("gy", y_near)
    return x_far, x_near, y_far, y_near


def far_partner(i, size):
    return (i + 1 if i % 2 else i - 1) % size


def partner_sum(values, axis, partners, riders):
    size, count = lax.axis_size(axis), values.shape[0]
    heard, faces = [], []
    for partner, rider in zip(partners, riders):
        load = values if rider is None else jnp.concatenate([values, rider])
        load = lax.ppermute(load, axis, [(i, partner(i)) for i in range(size)])
        heard.append(load[:count])
        if rider is not None:
            faces.append(load[count:])
    if len(heard) == 1:
        return values + heard[0], faces
    return (values + heard[0]) + (heard[1] + heard[2]), faces


def all_sum(values, axis, near, far):
    size = lax.axis_size(axis)
    half = size // 2

    def to_near(i):
        return i ^ 1

    def to_far(i):
        return far_partner(i, size)

    def across(i):
        return (i + half) % size

    def far_across(i):
        return across(to_far(i))

    if size == 4:
        values, (far, near) = partner_sum(values, axis, (to_far, to_near, across), (far, near, None))
        return values, near, far
    if size == 2:
        values, (far,) = partner_sum(values, axis, (to_far,), (far,))
        return values, lax.ppermute(near, axis, [(i, to_near(i)) for i in range(size)]), far
    values, (far,) = partner_sum(values, axis, (to_far, across, far_across), (far, None, None))
    values, (near,) = partner_sum(values, axis, (to_near,), (near,))
    bit = 4
    while bit < half:
        values, _ = partner_sum(values, axis, (lambda i, bit=bit: i ^ bit,), (None,))
        bit *= 2
    return values, near, far


def conjugate_coefficients(moments, centre, half):
    remaining, towards = list(moments), list(moments)
    one, zero = jnp.ones_like(moments[0]), jnp.zeros_like(moments[0])
    direction = [one] + [zero] * ITERS
    residual = list(direction)
    total = [zero] * ITERS
    for step in range(ITERS):
        count = len(towards) - 1
        image = []
        for level in range(count):
            side = (
                half * towards[1] if level == 0 else 0.5 * half * (towards[level + 1] + towards[level - 1])
            )
            image.append(centre * towards[level] + side)
        alpha = remaining[step] / image[step]
        total = [total[i] + alpha * direction[i] for i in range(ITERS)]
        if step == ITERS - 1:
            break
        applied = []
        for i in range(ITERS + 1):
            term = centre * direction[i]
            if i >= 1:
                term = term + (half if i == 1 else 0.5 * half) * direction[i - 1]
            if i < ITERS:
                term = term + 0.5 * half * direction[i + 1]
            applied.append(term)
        residual = [residual[i] - alpha * applied[i] for i in range(ITERS + 1)]
        following = [remaining[i] - alpha * image[i] for i in range(count)]
        beta = -alpha * (half if step == 0 else 0.5 * half) * following[step + 1] / remaining[step]
        towards = [following[i] + beta * towards[i] for i in range(count)]
        direction = [residual[i] + beta * direction[i] for i in range(ITERS + 1)]
        remaining = following
    return total


def on_device(old_fields, inverse_step, boundary):
    x, y, z = inverse_step.shape
    t = Tables(z)
    brick, four = (x, y, z), (4, x, y, z)
    faces = [(y, z)] * 2 + [(x, z)] * 2
    faces5 = [(5,) + f for f in faces]
    faces_back = [(y, z)] * 2 + [(x, z)] * 2

    place = [lax.axis_index(a) % 2 == 0 for a in ("gx", "gy")]
    even = jnp.stack([jnp.full((8, 128), p, jnp.float32) for p in place])

    local, x_near, x_far, y_near, y_far = call(
        load_local, "local_right", [(5,) + brick] + faces5, old_fields, inverse_step, even,
        scratch=[four, brick], far_in=2, copies=5,
    )
    received = swap_all(x_near, x_far, y_near, y_far)

    top = INTERVAL_SHARE * np.array([spectrum_top(c) for c in DIFFUSE])
    halves = [float(v) for v in 0.5 * top]
    scales = [float(v) for v in np.array(DIFFUSE) / (0.5 * top)]
    rates = [float(v) for v in 1.0 / (0.5 * top)]

    relayed = [(6,) + f for f in faces[2:]]
    right, *sent = call(start_field, "right_field", [four] + faces5[:2] + relayed, local, boundary, *received, even)
    heard = [swap_all(*sent)]
    reaction, free, ahead = call(
        functools.partial(start_sums, scales, rates), "right_sums", [brick, brick, four],
        local, boundary, *received, even, right, t.summed, t.share, t.stiff_y, t.stiff_z, cost=busy(8 << 20),
    )
    field, right, reaction, *slopes = call(
        functools.partial(second_field, scales, rates), "second_field", [four, four, brick] + faces_back + faces5,
        ahead, free, *received, *heard[0], even, t.summed, t.stiff_z, right, reaction,
        scratch=[(16, z)] * 2, aliases=[(13, 1), (14, 2)],
    )
    slopes, sent = slopes[:4], slopes[4:]
    heard[0] = slopes
    basis, sums = [right, field], []
    for k in range(1, ITERS - 1):
        heard.append(swap_all(*sent))
        outs = [four, (8, 128)] + ([(8, 128)] if k == 1 else [])
        ahead, *dots = call(
            functools.partial(basis_sums, scales, rates), "basis_sums", outs,
            basis[-1], basis[-2], reaction, free, t.summed, t.share, t.stiff_y, t.stiff_z, cost=busy(8 << 20),
        )
        sums += dots[::-1]
        if k == ITERS - 2:
            break
        field, *sent = call(
            functools.partial(grow_field, [2.0 * v for v in scales]), "basis_field", [four] + faces5,
            ahead, free, *heard[-1], even, t.summed,
        )
        basis.append(field)
    field, sums, x_near, x_far, y_near, y_far = call(
        functools.partial(last_field, scales, rates), "last_field", [four, (ITERS, 8, 128)] + faces,
        ahead, basis[-1], reaction, free, *heard[-1], even, t.summed, t.share, t.stiff_y, t.plain_z, t.local, *sums,
    )
    basis.append(field)
    sums = sums.reshape(ITERS * 8, z)
    sums, x_near, x_far = all_sum(sums, "gx", x_near, x_far)
    sums, y_near, y_far = all_sum(sums, "gy", y_near, y_far)
    sums = sums.reshape(ITERS, 8, z)
    slopes = (x_far, x_near, y_far, y_near)

    centre, half = chebyshev_bounds()
    factor = centre / half
    damping = 1.0 / factor
    fields, remainder, update, *sent = call(
        functools.partial(finish_fields, halves, 1.0 / centre), "fields", [four, brick, brick] + faces,
        sums, *basis, *[a for h in heard for a in h], *slopes, even, free, t.summed, t.slope_y, t.slope_z, t.inverse,
        scratch=[(ITERS, 8, 128), brick] + faces,
    )
    pressure = update
    for step in range(1, CHEB):
        last = step == CHEB - 1
        received = swap_all(*sent)
        (raw,) = call(
            pressure_sums, "pressure_sums", [brick],
            update, t.summed, t.shift, t.stiff_y, t.stiff_z, cost=busy(2 << 20),
        )
        following = 1.0 / (2.0 * factor - damping)
        keep, gain = following * damping, 2.0 * following / half
        damping = following
        kernel = functools.partial(pressure_step, last, keep, gain)
        args = [raw, free, *received, even, t.summed, t.inverse, remainder, update, pressure]
        if last:
            (pressure,) = call(
                kernel, "pressure_last", [brick], *args, scratch=[brick], far_out=1, copies=x // 8
            )
            break
        pressure, remainder, update, *sent = call(kernel, "pressure_step", [brick] * 3 + faces, *args)
    return (fields, pressure)


def solution(mesh):
    return jax.shard_map(
        on_device,
        mesh=mesh,
        in_specs=(P(None, "gx", "gy", None), P("gx", "gy", None), P("gx", "gy", None)),
        out_specs=(P(None, "gx", "gy", None), P("gx", "gy", None)),
        check_vma=False,
    )
```

```python
import functools

import jax
import jax.numpy as jnp
import ml_dtypes
import numpy as np
from jax import lax
from jax.experimental import pallas as pl
from jax.experimental.pallas import tpu as pltpu
from jax.sharding import PartitionSpec as P

ITERS = 6
CHEB = 6

SIGMA_SHIFT = 0.5
DIFFUSE = (1.0, 1.0, 1.0, 1.4)
COUPLING = 1.0
STRATIFY = 1.0
SPREAD = 20.0
STEP_MAX = 64.0
INTERVAL_SHARE = 0.82
HIGHEST_PRECISION = lax.Precision.HIGHEST
LOBATTO_POINTS = (
    -1.0,
    -0.8717401485096066,
    -0.5917001814331423,
    -0.2092992179024789,
    0.2092992179024789,
    0.5917001814331423,
    0.8717401485096066,
    1.0,
)


def legendre_value(points, degree):
    previous = points * 0.0 + 1.0
    current = points
    for order in range(1, degree):
        following = ((2 * order + 1) * points * current - order * previous) / (order + 1)
        previous = current
        current = following
    return current


def quadrature_tables():
    degree = 7
    points = np.array(LOBATTO_POINTS)
    values = legendre_value(points, degree)
    weights = 2.0 / (degree * (degree + 1) * values * values)
    derive = np.zeros((degree + 1, degree + 1))
    for row_index in range(degree + 1):
        for column_index in range(degree + 1):
            if row_index != column_index:
                derive[row_index, column_index] = values[row_index] / (
                    values[column_index] * (points[row_index] - points[column_index])
                )
    derive[0, 0] = -degree * (degree + 1) / 4.0
    derive[degree, degree] = degree * (degree + 1) / 4.0
    stiffness_table = derive.T @ (weights[:, None] * derive)
    return (weights, derive, stiffness_table)


WEIGHTS, DERIVE, STIFF = quadrature_tables()
SLOPE = WEIGHTS[:, None] * DERIVE
COPIES = np.where(np.arange(8) % 7 == 0, 2.0, 1.0)


def chebyshev_bounds():
    weight_matrix = np.eye(8) * WEIGHTS

    def kron3(a, b, c):
        return np.kron(np.kron(a, b), c)

    element_matrix = (
        kron3(STIFF, weight_matrix, weight_matrix)
        + kron3(weight_matrix, STIFF, weight_matrix)
        + kron3(weight_matrix, weight_matrix, STIFF)
        + SIGMA_SHIFT * kron3(weight_matrix, weight_matrix, weight_matrix)
    )
    bounds_ratio = np.sum(np.abs(element_matrix), axis=1) / np.diagonal(element_matrix)
    upper_bound = float(np.max(bounds_ratio))
    lower_bound = upper_bound / SPREAD
    return ((upper_bound + lower_bound) / 2.0, (upper_bound - lower_bound) / 2.0)


def spectrum_top(diffuse):
    root = np.sqrt(COPIES)
    stiff = root[:, None] * STIFF * root[None, :]
    weight = np.diag(WEIGHTS * COPIES)

    def kron3(a, b, c):
        return np.kron(np.kron(a, b), c)

    element = diffuse * (
        kron3(stiff, weight, weight) + kron3(weight, stiff, weight) + kron3(weight, weight, stiff)
    ) + STEP_MAX * kron3(weight, weight, weight)
    return float(np.linalg.eigvalsh(element)[-1])


def line_sums(table, length):
    matrix = np.kron(np.eye(length // 8), table)
    total = matrix.copy()
    for start in range(8, length, 8):
        total[start] += matrix[start - 1]
        total[start - 1] += matrix[start]
    return total


def depth_line(vector, length):
    line = np.tile(vector * COPIES, length // 8)
    line[0] = vector[0]
    line[-1] = vector[-1]
    return line


def f32(array):
    return np.ascontiguousarray(array, np.float32)


def rolled_rows(table):
    out = np.zeros((8, 8, 128))
    for shift in range(8):
        for row in range(8):
            out[shift, row] = table[row, (row - shift) % 8]
    return out


def block(a, b, c):
    return a[:, None, None] * b[:, None] * c


def parts_of(matrix):
    rest, parts = f32(matrix), []
    for _ in range(3):
        parts.append(rest.astype(ml_dtypes.bfloat16))
        rest = rest - parts[-1].astype(np.float32)
    hi, mid, lo = parts
    return np.block([[hi, mid], [hi, mid]]), np.concatenate([hi, lo])


class Tables:
    def __init__(self, depth):
        ones8, ones = np.ones(8), np.ones(depth)
        wide = WEIGHTS * COPIES
        deep = depth_line(WEIGHTS, depth)
        flat = np.tile(WEIGHTS, depth // 8)
        stiff = np.diagonal(STIFF)
        wide_s, deep_s = stiff * COPIES, depth_line(stiff, depth)
        share = 1.0 / COPIES
        share_z = np.tile(share, depth // 8)
        share_z[0] = share_z[-1] = 1.0
        self.summed = f32(
            np.stack([block(ones8, wide, deep), block(wide, ones8, deep), block(wide, wide, ones)])
        )
        self.local = f32(
            np.stack(
                [block(ones8, WEIGHTS, flat), block(WEIGHTS, ones8, flat), block(WEIGHTS, WEIGHTS, ones)]
            )
        )
        self.share = f32(block(share, share, share_z))
        diagonal = (
            block(wide_s, wide, deep)
            + block(wide, wide_s, deep)
            + block(wide, wide, deep_s)
            + SIGMA_SHIFT * block(wide, wide, deep)
        )
        self.inverse = f32(1.0 / diagonal)
        self.shift = f32(SIGMA_SHIFT * block(wide, wide, deep))
        self.stiff_y = f32(rolled_rows(STIFF))
        self.slope_y = f32(rolled_rows(SLOPE))
        self.stiff_z = parts_of(line_sums(STIFF, depth).T)
        self.plain_z = parts_of(np.kron(np.eye(depth // 8), STIFF).T)
        self.slope_z = parts_of(line_sums(SLOPE, depth).T)


def row_marks():
    row = lax.broadcasted_iota(jnp.int32, (8, 128), 0)
    return jnp.where(row == 0, 1.0, 0.0), jnp.where(row == 7, 1.0, 0.0)


def by_place(vector, place):
    out = jnp.full(place.shape, float(vector[0]), jnp.float32)
    for i in range(1, 8):
        out = jnp.where(place == i, float(vector[i]), out)
    return out


def along_x(rows, table):
    if np.allclose(table, table[::-1, ::-1]):
        even = 0.5 * (table[:4, :4] + table[:4, :3:-1])
        odd = 0.5 * (table[:4, :4] - table[:4, :3:-1])
        plus = [rows[i] + rows[7 - i] for i in range(4)]
        minus = [rows[i] - rows[7 - i] for i in range(4)]
        out = [None] * 8
        for a in range(4):
            p = sum(float(even[a, b]) * plus[b] for b in range(4))
            m = sum(float(odd[a, b]) * minus[b] for b in range(4))
            out[a], out[7 - a] = p + m, p - m
        return out
    return [sum(float(table[a, b]) * rows[b] for b in range(8)) for a in range(8)]


def along_y(tiles, factors):
    total = factors[0] * tiles
    for shift in range(1, 8):
        total = total + factors[shift] * pltpu.roll(tiles, shift, axis=1)
    return total


def along_z(tiles, matrix):
    wide, rest = matrix
    shape, depth = tiles.shape, tiles.shape[-1]
    flat = tiles.reshape(-1, depth)
    hi = flat.astype(jnp.bfloat16)
    flat = flat - hi.astype(jnp.float32)
    mid = flat.astype(jnp.bfloat16)
    lo = (flat - mid.astype(jnp.float32)).astype(jnp.bfloat16)
    first = jnp.dot(jnp.concatenate([hi, mid], axis=1), wide[...], preferred_element_type=jnp.float32)
    second = jnp.dot(jnp.concatenate([lo, hi], axis=1), rest[...], preferred_element_type=jnp.float32)
    return (first[:, :depth] + (first[:, depth:] + second)).reshape(shape)


def fill_z(out, field, matrix):
    for x in range(0, out.shape[0], 16):
        rows = pl.ds(x, min(16, out.shape[0] - x))
        out[rows] = along_z(field[rows], matrix)


def join_y(parts, low, high):
    out = list(parts)
    for e in range(1, len(parts)):
        out[e - 1] = out[e - 1] + high * pltpu.roll(parts[e], 7, axis=1)
        out[e] = out[e] + low * pltpu.roll(parts[e - 1], 1, axis=1)
    return out


def spread_rows(rows):
    return jnp.broadcast_to(rows[:, None, :], (rows.shape[0], 8, rows.shape[1]))


def column_sums(x_rows, y_parts, z_parts, summed, edges):
    y_parts = join_y(y_parts, edges[0], edges[1])
    return [
        jnp.stack(kx) * summed[0, 0] + ky * summed[1] + kz * summed[2]
        for kx, ky, kz in zip(x_rows, y_parts, z_parts)
    ]


def emit_column(ex, x_rows, y_parts, z_parts, summed, edges, out, state, finish=None, factor=None):
    rows = pl.ds(8 * ex, 8)
    parts = column_sums(x_rows, y_parts, z_parts, summed, edges)
    for e, part in enumerate(parts):
        ys = pl.ds(8 * e, 8)
        out[rows, ys] = part if finish is None else finish(e, part)
        if ex:
            for row, face in ((8 * ex, state[e]), (8 * ex - 1, x_rows[e][0])):
                face = face * summed[0, 0]
                out[row, ys] += face if factor is None else face * factor(row, ys)
    return [r[7] for r in x_rows]


def end_rows(table):
    row = lax.broadcasted_iota(jnp.int32, (8, 128), 0)
    return (table[0], table[7]), (by_place(table[0], row), by_place(table[7], row))


def store_faces(ex, e, columns, count, tile, even, ends, faces, x=True, y=True):
    x_near, x_far, y_near, y_far = faces
    (x_low, x_high), (y_low, y_high) = ends
    rows, ys = pl.ds(8 * ex, 8), pl.ds(8 * e, 8)
    if x and ex == 0:
        low = sum(float(x_low[i]) * tile[i] for i in range(8))
        x_near[ys] = low
        x_far[ys] = low
    if x and ex == columns - 1:
        high = sum(float(x_high[i]) * tile[i] for i in range(8))
        x_near[ys] = jnp.where(even[0], high, x_near[ys])
        x_far[ys] = jnp.where(even[0], x_far[ys], high)
    if y and e == 0:
        low = jnp.sum(tile * y_low, axis=1)
        y_near[rows] = low
        y_far[rows] = low
    if y and e == count - 1:
        high = jnp.sum(tile * y_high, axis=1)
        y_near[rows] = jnp.where(even[1], high, y_near[rows])
        y_far[rows] = jnp.where(even[1], y_far[rows], high)


def parity(even_ref):
    return even_ref[0] > 0.5, even_ref[1] > 0.5


def even_rows(even_ref):
    return even_ref[0, 0:1] > 0.5, even_ref[1, 0:1] > 0.5


def before_of(even, near, far):
    return jnp.where(even, far, near)


def after_of(even, near, far):
    return jnp.where(even, near, far)


def with_faces(tile, ex, e, columns, count, received, even, edges, weight_x=None, weight_y=None, mask=None):
    x_far, x_near, y_far, y_near = received
    rows, ys = pl.ds(8 * ex, 8), pl.ds(8 * e, 8)

    def weighted(face, weight):
        return face if weight is None else face * weight

    if e == 0:
        face = before_of(even[1], y_near[rows], y_far[rows])
        face = spread_rows(face) * weighted(edges[0], weight_y)
        tile = tile + weighted(face, mask)
    if e == count - 1:
        face = after_of(even[1], y_near[rows], y_far[rows])
        face = spread_rows(face) * weighted(edges[1], weight_y)
        tile = tile + weighted(face, mask)
    if ex == 0:
        face = before_of(even[0], x_near[ys], x_far[ys])
        face = weighted(face, weight_x) if mask is None else weighted(face, weight_x) * mask[0]
        tile = jnp.concatenate([tile[0:1] + face[None], tile[1:]], axis=0)
    if ex == columns - 1:
        face = after_of(even[0], x_near[ys], x_far[ys])
        face = weighted(face, weight_x) if mask is None else weighted(face, weight_x) * mask[7]
        tile = jnp.concatenate([tile[:7], tile[7:8] + face[None]], axis=0)
    return tile


def split_rows(block_rows):
    return [block_rows[i] for i in range(8)]


def load_local(old_far, step_far, even_ref, out, x_near, x_far, y_near, y_far, old, step, arrived):
    columns, count, depth = out.shape[1] // 8, out.shape[2] // 8, out.shape[3]
    copies = [pltpu.make_async_copy(step_far, step, arrived.at[4])]
    copies += [pltpu.make_async_copy(old_far.at[i], old.at[i], arrived.at[i]) for i in range(4)]
    for copy in copies:
        copy.start()
    even, edges = parity(even_ref), row_marks()
    row = lax.broadcasted_iota(jnp.int32, (8, depth), 0)
    lane = lax.broadcasted_iota(jnp.int32, (8, depth), 1)
    place = lane & 7
    after = jnp.where((place == 0) & (lane > 0), 1.0, 0.0)
    before_z = jnp.where((place == 7) & (lane < depth - 1), 1.0, 0.0)
    plane = by_place(WEIGHTS, row) * by_place(WEIGHTS, place)
    mass = jnp.stack([float(w) * plane for w in WEIGHTS])
    for field in (4, 0, 1, 2, 3):
        if field != 3:
            copies[0 if field == 4 else field + 1].wait()
        if field == 2:
            copies[4].wait()
        before = [None] * count
        for ex in range(columns):
            rows = pl.ds(8 * ex, 8)
            parts = []
            for e in range(count):
                ys = pl.ds(8 * e, 8)
                value = step[rows, ys]
                if field < 4:
                    value = value * old[field, rows, ys]
                if field == 2:
                    value = value + COUPLING * old[3, rows, ys]
                if field == 3:
                    value = value - STRATIFY * old[2, rows, ys]
                value = value * mass
                value = (
                    value
                    + after * pltpu.roll(value, 1, axis=2)
                    + before_z * pltpu.roll(value, depth - 1, axis=2)
                )
                parts.append(value)
            parts = join_y(parts, edges[0], edges[1])
            for e in range(count):
                ys = pl.ds(8 * e, 8)
                out[field, rows, ys] = parts[e]
                if ex:
                    out[field, 8 * ex, ys] += before[e]
                    out[field, 8 * ex - 1, ys] += parts[e][0]
                before[e] = parts[e][7]
        for e in range(count):
            ys = pl.ds(8 * e, 8)
            low, high = out[field, 0, ys], out[field, 8 * columns - 1, ys]
            x_near[field, ys] = jnp.where(even[0], high, low)
            x_far[field, ys] = jnp.where(even[0], low, high)
        for ex in range(columns):
            rows = pl.ds(8 * ex, 8)
            low = out[field, rows, pl.ds(0, 8)][:, 0]
            high = out[field, rows, pl.ds(8 * count - 8, 8)][:, 7]
            y_near[field, rows] = jnp.where(even[1], high, low)
            y_far[field, rows] = jnp.where(even[1], low, high)


def stiff_terms(ex, tiles, stiff_y, z_sums):
    x_rows = [along_x(split_rows(t), STIFF) for t in tiles]
    y_parts = [along_y(t, stiff_y) for t in tiles]
    z_parts = [z_sums[pl.ds(8 * ex, 8), pl.ds(8 * e, 8)] for e in range(len(tiles))]
    return x_rows, y_parts, z_parts


def square_sum(rows):
    total = 0.0
    for sign in (1.0, -1.0):
        form = 0.5 * (STIFF[:4, :4] + sign * STIFF[:4, :3:-1])
        part = [rows[i] + rows[7 - i] if sign > 0 else rows[i] - rows[7 - i] for i in range(4)]
        for i in range(4):
            pivot = form[i, i]
            if pivot < 1e-12:
                continue
            line = form[i] / np.sqrt(pivot)
            value = sum(float(line[b]) * part[b] for b in range(i, 4))
            total = total + value * value
            form = form - np.outer(line, line)
    return total


def half_y(tiles, factors):
    total = factors[0] * tiles
    for shift in range(1, 5):
        rolled = factors[shift] * pltpu.roll(tiles, shift, axis=1)
        total = total + (rolled if shift == 4 else 2.0 * rolled)
    return total


def field_faces(c, ex, e, columns, count, tile, even, ends, slope_ends, faces):
    store_faces(ex, e, columns, count, tile, even, ends, [f.at[c] for f in faces])
    slopes = [f.at[4] for f in faces]
    if isinstance(c, int):
        store_faces(ex, e, columns, count, tile, even, slope_ends, slopes, c == 0, c == 1)
        return

    @pl.when(c == 0)
    def _():
        store_faces(ex, e, columns, count, tile, even, slope_ends, slopes, True, False)

    @pl.when(c == 1)
    def _():
        store_faces(ex, e, columns, count, tile, even, slope_ends, slopes, False, True)


def start_field(local, boundary, x_far, x_near, y_far, y_near, even_ref, right, *faces):
    columns, count = right.shape[1] // 8, right.shape[2] // 8
    even, edges = parity(even_ref), row_marks()
    received = (x_far, x_near, y_far, y_near)
    ends, slope_ends = end_rows(STIFF), end_rows(SLOPE)
    for c in range(4):
        for ex in range(columns):
            for e in range(count):
                rows, ys = pl.ds(8 * ex, 8), pl.ds(8 * e, 8)
                tile = with_faces(local[c, rows, ys], ex, e, columns, count, [r.at[c] for r in received],
                                  even, edges)
                tile = tile * boundary[rows, ys].astype(jnp.float32)
                right[c, rows, ys] = tile
                field_faces(c, ex, e, columns, count, tile, even, ends, slope_ends, faces)
    even = even_rows(even_ref)
    near, far = faces[2:]
    near[5] = jnp.zeros(near.shape[1:], jnp.float32)
    far[5] = jnp.zeros(far.shape[1:], jnp.float32)
    for xi, side in enumerate((before_of, after_of)):
        for field in range(5):
            low, high = [
                side(even[0], x_near[field, y : y + 1], x_far[field, y : y + 1]) for y in (0, 8 * count - 1)
            ]
            row = 8 * xi + field
            near[5, row : row + 1] = jnp.where(even[1], high, low)
            far[5, row : row + 1] = jnp.where(even[1], low, high)


def pick(c, values):
    out = jnp.float32(values[0])
    for i in range(1, 4):
        out = jnp.where(c == i, jnp.float32(values[i]), out)
    return out


def start_sums(scales, rates, local, boundary, x_far, x_near, y_far, y_near, even_ref, right, summed, share, stiff_y,
               wide_z, rest_z, reaction, free, ahead, z_sums):
    columns, count = ahead.shape[1] // 8, ahead.shape[2] // 8
    even, edges = parity(even_ref), row_marks()
    received = [r.at[4] for r in (x_far, x_near, y_far, y_near)]
    for ex in range(columns):
        for e in range(count):
            rows, ys = pl.ds(8 * ex, 8), pl.ds(8 * e, 8)
            reaction[rows, ys] = with_faces(local[4, rows, ys], ex, e, columns, count, received, even, edges)
            free[rows, ys] = boundary[rows, ys].astype(jnp.float32)
    basis_fill(scales, rates, right, None, reaction, free, summed, share, stiff_y, (wide_z, rest_z), ahead, z_sums)


def basis_sums(scales, rates, newest, older, reaction, free, summed, share, stiff_y, wide_z, rest_z, ahead, *rest):
    *dots, z_sums = rest
    basis_fill(scales, rates, newest, older, reaction, free, summed, share, stiff_y, (wide_z, rest_z), ahead, z_sums, *dots)


def basis_fill(scales, rates, newest, older, reaction, free, summed, share, stiff_y, stiff_z, ahead, z_sums, dots=None,
               first=None):
    columns, count = ahead.shape[1] // 8, ahead.shape[2] // 8
    edges = row_marks()
    double = 1.0 if older is None else 2.0

    def component(c, carry):
        scale, rate = pick(c, [double * v for v in scales]), pick(c, [double * v for v in rates])
        same = jnp.zeros((8, 128), jnp.float32)
        cross = jnp.zeros((8, 128), jnp.float32)
        start = jnp.zeros((8, 128), jnp.float32)
        state = None
        fill_z(z_sums, newest.at[c], stiff_z)
        for ex in range(columns):
            rows = pl.ds(8 * ex, 8)
            tiles = []
            for e in range(count):
                ys = pl.ds(8 * e, 8)
                tile = newest[c, rows, ys]
                if older is not None:
                    weighted = tile * share[...]
                    same = same + jnp.sum(weighted * tile, axis=0)
                    cross = cross + jnp.sum(weighted * older[c, rows, ys], axis=0)
                if first is not None:
                    start = start + jnp.sum(older[c, rows, ys] * older[c, rows, ys] * share[...], axis=0)
                tiles.append(tile)
            x_rows, y_parts, z_parts = stiff_terms(ex, tiles, stiff_y, z_sums)

            def finish(e, part):
                ys = pl.ds(8 * e, 8)
                value = scale * part + (rate * reaction[rows, ys] - double) * tiles[e]
                value = value * free[rows, ys]
                return value if older is None else value - older[c, rows, ys]

            state = emit_column(ex, x_rows, y_parts, z_parts, summed, edges, ahead.at[c], state, finish,
                                lambda row, ys: scale * free[row, ys])
        if older is not None:
            dots[pl.ds(c, 1)] = jnp.sum(same, axis=0, keepdims=True)
            dots[pl.ds(c + 4, 1)] = jnp.sum(cross, axis=0, keepdims=True)
        if first is not None:
            first[pl.ds(c, 1)] = jnp.sum(start, axis=0, keepdims=True)
            first[pl.ds(c + 4, 1)] = jnp.zeros((1, 128), jnp.float32)
        return carry

    lax.fori_loop(0, 4, component, 0)


def next_field(c, ex, e, ahead, free, received, scale, summed, edges, even, columns, count):
    rows, ys = pl.ds(8 * ex, 8), pl.ds(8 * e, 8)
    return with_faces(ahead[c, rows, ys], ex, e, columns, count, [r.at[c] for r in received], even, edges,
                      summed[0, 0], summed[1], scale * free[rows, ys])


def grow_field(scales, ahead, free, x_far, x_near, y_far, y_near, even_ref, summed, out, *faces):
    received = (x_far, x_near, y_far, y_near)
    columns, count = out.shape[1] // 8, out.shape[2] // 8
    even, edges = parity(even_ref), row_marks()
    ends, slope_ends = end_rows(STIFF), end_rows(SLOPE)
    for c in range(4):
        for ex in range(columns):
            for e in range(count):
                tile = next_field(c, ex, e, ahead, free, received, scales[c], summed, edges, even, columns, count)
                out[c, pl.ds(8 * ex, 8), pl.ds(8 * e, 8)] = tile
                field_faces(c, ex, e, columns, count, tile, even, ends, slope_ends, faces)


def second_field(scales, rates, ahead, free, x_far0, x_near0, y_far0, y_near0, x_far, x_near, y_far, y_near, even_ref,
                 summed, wide_z, rest_z, right_in, reaction_in, out, right, reaction, sx_far, sx_near, sy_far, sy_near,
                 x_near_out, x_far_out, y_near_out, y_far_out, lines, depth_lines):
    columns, count = out.shape[1] // 8, out.shape[2] // 8
    even, edges, even_row = parity(even_ref), row_marks(), even_rows(even_ref)
    received = (x_far, x_near, y_far, y_near)
    faces = (x_near_out, x_far_out, y_near_out, y_far_out)
    ends, slope_ends = end_rows(STIFF), end_rows(SLOPE)
    end_x, end_y = (0, 8 * columns - 1), (0, 8 * count - 1)
    sides = (before_of, after_of)
    corners = [(xi, yi) for xi in (0, 1) for yi in (0, 1)]

    def at(array, xi, yi):
        return array[end_x[xi], end_y[yi] : end_y[yi] + 1]

    def diagonal(field, xi, yi):
        row = 8 * xi + field
        return sides[yi](even_row[1], y_near[5, row : row + 1], y_far[5, row : row + 1])

    def beside(field, xi, yi):
        row = end_y[yi]
        return sides[xi](even_row[0], x_near0[field, row : row + 1], x_far0[field, row : row + 1])

    def beyond(field, xi, yi):
        row = end_x[xi]
        return sides[yi](even_row[1], y_near0[field, row : row + 1], y_far0[field, row : row + 1])

    for c in range(4):
        for n, (xi, yi) in enumerate(corners):
            lines[4 * c + n : 4 * c + n + 1] = diagonal(c, xi, yi) * at(free, xi, yi)
    depth_lines[...] = along_z(lines[...], (wide_z, rest_z))

    def missed(c, ex, e):
        found = []
        for n, (xi, yi) in enumerate(corners):
            cx, ce, sx, sy = (columns - 1) * xi, (count - 1) * yi, 7 * xi, 7 * yi
            line = lines[4 * c + n : 4 * c + n + 1]
            weight_x, weight_y = summed[0, 0, sy : sy + 1], summed[1, sx, 0:1]
            along = scales[c] * line * weight_x
            across = scales[c] * line * weight_y
            if ex == cx and e == ce:
                for i in range(8):
                    found.append((i, float(STIFF[i, sx]) * along * edges[yi]))
                found.append((sx, across * ends[1][yi]))
                side = beyond(c, xi, yi) * weight_x + beside(c, xi, yi) * weight_y
                side = float(STIFF[0, 0]) * side
                depth = depth_lines[4 * c + n : 4 * c + n + 1] * summed[2, sx, sy : sy + 1]
                gained = diagonal(4, xi, yi)
                node = scales[c] * (side + depth)
                node = node + (rates[c] * (at(reaction_in, xi, yi) + gained) - 1.0) * line
                node = node + rates[c] * gained * at(right_in.at[c], xi, yi)
                found.append((sx, node * edges[yi]))
            elif e == ce and ex == cx + 1 - 2 * xi:
                found.append((sx, float(STIFF[7 - sx, sx]) * along * edges[yi]))
            elif ex == cx and e == ce + 1 - 2 * yi:
                found.append((sx, float(STIFF[7 - sy, sy]) * across * edges[yi]))
        return found

    for c in range(4):
        for ex in range(columns):
            for e in range(count):
                rows, ys = pl.ds(8 * ex, 8), pl.ds(8 * e, 8)
                tile = next_field(c, ex, e, ahead, free, received, scales[c], summed, edges, even, columns, count)
                found = missed(c, ex, e)
                if found:
                    parts = []
                    for i in range(8):
                        extra = [t for row, t in found if row == i]
                        parts.append(tile[i] + sum(extra) * free[8 * ex + i, ys] if extra else tile[i])
                    tile = jnp.stack(parts)
                out[c, rows, ys] = tile
                field_faces(c, ex, e, columns, count, tile, even, ends, slope_ends, faces)

    sx_far[...], sx_near[...], sy_far[...], sy_near[...] = x_far[4], x_near[4], y_far[4], y_near[4]
    low, high = float(SLOPE[7, 7]), float(SLOPE[0, 0])
    for i in (0, 1):
        y, x = end_y[i], end_x[i]
        before = low * beyond(0, 0, i) * at(free, 0, i)
        after = high * beyond(0, 1, i) * at(free, 1, i)
        sx_near[y : y + 1] += jnp.where(even_row[0], after, before)
        sx_far[y : y + 1] += jnp.where(even_row[0], before, after)
        before = low * beside(1, i, 0) * at(free, i, 0)
        after = high * beside(1, i, 1) * at(free, i, 1)
        sy_near[x : x + 1] += jnp.where(even_row[1], after, before)
        sy_far[x : x + 1] += jnp.where(even_row[1], before, after)
    for n, (xi, yi) in enumerate(corners):
        x, y = end_x[xi], end_y[yi]
        reaction[x, y : y + 1] = at(reaction_in, xi, yi) + diagonal(4, xi, yi)
        for c in range(4):
            right[c, x, y : y + 1] = at(right_in.at[c], xi, yi) + lines[4 * c + n : 4 * c + n + 1]


def last_field(scales, rates, *refs):
    refs = list(refs)
    ahead, newest, reaction, free, *received, even_ref, summed, share, stiff_y, wide_z, rest_z, local = refs[:15]
    dots, (out, sums, *slopes, z_sums) = refs[15:20], refs[20:]
    columns, count = out.shape[1] // 8, out.shape[2] // 8
    even, edges = parity(even_ref), row_marks()
    slope_ends = end_rows(SLOPE)
    for i in range(1, ITERS - 1):
        sums[i] = dots[i][...]
    for c in range(4):
        scale, rate = scales[c], rates[c]
        same = jnp.zeros((8, 128), jnp.float32)
        cross = jnp.zeros((8, 128), jnp.float32)
        work = jnp.zeros((8, 128), jnp.float32)
        for ex in range(columns):
            rows = pl.ds(8 * ex, 8)
            for e in range(count):
                ys = pl.ds(8 * e, 8)
                tile = next_field(c, ex, e, ahead, free, received, 2.0 * scale, summed, edges, even, columns, count)
                now = newest[c, rows, ys]
                out[c, rows, ys] = tile
                store_faces(ex, e, columns, count, tile, even, slope_ends, slopes, c == 0, c == 1)
                weighted = tile * share[...]
                same = same + jnp.sum(weighted * tile, axis=0)
                cross = cross + jnp.sum(weighted * now, axis=0)
                extra = (rate * reaction[rows, ys] - 1.0) * tile
                work = work + jnp.sum(weighted * extra, axis=0)
                work = work + scale * (square_sum(split_rows(tile)) * local[0, 0])
                term = half_y(tile, stiff_y) * local[1]
                work = work + scale * jnp.sum(term * tile, axis=0)
        fill_z(z_sums, out.at[c], (wide_z, rest_z))
        for ex in range(columns):
            for e in range(count):
                rows, ys = pl.ds(8 * ex, 8), pl.ds(8 * e, 8)
                work = work + scale * jnp.sum(z_sums[rows, ys] * local[2] * out[c, rows, ys], axis=0)
        sums[ITERS - 1, c : c + 1] = jnp.sum(same, axis=0, keepdims=True)
        sums[ITERS - 1, c + 4 : c + 5] = jnp.sum(cross, axis=0, keepdims=True)
        sums[0, c : c + 1] = dots[0][c : c + 1]
        sums[0, c + 4 : c + 5] = jnp.sum(work, axis=0, keepdims=True)


def slope_sums(*refs):
    fields, (summed, slope_y, wide_z, rest_z), outs = refs[:3], refs[3:7], refs[7:]
    columns, count = outs[0].shape[1] // 8, outs[0].shape[2] // 8
    edges = row_marks()
    for field, out in zip(fields, outs):
        fill_z(out.at[2], field.at[2], (wide_z, rest_z))
        state = None
        for ex in range(columns):
            rows, ends = pl.ds(8 * ex, 8), []
            y_parts = [along_y(field[1, rows, pl.ds(8 * e, 8)], slope_y) for e in range(count)]
            y_parts = join_y(y_parts, edges[0], edges[1])
            for e in range(count):
                ys = pl.ds(8 * e, 8)
                out[1, rows, ys] = y_parts[e] * summed[1]
                out[2, rows, ys] = out[2, rows, ys] * summed[2]
                x_rows = [r * summed[0, 0] for r in along_x(split_rows(field[0, rows, ys]), SLOPE)]
                out[0, rows, ys] = jnp.stack(x_rows)
                if ex:
                    out[0, 8 * ex, ys] += state[e]
                    out[0, 8 * ex - 1, ys] += x_rows[0]
                ends.append(x_rows[7])
            state = ends


def first_update(halves, gain, *refs):
    sums, *sloped = refs[: ITERS + 1]
    refs = refs[ITERS + 1 :]
    slopes = [refs[:4]]
    slopes += [[r.at[4] for r in refs[4 * k : 4 * k + 4]] for k in range(1, ITERS - 1)]
    refs = refs[4 * ITERS - 4 :]
    slopes.append(refs[:4])
    even_ref, free, summed, inverse = refs[4:8]
    weights, remainder, update, *faces = refs[8:15]
    joined = refs[15:]
    columns, count = update.shape[0] // 8, update.shape[1] // 8
    even, edges = parity(even_ref), row_marks()
    ends = end_rows(STIFF)
    total = [jnp.broadcast_to(jnp.sum(sums[i], axis=1, keepdims=True), (8, 128)) for i in range(ITERS)]
    other = [pltpu.roll(t, 4, axis=0) for t in total]
    row = lax.broadcasted_iota(jnp.int32, (8, 128), 0)
    half = jnp.full((8, 128), halves[0], jnp.float32)
    for i in range(1, 4):
        half = jnp.where(row == i, halves[i], half)
    moments = [total[0], other[1]]
    for level in range(2, 2 * ITERS - 1):
        inner = total[level // 2] if level % 2 == 0 else other[level // 2 + 1]
        moments.append(2.0 * inner - moments[level % 2])
    top = 2.0 * other[0] - other[5]
    moments.append(2.0 * top - moments[1])
    for i, value in enumerate(conjugate_coefficients(moments, half, half)):
        weights[i] = value
    for n in range(4):
        c = n // 2
        joined[n][...] = sum(slopes[i][n][...] * weights[i, c : c + 1] for i in range(ITERS))
    factor = [[weights[i, c : c + 1][None] for c in range(3)] for i in range(ITERS)]
    for ex in range(columns):
        for e in range(count):
            rows, ys = pl.ds(8 * ex, 8), pl.ds(8 * e, 8)
            tile = sum(sloped[i][c, rows, ys] * factor[i][c] for i in range(ITERS) for c in range(3))
            tile = with_faces(tile, ex, e, columns, count, joined, even, edges, summed[0, 0], summed[1])
            left = -tile * free[rows, ys]
            change = gain * inverse[...] * left
            remainder[rows, ys] = left
            update[rows, ys] = change
            store_faces(ex, e, columns, count, change, even, ends, faces)


def combine_fields(weights, *refs):
    *basis, fields = refs

    def combine(c, carry):
        factor = [weights[i, pl.ds(c, 1)] for i in range(ITERS)]
        for x in range(0, fields.shape[1], 8):
            rows = pl.ds(x, 8)
            value = basis[0][c, rows] * factor[0][None]
            for i in range(1, ITERS):
                value = value + basis[i][c, rows] * factor[i][None]
            fields[c, rows] = value
        return carry

    lax.fori_loop(0, 4, combine, 0)


def add_loads(count, *refs):
    *loads, rider, tick, out = refs
    del tick
    values = [load[:count] for load in loads]
    total = values[0] + values[1]
    if len(values) == 4:
        total = total + (values[2] + values[3])
    out[:count] = total
    out[count:] = rider[...]


def pressure_sums(update, summed, shift, stiff_y, wide_z, rest_z, raw, z_sums):
    columns, count = raw.shape[0] // 8, raw.shape[1] // 8
    edges = row_marks()
    state = None
    fill_z(z_sums, update, (wide_z, rest_z))
    for ex in range(columns):
        rows = pl.ds(8 * ex, 8)
        tiles = [update[rows, pl.ds(8 * e, 8)] for e in range(count)]
        x_rows, y_parts, z_parts = stiff_terms(ex, tiles, stiff_y, z_sums)
        state = emit_column(ex, x_rows, y_parts, z_parts, summed, edges, raw, state,
                            lambda e, part: part + shift[...] * tiles[e])


def pressure_step(last, keep, gain, *refs):
    raw, free, *received, even_ref, summed, inverse, remainder_in, update_in, pressure_in = refs[:12]
    if last:
        pressure_far, pressure, left_here = refs[12:]
    else:
        pressure, remainder, update, *faces = refs[12:]
    columns, count = raw.shape[0] // 8, raw.shape[1] // 8
    copies = []
    even, edges = parity(even_ref), row_marks()
    ends = end_rows(STIFF)
    for ex in range(columns):
        for e in range(count):
            rows, ys = pl.ds(8 * ex, 8), pl.ds(8 * e, 8)
            tile = with_faces(raw[rows, ys], ex, e, columns, count, received, even, edges,
                              summed[0, 0], summed[1])
            left = remainder_in[rows, ys] - tile * free[rows, ys]
            change = gain * inverse[...] * left + keep * update_in[rows, ys]
            pressure[rows, ys] = pressure_in[rows, ys] + change
            if not last:
                remainder[rows, ys] = left
                update[rows, ys] = change
                store_faces(ex, e, columns, count, change, even, ends, faces)
        if last:
            rows = pl.ds(8 * ex, 8)
            copies.append(pltpu.make_async_copy(pressure.at[rows], pressure_far.at[rows], left_here.at[ex]))
            copies[-1].start()
    for copy in copies:
        copy.wait()


VMEM_BYTES = 24 * 1024 * 1024


def call(kernel, name, outs, *args, scratch=(), cost=None, far_in=0, far_out=0, copies=0, aliases=()):
    held, far = pl.BlockSpec(memory_space=pltpu.VMEM), pl.BlockSpec(memory_space=pltpu.HBM)
    scratch_shapes = [pltpu.VMEM(s, jnp.float32) for s in scratch]
    if copies:
        scratch_shapes.append(pltpu.SemaphoreType.DMA((copies,)))
    return pl.pallas_call(
        kernel,
        name=name,
        out_shape=[jax.ShapeDtypeStruct(s, jnp.float32) for s in outs],
        in_specs=[far] * far_in + [held] * (len(args) - far_in),
        out_specs=[far] * far_out + [held] * (len(outs) - far_out),
        scratch_shapes=scratch_shapes,
        cost_estimate=cost,
        input_output_aliases=dict(aliases),
        compiler_params=pltpu.CompilerParams(vmem_limit_bytes=VMEM_BYTES),
    )(*[pltpu.with_memory_space_constraint(a, pltpu.HBM) for a in args[:far_in]], *args[far_in:])


def busy(bytes_accessed):
    return pl.CostEstimate(flops=0, bytes_accessed=bytes_accessed, transcendentals=0)


def swap_near(axis, face):
    return lax.ppermute(face, axis, [(i, i ^ 1) for i in range(lax.axis_size(axis))])


def swap_far(axis, face):
    size = lax.axis_size(axis)
    return lax.ppermute(face, axis, [(i, far_partner(i, size)) for i in range(size)])


def swap_all(x_near, x_far, y_near, y_far):
    y_far = swap_far("gy", y_far)
    x_far = swap_far("gx", x_far)
    x_near = swap_near("gx", x_near)
    y_near = swap_near("gy", y_near)
    return x_far, x_near, y_far, y_near


def far_partner(i, size):
    return (i + 1 if i % 2 else i - 1) % size


def partner_loads(load, axis, partners, riders, count):
    size, heard, faces = lax.axis_size(axis), [], []
    for n, (partner, rider) in enumerate(zip(partners, riders)):
        mine = load
        if n:
            mine = load[:count] if rider is None else jnp.concatenate([load[:count], rider])
        mine = lax.ppermute(mine, axis, [(i, partner(i)) for i in range(size)])
        heard.append(mine)
        if rider is not None:
            faces.append(mine[count:])
    return heard, faces


def all_sum(values, axis, near, far, following, meanwhile):
    size = lax.axis_size(axis)
    count = values.shape[0] - far.shape[0] if following is None else values.shape[0]
    half = size // 2

    def to_near(i):
        return i ^ 1

    def to_far(i):
        return far_partner(i, size)

    def across(i):
        return (i + half) % size

    def far_across(i):
        return across(to_far(i))

    rounds = [((to_far,), (far,))]
    if size == 4:
        rounds = [((to_far, to_near, across), (far, near, None))]
    elif size > 4:
        rounds = [((to_far, across, far_across), (far, None, None)), ((to_near,), (near,))]
        bit = 4
        while bit < half:
            rounds.append(((lambda i, bit=bit: i ^ bit,), (None,)))
            bit *= 2
    else:
        rounds.append(((), (near,)))
    faces = []
    load = values if following is None else jnp.concatenate([values, far])
    for n, (partners, riders) in enumerate(rounds):
        if not partners:
            faces.append(lax.ppermute(near, axis, [(i, to_near(i)) for i in range(size)]))
            continue
        heard, got = partner_loads(load, axis, partners, riders, count)
        faces += got
        rider = rounds[n + 1][1][0] if n + 1 < len(rounds) and rounds[n + 1][0] else following
        tail = jnp.zeros((8, values.shape[1]), jnp.float32) if rider is None else rider
        (load,) = call(
            functools.partial(add_loads, count), "add_loads", [(count + tail.shape[0], values.shape[1])],
            load, *heard, tail, meanwhile(),
        )
    if following is None:
        load = load[:count]
    return load, faces[1], faces[0]


def conjugate_coefficients(moments, centre, half):
    remaining, towards = list(moments), list(moments)
    one, zero = jnp.ones_like(moments[0]), jnp.zeros_like(moments[0])
    direction = [one] + [zero] * ITERS
    residual = list(direction)
    total = [zero] * ITERS
    for step in range(ITERS):
        count = len(towards) - 1
        image = []
        for level in range(count):
            side = (
                half * towards[1] if level == 0 else 0.5 * half * (towards[level + 1] + towards[level - 1])
            )
            image.append(centre * towards[level] + side)
        alpha = remaining[step] / image[step]
        total = [total[i] + alpha * direction[i] for i in range(ITERS)]
        if step == ITERS - 1:
            break
        applied = []
        for i in range(ITERS + 1):
            term = centre * direction[i]
            if i >= 1:
                term = term + (half if i == 1 else 0.5 * half) * direction[i - 1]
            if i < ITERS:
                term = term + 0.5 * half * direction[i + 1]
            applied.append(term)
        residual = [residual[i] - alpha * applied[i] for i in range(ITERS + 1)]
        following = [remaining[i] - alpha * image[i] for i in range(count)]
        beta = -alpha * (half if step == 0 else 0.5 * half) * following[step + 1] / remaining[step]
        towards = [following[i] + beta * towards[i] for i in range(count)]
        direction = [residual[i] + beta * direction[i] for i in range(ITERS + 1)]
        remaining = following
    return total


def on_device(old_fields, inverse_step, boundary):
    x, y, z = inverse_step.shape
    t = Tables(z)
    brick, four = (x, y, z), (4, x, y, z)
    faces = [(y, z)] * 2 + [(x, z)] * 2
    faces5 = [(5,) + f for f in faces]
    faces_back = [(y, z)] * 2 + [(x, z)] * 2

    place = [lax.axis_index(a) % 2 == 0 for a in ("gx", "gy")]
    even = jnp.stack([jnp.full((8, 128), p, jnp.float32) for p in place])

    local, x_near, x_far, y_near, y_far = call(
        load_local, "local_right", [(5,) + brick] + faces5, old_fields, inverse_step, even,
        scratch=[four, brick], far_in=2, copies=5,
    )
    received = swap_all(x_near, x_far, y_near, y_far)

    top = INTERVAL_SHARE * np.array([spectrum_top(c) for c in DIFFUSE])
    halves = [float(v) for v in 0.5 * top]
    scales = [float(v) for v in np.array(DIFFUSE) / (0.5 * top)]
    rates = [float(v) for v in 1.0 / (0.5 * top)]

    relayed = [(6,) + f for f in faces[2:]]
    right, *sent = call(start_field, "right_field", [four] + faces5[:2] + relayed, local, boundary, *received, even)
    heard = [swap_all(*sent)]
    reaction, free, ahead = call(
        functools.partial(start_sums, scales, rates), "right_sums", [brick, brick, four],
        local, boundary, *received, even, right, t.summed, t.share, t.stiff_y, *t.stiff_z, cost=busy(8 << 20),
        scratch=[brick],
    )
    field, right, reaction, *slopes = call(
        functools.partial(second_field, scales, rates), "second_field", [four, four, brick] + faces_back + faces5,
        ahead, free, *received, *heard[0], even, t.summed, *t.stiff_z, right, reaction,
        scratch=[(16, z)] * 2, aliases=[(14, 1), (15, 2)],
    )
    slopes, sent = slopes[:4], slopes[4:]
    heard[0] = slopes
    basis, sums = [right, field], []
    for k in range(1, ITERS - 1):
        heard.append(swap_all(*sent))
        outs = [four, (8, 128)] + ([(8, 128)] if k == 1 else [])
        ahead, *dots = call(
            functools.partial(basis_sums, scales, rates), "basis_sums", outs,
            basis[-1], basis[-2], reaction, free, t.summed, t.share, t.stiff_y, *t.stiff_z, cost=busy(8 << 20),
            scratch=[brick],
        )
        sums += dots[::-1]
        if k == ITERS - 2:
            break
        field, *sent = call(
            functools.partial(grow_field, [2.0 * v for v in scales]), "basis_field", [four] + faces5,
            ahead, free, *heard[-1], even, t.summed,
        )
        basis.append(field)
    field, sums, x_near, x_far, y_near, y_far = call(
        functools.partial(last_field, scales, rates), "last_field", [four, (ITERS, 8, 128)] + faces,
        ahead, basis[-1], reaction, free, *heard[-1], even, t.summed, t.share, t.stiff_y, *t.plain_z, t.local, *sums,
        scratch=[brick],
    )
    basis.append(field)
    sums = sums.reshape(ITERS * 8, z)
    sloped = []

    def meanwhile():
        if len(sloped) < ITERS:
            sloped.extend(
                call(
                    slope_sums, "slope_sums", [(3,) + brick] * 3,
                    *basis[len(sloped) : len(sloped) + 3], t.summed, t.slope_y, *t.slope_z, cost=busy(6 << 20),
                )
            )
        return sloped[-1]

    sums, x_near, x_far = all_sum(sums, "gx", x_near, x_far, y_far, meanwhile)
    sums, y_near, y_far = all_sum(sums, "gy", y_near, y_far, None, meanwhile)
    while len(sloped) < ITERS:
        meanwhile()
    sums = sums.reshape(ITERS, 8, z)
    slopes = (x_far, x_near, y_far, y_near)

    centre, half = chebyshev_bounds()
    factor = centre / half
    damping = 1.0 / factor
    weights, remainder, update, *sent = call(
        functools.partial(first_update, halves, 1.0 / centre), "first_update", [(ITERS, 8, 128), brick, brick] + faces,
        sums, *sloped, *[a for h in heard for a in h], *slopes, even, free, t.summed, t.inverse, scratch=faces_back,
    )
    pressure = update
    for step in range(1, CHEB):
        last = step == CHEB - 1
        received = swap_all(*sent)
        (raw,) = call(
            pressure_sums, "pressure_sums", [brick],
            update, t.summed, t.shift, t.stiff_y, *t.stiff_z, cost=busy(2 << 20), scratch=[brick],
        )
        if step == 1:
            (fields,) = call(combine_fields, "fields", [four], weights, *basis, cost=busy(4 << 20))
        following = 1.0 / (2.0 * factor - damping)
        keep, gain = following * damping, 2.0 * following / half
        damping = following
        kernel = functools.partial(pressure_step, last, keep, gain)
        args = [raw, free, *received, even, t.summed, t.inverse, remainder, update, pressure]
        if last:
            (pressure,) = call(
                kernel, "pressure_last", [brick], *args, scratch=[brick], far_out=1, copies=x // 8
            )
            break
        pressure, remainder, update, *sent = call(kernel, "pressure_step", [brick] * 3 + faces, *args)
    return (fields, pressure)


def solution(mesh):
    return jax.shard_map(
        on_device,
        mesh=mesh,
        in_specs=(P(None, "gx", "gy", None), P("gx", "gy", None), P("gx", "gy", None)),
        out_specs=(P(None, "gx", "gy", None), P("gx", "gy", None)),
        check_vma=False,
    )
```

```python
import functools

import jax
import jax.numpy as jnp
import ml_dtypes
import numpy as np
from jax import lax
from jax.experimental import pallas as pl
from jax.experimental.pallas import tpu as pltpu
from jax.sharding import PartitionSpec as P

ITERS = 6
CHEB = 6

SIGMA_SHIFT = 0.5
DIFFUSE = (1.0, 1.0, 1.0, 1.4)
COUPLING = 1.0
STRATIFY = 1.0
SPREAD = 20.0
STEP_MAX = 64.0
INTERVAL_SHARE = 0.82
HIGHEST_PRECISION = lax.Precision.HIGHEST
LOBATTO_POINTS = (
    -1.0,
    -0.8717401485096066,
    -0.5917001814331423,
    -0.2092992179024789,
    0.2092992179024789,
    0.5917001814331423,
    0.8717401485096066,
    1.0,
)


def legendre_value(points, degree):
    previous = points * 0.0 + 1.0
    current = points
    for order in range(1, degree):
        following = ((2 * order + 1) * points * current - order * previous) / (order + 1)
        previous = current
        current = following
    return current


def quadrature_tables():
    degree = 7
    points = np.array(LOBATTO_POINTS)
    values = legendre_value(points, degree)
    weights = 2.0 / (degree * (degree + 1) * values * values)
    derive = np.zeros((degree + 1, degree + 1))
    for row_index in range(degree + 1):
        for column_index in range(degree + 1):
            if row_index != column_index:
                derive[row_index, column_index] = values[row_index] / (
                    values[column_index] * (points[row_index] - points[column_index])
                )
    derive[0, 0] = -degree * (degree + 1) / 4.0
    derive[degree, degree] = degree * (degree + 1) / 4.0
    stiffness_table = derive.T @ (weights[:, None] * derive)
    return (weights, derive, stiffness_table)


WEIGHTS, DERIVE, STIFF = quadrature_tables()
SLOPE = WEIGHTS[:, None] * DERIVE
COPIES = np.where(np.arange(8) % 7 == 0, 2.0, 1.0)


def chebyshev_bounds():
    weight_matrix = np.eye(8) * WEIGHTS

    def kron3(a, b, c):
        return np.kron(np.kron(a, b), c)

    element_matrix = (
        kron3(STIFF, weight_matrix, weight_matrix)
        + kron3(weight_matrix, STIFF, weight_matrix)
        + kron3(weight_matrix, weight_matrix, STIFF)
        + SIGMA_SHIFT * kron3(weight_matrix, weight_matrix, weight_matrix)
    )
    bounds_ratio = np.sum(np.abs(element_matrix), axis=1) / np.diagonal(element_matrix)
    upper_bound = float(np.max(bounds_ratio))
    lower_bound = upper_bound / SPREAD
    return ((upper_bound + lower_bound) / 2.0, (upper_bound - lower_bound) / 2.0)


def spectrum_top(diffuse):
    root = np.sqrt(COPIES)
    stiff = root[:, None] * STIFF * root[None, :]
    weight = np.diag(WEIGHTS * COPIES)

    def kron3(a, b, c):
        return np.kron(np.kron(a, b), c)

    element = diffuse * (
        kron3(stiff, weight, weight) + kron3(weight, stiff, weight) + kron3(weight, weight, stiff)
    ) + STEP_MAX * kron3(weight, weight, weight)
    return float(np.linalg.eigvalsh(element)[-1])


def line_sums(table, length):
    matrix = np.kron(np.eye(length // 8), table)
    total = matrix.copy()
    for start in range(8, length, 8):
        total[start] += matrix[start - 1]
        total[start - 1] += matrix[start]
    return total


def depth_line(vector, length):
    line = np.tile(vector * COPIES, length // 8)
    line[0] = vector[0]
    line[-1] = vector[-1]
    return line


def f32(array):
    return np.ascontiguousarray(array, np.float32)


def rolled_rows(table):
    out = np.zeros((8, 8, 128))
    for shift in range(8):
        for row in range(8):
            out[shift, row] = table[row, (row - shift) % 8]
    return out


def block(a, b, c):
    return a[:, None, None] * b[:, None] * c


def parts_of(matrix):
    rest, parts = f32(matrix), []
    for _ in range(3):
        parts.append(rest.astype(ml_dtypes.bfloat16))
        rest = rest - parts[-1].astype(np.float32)
    hi, mid, lo = parts
    return np.block([[hi, mid], [hi, mid]]), np.concatenate([hi, lo])


class Tables:
    def __init__(self, depth):
        ones8, ones = np.ones(8), np.ones(depth)
        wide = WEIGHTS * COPIES
        deep = depth_line(WEIGHTS, depth)
        flat = np.tile(WEIGHTS, depth // 8)
        stiff = np.diagonal(STIFF)
        wide_s, deep_s = stiff * COPIES, depth_line(stiff, depth)
        share = 1.0 / COPIES
        share_z = np.tile(share, depth // 8)
        share_z[0] = share_z[-1] = 1.0
        self.summed = f32(
            np.stack([block(ones8, wide, deep), block(wide, ones8, deep), block(wide, wide, ones)])
        )
        self.local = f32(
            np.stack(
                [block(ones8, WEIGHTS, flat), block(WEIGHTS, ones8, flat), block(WEIGHTS, WEIGHTS, ones)]
            )
        )
        self.share = f32(block(share, share, share_z))
        diagonal = (
            block(wide_s, wide, deep)
            + block(wide, wide_s, deep)
            + block(wide, wide, deep_s)
            + SIGMA_SHIFT * block(wide, wide, deep)
        )
        self.inverse = f32(1.0 / diagonal)
        self.shift = f32(SIGMA_SHIFT * block(wide, wide, deep))
        self.stiff_y = f32(rolled_rows(STIFF))
        self.slope_y = f32(rolled_rows(SLOPE))
        self.stiff_z = parts_of(line_sums(STIFF, depth).T)
        self.plain_z = parts_of(np.kron(np.eye(depth // 8), STIFF).T)
        self.slope_z = parts_of(line_sums(SLOPE, depth).T)


def row_marks():
    row = lax.broadcasted_iota(jnp.int32, (8, 128), 0)
    return jnp.where(row == 0, 1.0, 0.0), jnp.where(row == 7, 1.0, 0.0)


def by_place(vector, place):
    out = jnp.full(place.shape, float(vector[0]), jnp.float32)
    for i in range(1, 8):
        out = jnp.where(place == i, float(vector[i]), out)
    return out


def along_x(rows, table):
    if np.allclose(table, table[::-1, ::-1]):
        even = 0.5 * (table[:4, :4] + table[:4, :3:-1])
        odd = 0.5 * (table[:4, :4] - table[:4, :3:-1])
        plus = [rows[i] + rows[7 - i] for i in range(4)]
        minus = [rows[i] - rows[7 - i] for i in range(4)]
        out = [None] * 8
        for a in range(4):
            p = sum(float(even[a, b]) * plus[b] for b in range(4))
            m = sum(float(odd[a, b]) * minus[b] for b in range(4))
            out[a], out[7 - a] = p + m, p - m
        return out
    return [sum(float(table[a, b]) * rows[b] for b in range(8)) for a in range(8)]


def along_y(tiles, factors):
    total = factors[0] * tiles
    for shift in range(1, 8):
        total = total + factors[shift] * pltpu.roll(tiles, shift, axis=1)
    return total


def along_z(tiles, matrix):
    wide, rest = matrix
    shape, depth = tiles.shape, tiles.shape[-1]
    flat = tiles.reshape(-1, depth)
    hi = flat.astype(jnp.bfloat16)
    flat = flat - hi.astype(jnp.float32)
    mid = flat.astype(jnp.bfloat16)
    lo = (flat - mid.astype(jnp.float32)).astype(jnp.bfloat16)
    first = jnp.dot(jnp.concatenate([hi, mid], axis=1), wide[...], preferred_element_type=jnp.float32)
    second = jnp.dot(jnp.concatenate([lo, hi], axis=1), rest[...], preferred_element_type=jnp.float32)
    return (first[:, :depth] + (first[:, depth:] + second)).reshape(shape)


def fill_z(out, field, matrix):
    for x in range(0, out.shape[0], 16):
        rows = pl.ds(x, min(16, out.shape[0] - x))
        out[rows] = along_z(field[rows], matrix)


def join_y(parts, low, high):
    out = list(parts)
    for e in range(1, len(parts)):
        out[e - 1] = out[e - 1] + high * pltpu.roll(parts[e], 7, axis=1)
        out[e] = out[e] + low * pltpu.roll(parts[e - 1], 1, axis=1)
    return out


def spread_rows(rows):
    return jnp.broadcast_to(rows[:, None, :], (rows.shape[0], 8, rows.shape[1]))


def column_sums(x_rows, y_parts, z_parts, summed, edges):
    y_parts = join_y(y_parts, edges[0], edges[1])
    return [
        jnp.stack(kx) * summed[0, 0] + ky * summed[1] + kz * summed[2]
        for kx, ky, kz in zip(x_rows, y_parts, z_parts)
    ]


def emit_column(ex, x_rows, y_parts, z_parts, summed, edges, out, state, finish=None, factor=None):
    rows = pl.ds(8 * ex, 8)
    parts = column_sums(x_rows, y_parts, z_parts, summed, edges)
    for e, part in enumerate(parts):
        ys = pl.ds(8 * e, 8)
        out[rows, ys] = part if finish is None else finish(e, part)
        if ex:
            for row, face in ((8 * ex, state[e]), (8 * ex - 1, x_rows[e][0])):
                face = face * summed[0, 0]
                out[row, ys] += face if factor is None else face * factor(row, ys)
    return [r[7] for r in x_rows]


def end_rows(table):
    row = lax.broadcasted_iota(jnp.int32, (8, 128), 0)
    return (table[0], table[7]), (by_place(table[0], row), by_place(table[7], row))


def store_faces(ex, e, columns, count, tile, even, ends, faces, x=True, y=True):
    x_near, x_far, y_near, y_far = faces
    (x_low, x_high), (y_low, y_high) = ends
    rows, ys = pl.ds(8 * ex, 8), pl.ds(8 * e, 8)
    if x and ex == 0:
        low = sum(float(x_low[i]) * tile[i] for i in range(8))
        x_near[ys] = low
        x_far[ys] = low
    if x and ex == columns - 1:
        high = sum(float(x_high[i]) * tile[i] for i in range(8))
        x_near[ys] = jnp.where(even[0], high, x_near[ys])
        x_far[ys] = jnp.where(even[0], x_far[ys], high)
    if y and e == 0:
        low = jnp.sum(tile * y_low, axis=1)
        y_near[rows] = low
        y_far[rows] = low
    if y and e == count - 1:
        high = jnp.sum(tile * y_high, axis=1)
        y_near[rows] = jnp.where(even[1], high, y_near[rows])
        y_far[rows] = jnp.where(even[1], y_far[rows], high)


def parity(even_ref):
    return even_ref[0] > 0.5, even_ref[1] > 0.5


def even_rows(even_ref):
    return even_ref[0, 0:1] > 0.5, even_ref[1, 0:1] > 0.5


def before_of(even, near, far):
    return jnp.where(even, far, near)


def after_of(even, near, far):
    return jnp.where(even, near, far)


def with_faces(tile, ex, e, columns, count, received, even, edges, weight_x=None, weight_y=None, mask=None, x=True):
    x_far, x_near, y_far, y_near = received
    rows, ys = pl.ds(8 * ex, 8), pl.ds(8 * e, 8)

    def weighted(face, weight):
        return face if weight is None else face * weight

    if e == 0:
        face = before_of(even[1], y_near[rows], y_far[rows])
        face = spread_rows(face) * weighted(edges[0], weight_y)
        tile = tile + weighted(face, mask)
    if e == count - 1:
        face = after_of(even[1], y_near[rows], y_far[rows])
        face = spread_rows(face) * weighted(edges[1], weight_y)
        tile = tile + weighted(face, mask)
    if x and ex == 0:
        face = before_of(even[0], x_near[ys], x_far[ys])
        face = weighted(face, weight_x) if mask is None else weighted(face, weight_x) * mask[0]
        tile = jnp.concatenate([tile[0:1] + face[None], tile[1:]], axis=0)
    if x and ex == columns - 1:
        face = after_of(even[0], x_near[ys], x_far[ys])
        face = weighted(face, weight_x) if mask is None else weighted(face, weight_x) * mask[7]
        tile = jnp.concatenate([tile[:7], tile[7:8] + face[None]], axis=0)
    return tile


def split_rows(block_rows):
    return [block_rows[i] for i in range(8)]


def load_local(old_far, step_far, even_ref, out, x_near, x_far, y_near, y_far, old, step, arrived):
    columns, count, depth = out.shape[1] // 8, out.shape[2] // 8, out.shape[3]
    copies = [pltpu.make_async_copy(step_far, step, arrived.at[4])]
    copies += [pltpu.make_async_copy(old_far.at[i], old.at[i], arrived.at[i]) for i in range(4)]
    for copy in copies:
        copy.start()
    even, edges = parity(even_ref), row_marks()
    row = lax.broadcasted_iota(jnp.int32, (8, depth), 0)
    lane = lax.broadcasted_iota(jnp.int32, (8, depth), 1)
    place = lane & 7
    after = jnp.where((place == 0) & (lane > 0), 1.0, 0.0)
    before_z = jnp.where((place == 7) & (lane < depth - 1), 1.0, 0.0)
    plane = by_place(WEIGHTS, row) * by_place(WEIGHTS, place)
    mass = jnp.stack([float(w) * plane for w in WEIGHTS])
    for field in (4, 0, 1, 2, 3):
        if field != 3:
            copies[0 if field == 4 else field + 1].wait()
        if field == 2:
            copies[4].wait()
        before = [None] * count
        for ex in range(columns):
            rows = pl.ds(8 * ex, 8)
            parts = []
            for e in range(count):
                ys = pl.ds(8 * e, 8)
                value = step[rows, ys]
                if field < 4:
                    value = value * old[field, rows, ys]
                if field == 2:
                    value = value + COUPLING * old[3, rows, ys]
                if field == 3:
                    value = value - STRATIFY * old[2, rows, ys]
                value = value * mass
                value = (
                    value
                    + after * pltpu.roll(value, 1, axis=2)
                    + before_z * pltpu.roll(value, depth - 1, axis=2)
                )
                parts.append(value)
            parts = join_y(parts, edges[0], edges[1])
            for e in range(count):
                ys = pl.ds(8 * e, 8)
                out[field, rows, ys] = parts[e]
                if ex:
                    out[field, 8 * ex, ys] += before[e]
                    out[field, 8 * ex - 1, ys] += parts[e][0]
                before[e] = parts[e][7]
        for e in range(count):
            ys = pl.ds(8 * e, 8)
            low, high = out[field, 0, ys], out[field, 8 * columns - 1, ys]
            x_near[field, ys] = jnp.where(even[0], high, low)
            x_far[field, ys] = jnp.where(even[0], low, high)
        for ex in range(columns):
            rows = pl.ds(8 * ex, 8)
            low = out[field, rows, pl.ds(0, 8)][:, 0]
            high = out[field, rows, pl.ds(8 * count - 8, 8)][:, 7]
            y_near[field, rows] = jnp.where(even[1], high, low)
            y_far[field, rows] = jnp.where(even[1], low, high)


def stiff_terms(ex, tiles, stiff_y, z_sums):
    x_rows = [along_x(split_rows(t), STIFF) for t in tiles]
    y_parts = [along_y(t, stiff_y) for t in tiles]
    z_parts = [z_sums[pl.ds(8 * ex, 8), pl.ds(8 * e, 8)] for e in range(len(tiles))]
    return x_rows, y_parts, z_parts


def square_sum(rows):
    total = 0.0
    for sign in (1.0, -1.0):
        form = 0.5 * (STIFF[:4, :4] + sign * STIFF[:4, :3:-1])
        part = [rows[i] + rows[7 - i] if sign > 0 else rows[i] - rows[7 - i] for i in range(4)]
        for i in range(4):
            pivot = form[i, i]
            if pivot < 1e-12:
                continue
            line = form[i] / np.sqrt(pivot)
            value = sum(float(line[b]) * part[b] for b in range(i, 4))
            total = total + value * value
            form = form - np.outer(line, line)
    return total


def half_y(tiles, factors):
    total = factors[0] * tiles
    for shift in range(1, 5):
        rolled = factors[shift] * pltpu.roll(tiles, shift, axis=1)
        total = total + (rolled if shift == 4 else 2.0 * rolled)
    return total


def join_x(c, out, x_far, x_near, even, even_row, ends, weight, mask, faces, slopes, slope_ends):
    columns, count = out.shape[0] // 8, out.shape[1] // 8
    for xi, side in enumerate((before_of, after_of)):
        row = (8 * columns - 1) * xi
        mended = [[0.0, 0.0], [0.0, 0.0]]
        for e in range(count):
            ys = pl.ds(8 * e, 8)
            change = side(even[0], x_near[c, ys], x_far[c, ys]) * weight * mask(row, ys)
            out[row, ys] += change
            for kind, (low, high) in enumerate((ends[1], slope_ends[1])):
                if e == 0:
                    mended[kind][0] = jnp.sum(change * low, axis=0, keepdims=True)
                if e == count - 1:
                    mended[kind][1] = jnp.sum(change * high, axis=0, keepdims=True)
        for kind, where in enumerate((faces, slopes if c == 1 else None)):
            if where is not None:
                low, high = mended[kind]
                where[2][row : row + 1] += jnp.where(even_row[1], high, low)
                where[3][row : row + 1] += jnp.where(even_row[1], low, high)
    for ex in sorted({0, columns - 1}):
        for e in range(count):
            tile = out[pl.ds(8 * ex, 8), pl.ds(8 * e, 8)]
            if faces is not None:
                store_faces(ex, e, columns, count, tile, even, ends, faces, True, False)
            if slopes is not None and c == 0:
                store_faces(ex, e, columns, count, tile, even, slope_ends, slopes, True, False)


def y_faces(c, ex, e, columns, count, tile, even, ends, slope_ends, y_near, y_far):
    store_faces(ex, e, columns, count, tile, even, ends, (None, None, y_near.at[c], y_far.at[c]), False, True)
    if c == 1:
        slopes = (None, None, y_near.at[4], y_far.at[4])
        store_faces(ex, e, columns, count, tile, even, slope_ends, slopes, False, True)


def first_y(local, boundary, y_far, y_near, even_ref, part, y_near_out, y_far_out):
    columns, count = part.shape[1] // 8, part.shape[2] // 8
    even, edges = parity(even_ref), row_marks()
    ends, slope_ends = end_rows(STIFF), end_rows(SLOPE)
    for c in range(4):
        for ex in range(columns):
            for e in range(count):
                rows, ys = pl.ds(8 * ex, 8), pl.ds(8 * e, 8)
                tile = with_faces(local[c, rows, ys], ex, e, columns, count, (None, None, y_far.at[c], y_near.at[c]),
                                  even, edges, x=False)
                tile = tile * boundary[rows, ys].astype(jnp.float32)
                part[c, rows, ys] = tile
                y_faces(c, ex, e, columns, count, tile, even, ends, slope_ends, y_near_out, y_far_out)


def first_x(part, y_near_in, y_far_in, boundary, x_far, x_near, even_ref, right, near, far, x_near_out, x_far_out):
    del part, y_near_in, y_far_in
    columns, count = right.shape[1] // 8, right.shape[2] // 8
    even, even_row = parity(even_ref), even_rows(even_ref)
    ends, slope_ends = end_rows(STIFF), end_rows(SLOPE)
    faces = (x_near_out, x_far_out, near, far)
    for c in range(4):
        join_x(c, right.at[c], x_far, x_near, even, even_row, ends, 1.0,
               lambda row, ys: boundary[row, ys].astype(jnp.float32),
               [f.at[c] for f in faces], [f.at[4] for f in faces], slope_ends)
    near[5] = jnp.zeros(near.shape[1:], jnp.float32)
    far[5] = jnp.zeros(far.shape[1:], jnp.float32)
    for xi, side in enumerate((before_of, after_of)):
        for field in range(5):
            low, high = [
                side(even_row[0], x_near[field, y : y + 1], x_far[field, y : y + 1]) for y in (0, 8 * count - 1)
            ]
            row = 8 * xi + field
            near[5, row : row + 1] = jnp.where(even_row[1], high, low)
            far[5, row : row + 1] = jnp.where(even_row[1], low, high)


def pick(c, values):
    out = jnp.float32(values[0])
    for i in range(1, 4):
        out = jnp.where(c == i, jnp.float32(values[i]), out)
    return out


def start_sums(scales, rates, local, boundary, x_far, x_near, y_far, y_near, even_ref, right, summed, share, stiff_y,
               wide_z, rest_z, reaction, free, ahead, z_sums):
    columns, count = ahead.shape[1] // 8, ahead.shape[2] // 8
    even, edges = parity(even_ref), row_marks()
    received = [r.at[4] for r in (x_far, x_near, y_far, y_near)]
    for ex in range(columns):
        for e in range(count):
            rows, ys = pl.ds(8 * ex, 8), pl.ds(8 * e, 8)
            reaction[rows, ys] = with_faces(local[4, rows, ys], ex, e, columns, count, received, even, edges)
            free[rows, ys] = boundary[rows, ys].astype(jnp.float32)
    basis_fill(scales, rates, right, None, reaction, free, summed, share, stiff_y, (wide_z, rest_z), ahead, z_sums)


def basis_sums(scales, rates, newest, older, reaction, free, summed, share, stiff_y, wide_z, rest_z, ahead, *rest):
    *dots, z_sums = rest
    basis_fill(scales, rates, newest, older, reaction, free, summed, share, stiff_y, (wide_z, rest_z), ahead, z_sums, *dots)


def basis_fill(scales, rates, newest, older, reaction, free, summed, share, stiff_y, stiff_z, ahead, z_sums, dots=None,
               first=None):
    columns, count = ahead.shape[1] // 8, ahead.shape[2] // 8
    edges = row_marks()
    double = 1.0 if older is None else 2.0

    def component(c, carry):
        scale, rate = pick(c, [double * v for v in scales]), pick(c, [double * v for v in rates])
        same = jnp.zeros((8, 128), jnp.float32)
        cross = jnp.zeros((8, 128), jnp.float32)
        start = jnp.zeros((8, 128), jnp.float32)
        state = None
        fill_z(z_sums, newest.at[c], stiff_z)
        for ex in range(columns):
            rows = pl.ds(8 * ex, 8)
            tiles = []
            for e in range(count):
                ys = pl.ds(8 * e, 8)
                tile = newest[c, rows, ys]
                if older is not None:
                    weighted = tile * share[...]
                    same = same + jnp.sum(weighted * tile, axis=0)
                    cross = cross + jnp.sum(weighted * older[c, rows, ys], axis=0)
                if first is not None:
                    start = start + jnp.sum(older[c, rows, ys] * older[c, rows, ys] * share[...], axis=0)
                tiles.append(tile)
            x_rows, y_parts, z_parts = stiff_terms(ex, tiles, stiff_y, z_sums)

            def finish(e, part):
                ys = pl.ds(8 * e, 8)
                value = scale * part + (rate * reaction[rows, ys] - double) * tiles[e]
                value = value * free[rows, ys]
                return value if older is None else value - older[c, rows, ys]

            state = emit_column(ex, x_rows, y_parts, z_parts, summed, edges, ahead.at[c], state, finish,
                                lambda row, ys: scale * free[row, ys])
        if older is not None:
            dots[pl.ds(c, 1)] = jnp.sum(same, axis=0, keepdims=True)
            dots[pl.ds(c + 4, 1)] = jnp.sum(cross, axis=0, keepdims=True)
        if first is not None:
            first[pl.ds(c, 1)] = jnp.sum(start, axis=0, keepdims=True)
            first[pl.ds(c + 4, 1)] = jnp.zeros((1, 128), jnp.float32)
        return carry

    lax.fori_loop(0, 4, component, 0)


def y_field(c, ex, e, ahead, free, y_far, y_near, scale, summed, edges, even, columns, count):
    rows, ys = pl.ds(8 * ex, 8), pl.ds(8 * e, 8)
    return with_faces(ahead[c, rows, ys], ex, e, columns, count, (None, None, y_far.at[c], y_near.at[c]), even, edges,
                      None, summed[1], scale * free[rows, ys], x=False)


def grow_y(scales, ahead, free, y_far, y_near, even_ref, summed, part, y_near_out, y_far_out):
    columns, count = part.shape[1] // 8, part.shape[2] // 8
    even, edges = parity(even_ref), row_marks()
    ends, slope_ends = end_rows(STIFF), end_rows(SLOPE)
    for c in range(4):
        for ex in range(columns):
            for e in range(count):
                tile = y_field(c, ex, e, ahead, free, y_far, y_near, scales[c], summed, edges, even, columns, count)
                part[c, pl.ds(8 * ex, 8), pl.ds(8 * e, 8)] = tile
                y_faces(c, ex, e, columns, count, tile, even, ends, slope_ends, y_near_out, y_far_out)


def grow_x(scales, part, y_near_in, y_far_in, free, x_far, x_near, even_ref, summed, out, y_near_out, y_far_out,
           x_near_out, x_far_out):
    del part, y_near_in, y_far_in
    even, even_row = parity(even_ref), even_rows(even_ref)
    ends, slope_ends = end_rows(STIFF), end_rows(SLOPE)
    faces = (x_near_out, x_far_out, y_near_out, y_far_out)
    for c in range(4):
        join_x(c, out.at[c], x_far, x_near, even, even_row, ends, scales[c] * summed[0, 0],
               lambda row, ys: free[row, ys], [f.at[c] for f in faces], [f.at[4] for f in faces], slope_ends)


def second_y(scales, rates, ahead, free, x_far0, x_near0, y_far0, y_near0, y_far, y_near, even_ref, summed, wide_z,
             rest_z, right_in, reaction_in, out, right, reaction, y_near_out, y_far_out, lines, depth_lines):
    columns, count = out.shape[1] // 8, out.shape[2] // 8
    even, edges, even_row = parity(even_ref), row_marks(), even_rows(even_ref)
    ends, slope_ends = end_rows(STIFF), end_rows(SLOPE)
    end_x, end_y = (0, 8 * columns - 1), (0, 8 * count - 1)
    sides = (before_of, after_of)
    corners = [(xi, yi) for xi in (0, 1) for yi in (0, 1)]

    def at(array, xi, yi):
        return array[end_x[xi], end_y[yi] : end_y[yi] + 1]

    def diagonal(field, xi, yi):
        row = 8 * xi + field
        return sides[yi](even_row[1], y_near[5, row : row + 1], y_far[5, row : row + 1])

    def beside(field, xi, yi):
        row = end_y[yi]
        return sides[xi](even_row[0], x_near0[field, row : row + 1], x_far0[field, row : row + 1])

    def beyond(field, xi, yi):
        row = end_x[xi]
        return sides[yi](even_row[1], y_near0[field, row : row + 1], y_far0[field, row : row + 1])

    for c in range(4):
        for n, (xi, yi) in enumerate(corners):
            lines[4 * c + n : 4 * c + n + 1] = diagonal(c, xi, yi) * at(free, xi, yi)
    depth_lines[...] = along_z(lines[...], (wide_z, rest_z))

    def missed(c, ex, e):
        found = []
        for n, (xi, yi) in enumerate(corners):
            cx, ce, sx, sy = (columns - 1) * xi, (count - 1) * yi, 7 * xi, 7 * yi
            line = lines[4 * c + n : 4 * c + n + 1]
            weight_x, weight_y = summed[0, 0, sy : sy + 1], summed[1, sx, 0:1]
            along = scales[c] * line * weight_x
            across = scales[c] * line * weight_y
            if ex == cx and e == ce:
                for i in range(8):
                    found.append((i, float(STIFF[i, sx]) * along * edges[yi]))
                found.append((sx, across * ends[1][yi]))
                side = beyond(c, xi, yi) * weight_x + beside(c, xi, yi) * weight_y
                side = float(STIFF[0, 0]) * side
                depth = depth_lines[4 * c + n : 4 * c + n + 1] * summed[2, sx, sy : sy + 1]
                gained = diagonal(4, xi, yi)
                node = scales[c] * (side + depth)
                node = node + (rates[c] * (at(reaction_in, xi, yi) + gained) - 1.0) * line
                node = node + rates[c] * gained * at(right_in.at[c], xi, yi)
                found.append((sx, node * edges[yi]))
            elif e == ce and ex == cx + 1 - 2 * xi:
                found.append((sx, float(STIFF[7 - sx, sx]) * along * edges[yi]))
            elif ex == cx and e == ce + 1 - 2 * yi:
                found.append((sx, float(STIFF[7 - sy, sy]) * across * edges[yi]))
        return found

    for c in range(4):
        for ex in range(columns):
            for e in range(count):
                rows, ys = pl.ds(8 * ex, 8), pl.ds(8 * e, 8)
                tile = y_field(c, ex, e, ahead, free, y_far, y_near, scales[c], summed, edges, even, columns, count)
                found = missed(c, ex, e)
                if found:
                    parts = []
                    for i in range(8):
                        extra = [t for row, t in found if row == i]
                        parts.append(tile[i] + sum(extra) * free[8 * ex + i, ys] if extra else tile[i])
                    tile = jnp.stack(parts)
                out[c, rows, ys] = tile
                y_faces(c, ex, e, columns, count, tile, even, ends, slope_ends, y_near_out, y_far_out)

    for n, (xi, yi) in enumerate(corners):
        x, y = end_x[xi], end_y[yi]
        reaction[x, y : y + 1] = at(reaction_in, xi, yi) + diagonal(4, xi, yi)
        for c in range(4):
            right[c, x, y : y + 1] = at(right_in.at[c], xi, yi) + lines[4 * c + n : 4 * c + n + 1]


def mend_slopes(x_far0, x_near0, y_far0, y_near0, x_far, x_near, y_far, y_near, free, even_ref,
                sx_far, sx_near, sy_far, sy_near):
    even_row = even_rows(even_ref)
    end_x, end_y = (0, free.shape[0] - 1), (0, free.shape[1] - 1)
    sides = (before_of, after_of)

    def at(array, xi, yi):
        return array[end_x[xi], end_y[yi] : end_y[yi] + 1]

    def beside(field, xi, yi):
        row = end_y[yi]
        return sides[xi](even_row[0], x_near0[field, row : row + 1], x_far0[field, row : row + 1])

    def beyond(field, xi, yi):
        row = end_x[xi]
        return sides[yi](even_row[1], y_near0[field, row : row + 1], y_far0[field, row : row + 1])

    sx_far[...], sx_near[...], sy_far[...], sy_near[...] = x_far[4], x_near[4], y_far[4], y_near[4]
    low, high = float(SLOPE[7, 7]), float(SLOPE[0, 0])
    for i in (0, 1):
        y, x = end_y[i], end_x[i]
        before = low * beyond(0, 0, i) * at(free, 0, i)
        after = high * beyond(0, 1, i) * at(free, 1, i)
        sx_near[y : y + 1] += jnp.where(even_row[0], after, before)
        sx_far[y : y + 1] += jnp.where(even_row[0], before, after)
        before = low * beside(1, i, 0) * at(free, i, 0)
        after = high * beside(1, i, 1) * at(free, i, 1)
        sy_near[x : x + 1] += jnp.where(even_row[1], after, before)
        sy_far[x : x + 1] += jnp.where(even_row[1], before, after)


def column_products(c, ex, out, newest, reaction, share, stiff_y, stiff_z, local, scale, rate, z_sums):
    count = out.shape[2] // 8
    rows = pl.ds(8 * ex, 8)
    same = jnp.zeros((8, 128), jnp.float32)
    cross = jnp.zeros((8, 128), jnp.float32)
    work = jnp.zeros((8, 128), jnp.float32)
    z_sums[...] = along_z(out[c, rows], stiff_z)
    for e in range(count):
        ys = pl.ds(8 * e, 8)
        tile = out[c, rows, ys]
        weighted = tile * share[...]
        same = same + jnp.sum(weighted * tile, axis=0)
        cross = cross + jnp.sum(weighted * newest[c, rows, ys], axis=0)
        extra = (rate * reaction[rows, ys] - 1.0) * tile
        work = work + jnp.sum(weighted * extra, axis=0)
        work = work + scale * (square_sum(split_rows(tile)) * local[0, 0])
        term = half_y(tile, stiff_y) * local[1] + z_sums[:, ys] * local[2]
        work = work + scale * jnp.sum(term * tile, axis=0)
    return same, cross, work


def last_y(scales, rates, ahead, newest, reaction, free, y_far, y_near, even_ref, summed, share, stiff_y, wide_z, rest_z,
           local, part, sy_near, sy_far, products, z_sums):
    columns, count = part.shape[1] // 8, part.shape[2] // 8
    even, edges = parity(even_ref), row_marks()
    slope_ends = end_rows(SLOPE)
    for c in range(4):
        total = [jnp.zeros((8, 128), jnp.float32)] * 3
        for ex in range(columns):
            for e in range(count):
                tile = y_field(c, ex, e, ahead, free, y_far, y_near, 2.0 * scales[c], summed, edges, even, columns, count)
                part[c, pl.ds(8 * ex, 8), pl.ds(8 * e, 8)] = tile
                if c == 1:
                    store_faces(ex, e, columns, count, tile, even, slope_ends, (None, None, sy_near, sy_far), False, True)
            if 0 < ex < columns - 1:
                found = column_products(c, ex, part, newest, reaction, share, stiff_y, (wide_z, rest_z), local, scales[c],
                                        rates[c], z_sums)
                total = [a + b for a, b in zip(total, found)]
        for n in range(3):
            products[c, n] = total[n]


def last_x(scales, rates, part, sy_near_in, sy_far_in, products, newest, reaction, free, x_far, x_near, even_ref, summed,
           share, stiff_y, wide_z, rest_z, local, d0, d1, d2, d3, d4, out, sy_near, sy_far, sums, sx_near, sx_far, z_sums):
    del part, sy_near_in, sy_far_in
    dots = (d0, d1, d2, d3, d4)
    columns = out.shape[1] // 8
    even, even_row = parity(even_ref), even_rows(even_ref)
    ends, slope_ends = end_rows(STIFF), end_rows(SLOPE)
    for i in range(1, ITERS - 1):
        sums[i] = dots[i][...]
    for c in range(4):
        join_x(c, out.at[c], x_far, x_near, even, even_row, ends, 2.0 * scales[c] * summed[0, 0],
               lambda row, ys: free[row, ys], None, (sx_near, sx_far, sy_near, sy_far), slope_ends)
        total = [products[c, n] for n in range(3)]
        for ex in sorted({0, columns - 1}):
            found = column_products(c, ex, out, newest, reaction, share, stiff_y, (wide_z, rest_z), local, scales[c],
                                    rates[c], z_sums)
            total = [a + b for a, b in zip(total, found)]
        same, cross, work = [jnp.sum(t, axis=0, keepdims=True) for t in total]
        sums[ITERS - 1, c : c + 1] = same
        sums[ITERS - 1, c + 4 : c + 5] = cross
        sums[0, c : c + 1] = dots[0][c : c + 1]
        sums[0, c + 4 : c + 5] = work


def slope_sums(*refs):
    fields, (summed, slope_y, wide_z, rest_z), outs = refs[:3], refs[3:7], refs[7:]
    columns, count = outs[0].shape[1] // 8, outs[0].shape[2] // 8
    edges = row_marks()
    for field, out in zip(fields, outs):
        fill_z(out.at[2], field.at[2], (wide_z, rest_z))
        state = None
        for ex in range(columns):
            rows, ends = pl.ds(8 * ex, 8), []
            y_parts = [along_y(field[1, rows, pl.ds(8 * e, 8)], slope_y) for e in range(count)]
            y_parts = join_y(y_parts, edges[0], edges[1])
            for e in range(count):
                ys = pl.ds(8 * e, 8)
                out[1, rows, ys] = y_parts[e] * summed[1]
                out[2, rows, ys] = out[2, rows, ys] * summed[2]
                x_rows = [r * summed[0, 0] for r in along_x(split_rows(field[0, rows, ys]), SLOPE)]
                out[0, rows, ys] = jnp.stack(x_rows)
                if ex:
                    out[0, 8 * ex, ys] += state[e]
                    out[0, 8 * ex - 1, ys] += x_rows[0]
                ends.append(x_rows[7])
            state = ends


def first_update(halves, gain, *refs):
    sums, *sloped = refs[: ITERS + 1]
    refs = refs[ITERS + 1 :]
    slopes = [refs[:4]]
    slopes += [[r.at[4] for r in refs[4 * k : 4 * k + 4]] for k in range(1, ITERS - 1)]
    refs = refs[4 * ITERS - 4 :]
    slopes.append(refs[:4])
    even_ref, free, summed, inverse = refs[4:8]
    weights, remainder, update, *faces = refs[8:15]
    joined = refs[15:]
    columns, count = update.shape[0] // 8, update.shape[1] // 8
    even, edges = parity(even_ref), row_marks()
    ends = end_rows(STIFF)
    total = [jnp.broadcast_to(jnp.sum(sums[i], axis=1, keepdims=True), (8, 128)) for i in range(ITERS)]
    other = [pltpu.roll(t, 4, axis=0) for t in total]
    row = lax.broadcasted_iota(jnp.int32, (8, 128), 0)
    half = jnp.full((8, 128), halves[0], jnp.float32)
    for i in range(1, 4):
        half = jnp.where(row == i, halves[i], half)
    moments = [total[0], other[1]]
    for level in range(2, 2 * ITERS - 1):
        inner = total[level // 2] if level % 2 == 0 else other[level // 2 + 1]
        moments.append(2.0 * inner - moments[level % 2])
    top = 2.0 * other[0] - other[5]
    moments.append(2.0 * top - moments[1])
    for i, value in enumerate(conjugate_coefficients(moments, half, half)):
        weights[i] = value
    for n in range(4):
        c = n // 2
        joined[n][...] = sum(slopes[i][n][...] * weights[i, c : c + 1] for i in range(ITERS))
    factor = [[weights[i, c : c + 1][None] for c in range(3)] for i in range(ITERS)]
    for ex in range(columns):
        for e in range(count):
            rows, ys = pl.ds(8 * ex, 8), pl.ds(8 * e, 8)
            tile = sum(sloped[i][c, rows, ys] * factor[i][c] for i in range(ITERS) for c in range(3))
            tile = with_faces(tile, ex, e, columns, count, joined, even, edges, summed[0, 0], summed[1])
            left = -tile * free[rows, ys]
            change = gain * inverse[...] * left
            remainder[rows, ys] = left
            update[rows, ys] = change
            store_faces(ex, e, columns, count, change, even, ends, faces)


def combine_fields(weights, *refs):
    *basis, fields = refs

    def combine(c, carry):
        factor = [weights[i, pl.ds(c, 1)] for i in range(ITERS)]
        for x in range(0, fields.shape[1], 8):
            rows = pl.ds(x, 8)
            value = basis[0][c, rows] * factor[0][None]
            for i in range(1, ITERS):
                value = value + basis[i][c, rows] * factor[i][None]
            fields[c, rows] = value
        return carry

    lax.fori_loop(0, 4, combine, 0)


def add_loads(count, *refs):
    *loads, rider, tick, out = refs
    del tick
    values = [load[:count] for load in loads]
    total = values[0] + values[1]
    if len(values) == 4:
        total = total + (values[2] + values[3])
    out[:count] = total
    out[count:] = rider[...]


def pressure_sums(update, summed, shift, stiff_y, wide_z, rest_z, raw, z_sums):
    columns, count = raw.shape[0] // 8, raw.shape[1] // 8
    edges = row_marks()
    state = None
    fill_z(z_sums, update, (wide_z, rest_z))
    for ex in range(columns):
        rows = pl.ds(8 * ex, 8)
        tiles = [update[rows, pl.ds(8 * e, 8)] for e in range(count)]
        x_rows, y_parts, z_parts = stiff_terms(ex, tiles, stiff_y, z_sums)
        state = emit_column(ex, x_rows, y_parts, z_parts, summed, edges, raw, state,
                            lambda e, part: part + shift[...] * tiles[e])


def pressure_step(last, keep, gain, *refs):
    raw, free, *received, even_ref, summed, inverse, remainder_in, update_in, pressure_in = refs[:12]
    if last:
        pressure_far, pressure, left_here = refs[12:]
    else:
        pressure, remainder, update, *faces = refs[12:]
    columns, count = raw.shape[0] // 8, raw.shape[1] // 8
    copies = []
    even, edges = parity(even_ref), row_marks()
    ends = end_rows(STIFF)
    for ex in range(columns):
        for e in range(count):
            rows, ys = pl.ds(8 * ex, 8), pl.ds(8 * e, 8)
            tile = with_faces(raw[rows, ys], ex, e, columns, count, received, even, edges,
                              summed[0, 0], summed[1])
            left = remainder_in[rows, ys] - tile * free[rows, ys]
            change = gain * inverse[...] * left + keep * update_in[rows, ys]
            pressure[rows, ys] = pressure_in[rows, ys] + change
            if not last:
                remainder[rows, ys] = left
                update[rows, ys] = change
                store_faces(ex, e, columns, count, change, even, ends, faces)
        if last:
            rows = pl.ds(8 * ex, 8)
            copies.append(pltpu.make_async_copy(pressure.at[rows], pressure_far.at[rows], left_here.at[ex]))
            copies[-1].start()
    for copy in copies:
        copy.wait()


VMEM_BYTES = 24 * 1024 * 1024


def call(kernel, name, outs, *args, scratch=(), cost=None, far_in=0, far_out=0, copies=0, aliases=()):
    held, far = pl.BlockSpec(memory_space=pltpu.VMEM), pl.BlockSpec(memory_space=pltpu.HBM)
    scratch_shapes = [pltpu.VMEM(s, jnp.float32) for s in scratch]
    if copies:
        scratch_shapes.append(pltpu.SemaphoreType.DMA((copies,)))
    return pl.pallas_call(
        kernel,
        name=name,
        out_shape=[jax.ShapeDtypeStruct(s, jnp.float32) for s in outs],
        in_specs=[far] * far_in + [held] * (len(args) - far_in),
        out_specs=[far] * far_out + [held] * (len(outs) - far_out),
        scratch_shapes=scratch_shapes,
        cost_estimate=cost,
        input_output_aliases=dict(aliases),
        compiler_params=pltpu.CompilerParams(vmem_limit_bytes=VMEM_BYTES),
    )(*[pltpu.with_memory_space_constraint(a, pltpu.HBM) for a in args[:far_in]], *args[far_in:])


def busy(bytes_accessed):
    return pl.CostEstimate(flops=0, bytes_accessed=bytes_accessed, transcendentals=0)


def swap_near(axis, face):
    return lax.ppermute(face, axis, [(i, i ^ 1) for i in range(lax.axis_size(axis))])


def swap_far(axis, face):
    size = lax.axis_size(axis)
    return lax.ppermute(face, axis, [(i, far_partner(i, size)) for i in range(size)])


def swap_all(x_near, x_far, y_near, y_far):
    y_far = swap_far("gy", y_far)
    x_far = swap_far("gx", x_far)
    x_near = swap_near("gx", x_near)
    y_near = swap_near("gy", y_near)
    return x_far, x_near, y_far, y_near


def far_partner(i, size):
    return (i + 1 if i % 2 else i - 1) % size


def partner_loads(load, axis, partners, riders, count):
    size, heard, faces = lax.axis_size(axis), [], []
    for n, (partner, rider) in enumerate(zip(partners, riders)):
        mine = load
        if n:
            mine = load[:count] if rider is None else jnp.concatenate([load[:count], rider])
        mine = lax.ppermute(mine, axis, [(i, partner(i)) for i in range(size)])
        heard.append(mine)
        if rider is not None:
            faces.append(mine[count:])
    return heard, faces


def all_sum(values, axis, near, far, following, meanwhile):
    size = lax.axis_size(axis)
    count = values.shape[0] - far.shape[0] if following is None else values.shape[0]
    half = size // 2

    def to_near(i):
        return i ^ 1

    def to_far(i):
        return far_partner(i, size)

    def across(i):
        return (i + half) % size

    def far_across(i):
        return across(to_far(i))

    rounds = [((to_far,), (far,))]
    if size == 4:
        rounds = [((to_far, to_near, across), (far, near, None))]
    elif size > 4:
        rounds = [((to_far, across, far_across), (far, None, None)), ((to_near,), (near,))]
        bit = 4
        while bit < half:
            rounds.append(((lambda i, bit=bit: i ^ bit,), (None,)))
            bit *= 2
    else:
        rounds.append(((), (near,)))
    faces = []
    load = values if following is None else jnp.concatenate([values, far])
    for n, (partners, riders) in enumerate(rounds):
        if not partners:
            faces.append(lax.ppermute(near, axis, [(i, to_near(i)) for i in range(size)]))
            continue
        heard, got = partner_loads(load, axis, partners, riders, count)
        faces += got
        rider = rounds[n + 1][1][0] if n + 1 < len(rounds) and rounds[n + 1][0] else following
        tail = jnp.zeros((8, values.shape[1]), jnp.float32) if rider is None else rider
        (load,) = call(
            functools.partial(add_loads, count), "add_loads", [(count + tail.shape[0], values.shape[1])],
            load, *heard, tail, meanwhile(),
        )
    if following is None:
        load = load[:count]
    return load, faces[1], faces[0]


def conjugate_coefficients(moments, centre, half):
    remaining, towards = list(moments), list(moments)
    one, zero = jnp.ones_like(moments[0]), jnp.zeros_like(moments[0])
    direction = [one] + [zero] * ITERS
    residual = list(direction)
    total = [zero] * ITERS
    for step in range(ITERS):
        count = len(towards) - 1
        image = []
        for level in range(count):
            side = (
                half * towards[1] if level == 0 else 0.5 * half * (towards[level + 1] + towards[level - 1])
            )
            image.append(centre * towards[level] + side)
        alpha = remaining[step] / image[step]
        total = [total[i] + alpha * direction[i] for i in range(ITERS)]
        if step == ITERS - 1:
            break
        applied = []
        for i in range(ITERS + 1):
            term = centre * direction[i]
            if i >= 1:
                term = term + (half if i == 1 else 0.5 * half) * direction[i - 1]
            if i < ITERS:
                term = term + 0.5 * half * direction[i + 1]
            applied.append(term)
        residual = [residual[i] - alpha * applied[i] for i in range(ITERS + 1)]
        following = [remaining[i] - alpha * image[i] for i in range(count)]
        beta = -alpha * (half if step == 0 else 0.5 * half) * following[step + 1] / remaining[step]
        towards = [following[i] + beta * towards[i] for i in range(count)]
        direction = [residual[i] + beta * direction[i] for i in range(ITERS + 1)]
        remaining = following
    return total


def on_device(old_fields, inverse_step, boundary):
    x, y, z = inverse_step.shape
    t = Tables(z)
    brick, four = (x, y, z), (4, x, y, z)
    faces = [(y, z)] * 2 + [(x, z)] * 2
    faces5 = [(5,) + f for f in faces]
    faces_back = [(y, z)] * 2 + [(x, z)] * 2

    place = [lax.axis_index(a) % 2 == 0 for a in ("gx", "gy")]
    even = jnp.stack([jnp.full((8, 128), p, jnp.float32) for p in place])

    local, x_near, x_far, y_near, y_far = call(
        load_local, "local_right", [(5,) + brick] + faces5, old_fields, inverse_step, even,
        scratch=[four, brick], far_in=2, copies=5,
    )
    received = swap_all(x_near, x_far, y_near, y_far)

    top = INTERVAL_SHARE * np.array([spectrum_top(c) for c in DIFFUSE])
    halves = [float(v) for v in 0.5 * top]
    scales = [float(v) for v in np.array(DIFFUSE) / (0.5 * top)]
    rates = [float(v) for v in 1.0 / (0.5 * top)]

    x_far, x_near, y_far, y_near = received
    relayed = [(6, x, z)] * 2
    x_faces, y_faces5 = [(5, y, z)] * 2, [(5, x, z)] * 2
    part, near, far = call(first_y, "first_y", [four] + relayed, local, boundary, y_far, y_near, even, cost=busy(2 << 20))
    right, y_near, y_far, x_near, x_far = call(
        first_x, "first_x", [four] + relayed + x_faces, part, near, far, boundary, x_far, x_near, even,
        aliases=[(0, 0), (1, 1), (2, 2)],
    )
    heard = [swap_all(x_near, x_far, y_near, y_far)]
    reaction, free, ahead = call(
        functools.partial(start_sums, scales, rates), "right_sums", [brick, brick, four],
        local, boundary, *received, even, right, t.summed, t.share, t.stiff_y, *t.stiff_z, cost=busy(8 << 20),
        scratch=[brick],
    )
    x_far, x_near, y_far, y_near = heard[0]
    part, right, reaction, near, far = call(
        functools.partial(second_y, scales, rates), "second_y", [four, four, brick] + y_faces5,
        ahead, free, *received, y_far, y_near, even, t.summed, *t.stiff_z, right, reaction,
        scratch=[(16, z)] * 2, aliases=[(12, 1), (13, 2)], cost=busy(3 << 20),
    )
    basis, sums = [right], []
    here = scales
    for k in range(1, ITERS - 1):
        field, y_near, y_far, x_near, x_far = call(
            functools.partial(grow_x, here), "basis_x", [four] + y_faces5 + x_faces,
            part, near, far, free, x_far, x_near, even, t.summed, aliases=[(0, 0), (1, 1), (2, 2)],
        )
        basis.append(field)
        heard.append(swap_all(x_near, x_far, y_near, y_far))
        x_far, x_near, y_far, y_near = heard[-1]
        outs = [four, (8, 128)] + ([(8, 128)] if k == 1 else [])
        ahead, *dots = call(
            functools.partial(basis_sums, scales, rates), "basis_sums", outs,
            basis[-1], basis[-2], reaction, free, t.summed, t.share, t.stiff_y, *t.stiff_z, cost=busy(8 << 20),
            scratch=[brick],
        )
        sums += dots[::-1]
        here = [2.0 * v for v in scales]
        if k < ITERS - 2:
            part, near, far = call(
                functools.partial(grow_y, here), "basis_y", [four] + y_faces5,
                ahead, free, y_far, y_near, even, t.summed, cost=busy(2 << 20),
            )
    part, near, far, products = call(
        functools.partial(last_y, scales, rates), "last_y", [four] + [(x, z)] * 2 + [(4, 3, 8, 128)],
        ahead, basis[-1], reaction, free, y_far, y_near, even, t.summed, t.share, t.stiff_y, *t.plain_z, t.local,
        scratch=[(8, y, z)], cost=busy(4 << 20),
    )
    field, y_near, y_far, sums, x_near, x_far = call(
        functools.partial(last_x, scales, rates), "last_x",
        [four] + [(x, z)] * 2 + [(ITERS, 8, 128)] + [(y, z)] * 2,
        part, near, far, products, basis[-1], reaction, free, x_far, x_near, even, t.summed, t.share, t.stiff_y,
        *t.plain_z, t.local, *sums, scratch=[(8, y, z)], aliases=[(0, 0), (1, 1), (2, 2)],
    )
    basis.append(field)
    heard[0] = call(mend_slopes, "slopes", faces_back, *received, *heard[0], free, even)
    sums = sums.reshape(ITERS * 8, z)
    sloped = []

    def meanwhile():
        if len(sloped) < ITERS:
            sloped.extend(
                call(
                    slope_sums, "slope_sums", [(3,) + brick] * 3,
                    *basis[len(sloped) : len(sloped) + 3], t.summed, t.slope_y, *t.slope_z, cost=busy(6 << 20),
                )
            )
        return sloped[-1]

    sums, x_near, x_far = all_sum(sums, "gx", x_near, x_far, y_far, meanwhile)
    sums, y_near, y_far = all_sum(sums, "gy", y_near, y_far, None, meanwhile)
    while len(sloped) < ITERS:
        meanwhile()
    sums = sums.reshape(ITERS, 8, z)
    slopes = (x_far, x_near, y_far, y_near)

    centre, half = chebyshev_bounds()
    factor = centre / half
    damping = 1.0 / factor
    weights, remainder, update, *sent = call(
        functools.partial(first_update, halves, 1.0 / centre), "first_update", [(ITERS, 8, 128), brick, brick] + faces,
        sums, *sloped, *[a for h in heard for a in h], *slopes, even, free, t.summed, t.inverse, scratch=faces_back,
    )
    pressure = update
    for step in range(1, CHEB):
        last = step == CHEB - 1
        received = swap_all(*sent)
        (raw,) = call(
            pressure_sums, "pressure_sums", [brick],
            update, t.summed, t.shift, t.stiff_y, *t.stiff_z, cost=busy(2 << 20), scratch=[brick],
        )
        if step == 1:
            (fields,) = call(combine_fields, "fields", [four], weights, *basis, cost=busy(4 << 20))
        following = 1.0 / (2.0 * factor - damping)
        keep, gain = following * damping, 2.0 * following / half
        damping = following
        kernel = functools.partial(pressure_step, last, keep, gain)
        args = [raw, free, *received, even, t.summed, t.inverse, remainder, update, pressure]
        if last:
            (pressure,) = call(
                kernel, "pressure_last", [brick], *args, scratch=[brick], far_out=1, copies=x // 8
            )
            break
        pressure, remainder, update, *sent = call(kernel, "pressure_step", [brick] * 3 + faces, *args)
    return (fields, pressure)


def solution(mesh):
    return jax.shard_map(
        on_device,
        mesh=mesh,
        in_specs=(P(None, "gx", "gy", None), P("gx", "gy", None), P("gx", "gy", None)),
        out_specs=(P(None, "gx", "gy", None), P("gx", "gy", None)),
        check_vma=False,
    )
```

```python
import functools

import jax
import jax.numpy as jnp
import ml_dtypes
import numpy as np
from jax import lax
from jax.experimental import pallas as pl
from jax.experimental.pallas import tpu as pltpu
from jax.sharding import PartitionSpec as P

ITERS = 6
CHEB = 6

SIGMA_SHIFT = 0.5
DIFFUSE = (1.0, 1.0, 1.0, 1.4)
COUPLING = 1.0
STRATIFY = 1.0
SPREAD = 20.0
STEP_MAX = 64.0
INTERVAL_SHARE = 0.82
HIGHEST_PRECISION = lax.Precision.HIGHEST
LOBATTO_POINTS = (
    -1.0,
    -0.8717401485096066,
    -0.5917001814331423,
    -0.2092992179024789,
    0.2092992179024789,
    0.5917001814331423,
    0.8717401485096066,
    1.0,
)


def legendre_value(points, degree):
    previous = points * 0.0 + 1.0
    current = points
    for order in range(1, degree):
        following = ((2 * order + 1) * points * current - order * previous) / (order + 1)
        previous = current
        current = following
    return current


def quadrature_tables():
    degree = 7
    points = np.array(LOBATTO_POINTS)
    values = legendre_value(points, degree)
    weights = 2.0 / (degree * (degree + 1) * values * values)
    derive = np.zeros((degree + 1, degree + 1))
    for row_index in range(degree + 1):
        for column_index in range(degree + 1):
            if row_index != column_index:
                derive[row_index, column_index] = values[row_index] / (
                    values[column_index] * (points[row_index] - points[column_index])
                )
    derive[0, 0] = -degree * (degree + 1) / 4.0
    derive[degree, degree] = degree * (degree + 1) / 4.0
    stiffness_table = derive.T @ (weights[:, None] * derive)
    return (weights, derive, stiffness_table)


WEIGHTS, DERIVE, STIFF = quadrature_tables()
SLOPE = WEIGHTS[:, None] * DERIVE
COPIES = np.where(np.arange(8) % 7 == 0, 2.0, 1.0)


def chebyshev_bounds():
    weight_matrix = np.eye(8) * WEIGHTS

    def kron3(a, b, c):
        return np.kron(np.kron(a, b), c)

    element_matrix = (
        kron3(STIFF, weight_matrix, weight_matrix)
        + kron3(weight_matrix, STIFF, weight_matrix)
        + kron3(weight_matrix, weight_matrix, STIFF)
        + SIGMA_SHIFT * kron3(weight_matrix, weight_matrix, weight_matrix)
    )
    bounds_ratio = np.sum(np.abs(element_matrix), axis=1) / np.diagonal(element_matrix)
    upper_bound = float(np.max(bounds_ratio))
    lower_bound = upper_bound / SPREAD
    return ((upper_bound + lower_bound) / 2.0, (upper_bound - lower_bound) / 2.0)


def spectrum_top(diffuse):
    root = np.sqrt(COPIES)
    stiff = root[:, None] * STIFF * root[None, :]
    weight = np.diag(WEIGHTS * COPIES)

    def kron3(a, b, c):
        return np.kron(np.kron(a, b), c)

    element = diffuse * (
        kron3(stiff, weight, weight) + kron3(weight, stiff, weight) + kron3(weight, weight, stiff)
    ) + STEP_MAX * kron3(weight, weight, weight)
    return float(np.linalg.eigvalsh(element)[-1])


def line_sums(table, length):
    matrix = np.kron(np.eye(length // 8), table)
    total = matrix.copy()
    for start in range(8, length, 8):
        total[start] += matrix[start - 1]
        total[start - 1] += matrix[start]
    return total


def depth_line(vector, length):
    line = np.tile(vector * COPIES, length // 8)
    line[0] = vector[0]
    line[-1] = vector[-1]
    return line


def f32(array):
    return np.ascontiguousarray(array, np.float32)


def rolled_rows(table):
    out = np.zeros((8, 8, 128))
    for shift in range(8):
        for row in range(8):
            out[shift, row] = table[row, (row - shift) % 8]
    return out


def block(a, b, c):
    return a[:, None, None] * b[:, None] * c


def parts_of(matrix):
    rest, parts = f32(matrix), []
    for _ in range(3):
        parts.append(rest.astype(ml_dtypes.bfloat16))
        rest = rest - parts[-1].astype(np.float32)
    hi, mid, lo = parts
    return np.block([[hi, mid], [hi, mid]]), np.concatenate([hi, lo])


def left_parts(table):
    rest, parts = f32(np.kron(np.eye(8), table)), []
    for _ in range(3):
        parts.append(rest.astype(ml_dtypes.bfloat16))
        rest = rest - parts[-1].astype(np.float32)
    hi, mid, lo = parts
    return np.block([[hi, hi], [mid, mid]]), np.concatenate([hi, lo], axis=1)


class Tables:
    def __init__(self, width, depth):
        self.left_y = left_parts(line_sums(STIFF, width))
        self.plain_y = left_parts(np.kron(np.eye(width // 8), STIFF))
        ones8, ones = np.ones(8), np.ones(depth)
        wide = WEIGHTS * COPIES
        deep = depth_line(WEIGHTS, depth)
        flat = np.tile(WEIGHTS, depth // 8)
        stiff = np.diagonal(STIFF)
        wide_s, deep_s = stiff * COPIES, depth_line(stiff, depth)
        share = 1.0 / COPIES
        share_z = np.tile(share, depth // 8)
        share_z[0] = share_z[-1] = 1.0
        self.summed = f32(
            np.stack([block(ones8, wide, deep), block(wide, ones8, deep), block(wide, wide, ones)])
        )
        self.local = f32(
            np.stack(
                [block(ones8, WEIGHTS, flat), block(WEIGHTS, ones8, flat), block(WEIGHTS, WEIGHTS, ones)]
            )
        )
        self.share = f32(block(share, share, share_z))
        diagonal = (
            block(wide_s, wide, deep)
            + block(wide, wide_s, deep)
            + block(wide, wide, deep_s)
            + SIGMA_SHIFT * block(wide, wide, deep)
        )
        self.inverse = f32(1.0 / diagonal)
        self.shift = f32(SIGMA_SHIFT * block(wide, wide, deep))
        self.stiff_y = f32(rolled_rows(STIFF))
        self.slope_y = f32(rolled_rows(SLOPE))
        self.stiff_z = parts_of(line_sums(STIFF, depth).T)
        self.plain_z = parts_of(np.kron(np.eye(depth // 8), STIFF).T)
        self.slope_z = parts_of(line_sums(SLOPE, depth).T)


def row_marks():
    row = lax.broadcasted_iota(jnp.int32, (8, 128), 0)
    return jnp.where(row == 0, 1.0, 0.0), jnp.where(row == 7, 1.0, 0.0)


def by_place(vector, place):
    out = jnp.full(place.shape, float(vector[0]), jnp.float32)
    for i in range(1, 8):
        out = jnp.where(place == i, float(vector[i]), out)
    return out


def along_x(rows, table):
    if np.allclose(table, table[::-1, ::-1]):
        even = 0.5 * (table[:4, :4] + table[:4, :3:-1])
        odd = 0.5 * (table[:4, :4] - table[:4, :3:-1])
        plus = [rows[i] + rows[7 - i] for i in range(4)]
        minus = [rows[i] - rows[7 - i] for i in range(4)]
        out = [None] * 8
        for a in range(4):
            p = sum(float(even[a, b]) * plus[b] for b in range(4))
            m = sum(float(odd[a, b]) * minus[b] for b in range(4))
            out[a], out[7 - a] = p + m, p - m
        return out
    return [sum(float(table[a, b]) * rows[b] for b in range(8)) for a in range(8)]


def along_y(tiles, factors):
    total = factors[0] * tiles
    for shift in range(1, 8):
        total = total + factors[shift] * pltpu.roll(tiles, shift, axis=1)
    return total


def along_z(tiles, matrix):
    wide, rest = matrix
    shape, depth = tiles.shape, tiles.shape[-1]
    flat = tiles.reshape(-1, depth)
    hi = flat.astype(jnp.bfloat16)
    flat = flat - hi.astype(jnp.float32)
    mid = flat.astype(jnp.bfloat16)
    lo = (flat - mid.astype(jnp.float32)).astype(jnp.bfloat16)
    first = jnp.dot(jnp.concatenate([hi, mid], axis=1), wide[...], preferred_element_type=jnp.float32)
    second = jnp.dot(jnp.concatenate([lo, hi], axis=1), rest[...], preferred_element_type=jnp.float32)
    return (first[:, :depth] + (first[:, depth:] + second)).reshape(shape)


def along_both(tiles, matrix, left):
    wide, rest = matrix
    tall, short = left
    shape, depth = tiles.shape, tiles.shape[-1]
    flat = tiles.reshape(-1, depth)
    lines = flat.shape[0]
    hi = flat.astype(jnp.bfloat16)
    flat = flat - hi.astype(jnp.float32)
    mid = flat.astype(jnp.bfloat16)
    lo = (flat - mid.astype(jnp.float32)).astype(jnp.bfloat16)

    def dot(a, b):
        return jnp.dot(a, b, preferred_element_type=jnp.float32)

    first = dot(jnp.concatenate([hi, mid], axis=1), wide[...])
    second = dot(jnp.concatenate([lo, hi], axis=1), rest[...])
    z_sums = first[:, :depth] + (first[:, depth:] + second)
    first = dot(tall[...], jnp.concatenate([hi, mid], axis=0))
    second = dot(short[...], jnp.concatenate([lo, hi], axis=0))
    y_sums = first[:lines] + (first[lines:] + second)
    return y_sums.reshape(shape), z_sums.reshape(shape)


def fill_z(out, field, matrix):
    for x in range(0, out.shape[0], 16):
        rows = pl.ds(x, min(16, out.shape[0] - x))
        out[rows] = along_z(field[rows], matrix)


def join_y(parts, low, high):
    out = list(parts)
    for e in range(1, len(parts)):
        out[e - 1] = out[e - 1] + high * pltpu.roll(parts[e], 7, axis=1)
        out[e] = out[e] + low * pltpu.roll(parts[e - 1], 1, axis=1)
    return out


def spread_rows(rows):
    return jnp.broadcast_to(rows[:, None, :], (rows.shape[0], 8, rows.shape[1]))


def column_sums(x_rows, y_parts, z_parts, summed, edges):
    if edges is not None:
        y_parts = join_y(y_parts, edges[0], edges[1])
    return [
        jnp.stack(kx) * summed[0, 0] + ky * summed[1] + kz * summed[2]
        for kx, ky, kz in zip(x_rows, y_parts, z_parts)
    ]


def emit_column(ex, x_rows, y_parts, z_parts, summed, edges, out, state, finish=None, factor=None):
    rows = pl.ds(8 * ex, 8)
    parts = column_sums(x_rows, y_parts, z_parts, summed, edges)
    for e, part in enumerate(parts):
        ys = pl.ds(8 * e, 8)
        out[rows, ys] = part if finish is None else finish(e, part)
        if ex:
            for row, face in ((8 * ex, state[e]), (8 * ex - 1, x_rows[e][0])):
                face = face * summed[0, 0]
                out[row, ys] += face if factor is None else face * factor(row, ys)
    return [r[7] for r in x_rows]


def end_rows(table):
    row = lax.broadcasted_iota(jnp.int32, (8, 128), 0)
    return (table[0], table[7]), (by_place(table[0], row), by_place(table[7], row))


def store_faces(ex, e, columns, count, tile, even, ends, faces, x=True, y=True):
    x_near, x_far, y_near, y_far = faces
    (x_low, x_high), (y_low, y_high) = ends
    rows, ys = pl.ds(8 * ex, 8), pl.ds(8 * e, 8)
    if x and ex == 0:
        low = sum(float(x_low[i]) * tile[i] for i in range(8))
        x_near[ys] = low
        x_far[ys] = low
    if x and ex == columns - 1:
        high = sum(float(x_high[i]) * tile[i] for i in range(8))
        x_near[ys] = jnp.where(even[0], high, x_near[ys])
        x_far[ys] = jnp.where(even[0], x_far[ys], high)
    if y and e == 0:
        low = jnp.sum(tile * y_low, axis=1)
        y_near[rows] = low
        y_far[rows] = low
    if y and e == count - 1:
        high = jnp.sum(tile * y_high, axis=1)
        y_near[rows] = jnp.where(even[1], high, y_near[rows])
        y_far[rows] = jnp.where(even[1], y_far[rows], high)


def parity(even_ref):
    return even_ref[0] > 0.5, even_ref[1] > 0.5


def even_rows(even_ref):
    return even_ref[0, 0:1] > 0.5, even_ref[1, 0:1] > 0.5


def before_of(even, near, far):
    return jnp.where(even, far, near)


def after_of(even, near, far):
    return jnp.where(even, near, far)


def with_faces(tile, ex, e, columns, count, received, even, edges, weight_x=None, weight_y=None, mask=None, x=True):
    x_far, x_near, y_far, y_near = received
    rows, ys = pl.ds(8 * ex, 8), pl.ds(8 * e, 8)

    def weighted(face, weight):
        return face if weight is None else face * weight

    if e == 0:
        face = before_of(even[1], y_near[rows], y_far[rows])
        face = spread_rows(face) * weighted(edges[0], weight_y)
        tile = tile + weighted(face, mask)
    if e == count - 1:
        face = after_of(even[1], y_near[rows], y_far[rows])
        face = spread_rows(face) * weighted(edges[1], weight_y)
        tile = tile + weighted(face, mask)
    if x and ex == 0:
        face = before_of(even[0], x_near[ys], x_far[ys])
        face = weighted(face, weight_x) if mask is None else weighted(face, weight_x) * mask[0]
        tile = jnp.concatenate([tile[0:1] + face[None], tile[1:]], axis=0)
    if x and ex == columns - 1:
        face = after_of(even[0], x_near[ys], x_far[ys])
        face = weighted(face, weight_x) if mask is None else weighted(face, weight_x) * mask[7]
        tile = jnp.concatenate([tile[:7], tile[7:8] + face[None]], axis=0)
    return tile


def split_rows(block_rows):
    return [block_rows[i] for i in range(8)]


def load_local(old_far, step_far, even_ref, out, x_near, x_far, y_near, y_far, old, step, arrived):
    columns, count, depth = out.shape[1] // 8, out.shape[2] // 8, out.shape[3]
    copies = [pltpu.make_async_copy(step_far, step, arrived.at[4])]
    copies += [pltpu.make_async_copy(old_far.at[i], old.at[i], arrived.at[i]) for i in range(4)]
    for copy in copies:
        copy.start()
    even, edges = parity(even_ref), row_marks()
    row = lax.broadcasted_iota(jnp.int32, (8, depth), 0)
    lane = lax.broadcasted_iota(jnp.int32, (8, depth), 1)
    place = lane & 7
    after = jnp.where((place == 0) & (lane > 0), 1.0, 0.0)
    before_z = jnp.where((place == 7) & (lane < depth - 1), 1.0, 0.0)
    plane = by_place(WEIGHTS, row) * by_place(WEIGHTS, place)
    mass = jnp.stack([float(w) * plane for w in WEIGHTS])
    for field in (4, 0, 1, 2, 3):
        if field != 3:
            copies[0 if field == 4 else field + 1].wait()
        if field == 2:
            copies[4].wait()
        before = [None] * count
        for ex in range(columns):
            rows = pl.ds(8 * ex, 8)
            parts = []
            for e in range(count):
                ys = pl.ds(8 * e, 8)
                value = step[rows, ys]
                if field < 4:
                    value = value * old[field, rows, ys]
                if field == 2:
                    value = value + COUPLING * old[3, rows, ys]
                if field == 3:
                    value = value - STRATIFY * old[2, rows, ys]
                value = value * mass
                value = (
                    value
                    + after * pltpu.roll(value, 1, axis=2)
                    + before_z * pltpu.roll(value, depth - 1, axis=2)
                )
                parts.append(value)
            parts = join_y(parts, edges[0], edges[1])
            for e in range(count):
                ys = pl.ds(8 * e, 8)
                out[field, rows, ys] = parts[e]
                if ex:
                    out[field, 8 * ex, ys] += before[e]
                    out[field, 8 * ex - 1, ys] += parts[e][0]
                before[e] = parts[e][7]
        for e in range(count):
            ys = pl.ds(8 * e, 8)
            low, high = out[field, 0, ys], out[field, 8 * columns - 1, ys]
            x_near[field, ys] = jnp.where(even[0], high, low)
            x_far[field, ys] = jnp.where(even[0], low, high)
        for ex in range(columns):
            rows = pl.ds(8 * ex, 8)
            low = out[field, rows, pl.ds(0, 8)][:, 0]
            high = out[field, rows, pl.ds(8 * count - 8, 8)][:, 7]
            y_near[field, rows] = jnp.where(even[1], high, low)
            y_far[field, rows] = jnp.where(even[1], low, high)


def stiff_terms(ex, tiles, stiff_y, z_sums):
    x_rows = [along_x(split_rows(t), STIFF) for t in tiles]
    y_parts = [along_y(t, stiff_y) for t in tiles]
    z_parts = [z_sums[pl.ds(8 * ex, 8), pl.ds(8 * e, 8)] for e in range(len(tiles))]
    return x_rows, y_parts, z_parts


def square_sum(rows):
    total = 0.0
    for sign in (1.0, -1.0):
        form = 0.5 * (STIFF[:4, :4] + sign * STIFF[:4, :3:-1])
        part = [rows[i] + rows[7 - i] if sign > 0 else rows[i] - rows[7 - i] for i in range(4)]
        for i in range(4):
            pivot = form[i, i]
            if pivot < 1e-12:
                continue
            line = form[i] / np.sqrt(pivot)
            value = sum(float(line[b]) * part[b] for b in range(i, 4))
            total = total + value * value
            form = form - np.outer(line, line)
    return total


def join_x(c, out, x_far, x_near, even, even_row, ends, weight, mask, faces, slopes, slope_ends):
    columns, count = out.shape[0] // 8, out.shape[1] // 8
    for xi, side in enumerate((before_of, after_of)):
        row = (8 * columns - 1) * xi
        mended = [[0.0, 0.0], [0.0, 0.0]]
        for e in range(count):
            ys = pl.ds(8 * e, 8)
            change = side(even[0], x_near[c, ys], x_far[c, ys]) * weight * mask(row, ys)
            out[row, ys] += change
            for kind, (low, high) in enumerate((ends[1], slope_ends[1])):
                if e == 0:
                    mended[kind][0] = jnp.sum(change * low, axis=0, keepdims=True)
                if e == count - 1:
                    mended[kind][1] = jnp.sum(change * high, axis=0, keepdims=True)
        for kind, where in enumerate((faces, slopes if c == 1 else None)):
            if where is not None:
                low, high = mended[kind]
                where[2][row : row + 1] += jnp.where(even_row[1], high, low)
                where[3][row : row + 1] += jnp.where(even_row[1], low, high)
    for ex in sorted({0, columns - 1}):
        for e in range(count):
            tile = out[pl.ds(8 * ex, 8), pl.ds(8 * e, 8)]
            if faces is not None:
                store_faces(ex, e, columns, count, tile, even, ends, faces, True, False)
            if slopes is not None and c == 0:
                store_faces(ex, e, columns, count, tile, even, slope_ends, slopes, True, False)


def y_faces(c, ex, e, columns, count, tile, even, ends, slope_ends, y_near, y_far):
    store_faces(ex, e, columns, count, tile, even, ends, (None, None, y_near.at[c], y_far.at[c]), False, True)
    if c == 1:
        slopes = (None, None, y_near.at[4], y_far.at[4])
        store_faces(ex, e, columns, count, tile, even, slope_ends, slopes, False, True)


def first_y(local, boundary, y_far, y_near, even_ref, part, y_near_out, y_far_out):
    columns, count = part.shape[1] // 8, part.shape[2] // 8
    even, edges = parity(even_ref), row_marks()
    ends, slope_ends = end_rows(STIFF), end_rows(SLOPE)
    for c in range(4):
        for ex in range(columns):
            for e in range(count):
                rows, ys = pl.ds(8 * ex, 8), pl.ds(8 * e, 8)
                tile = with_faces(local[c, rows, ys], ex, e, columns, count, (None, None, y_far.at[c], y_near.at[c]),
                                  even, edges, x=False)
                tile = tile * boundary[rows, ys].astype(jnp.float32)
                part[c, rows, ys] = tile
                y_faces(c, ex, e, columns, count, tile, even, ends, slope_ends, y_near_out, y_far_out)


def first_x(part, y_near_in, y_far_in, boundary, x_far, x_near, even_ref, right, near, far, x_near_out, x_far_out):
    del part, y_near_in, y_far_in
    columns, count = right.shape[1] // 8, right.shape[2] // 8
    even, even_row = parity(even_ref), even_rows(even_ref)
    ends, slope_ends = end_rows(STIFF), end_rows(SLOPE)
    faces = (x_near_out, x_far_out, near, far)
    for c in range(4):
        join_x(c, right.at[c], x_far, x_near, even, even_row, ends, 1.0,
               lambda row, ys: boundary[row, ys].astype(jnp.float32),
               [f.at[c] for f in faces], [f.at[4] for f in faces], slope_ends)
    near[5] = jnp.zeros(near.shape[1:], jnp.float32)
    far[5] = jnp.zeros(far.shape[1:], jnp.float32)
    for xi, side in enumerate((before_of, after_of)):
        for field in range(5):
            low, high = [
                side(even_row[0], x_near[field, y : y + 1], x_far[field, y : y + 1]) for y in (0, 8 * count - 1)
            ]
            row = 8 * xi + field
            near[5, row : row + 1] = jnp.where(even_row[1], high, low)
            far[5, row : row + 1] = jnp.where(even_row[1], low, high)


def pick(c, values):
    out = jnp.float32(values[0])
    for i in range(1, 4):
        out = jnp.where(c == i, jnp.float32(values[i]), out)
    return out


def start_sums(scales, rates, local, boundary, x_far, x_near, y_far, y_near, even_ref, right, summed, share, tall_y,
               short_y, wide_z, rest_z, reaction, free, ahead):
    columns, count = ahead.shape[1] // 8, ahead.shape[2] // 8
    even, edges = parity(even_ref), row_marks()
    received = [r.at[4] for r in (x_far, x_near, y_far, y_near)]
    for ex in range(columns):
        for e in range(count):
            rows, ys = pl.ds(8 * ex, 8), pl.ds(8 * e, 8)
            reaction[rows, ys] = with_faces(local[4, rows, ys], ex, e, columns, count, received, even, edges)
            free[rows, ys] = boundary[rows, ys].astype(jnp.float32)
    basis_fill(scales, rates, right, None, reaction, free, summed, share, (tall_y, short_y), (wide_z, rest_z), ahead)


def basis_sums(scales, rates, newest, older, reaction, free, summed, share, tall_y, short_y, wide_z, rest_z, ahead, *dots):
    left, matrix = (tall_y, short_y), (wide_z, rest_z)
    basis_fill(scales, rates, newest, older, reaction, free, summed, share, left, matrix, ahead, *dots)


def basis_fill(scales, rates, newest, older, reaction, free, summed, share, left, matrix, ahead, dots=None, first=None):
    columns, count = ahead.shape[1] // 8, ahead.shape[2] // 8
    double = 1.0 if older is None else 2.0

    def component(c, carry):
        scale, rate = pick(c, [double * v for v in scales]), pick(c, [double * v for v in rates])
        same = jnp.zeros((8, 128), jnp.float32)
        cross = jnp.zeros((8, 128), jnp.float32)
        start = jnp.zeros((8, 128), jnp.float32)
        state = None
        for ex in range(columns):
            rows = pl.ds(8 * ex, 8)
            tiles = []
            for e in range(count):
                ys = pl.ds(8 * e, 8)
                tile = newest[c, rows, ys]
                if older is not None:
                    weighted = tile * share[...]
                    same = same + jnp.sum(weighted * tile, axis=0)
                    cross = cross + jnp.sum(weighted * older[c, rows, ys], axis=0)
                if first is not None:
                    start = start + jnp.sum(older[c, rows, ys] * older[c, rows, ys] * share[...], axis=0)
                tiles.append(tile)
            x_rows = [along_x(split_rows(t), STIFF) for t in tiles]
            y_all, z_all = along_both(newest[c, rows], matrix, left)
            y_parts = [y_all[:, 8 * e : 8 * e + 8] for e in range(count)]
            z_parts = [z_all[:, 8 * e : 8 * e + 8] for e in range(count)]

            def finish(e, part):
                ys = pl.ds(8 * e, 8)
                value = scale * part + (rate * reaction[rows, ys] - double) * tiles[e]
                value = value * free[rows, ys]
                return value if older is None else value - older[c, rows, ys]

            state = emit_column(ex, x_rows, y_parts, z_parts, summed, None, ahead.at[c], state, finish,
                                lambda row, ys: scale * free[row, ys])
        if older is not None:
            dots[pl.ds(c, 1)] = jnp.sum(same, axis=0, keepdims=True)
            dots[pl.ds(c + 4, 1)] = jnp.sum(cross, axis=0, keepdims=True)
        if first is not None:
            first[pl.ds(c, 1)] = jnp.sum(start, axis=0, keepdims=True)
            first[pl.ds(c + 4, 1)] = jnp.zeros((1, 128), jnp.float32)
        return carry

    lax.fori_loop(0, 4, component, 0)


def y_field(c, ex, e, ahead, free, y_far, y_near, scale, summed, edges, even, columns, count):
    rows, ys = pl.ds(8 * ex, 8), pl.ds(8 * e, 8)
    return with_faces(ahead[c, rows, ys], ex, e, columns, count, (None, None, y_far.at[c], y_near.at[c]), even, edges,
                      None, summed[1], scale * free[rows, ys], x=False)


def grow_y(scales, ahead, free, y_far, y_near, even_ref, summed, part, y_near_out, y_far_out):
    columns, count = part.shape[1] // 8, part.shape[2] // 8
    even, edges = parity(even_ref), row_marks()
    ends, slope_ends = end_rows(STIFF), end_rows(SLOPE)
    for c in range(4):
        for ex in range(columns):
            for e in range(count):
                tile = y_field(c, ex, e, ahead, free, y_far, y_near, scales[c], summed, edges, even, columns, count)
                part[c, pl.ds(8 * ex, 8), pl.ds(8 * e, 8)] = tile
                y_faces(c, ex, e, columns, count, tile, even, ends, slope_ends, y_near_out, y_far_out)


def grow_x(scales, part, y_near_in, y_far_in, free, x_far, x_near, even_ref, summed, out, y_near_out, y_far_out,
           x_near_out, x_far_out):
    del part, y_near_in, y_far_in
    even, even_row = parity(even_ref), even_rows(even_ref)
    ends, slope_ends = end_rows(STIFF), end_rows(SLOPE)
    faces = (x_near_out, x_far_out, y_near_out, y_far_out)
    for c in range(4):
        join_x(c, out.at[c], x_far, x_near, even, even_row, ends, scales[c] * summed[0, 0],
               lambda row, ys: free[row, ys], [f.at[c] for f in faces], [f.at[4] for f in faces], slope_ends)


def second_y(scales, rates, ahead, free, x_far0, x_near0, y_far0, y_near0, y_far, y_near, even_ref, summed, wide_z,
             rest_z, right_in, reaction_in, out, right, reaction, y_near_out, y_far_out, lines, depth_lines):
    columns, count = out.shape[1] // 8, out.shape[2] // 8
    even, edges, even_row = parity(even_ref), row_marks(), even_rows(even_ref)
    ends, slope_ends = end_rows(STIFF), end_rows(SLOPE)
    end_x, end_y = (0, 8 * columns - 1), (0, 8 * count - 1)
    sides = (before_of, after_of)
    corners = [(xi, yi) for xi in (0, 1) for yi in (0, 1)]

    def at(array, xi, yi):
        return array[end_x[xi], end_y[yi] : end_y[yi] + 1]

    def diagonal(field, xi, yi):
        row = 8 * xi + field
        return sides[yi](even_row[1], y_near[5, row : row + 1], y_far[5, row : row + 1])

    def beside(field, xi, yi):
        row = end_y[yi]
        return sides[xi](even_row[0], x_near0[field, row : row + 1], x_far0[field, row : row + 1])

    def beyond(field, xi, yi):
        row = end_x[xi]
        return sides[yi](even_row[1], y_near0[field, row : row + 1], y_far0[field, row : row + 1])

    for c in range(4):
        for n, (xi, yi) in enumerate(corners):
            lines[4 * c + n : 4 * c + n + 1] = diagonal(c, xi, yi) * at(free, xi, yi)
    depth_lines[...] = along_z(lines[...], (wide_z, rest_z))

    def missed(c, ex, e):
        found = []
        for n, (xi, yi) in enumerate(corners):
            cx, ce, sx, sy = (columns - 1) * xi, (count - 1) * yi, 7 * xi, 7 * yi
            line = lines[4 * c + n : 4 * c + n + 1]
            weight_x, weight_y = summed[0, 0, sy : sy + 1], summed[1, sx, 0:1]
            along = scales[c] * line * weight_x
            across = scales[c] * line * weight_y
            if ex == cx and e == ce:
                for i in range(8):
                    found.append((i, float(STIFF[i, sx]) * along * edges[yi]))
                found.append((sx, across * ends[1][yi]))
                side = beyond(c, xi, yi) * weight_x + beside(c, xi, yi) * weight_y
                side = float(STIFF[0, 0]) * side
                depth = depth_lines[4 * c + n : 4 * c + n + 1] * summed[2, sx, sy : sy + 1]
                gained = diagonal(4, xi, yi)
                node = scales[c] * (side + depth)
                node = node + (rates[c] * (at(reaction_in, xi, yi) + gained) - 1.0) * line
                node = node + rates[c] * gained * at(right_in.at[c], xi, yi)
                found.append((sx, node * edges[yi]))
            elif e == ce and ex == cx + 1 - 2 * xi:
                found.append((sx, float(STIFF[7 - sx, sx]) * along * edges[yi]))
            elif ex == cx and e == ce + 1 - 2 * yi:
                found.append((sx, float(STIFF[7 - sy, sy]) * across * edges[yi]))
        return found

    for c in range(4):
        for ex in range(columns):
            for e in range(count):
                rows, ys = pl.ds(8 * ex, 8), pl.ds(8 * e, 8)
                tile = y_field(c, ex, e, ahead, free, y_far, y_near, scales[c], summed, edges, even, columns, count)
                found = missed(c, ex, e)
                if found:
                    parts = []
                    for i in range(8):
                        extra = [t for row, t in found if row == i]
                        parts.append(tile[i] + sum(extra) * free[8 * ex + i, ys] if extra else tile[i])
                    tile = jnp.stack(parts)
                out[c, rows, ys] = tile
                y_faces(c, ex, e, columns, count, tile, even, ends, slope_ends, y_near_out, y_far_out)

    for n, (xi, yi) in enumerate(corners):
        x, y = end_x[xi], end_y[yi]
        reaction[x, y : y + 1] = at(reaction_in, xi, yi) + diagonal(4, xi, yi)
        for c in range(4):
            right[c, x, y : y + 1] = at(right_in.at[c], xi, yi) + lines[4 * c + n : 4 * c + n + 1]


def mend_slopes(x_far0, x_near0, y_far0, y_near0, x_far, x_near, y_far, y_near, free, even_ref,
                sx_far, sx_near, sy_far, sy_near):
    even_row = even_rows(even_ref)
    end_x, end_y = (0, free.shape[0] - 1), (0, free.shape[1] - 1)
    sides = (before_of, after_of)

    def at(array, xi, yi):
        return array[end_x[xi], end_y[yi] : end_y[yi] + 1]

    def beside(field, xi, yi):
        row = end_y[yi]
        return sides[xi](even_row[0], x_near0[field, row : row + 1], x_far0[field, row : row + 1])

    def beyond(field, xi, yi):
        row = end_x[xi]
        return sides[yi](even_row[1], y_near0[field, row : row + 1], y_far0[field, row : row + 1])

    sx_far[...], sx_near[...], sy_far[...], sy_near[...] = x_far[4], x_near[4], y_far[4], y_near[4]
    low, high = float(SLOPE[7, 7]), float(SLOPE[0, 0])
    for i in (0, 1):
        y, x = end_y[i], end_x[i]
        before = low * beyond(0, 0, i) * at(free, 0, i)
        after = high * beyond(0, 1, i) * at(free, 1, i)
        sx_near[y : y + 1] += jnp.where(even_row[0], after, before)
        sx_far[y : y + 1] += jnp.where(even_row[0], before, after)
        before = low * beside(1, i, 0) * at(free, i, 0)
        after = high * beside(1, i, 1) * at(free, i, 1)
        sy_near[x : x + 1] += jnp.where(even_row[1], after, before)
        sy_far[x : x + 1] += jnp.where(even_row[1], before, after)


def column_products(c, ex, out, newest, reaction, share, left, matrix, local, scale, rate):
    count = out.shape[2] // 8
    rows = pl.ds(8 * ex, 8)
    same = jnp.zeros((8, 128), jnp.float32)
    cross = jnp.zeros((8, 128), jnp.float32)
    work = jnp.zeros((8, 128), jnp.float32)
    y_sums, z_sums = along_both(out[c, rows], matrix, left)
    for e in range(count):
        ys = pl.ds(8 * e, 8)
        tile = out[c, rows, ys]
        weighted = tile * share[...]
        same = same + jnp.sum(weighted * tile, axis=0)
        cross = cross + jnp.sum(weighted * newest[c, rows, ys], axis=0)
        extra = (rate * reaction[rows, ys] - 1.0) * tile
        work = work + jnp.sum(weighted * extra, axis=0)
        work = work + scale * (square_sum(split_rows(tile)) * local[0, 0])
        term = y_sums[:, 8 * e : 8 * e + 8] * local[1] + z_sums[:, 8 * e : 8 * e + 8] * local[2]
        work = work + scale * jnp.sum(term * tile, axis=0)
    return same, cross, work


def last_y(scales, rates, ahead, newest, reaction, free, y_far, y_near, even_ref, summed, share, tall_y, short_y, wide_z,
           rest_z, local, part, sy_near, sy_far, products):
    columns, count = part.shape[1] // 8, part.shape[2] // 8
    even, edges = parity(even_ref), row_marks()
    slope_ends = end_rows(SLOPE)
    for c in range(4):
        total = [jnp.zeros((8, 128), jnp.float32)] * 3
        for ex in range(columns):
            for e in range(count):
                tile = y_field(c, ex, e, ahead, free, y_far, y_near, 2.0 * scales[c], summed, edges, even, columns, count)
                part[c, pl.ds(8 * ex, 8), pl.ds(8 * e, 8)] = tile
                if c == 1:
                    store_faces(ex, e, columns, count, tile, even, slope_ends, (None, None, sy_near, sy_far), False, True)
            if 0 < ex < columns - 1:
                found = column_products(c, ex, part, newest, reaction, share, (tall_y, short_y), (wide_z, rest_z), local,
                                        scales[c], rates[c])
                total = [a + b for a, b in zip(total, found)]
        for n in range(3):
            products[c, n] = total[n]


def last_x(scales, rates, part, sy_near_in, sy_far_in, products, newest, reaction, free, x_far, x_near, even_ref, summed,
           share, tall_y, short_y, wide_z, rest_z, local, d0, d1, d2, d3, d4, out, sy_near, sy_far, sums, sx_near, sx_far):
    del part, sy_near_in, sy_far_in
    dots = (d0, d1, d2, d3, d4)
    columns = out.shape[1] // 8
    even, even_row = parity(even_ref), even_rows(even_ref)
    ends, slope_ends = end_rows(STIFF), end_rows(SLOPE)
    for i in range(1, ITERS - 1):
        sums[i] = dots[i][...]
    for c in range(4):
        join_x(c, out.at[c], x_far, x_near, even, even_row, ends, 2.0 * scales[c] * summed[0, 0],
               lambda row, ys: free[row, ys], None, (sx_near, sx_far, sy_near, sy_far), slope_ends)
        total = [products[c, n] for n in range(3)]
        for ex in sorted({0, columns - 1}):
            found = column_products(c, ex, out, newest, reaction, share, (tall_y, short_y), (wide_z, rest_z), local,
                                    scales[c], rates[c])
            total = [a + b for a, b in zip(total, found)]
        same, cross, work = [jnp.sum(t, axis=0, keepdims=True) for t in total]
        sums[ITERS - 1, c : c + 1] = same
        sums[ITERS - 1, c + 4 : c + 5] = cross
        sums[0, c : c + 1] = dots[0][c : c + 1]
        sums[0, c + 4 : c + 5] = work


def slope_sums(*refs):
    fields, (summed, slope_y, wide_z, rest_z), outs = refs[:3], refs[3:7], refs[7:]
    columns, count = outs[0].shape[1] // 8, outs[0].shape[2] // 8
    edges = row_marks()
    for field, out in zip(fields, outs):
        fill_z(out.at[2], field.at[2], (wide_z, rest_z))
        state = None
        for ex in range(columns):
            rows, ends = pl.ds(8 * ex, 8), []
            y_parts = [along_y(field[1, rows, pl.ds(8 * e, 8)], slope_y) for e in range(count)]
            y_parts = join_y(y_parts, edges[0], edges[1])
            for e in range(count):
                ys = pl.ds(8 * e, 8)
                out[1, rows, ys] = y_parts[e] * summed[1]
                out[2, rows, ys] = out[2, rows, ys] * summed[2]
                x_rows = [r * summed[0, 0] for r in along_x(split_rows(field[0, rows, ys]), SLOPE)]
                out[0, rows, ys] = jnp.stack(x_rows)
                if ex:
                    out[0, 8 * ex, ys] += state[e]
                    out[0, 8 * ex - 1, ys] += x_rows[0]
                ends.append(x_rows[7])
            state = ends


def first_update(halves, gain, *refs):
    sums, *sloped = refs[: ITERS + 1]
    refs = refs[ITERS + 1 :]
    slopes = [refs[:4]]
    slopes += [[r.at[4] for r in refs[4 * k : 4 * k + 4]] for k in range(1, ITERS - 1)]
    refs = refs[4 * ITERS - 4 :]
    slopes.append(refs[:4])
    even_ref, free, summed, inverse = refs[4:8]
    weights, remainder, update, *faces = refs[8:15]
    joined = refs[15:]
    columns, count = update.shape[0] // 8, update.shape[1] // 8
    even, edges = parity(even_ref), row_marks()
    ends = end_rows(STIFF)
    total = [jnp.broadcast_to(jnp.sum(sums[i], axis=1, keepdims=True), (8, 128)) for i in range(ITERS)]
    other = [pltpu.roll(t, 4, axis=0) for t in total]
    row = lax.broadcasted_iota(jnp.int32, (8, 128), 0)
    half = jnp.full((8, 128), halves[0], jnp.float32)
    for i in range(1, 4):
        half = jnp.where(row == i, halves[i], half)
    moments = [total[0], other[1]]
    for level in range(2, 2 * ITERS - 1):
        inner = total[level // 2] if level % 2 == 0 else other[level // 2 + 1]
        moments.append(2.0 * inner - moments[level % 2])
    top = 2.0 * other[0] - other[5]
    moments.append(2.0 * top - moments[1])
    for i, value in enumerate(conjugate_coefficients(moments, half, half)):
        weights[i] = value
    for n in range(4):
        c = n // 2
        joined[n][...] = sum(slopes[i][n][...] * weights[i, c : c + 1] for i in range(ITERS))
    factor = [[weights[i, c : c + 1][None] for c in range(3)] for i in range(ITERS)]
    for ex in range(columns):
        for e in range(count):
            rows, ys = pl.ds(8 * ex, 8), pl.ds(8 * e, 8)
            tile = sum(sloped[i][c, rows, ys] * factor[i][c] for i in range(ITERS) for c in range(3))
            tile = with_faces(tile, ex, e, columns, count, joined, even, edges, summed[0, 0], summed[1])
            left = -tile * free[rows, ys]
            change = gain * inverse[...] * left
            remainder[rows, ys] = left
            update[rows, ys] = change
            store_faces(ex, e, columns, count, change, even, ends, faces)


def combine_fields(weights, *refs):
    *basis, fields = refs

    def combine(c, carry):
        factor = [weights[i, pl.ds(c, 1)] for i in range(ITERS)]
        for x in range(0, fields.shape[1], 8):
            rows = pl.ds(x, 8)
            value = basis[0][c, rows] * factor[0][None]
            for i in range(1, ITERS):
                value = value + basis[i][c, rows] * factor[i][None]
            fields[c, rows] = value
        return carry

    lax.fori_loop(0, 4, combine, 0)


def add_loads(count, *refs):
    *loads, rider, tick, out = refs
    del tick
    values = [load[:count] for load in loads]
    total = values[0] + values[1]
    if len(values) == 4:
        total = total + (values[2] + values[3])
    out[:count] = total
    out[count:] = rider[...]


def pressure_sums(update, summed, shift, stiff_y, wide_z, rest_z, raw, z_sums):
    columns, count = raw.shape[0] // 8, raw.shape[1] // 8
    edges = row_marks()
    state = None
    fill_z(z_sums, update, (wide_z, rest_z))
    for ex in range(columns):
        rows = pl.ds(8 * ex, 8)
        tiles = [update[rows, pl.ds(8 * e, 8)] for e in range(count)]
        x_rows, y_parts, z_parts = stiff_terms(ex, tiles, stiff_y, z_sums)
        state = emit_column(ex, x_rows, y_parts, z_parts, summed, edges, raw, state,
                            lambda e, part: part + shift[...] * tiles[e])


def pressure_step(last, keep, gain, *refs):
    raw, free, *received, even_ref, summed, inverse, remainder_in, update_in, pressure_in = refs[:12]
    if last:
        pressure_far, pressure, left_here = refs[12:]
    else:
        pressure, remainder, update, *faces = refs[12:]
    columns, count = raw.shape[0] // 8, raw.shape[1] // 8
    copies = []
    even, edges = parity(even_ref), row_marks()
    ends = end_rows(STIFF)
    for ex in range(columns):
        for e in range(count):
            rows, ys = pl.ds(8 * ex, 8), pl.ds(8 * e, 8)
            tile = with_faces(raw[rows, ys], ex, e, columns, count, received, even, edges,
                              summed[0, 0], summed[1])
            left = remainder_in[rows, ys] - tile * free[rows, ys]
            change = gain * inverse[...] * left + keep * update_in[rows, ys]
            pressure[rows, ys] = pressure_in[rows, ys] + change
            if not last:
                remainder[rows, ys] = left
                update[rows, ys] = change
                store_faces(ex, e, columns, count, change, even, ends, faces)
        if last:
            rows = pl.ds(8 * ex, 8)
            copies.append(pltpu.make_async_copy(pressure.at[rows], pressure_far.at[rows], left_here.at[ex]))
            copies[-1].start()
    for copy in copies:
        copy.wait()


VMEM_BYTES = 24 * 1024 * 1024


def call(kernel, name, outs, *args, scratch=(), cost=None, far_in=0, far_out=0, copies=0, aliases=()):
    held, far = pl.BlockSpec(memory_space=pltpu.VMEM), pl.BlockSpec(memory_space=pltpu.HBM)
    scratch_shapes = [pltpu.VMEM(s, jnp.float32) for s in scratch]
    if copies:
        scratch_shapes.append(pltpu.SemaphoreType.DMA((copies,)))
    return pl.pallas_call(
        kernel,
        name=name,
        out_shape=[jax.ShapeDtypeStruct(s, jnp.float32) for s in outs],
        in_specs=[far] * far_in + [held] * (len(args) - far_in),
        out_specs=[far] * far_out + [held] * (len(outs) - far_out),
        scratch_shapes=scratch_shapes,
        cost_estimate=cost,
        input_output_aliases=dict(aliases),
        compiler_params=pltpu.CompilerParams(vmem_limit_bytes=VMEM_BYTES),
    )(*[pltpu.with_memory_space_constraint(a, pltpu.HBM) for a in args[:far_in]], *args[far_in:])


def busy(bytes_accessed):
    return pl.CostEstimate(flops=0, bytes_accessed=bytes_accessed, transcendentals=0)


def swap_near(axis, face):
    return lax.ppermute(face, axis, [(i, i ^ 1) for i in range(lax.axis_size(axis))])


def swap_far(axis, face):
    size = lax.axis_size(axis)
    return lax.ppermute(face, axis, [(i, far_partner(i, size)) for i in range(size)])


def swap_all(x_near, x_far, y_near, y_far):
    y_far = swap_far("gy", y_far)
    x_far = swap_far("gx", x_far)
    x_near = swap_near("gx", x_near)
    y_near = swap_near("gy", y_near)
    return x_far, x_near, y_far, y_near


def far_partner(i, size):
    return (i + 1 if i % 2 else i - 1) % size


def partner_loads(load, axis, partners, riders, count):
    size, heard, faces = lax.axis_size(axis), [], []
    for n, (partner, rider) in enumerate(zip(partners, riders)):
        mine = load
        if n:
            mine = load[:count] if rider is None else jnp.concatenate([load[:count], rider])
        mine = lax.ppermute(mine, axis, [(i, partner(i)) for i in range(size)])
        heard.append(mine)
        if rider is not None:
            faces.append(mine[count:])
    return heard, faces


def all_sum(values, axis, near, far, following, meanwhile):
    size = lax.axis_size(axis)
    count = values.shape[0] - far.shape[0] if following is None else values.shape[0]
    half = size // 2

    def to_near(i):
        return i ^ 1

    def to_far(i):
        return far_partner(i, size)

    def across(i):
        return (i + half) % size

    def far_across(i):
        return across(to_far(i))

    rounds = [((to_far,), (far,))]
    if size == 4:
        rounds = [((to_far, to_near, across), (far, near, None))]
    elif size > 4:
        rounds = [((to_far, across, far_across), (far, None, None)), ((to_near,), (near,))]
        bit = 4
        while bit < half:
            rounds.append(((lambda i, bit=bit: i ^ bit,), (None,)))
            bit *= 2
    else:
        rounds.append(((), (near,)))
    faces = []
    load = values if following is None else jnp.concatenate([values, far])
    for n, (partners, riders) in enumerate(rounds):
        if not partners:
            faces.append(lax.ppermute(near, axis, [(i, to_near(i)) for i in range(size)]))
            continue
        heard, got = partner_loads(load, axis, partners, riders, count)
        faces += got
        rider = rounds[n + 1][1][0] if n + 1 < len(rounds) and rounds[n + 1][0] else following
        tail = jnp.zeros((8, values.shape[1]), jnp.float32) if rider is None else rider
        (load,) = call(
            functools.partial(add_loads, count), "add_loads", [(count + tail.shape[0], values.shape[1])],
            load, *heard, tail, meanwhile(),
        )
    if following is None:
        load = load[:count]
    return load, faces[1], faces[0]


def conjugate_coefficients(moments, centre, half):
    remaining, towards = list(moments), list(moments)
    one, zero = jnp.ones_like(moments[0]), jnp.zeros_like(moments[0])
    direction = [one] + [zero] * ITERS
    residual = list(direction)
    total = [zero] * ITERS
    for step in range(ITERS):
        count = len(towards) - 1
        image = []
        for level in range(count):
            side = (
                half * towards[1] if level == 0 else 0.5 * half * (towards[level + 1] + towards[level - 1])
            )
            image.append(centre * towards[level] + side)
        alpha = remaining[step] / image[step]
        total = [total[i] + alpha * direction[i] for i in range(ITERS)]
        if step == ITERS - 1:
            break
        applied = []
        for i in range(ITERS + 1):
            term = centre * direction[i]
            if i >= 1:
                term = term + (half if i == 1 else 0.5 * half) * direction[i - 1]
            if i < ITERS:
                term = term + 0.5 * half * direction[i + 1]
            applied.append(term)
        residual = [residual[i] - alpha * applied[i] for i in range(ITERS + 1)]
        following = [remaining[i] - alpha * image[i] for i in range(count)]
        beta = -alpha * (half if step == 0 else 0.5 * half) * following[step + 1] / remaining[step]
        towards = [following[i] + beta * towards[i] for i in range(count)]
        direction = [residual[i] + beta * direction[i] for i in range(ITERS + 1)]
        remaining = following
    return total


def on_device(old_fields, inverse_step, boundary):
    x, y, z = inverse_step.shape
    t = Tables(y, z)
    brick, four = (x, y, z), (4, x, y, z)
    faces = [(y, z)] * 2 + [(x, z)] * 2
    faces5 = [(5,) + f for f in faces]
    faces_back = [(y, z)] * 2 + [(x, z)] * 2

    place = [lax.axis_index(a) % 2 == 0 for a in ("gx", "gy")]
    even = jnp.stack([jnp.full((8, 128), p, jnp.float32) for p in place])

    local, x_near, x_far, y_near, y_far = call(
        load_local, "local_right", [(5,) + brick] + faces5, old_fields, inverse_step, even,
        scratch=[four, brick], far_in=2, copies=5,
    )
    received = swap_all(x_near, x_far, y_near, y_far)

    top = INTERVAL_SHARE * np.array([spectrum_top(c) for c in DIFFUSE])
    halves = [float(v) for v in 0.5 * top]
    scales = [float(v) for v in np.array(DIFFUSE) / (0.5 * top)]
    rates = [float(v) for v in 1.0 / (0.5 * top)]

    x_far, x_near, y_far, y_near = received
    relayed = [(6, x, z)] * 2
    x_faces, y_faces5 = [(5, y, z)] * 2, [(5, x, z)] * 2
    part, near, far = call(first_y, "first_y", [four] + relayed, local, boundary, y_far, y_near, even, cost=busy(2 << 20))
    right, y_near, y_far, x_near, x_far = call(
        first_x, "first_x", [four] + relayed + x_faces, part, near, far, boundary, x_far, x_near, even,
        aliases=[(0, 0), (1, 1), (2, 2)],
    )
    heard = [swap_all(x_near, x_far, y_near, y_far)]
    reaction, free, ahead = call(
        functools.partial(start_sums, scales, rates), "right_sums", [brick, brick, four],
        local, boundary, *received, even, right, t.summed, t.share, *t.left_y, *t.stiff_z, cost=busy(8 << 20),
    )
    x_far, x_near, y_far, y_near = heard[0]
    part, right, reaction, near, far = call(
        functools.partial(second_y, scales, rates), "second_y", [four, four, brick] + y_faces5,
        ahead, free, *received, y_far, y_near, even, t.summed, *t.stiff_z, right, reaction,
        scratch=[(16, z)] * 2, aliases=[(12, 1), (13, 2)], cost=busy(3 << 20),
    )
    basis, sums = [right], []
    here = scales
    for k in range(1, ITERS - 1):
        field, y_near, y_far, x_near, x_far = call(
            functools.partial(grow_x, here), "basis_x", [four] + y_faces5 + x_faces,
            part, near, far, free, x_far, x_near, even, t.summed, aliases=[(0, 0), (1, 1), (2, 2)],
        )
        basis.append(field)
        heard.append(swap_all(x_near, x_far, y_near, y_far))
        x_far, x_near, y_far, y_near = heard[-1]
        outs = [four, (8, 128)] + ([(8, 128)] if k == 1 else [])
        ahead, *dots = call(
            functools.partial(basis_sums, scales, rates), "basis_sums", outs,
            basis[-1], basis[-2], reaction, free, t.summed, t.share, *t.left_y, *t.stiff_z, cost=busy(8 << 20),
        )
        sums += dots[::-1]
        here = [2.0 * v for v in scales]
        if k < ITERS - 2:
            part, near, far = call(
                functools.partial(grow_y, here), "basis_y", [four] + y_faces5,
                ahead, free, y_far, y_near, even, t.summed, cost=busy(2 << 20),
            )
    part, near, far, products = call(
        functools.partial(last_y, scales, rates), "last_y", [four] + [(x, z)] * 2 + [(4, 3, 8, 128)],
        ahead, basis[-1], reaction, free, y_far, y_near, even, t.summed, t.share, *t.plain_y, *t.plain_z, t.local,
        cost=busy(4 << 20),
    )
    field, y_near, y_far, sums, x_near, x_far = call(
        functools.partial(last_x, scales, rates), "last_x",
        [four] + [(x, z)] * 2 + [(ITERS, 8, 128)] + [(y, z)] * 2,
        part, near, far, products, basis[-1], reaction, free, x_far, x_near, even, t.summed, t.share,
        *t.plain_y, *t.plain_z, t.local, *sums, aliases=[(0, 0), (1, 1), (2, 2)],
    )
    basis.append(field)
    heard[0] = call(mend_slopes, "slopes", faces_back, *received, *heard[0], free, even)
    sums = sums.reshape(ITERS * 8, z)
    sloped = []

    def meanwhile():
        if len(sloped) < ITERS:
            sloped.extend(
                call(
                    slope_sums, "slope_sums", [(3,) + brick] * 3,
                    *basis[len(sloped) : len(sloped) + 3], t.summed, t.slope_y, *t.slope_z, cost=busy(6 << 20),
                )
            )
        return sloped[-1]

    sums, x_near, x_far = all_sum(sums, "gx", x_near, x_far, y_far, meanwhile)
    sums, y_near, y_far = all_sum(sums, "gy", y_near, y_far, None, meanwhile)
    while len(sloped) < ITERS:
        meanwhile()
    sums = sums.reshape(ITERS, 8, z)
    slopes = (x_far, x_near, y_far, y_near)

    centre, half = chebyshev_bounds()
    factor = centre / half
    damping = 1.0 / factor
    weights, remainder, update, *sent = call(
        functools.partial(first_update, halves, 1.0 / centre), "first_update", [(ITERS, 8, 128), brick, brick] + faces,
        sums, *sloped, *[a for h in heard for a in h], *slopes, even, free, t.summed, t.inverse, scratch=faces_back,
    )
    pressure = update
    for step in range(1, CHEB):
        last = step == CHEB - 1
        received = swap_all(*sent)
        (raw,) = call(
            pressure_sums, "pressure_sums", [brick],
            update, t.summed, t.shift, t.stiff_y, *t.stiff_z, cost=busy(2 << 20), scratch=[brick],
        )
        if step == 1:
            (fields,) = call(combine_fields, "fields", [four], weights, *basis, cost=busy(4 << 20))
        following = 1.0 / (2.0 * factor - damping)
        keep, gain = following * damping, 2.0 * following / half
        damping = following
        kernel = functools.partial(pressure_step, last, keep, gain)
        args = [raw, free, *received, even, t.summed, t.inverse, remainder, update, pressure]
        if last:
            (pressure,) = call(
                kernel, "pressure_last", [brick], *args, scratch=[brick], far_out=1, copies=x // 8
            )
            break
        pressure, remainder, update, *sent = call(kernel, "pressure_step", [brick] * 3 + faces, *args)
    return (fields, pressure)


def solution(mesh):
    return jax.shard_map(
        on_device,
        mesh=mesh,
        in_specs=(P(None, "gx", "gy", None), P("gx", "gy", None), P("gx", "gy", None)),
        out_specs=(P(None, "gx", "gy", None), P("gx", "gy", None)),
        check_vma=False,
    )
```

```python
import functools

import jax
import jax.numpy as jnp
import ml_dtypes
import numpy as np
from jax import lax
from jax.experimental import pallas as pl
from jax.experimental.pallas import tpu as pltpu
from jax.sharding import PartitionSpec as P

ITERS = 6
CHEB = 6

SIGMA_SHIFT = 0.5
DIFFUSE = (1.0, 1.0, 1.0, 1.4)
COUPLING = 1.0
STRATIFY = 1.0
SPREAD = 20.0
STEP_MAX = 64.0
INTERVAL_SHARE = 0.82
HIGHEST_PRECISION = lax.Precision.HIGHEST
LOBATTO_POINTS = (
    -1.0,
    -0.8717401485096066,
    -0.5917001814331423,
    -0.2092992179024789,
    0.2092992179024789,
    0.5917001814331423,
    0.8717401485096066,
    1.0,
)


def legendre_value(points, degree):
    previous = points * 0.0 + 1.0
    current = points
    for order in range(1, degree):
        following = ((2 * order + 1) * points * current - order * previous) / (order + 1)
        previous = current
        current = following
    return current


def quadrature_tables():
    degree = 7
    points = np.array(LOBATTO_POINTS)
    values = legendre_value(points, degree)
    weights = 2.0 / (degree * (degree + 1) * values * values)
    derive = np.zeros((degree + 1, degree + 1))
    for row_index in range(degree + 1):
        for column_index in range(degree + 1):
            if row_index != column_index:
                derive[row_index, column_index] = values[row_index] / (
                    values[column_index] * (points[row_index] - points[column_index])
                )
    derive[0, 0] = -degree * (degree + 1) / 4.0
    derive[degree, degree] = degree * (degree + 1) / 4.0
    stiffness_table = derive.T @ (weights[:, None] * derive)
    return (weights, derive, stiffness_table)


WEIGHTS, DERIVE, STIFF = quadrature_tables()
SLOPE = WEIGHTS[:, None] * DERIVE
COPIES = np.where(np.arange(8) % 7 == 0, 2.0, 1.0)


def chebyshev_bounds():
    weight_matrix = np.eye(8) * WEIGHTS

    def kron3(a, b, c):
        return np.kron(np.kron(a, b), c)

    element_matrix = (
        kron3(STIFF, weight_matrix, weight_matrix)
        + kron3(weight_matrix, STIFF, weight_matrix)
        + kron3(weight_matrix, weight_matrix, STIFF)
        + SIGMA_SHIFT * kron3(weight_matrix, weight_matrix, weight_matrix)
    )
    bounds_ratio = np.sum(np.abs(element_matrix), axis=1) / np.diagonal(element_matrix)
    upper_bound = float(np.max(bounds_ratio))
    lower_bound = upper_bound / SPREAD
    return ((upper_bound + lower_bound) / 2.0, (upper_bound - lower_bound) / 2.0)


def spectrum_top(diffuse):
    root = np.sqrt(COPIES)
    stiff = root[:, None] * STIFF * root[None, :]
    weight = np.diag(WEIGHTS * COPIES)

    def kron3(a, b, c):
        return np.kron(np.kron(a, b), c)

    element = diffuse * (
        kron3(stiff, weight, weight) + kron3(weight, stiff, weight) + kron3(weight, weight, stiff)
    ) + STEP_MAX * kron3(weight, weight, weight)
    return float(np.linalg.eigvalsh(element)[-1])


def line_sums(table, length):
    matrix = np.kron(np.eye(length // 8), table)
    total = matrix.copy()
    for start in range(8, length, 8):
        total[start] += matrix[start - 1]
        total[start - 1] += matrix[start]
    return total


def depth_line(vector, length):
    line = np.tile(vector * COPIES, length // 8)
    line[0] = vector[0]
    line[-1] = vector[-1]
    return line


def f32(array):
    return np.ascontiguousarray(array, np.float32)


def rolled_rows(table):
    out = np.zeros((8, 8, 128))
    for shift in range(8):
        for row in range(8):
            out[shift, row] = table[row, (row - shift) % 8]
    return out


def block(a, b, c):
    return a[:, None, None] * b[:, None] * c


def parts_of(matrix):
    rest, parts = f32(matrix), []
    for _ in range(3):
        parts.append(rest.astype(ml_dtypes.bfloat16))
        rest = rest - parts[-1].astype(np.float32)
    hi, mid, lo = parts
    return np.block([[hi, mid], [hi, mid]]), np.concatenate([hi, lo])


class Tables:
    def __init__(self, depth):
        ones8, ones = np.ones(8), np.ones(depth)
        wide = WEIGHTS * COPIES
        deep = depth_line(WEIGHTS, depth)
        flat = np.tile(WEIGHTS, depth // 8)
        stiff = np.diagonal(STIFF)
        wide_s, deep_s = stiff * COPIES, depth_line(stiff, depth)
        share = 1.0 / COPIES
        share_z = np.tile(share, depth // 8)
        share_z[0] = share_z[-1] = 1.0
        self.summed = f32(
            np.stack([block(ones8, wide, deep), block(wide, ones8, deep), block(wide, wide, ones)])
        )
        self.local = f32(
            np.stack(
                [block(ones8, WEIGHTS, flat), block(WEIGHTS, ones8, flat), block(WEIGHTS, WEIGHTS, ones)]
            )
        )
        self.share = f32(block(share, share, share_z))
        diagonal = (
            block(wide_s, wide, deep)
            + block(wide, wide_s, deep)
            + block(wide, wide, deep_s)
            + SIGMA_SHIFT * block(wide, wide, deep)
        )
        self.inverse = f32(1.0 / diagonal)
        self.shift = f32(SIGMA_SHIFT * block(wide, wide, deep))
        self.stiff_y = f32(rolled_rows(STIFF))
        self.slope_y = f32(rolled_rows(SLOPE))
        self.stiff_z = parts_of(line_sums(STIFF, depth).T)
        self.plain_z = parts_of(np.kron(np.eye(depth // 8), STIFF).T)
        self.slope_z = parts_of(line_sums(SLOPE, depth).T)


def row_marks():
    row = lax.broadcasted_iota(jnp.int32, (8, 128), 0)
    return jnp.where(row == 0, 1.0, 0.0), jnp.where(row == 7, 1.0, 0.0)


def by_place(vector, place):
    out = jnp.full(place.shape, float(vector[0]), jnp.float32)
    for i in range(1, 8):
        out = jnp.where(place == i, float(vector[i]), out)
    return out


def along_x(rows, table):
    if np.allclose(table, table[::-1, ::-1]):
        even = 0.5 * (table[:4, :4] + table[:4, :3:-1])
        odd = 0.5 * (table[:4, :4] - table[:4, :3:-1])
        plus = [rows[i] + rows[7 - i] for i in range(4)]
        minus = [rows[i] - rows[7 - i] for i in range(4)]
        out = [None] * 8
        for a in range(4):
            p = sum(float(even[a, b]) * plus[b] for b in range(4))
            m = sum(float(odd[a, b]) * minus[b] for b in range(4))
            out[a], out[7 - a] = p + m, p - m
        return out
    return [sum(float(table[a, b]) * rows[b] for b in range(8)) for a in range(8)]


def along_y(tiles, factors):
    total = factors[0] * tiles
    for shift in range(1, 8):
        total = total + factors[shift] * pltpu.roll(tiles, shift, axis=1)
    return total


def along_z(tiles, matrix):
    wide, rest = matrix
    shape, depth = tiles.shape, tiles.shape[-1]
    flat = tiles.reshape(-1, depth)
    hi = flat.astype(jnp.bfloat16)
    flat = flat - hi.astype(jnp.float32)
    mid = flat.astype(jnp.bfloat16)
    lo = (flat - mid.astype(jnp.float32)).astype(jnp.bfloat16)
    first = jnp.dot(jnp.concatenate([hi, mid], axis=1), wide[...], preferred_element_type=jnp.float32)
    second = jnp.dot(jnp.concatenate([lo, hi], axis=1), rest[...], preferred_element_type=jnp.float32)
    return (first[:, :depth] + (first[:, depth:] + second)).reshape(shape)


def fill_z(out, field, matrix):
    for x in range(0, out.shape[0], 16):
        rows = pl.ds(x, min(16, out.shape[0] - x))
        out[rows] = along_z(field[rows], matrix)


def join_y(parts, low, high):
    out = list(parts)
    for e in range(1, len(parts)):
        out[e - 1] = out[e - 1] + high * pltpu.roll(parts[e], 7, axis=1)
        out[e] = out[e] + low * pltpu.roll(parts[e - 1], 1, axis=1)
    return out


def spread_rows(rows):
    return jnp.broadcast_to(rows[:, None, :], (rows.shape[0], 8, rows.shape[1]))


def column_sums(x_rows, y_parts, z_parts, summed, edges):
    y_parts = join_y(y_parts, edges[0], edges[1])
    return [
        jnp.stack(kx) * summed[0, 0] + ky * summed[1] + kz * summed[2]
        for kx, ky, kz in zip(x_rows, y_parts, z_parts)
    ]


def emit_column(ex, x_rows, y_parts, z_parts, summed, edges, out, state, finish=None, factor=None):
    rows = pl.ds(8 * ex, 8)
    parts = column_sums(x_rows, y_parts, z_parts, summed, edges)
    for e, part in enumerate(parts):
        ys = pl.ds(8 * e, 8)
        out[rows, ys] = part if finish is None else finish(e, part)
        if ex:
            for row, face in ((8 * ex, state[e]), (8 * ex - 1, x_rows[e][0])):
                face = face * summed[0, 0]
                out[row, ys] += face if factor is None else face * factor(row, ys)
    return [r[7] for r in x_rows]


def end_rows(table):
    row = lax.broadcasted_iota(jnp.int32, (8, 128), 0)
    return (table[0], table[7]), (by_place(table[0], row), by_place(table[7], row))


def store_faces(ex, e, columns, count, tile, even, ends, faces, x=True, y=True):
    x_near, x_far, y_near, y_far = faces
    (x_low, x_high), (y_low, y_high) = ends
    rows, ys = pl.ds(8 * ex, 8), pl.ds(8 * e, 8)
    if x and ex == 0:
        low = sum(float(x_low[i]) * tile[i] for i in range(8))
        x_near[ys] = low
        x_far[ys] = low
    if x and ex == columns - 1:
        high = sum(float(x_high[i]) * tile[i] for i in range(8))
        x_near[ys] = jnp.where(even[0], high, x_near[ys])
        x_far[ys] = jnp.where(even[0], x_far[ys], high)
    if y and e == 0:
        low = jnp.sum(tile * y_low, axis=1)
        y_near[rows] = low
        y_far[rows] = low
    if y and e == count - 1:
        high = jnp.sum(tile * y_high, axis=1)
        y_near[rows] = jnp.where(even[1], high, y_near[rows])
        y_far[rows] = jnp.where(even[1], y_far[rows], high)


def parity(even_ref):
    return even_ref[0] > 0.5, even_ref[1] > 0.5


def even_rows(even_ref):
    return even_ref[0, 0:1] > 0.5, even_ref[1, 0:1] > 0.5


def before_of(even, near, far):
    return jnp.where(even, far, near)


def after_of(even, near, far):
    return jnp.where(even, near, far)


def with_faces(tile, ex, e, columns, count, received, even, edges, weight_x=None, weight_y=None, mask=None, x=True):
    x_far, x_near, y_far, y_near = received
    rows, ys = pl.ds(8 * ex, 8), pl.ds(8 * e, 8)

    def weighted(face, weight):
        return face if weight is None else face * weight

    if e == 0:
        face = before_of(even[1], y_near[rows], y_far[rows])
        face = spread_rows(face) * weighted(edges[0], weight_y)
        tile = tile + weighted(face, mask)
    if e == count - 1:
        face = after_of(even[1], y_near[rows], y_far[rows])
        face = spread_rows(face) * weighted(edges[1], weight_y)
        tile = tile + weighted(face, mask)
    if x and ex == 0:
        face = before_of(even[0], x_near[ys], x_far[ys])
        face = weighted(face, weight_x) if mask is None else weighted(face, weight_x) * mask[0]
        tile = jnp.concatenate([tile[0:1] + face[None], tile[1:]], axis=0)
    if x and ex == columns - 1:
        face = after_of(even[0], x_near[ys], x_far[ys])
        face = weighted(face, weight_x) if mask is None else weighted(face, weight_x) * mask[7]
        tile = jnp.concatenate([tile[:7], tile[7:8] + face[None]], axis=0)
    return tile


def split_rows(block_rows):
    return [block_rows[i] for i in range(8)]


def join_rows(parts, low, high):
    out = list(parts)
    for e in range(1, len(parts)):
        out[e - 1] = out[e - 1] + high * pltpu.roll(parts[e], 7, axis=0)
        out[e] = out[e] + low * pltpu.roll(parts[e - 1], 1, axis=0)
    return out


def depth_marks(depth):
    lane = lax.broadcasted_iota(jnp.int32, (8, depth), 1)
    place = lane & 7
    after = jnp.where((place == 0) & (lane > 0), 1.0, 0.0)
    before = jnp.where((place == 7) & (lane < depth - 1), 1.0, 0.0)
    return by_place(WEIGHTS, place), after, before


def join_depth(value, after, before):
    axis, depth = value.ndim - 1, value.shape[-1]
    return value + after * pltpu.roll(value, 1, axis=axis) + before * pltpu.roll(value, depth - 1, axis=axis)


def forced(field, old, step):
    if field == 4:
        return step
    value = step * old(field)
    if field == 2:
        value = value + COUPLING * old(3)
    if field == 3:
        value = value - STRATIFY * old(2)
    return value


def load_faces(old_far, step_far, even_ref, old, step, x_near, x_far, y_near, y_far, arrived):
    length, width, depth = step.shape
    columns, count = length // 8, width // 8
    copies = [pltpu.make_async_copy(step_far, step, arrived.at[4])]
    copies += [pltpu.make_async_copy(old_far.at[i], old.at[i], arrived.at[i]) for i in range(4)]
    for copy in copies:
        copy.start()
    even, (low, high) = parity(even_ref), row_marks()
    row = lax.broadcasted_iota(jnp.int32, (8, depth), 0)
    line, after, before = depth_marks(depth)
    mass = by_place(WEIGHTS, row) * line
    for field in (4, 0, 1, 2, 3):
        if field != 3:
            copies[0 if field == 4 else field + 1].wait()
        if field == 2:
            copies[4].wait()
        found = []
        for x in (0, length - 1):
            parts = []
            for e in range(count):
                ys = pl.ds(8 * e, 8)
                value = forced(field, lambda f: old[f, x, ys], step[x, ys])
                parts.append(join_depth(value * (float(WEIGHTS[x % 8]) * mass), after, before))
            found.append(join_rows(parts, low, high))
        for e in range(count):
            ys = pl.ds(8 * e, 8)
            x_near[field, ys] = jnp.where(even[0], found[1][e], found[0][e])
            x_far[field, ys] = jnp.where(even[0], found[0][e], found[1][e])
        found = []
        for y in (0, width - 1):
            parts = []
            for ex in range(columns):
                rows, ys = pl.ds(8 * ex, 8), pl.ds(y // 8 * 8, 8)
                value = forced(field, lambda f: old[f, rows, ys][:, y % 8], step[rows, ys][:, y % 8])
                parts.append(join_depth(value * (float(WEIGHTS[y % 8]) * mass), after, before))
            found.append(join_rows(parts, low, high))
        for ex in range(columns):
            rows = pl.ds(8 * ex, 8)
            y_near[field, rows] = jnp.where(even[1], found[1][ex], found[0][ex])
            y_far[field, rows] = jnp.where(even[1], found[0][ex], found[1][ex])


def load_local(old, step, out):
    columns, count, depth = out.shape[1] // 8, out.shape[2] // 8, out.shape[3]
    edges = row_marks()
    row = lax.broadcasted_iota(jnp.int32, (8, depth), 0)
    line, after, before = depth_marks(depth)
    plane = by_place(WEIGHTS, row) * line
    mass = jnp.stack([float(w) * plane for w in WEIGHTS])
    for field in range(5):
        state = [None] * count
        for ex in range(columns):
            rows = pl.ds(8 * ex, 8)
            parts = []
            for e in range(count):
                ys = pl.ds(8 * e, 8)
                value = forced(field, lambda f: old[f, rows, ys], step[rows, ys])
                parts.append(join_depth(value * mass, after, before))
            parts = join_y(parts, edges[0], edges[1])
            for e in range(count):
                ys = pl.ds(8 * e, 8)
                out[field, rows, ys] = parts[e]
                if ex:
                    out[field, 8 * ex, ys] += state[e]
                    out[field, 8 * ex - 1, ys] += parts[e][0]
                state[e] = parts[e][7]


def stiff_terms(ex, tiles, stiff_y, z_sums):
    x_rows = [along_x(split_rows(t), STIFF) for t in tiles]
    y_parts = [along_y(t, stiff_y) for t in tiles]
    z_parts = [z_sums[pl.ds(8 * ex, 8), pl.ds(8 * e, 8)] for e in range(len(tiles))]
    return x_rows, y_parts, z_parts


def square_sum(rows):
    total = 0.0
    for sign in (1.0, -1.0):
        form = 0.5 * (STIFF[:4, :4] + sign * STIFF[:4, :3:-1])
        part = [rows[i] + rows[7 - i] if sign > 0 else rows[i] - rows[7 - i] for i in range(4)]
        for i in range(4):
            pivot = form[i, i]
            if pivot < 1e-12:
                continue
            line = form[i] / np.sqrt(pivot)
            value = sum(float(line[b]) * part[b] for b in range(i, 4))
            total = total + value * value
            form = form - np.outer(line, line)
    return total


def half_y(tiles, factors):
    total = factors[0] * tiles
    for shift in range(1, 5):
        rolled = factors[shift] * pltpu.roll(tiles, shift, axis=1)
        total = total + (rolled if shift == 4 else 2.0 * rolled)
    return total


def join_x(c, out, x_far, x_near, even, even_row, ends, weight, mask, faces, slopes, slope_ends):
    columns, count = out.shape[0] // 8, out.shape[1] // 8
    for xi, side in enumerate((before_of, after_of)):
        row = (8 * columns - 1) * xi
        mended = [[0.0, 0.0], [0.0, 0.0]]
        for e in range(count):
            ys = pl.ds(8 * e, 8)
            change = side(even[0], x_near[c, ys], x_far[c, ys]) * weight * mask(row, ys)
            out[row, ys] += change
            for kind, (low, high) in enumerate((ends[1], slope_ends[1])):
                if e == 0:
                    mended[kind][0] = jnp.sum(change * low, axis=0, keepdims=True)
                if e == count - 1:
                    mended[kind][1] = jnp.sum(change * high, axis=0, keepdims=True)
        for kind, where in enumerate((faces, slopes if c == 1 else None)):
            if where is not None:
                low, high = mended[kind]
                where[2][row : row + 1] += jnp.where(even_row[1], high, low)
                where[3][row : row + 1] += jnp.where(even_row[1], low, high)
    for ex in sorted({0, columns - 1}):
        for e in range(count):
            tile = out[pl.ds(8 * ex, 8), pl.ds(8 * e, 8)]
            if faces is not None:
                store_faces(ex, e, columns, count, tile, even, ends, faces, True, False)
            if slopes is not None and c == 0:
                store_faces(ex, e, columns, count, tile, even, slope_ends, slopes, True, False)


def y_faces(c, ex, e, columns, count, tile, even, ends, slope_ends, y_near, y_far):
    store_faces(ex, e, columns, count, tile, even, ends, (None, None, y_near.at[c], y_far.at[c]), False, True)
    if c == 1:
        slopes = (None, None, y_near.at[4], y_far.at[4])
        store_faces(ex, e, columns, count, tile, even, slope_ends, slopes, False, True)


def first_y(local, boundary, y_far, y_near, even_ref, part, y_near_out, y_far_out):
    columns, count = part.shape[1] // 8, part.shape[2] // 8
    even, edges = parity(even_ref), row_marks()
    ends, slope_ends = end_rows(STIFF), end_rows(SLOPE)
    for c in range(4):
        for ex in range(columns):
            for e in range(count):
                rows, ys = pl.ds(8 * ex, 8), pl.ds(8 * e, 8)
                tile = with_faces(local[c, rows, ys], ex, e, columns, count, (None, None, y_far.at[c], y_near.at[c]),
                                  even, edges, x=False)
                tile = tile * boundary[rows, ys].astype(jnp.float32)
                part[c, rows, ys] = tile
                y_faces(c, ex, e, columns, count, tile, even, ends, slope_ends, y_near_out, y_far_out)


def first_x(part, y_near_in, y_far_in, boundary, x_far, x_near, even_ref, right, near, far, x_near_out, x_far_out):
    del part, y_near_in, y_far_in
    columns, count = right.shape[1] // 8, right.shape[2] // 8
    even, even_row = parity(even_ref), even_rows(even_ref)
    ends, slope_ends = end_rows(STIFF), end_rows(SLOPE)
    faces = (x_near_out, x_far_out, near, far)
    for c in range(4):
        join_x(c, right.at[c], x_far, x_near, even, even_row, ends, 1.0,
               lambda row, ys: boundary[row, ys].astype(jnp.float32),
               [f.at[c] for f in faces], [f.at[4] for f in faces], slope_ends)
    near[5] = jnp.zeros(near.shape[1:], jnp.float32)
    far[5] = jnp.zeros(far.shape[1:], jnp.float32)
    for xi, side in enumerate((before_of, after_of)):
        for field in range(5):
            low, high = [
                side(even_row[0], x_near[field, y : y + 1], x_far[field, y : y + 1]) for y in (0, 8 * count - 1)
            ]
            row = 8 * xi + field
            near[5, row : row + 1] = jnp.where(even_row[1], high, low)
            far[5, row : row + 1] = jnp.where(even_row[1], low, high)


def pick(c, values):
    out = jnp.float32(values[0])
    for i in range(1, 4):
        out = jnp.where(c == i, jnp.float32(values[i]), out)
    return out


def start_sums(scales, rates, local, boundary, x_far, x_near, y_far, y_near, even_ref, right, summed, share, stiff_y,
               wide_z, rest_z, reaction, free, ahead, z_sums):
    columns, count = ahead.shape[1] // 8, ahead.shape[2] // 8
    even, edges = parity(even_ref), row_marks()
    received = [r.at[4] for r in (x_far, x_near, y_far, y_near)]
    for ex in range(columns):
        for e in range(count):
            rows, ys = pl.ds(8 * ex, 8), pl.ds(8 * e, 8)
            reaction[rows, ys] = with_faces(local[4, rows, ys], ex, e, columns, count, received, even, edges)
            free[rows, ys] = boundary[rows, ys].astype(jnp.float32)
    basis_fill(scales, rates, right, None, reaction, free, summed, share, stiff_y, (wide_z, rest_z), ahead, z_sums)


def basis_sums(scales, rates, newest, older, reaction, free, summed, share, stiff_y, wide_z, rest_z, ahead, *rest):
    *dots, z_sums = rest
    basis_fill(scales, rates, newest, older, reaction, free, summed, share, stiff_y, (wide_z, rest_z), ahead, z_sums, *dots)


def basis_fill(scales, rates, newest, older, reaction, free, summed, share, stiff_y, stiff_z, ahead, z_sums, dots=None,
               first=None):
    columns, count = ahead.shape[1] // 8, ahead.shape[2] // 8
    edges = row_marks()
    double = 1.0 if older is None else 2.0

    def component(c, carry):
        scale, rate = pick(c, [double * v for v in scales]), pick(c, [double * v for v in rates])
        same = jnp.zeros((8, 128), jnp.float32)
        cross = jnp.zeros((8, 128), jnp.float32)
        start = jnp.zeros((8, 128), jnp.float32)
        state = None
        fill_z(z_sums, newest.at[c], stiff_z)
        for ex in range(columns):
            rows = pl.ds(8 * ex, 8)
            tiles = []
            for e in range(count):
                ys = pl.ds(8 * e, 8)
                tile = newest[c, rows, ys]
                if older is not None:
                    weighted = tile * share[...]
                    same = same + jnp.sum(weighted * tile, axis=0)
                    cross = cross + jnp.sum(weighted * older[c, rows, ys], axis=0)
                if first is not None:
                    start = start + jnp.sum(older[c, rows, ys] * older[c, rows, ys] * share[...], axis=0)
                tiles.append(tile)
            x_rows, y_parts, z_parts = stiff_terms(ex, tiles, stiff_y, z_sums)

            def finish(e, part):
                ys = pl.ds(8 * e, 8)
                value = scale * part + (rate * reaction[rows, ys] - double) * tiles[e]
                value = value * free[rows, ys]
                return value if older is None else value - older[c, rows, ys]

            state = emit_column(ex, x_rows, y_parts, z_parts, summed, edges, ahead.at[c], state, finish,
                                lambda row, ys: scale * free[row, ys])
        if older is not None:
            dots[pl.ds(c, 1)] = jnp.sum(same, axis=0, keepdims=True)
            dots[pl.ds(c + 4, 1)] = jnp.sum(cross, axis=0, keepdims=True)
        if first is not None:
            first[pl.ds(c, 1)] = jnp.sum(start, axis=0, keepdims=True)
            first[pl.ds(c + 4, 1)] = jnp.zeros((1, 128), jnp.float32)
        return carry

    lax.fori_loop(0, 4, component, 0)


def y_field(c, ex, e, ahead, free, y_far, y_near, scale, summed, edges, even, columns, count):
    rows, ys = pl.ds(8 * ex, 8), pl.ds(8 * e, 8)
    return with_faces(ahead[c, rows, ys], ex, e, columns, count, (None, None, y_far.at[c], y_near.at[c]), even, edges,
                      None, summed[1], scale * free[rows, ys], x=False)


def grow_y(scales, ahead, free, y_far, y_near, even_ref, summed, part, y_near_out, y_far_out):
    columns, count = part.shape[1] // 8, part.shape[2] // 8
    even, edges = parity(even_ref), row_marks()
    ends, slope_ends = end_rows(STIFF), end_rows(SLOPE)
    for c in range(4):
        for ex in range(columns):
            for e in range(count):
                tile = y_field(c, ex, e, ahead, free, y_far, y_near, scales[c], summed, edges, even, columns, count)
                part[c, pl.ds(8 * ex, 8), pl.ds(8 * e, 8)] = tile
                y_faces(c, ex, e, columns, count, tile, even, ends, slope_ends, y_near_out, y_far_out)


def grow_x(scales, part, y_near_in, y_far_in, free, x_far, x_near, even_ref, summed, out, y_near_out, y_far_out,
           x_near_out, x_far_out):
    del part, y_near_in, y_far_in
    even, even_row = parity(even_ref), even_rows(even_ref)
    ends, slope_ends = end_rows(STIFF), end_rows(SLOPE)
    faces = (x_near_out, x_far_out, y_near_out, y_far_out)
    for c in range(4):
        join_x(c, out.at[c], x_far, x_near, even, even_row, ends, scales[c] * summed[0, 0],
               lambda row, ys: free[row, ys], [f.at[c] for f in faces], [f.at[4] for f in faces], slope_ends)


def second_y(scales, rates, ahead, free, x_far0, x_near0, y_far0, y_near0, y_far, y_near, even_ref, summed, wide_z,
             rest_z, right_in, reaction_in, out, right, reaction, y_near_out, y_far_out, lines, depth_lines):
    columns, count = out.shape[1] // 8, out.shape[2] // 8
    even, edges, even_row = parity(even_ref), row_marks(), even_rows(even_ref)
    ends, slope_ends = end_rows(STIFF), end_rows(SLOPE)
    end_x, end_y = (0, 8 * columns - 1), (0, 8 * count - 1)
    sides = (before_of, after_of)
    corners = [(xi, yi) for xi in (0, 1) for yi in (0, 1)]

    def at(array, xi, yi):
        return array[end_x[xi], end_y[yi] : end_y[yi] + 1]

    def diagonal(field, xi, yi):
        row = 8 * xi + field
        return sides[yi](even_row[1], y_near[5, row : row + 1], y_far[5, row : row + 1])

    def beside(field, xi, yi):
        row = end_y[yi]
        return sides[xi](even_row[0], x_near0[field, row : row + 1], x_far0[field, row : row + 1])

    def beyond(field, xi, yi):
        row = end_x[xi]
        return sides[yi](even_row[1], y_near0[field, row : row + 1], y_far0[field, row : row + 1])

    for c in range(4):
        for n, (xi, yi) in enumerate(corners):
            lines[4 * c + n : 4 * c + n + 1] = diagonal(c, xi, yi) * at(free, xi, yi)
    depth_lines[...] = along_z(lines[...], (wide_z, rest_z))

    def missed(c, ex, e):
        found = []
        for n, (xi, yi) in enumerate(corners):
            cx, ce, sx, sy = (columns - 1) * xi, (count - 1) * yi, 7 * xi, 7 * yi
            line = lines[4 * c + n : 4 * c + n + 1]
            weight_x, weight_y = summed[0, 0, sy : sy + 1], summed[1, sx, 0:1]
            along = scales[c] * line * weight_x
            across = scales[c] * line * weight_y
            if ex == cx and e == ce:
                for i in range(8):
                    found.append((i, float(STIFF[i, sx]) * along * edges[yi]))
                found.append((sx, across * ends[1][yi]))
                side = beyond(c, xi, yi) * weight_x + beside(c, xi, yi) * weight_y
                side = float(STIFF[0, 0]) * side
                depth = depth_lines[4 * c + n : 4 * c + n + 1] * summed[2, sx, sy : sy + 1]
                gained = diagonal(4, xi, yi)
                node = scales[c] * (side + depth)
                node = node + (rates[c] * (at(reaction_in, xi, yi) + gained) - 1.0) * line
                node = node + rates[c] * gained * at(right_in.at[c], xi, yi)
                found.append((sx, node * edges[yi]))
            elif e == ce and ex == cx + 1 - 2 * xi:
                found.append((sx, float(STIFF[7 - sx, sx]) * along * edges[yi]))
            elif ex == cx and e == ce + 1 - 2 * yi:
                found.append((sx, float(STIFF[7 - sy, sy]) * across * edges[yi]))
        return found

    for c in range(4):
        for ex in range(columns):
            for e in range(count):
                rows, ys = pl.ds(8 * ex, 8), pl.ds(8 * e, 8)
                tile = y_field(c, ex, e, ahead, free, y_far, y_near, scales[c], summed, edges, even, columns, count)
                found = missed(c, ex, e)
                if found:
                    parts = []
                    for i in range(8):
                        extra = [t for row, t in found if row == i]
                        parts.append(tile[i] + sum(extra) * free[8 * ex + i, ys] if extra else tile[i])
                    tile = jnp.stack(parts)
                out[c, rows, ys] = tile
                y_faces(c, ex, e, columns, count, tile, even, ends, slope_ends, y_near_out, y_far_out)

    for n, (xi, yi) in enumerate(corners):
        x, y = end_x[xi], end_y[yi]
        reaction[x, y : y + 1] = at(reaction_in, xi, yi) + diagonal(4, xi, yi)
        for c in range(4):
            right[c, x, y : y + 1] = at(right_in.at[c], xi, yi) + lines[4 * c + n : 4 * c + n + 1]


def mend_slopes(x_far0, x_near0, y_far0, y_near0, x_far, x_near, y_far, y_near, free, even_ref,
                sx_far, sx_near, sy_far, sy_near):
    even_row = even_rows(even_ref)
    end_x, end_y = (0, free.shape[0] - 1), (0, free.shape[1] - 1)
    sides = (before_of, after_of)

    def at(array, xi, yi):
        return array[end_x[xi], end_y[yi] : end_y[yi] + 1]

    def beside(field, xi, yi):
        row = end_y[yi]
        return sides[xi](even_row[0], x_near0[field, row : row + 1], x_far0[field, row : row + 1])

    def beyond(field, xi, yi):
        row = end_x[xi]
        return sides[yi](even_row[1], y_near0[field, row : row + 1], y_far0[field, row : row + 1])

    sx_far[...], sx_near[...], sy_far[...], sy_near[...] = x_far[4], x_near[4], y_far[4], y_near[4]
    low, high = float(SLOPE[7, 7]), float(SLOPE[0, 0])
    for i in (0, 1):
        y, x = end_y[i], end_x[i]
        before = low * beyond(0, 0, i) * at(free, 0, i)
        after = high * beyond(0, 1, i) * at(free, 1, i)
        sx_near[y : y + 1] += jnp.where(even_row[0], after, before)
        sx_far[y : y + 1] += jnp.where(even_row[0], before, after)
        before = low * beside(1, i, 0) * at(free, i, 0)
        after = high * beside(1, i, 1) * at(free, i, 1)
        sy_near[x : x + 1] += jnp.where(even_row[1], after, before)
        sy_far[x : x + 1] += jnp.where(even_row[1], before, after)


def column_products(c, ex, out, newest, reaction, share, stiff_y, stiff_z, local, scale, rate, z_sums):
    count = out.shape[2] // 8
    rows = pl.ds(8 * ex, 8)
    same = jnp.zeros((8, 128), jnp.float32)
    cross = jnp.zeros((8, 128), jnp.float32)
    work = jnp.zeros((8, 128), jnp.float32)
    z_sums[...] = along_z(out[c, rows], stiff_z)
    for e in range(count):
        ys = pl.ds(8 * e, 8)
        tile = out[c, rows, ys]
        weighted = tile * share[...]
        same = same + jnp.sum(weighted * tile, axis=0)
        cross = cross + jnp.sum(weighted * newest[c, rows, ys], axis=0)
        extra = (rate * reaction[rows, ys] - 1.0) * tile
        work = work + jnp.sum(weighted * extra, axis=0)
        work = work + scale * (square_sum(split_rows(tile)) * local[0, 0])
        term = half_y(tile, stiff_y) * local[1] + z_sums[:, ys] * local[2]
        work = work + scale * jnp.sum(term * tile, axis=0)
    return same, cross, work


def last_y(scales, rates, ahead, newest, reaction, free, y_far, y_near, even_ref, summed, share, stiff_y, wide_z, rest_z,
           local, part, sy_near, sy_far, products, z_sums):
    columns, count = part.shape[1] // 8, part.shape[2] // 8
    even, edges = parity(even_ref), row_marks()
    slope_ends = end_rows(SLOPE)
    for c in range(4):
        total = [jnp.zeros((8, 128), jnp.float32)] * 3
        for ex in range(columns):
            for e in range(count):
                tile = y_field(c, ex, e, ahead, free, y_far, y_near, 2.0 * scales[c], summed, edges, even, columns, count)
                part[c, pl.ds(8 * ex, 8), pl.ds(8 * e, 8)] = tile
                if c == 1:
                    store_faces(ex, e, columns, count, tile, even, slope_ends, (None, None, sy_near, sy_far), False, True)
            if 0 < ex < columns - 1:
                found = column_products(c, ex, part, newest, reaction, share, stiff_y, (wide_z, rest_z), local, scales[c],
                                        rates[c], z_sums)
                total = [a + b for a, b in zip(total, found)]
        for n in range(3):
            products[c, n] = total[n]


def last_x(scales, rates, part, sy_near_in, sy_far_in, products, newest, reaction, free, x_far, x_near, even_ref, summed,
           share, stiff_y, wide_z, rest_z, local, d0, d1, d2, d3, d4, out, sy_near, sy_far, sums, sx_near, sx_far, z_sums):
    del part, sy_near_in, sy_far_in
    dots = (d0, d1, d2, d3, d4)
    columns = out.shape[1] // 8
    even, even_row = parity(even_ref), even_rows(even_ref)
    ends, slope_ends = end_rows(STIFF), end_rows(SLOPE)
    for i in range(1, ITERS - 1):
        sums[i] = dots[i][...]
    for c in range(4):
        join_x(c, out.at[c], x_far, x_near, even, even_row, ends, 2.0 * scales[c] * summed[0, 0],
               lambda row, ys: free[row, ys], None, (sx_near, sx_far, sy_near, sy_far), slope_ends)
        total = [products[c, n] for n in range(3)]
        for ex in sorted({0, columns - 1}):
            found = column_products(c, ex, out, newest, reaction, share, stiff_y, (wide_z, rest_z), local, scales[c],
                                    rates[c], z_sums)
            total = [a + b for a, b in zip(total, found)]
        same, cross, work = [jnp.sum(t, axis=0, keepdims=True) for t in total]
        sums[ITERS - 1, c : c + 1] = same
        sums[ITERS - 1, c + 4 : c + 5] = cross
        sums[0, c : c + 1] = dots[0][c : c + 1]
        sums[0, c + 4 : c + 5] = work


def slope_sums(*refs):
    fields, (summed, slope_y, wide_z, rest_z), outs = refs[:3], refs[3:7], refs[7:]
    columns, count = outs[0].shape[1] // 8, outs[0].shape[2] // 8
    edges = row_marks()
    for field, out in zip(fields, outs):
        fill_z(out.at[2], field.at[2], (wide_z, rest_z))
        state = None
        for ex in range(columns):
            rows, ends = pl.ds(8 * ex, 8), []
            y_parts = [along_y(field[1, rows, pl.ds(8 * e, 8)], slope_y) for e in range(count)]
            y_parts = join_y(y_parts, edges[0], edges[1])
            for e in range(count):
                ys = pl.ds(8 * e, 8)
                out[1, rows, ys] = y_parts[e] * summed[1]
                out[2, rows, ys] = out[2, rows, ys] * summed[2]
                x_rows = [r * summed[0, 0] for r in along_x(split_rows(field[0, rows, ys]), SLOPE)]
                out[0, rows, ys] = jnp.stack(x_rows)
                if ex:
                    out[0, 8 * ex, ys] += state[e]
                    out[0, 8 * ex - 1, ys] += x_rows[0]
                ends.append(x_rows[7])
            state = ends


def first_update(halves, gain, *refs):
    sums, *sloped = refs[: ITERS + 1]
    refs = refs[ITERS + 1 :]
    slopes = [refs[:4]]
    slopes += [[r.at[4] for r in refs[4 * k : 4 * k + 4]] for k in range(1, ITERS - 1)]
    refs = refs[4 * ITERS - 4 :]
    slopes.append(refs[:4])
    even_ref, free, summed, inverse = refs[4:8]
    weights, remainder, update, *faces = refs[8:15]
    joined = refs[15:]
    columns, count = update.shape[0] // 8, update.shape[1] // 8
    even, edges = parity(even_ref), row_marks()
    ends = end_rows(STIFF)
    total = [jnp.broadcast_to(jnp.sum(sums[i], axis=1, keepdims=True), (8, 128)) for i in range(ITERS)]
    other = [pltpu.roll(t, 4, axis=0) for t in total]
    row = lax.broadcasted_iota(jnp.int32, (8, 128), 0)
    half = jnp.full((8, 128), halves[0], jnp.float32)
    for i in range(1, 4):
        half = jnp.where(row == i, halves[i], half)
    moments = [total[0], other[1]]
    for level in range(2, 2 * ITERS - 1):
        inner = total[level // 2] if level % 2 == 0 else other[level // 2 + 1]
        moments.append(2.0 * inner - moments[level % 2])
    top = 2.0 * other[0] - other[5]
    moments.append(2.0 * top - moments[1])
    for i, value in enumerate(conjugate_coefficients(moments, half, half)):
        weights[i] = value
    for n in range(4):
        c = n // 2
        joined[n][...] = sum(slopes[i][n][...] * weights[i, c : c + 1] for i in range(ITERS))
    factor = [[weights[i, c : c + 1][None] for c in range(3)] for i in range(ITERS)]
    for ex in range(columns):
        for e in range(count):
            rows, ys = pl.ds(8 * ex, 8), pl.ds(8 * e, 8)
            tile = sum(sloped[i][c, rows, ys] * factor[i][c] for i in range(ITERS) for c in range(3))
            tile = with_faces(tile, ex, e, columns, count, joined, even, edges, summed[0, 0], summed[1])
            left = -tile * free[rows, ys]
            change = gain * inverse[...] * left
            remainder[rows, ys] = left
            update[rows, ys] = change
            store_faces(ex, e, columns, count, change, even, ends, faces)


def combine_fields(weights, *refs):
    *basis, fields = refs

    def combine(c, carry):
        factor = [weights[i, pl.ds(c, 1)] for i in range(ITERS)]
        for x in range(0, fields.shape[1], 8):
            rows = pl.ds(x, 8)
            value = basis[0][c, rows] * factor[0][None]
            for i in range(1, ITERS):
                value = value + basis[i][c, rows] * factor[i][None]
            fields[c, rows] = value
        return carry

    lax.fori_loop(0, 4, combine, 0)


def add_loads(count, *refs):
    *loads, rider, tick, out = refs
    del tick
    values = [load[:count] for load in loads]
    total = values[0] + values[1]
    if len(values) == 4:
        total = total + (values[2] + values[3])
    out[:count] = total
    out[count:] = rider[...]


def pressure_sums(update, summed, shift, stiff_y, wide_z, rest_z, raw, z_sums):
    columns, count = raw.shape[0] // 8, raw.shape[1] // 8
    edges = row_marks()
    state = None
    fill_z(z_sums, update, (wide_z, rest_z))
    for ex in range(columns):
        rows = pl.ds(8 * ex, 8)
        tiles = [update[rows, pl.ds(8 * e, 8)] for e in range(count)]
        x_rows, y_parts, z_parts = stiff_terms(ex, tiles, stiff_y, z_sums)
        state = emit_column(ex, x_rows, y_parts, z_parts, summed, edges, raw, state,
                            lambda e, part: part + shift[...] * tiles[e])


def pressure_step(last, keep, gain, *refs):
    raw, free, *received, even_ref, summed, inverse, remainder_in, update_in, pressure_in = refs[:12]
    if last:
        pressure_far, pressure, left_here = refs[12:]
    else:
        pressure, remainder, update, *faces = refs[12:]
    columns, count = raw.shape[0] // 8, raw.shape[1] // 8
    copies = []
    even, edges = parity(even_ref), row_marks()
    ends = end_rows(STIFF)
    for ex in range(columns):
        for e in range(count):
            rows, ys = pl.ds(8 * ex, 8), pl.ds(8 * e, 8)
            tile = with_faces(raw[rows, ys], ex, e, columns, count, received, even, edges,
                              summed[0, 0], summed[1])
            left = remainder_in[rows, ys] - tile * free[rows, ys]
            change = gain * inverse[...] * left + keep * update_in[rows, ys]
            pressure[rows, ys] = pressure_in[rows, ys] + change
            if not last:
                remainder[rows, ys] = left
                update[rows, ys] = change
                store_faces(ex, e, columns, count, change, even, ends, faces)
        if last:
            rows = pl.ds(8 * ex, 8)
            copies.append(pltpu.make_async_copy(pressure.at[rows], pressure_far.at[rows], left_here.at[ex]))
            copies[-1].start()
    for copy in copies:
        copy.wait()


VMEM_BYTES = 24 * 1024 * 1024


def call(kernel, name, outs, *args, scratch=(), cost=None, far_in=0, far_out=0, copies=0, aliases=()):
    held, far = pl.BlockSpec(memory_space=pltpu.VMEM), pl.BlockSpec(memory_space=pltpu.HBM)
    scratch_shapes = [pltpu.VMEM(s, jnp.float32) for s in scratch]
    if copies:
        scratch_shapes.append(pltpu.SemaphoreType.DMA((copies,)))
    return pl.pallas_call(
        kernel,
        name=name,
        out_shape=[jax.ShapeDtypeStruct(s, jnp.float32) for s in outs],
        in_specs=[far] * far_in + [held] * (len(args) - far_in),
        out_specs=[far] * far_out + [held] * (len(outs) - far_out),
        scratch_shapes=scratch_shapes,
        cost_estimate=cost,
        input_output_aliases=dict(aliases),
        compiler_params=pltpu.CompilerParams(vmem_limit_bytes=VMEM_BYTES),
    )(*[pltpu.with_memory_space_constraint(a, pltpu.HBM) for a in args[:far_in]], *args[far_in:])


def busy(bytes_accessed):
    return pl.CostEstimate(flops=0, bytes_accessed=bytes_accessed, transcendentals=0)


def swap_near(axis, face):
    return lax.ppermute(face, axis, [(i, i ^ 1) for i in range(lax.axis_size(axis))])


def swap_far(axis, face):
    size = lax.axis_size(axis)
    return lax.ppermute(face, axis, [(i, far_partner(i, size)) for i in range(size)])


def swap_all(x_near, x_far, y_near, y_far):
    y_far = swap_far("gy", y_far)
    x_far = swap_far("gx", x_far)
    x_near = swap_near("gx", x_near)
    y_near = swap_near("gy", y_near)
    return x_far, x_near, y_far, y_near


def far_partner(i, size):
    return (i + 1 if i % 2 else i - 1) % size


def partner_loads(load, axis, partners, riders, count):
    size, heard, faces = lax.axis_size(axis), [], []
    for n, (partner, rider) in enumerate(zip(partners, riders)):
        mine = load
        if n:
            mine = load[:count] if rider is None else jnp.concatenate([load[:count], rider])
        mine = lax.ppermute(mine, axis, [(i, partner(i)) for i in range(size)])
        heard.append(mine)
        if rider is not None:
            faces.append(mine[count:])
    return heard, faces


def all_sum(values, axis, near, far, following, meanwhile):
    size = lax.axis_size(axis)
    count = values.shape[0] - far.shape[0] if following is None else values.shape[0]
    half = size // 2

    def to_near(i):
        return i ^ 1

    def to_far(i):
        return far_partner(i, size)

    def across(i):
        return (i + half) % size

    def far_across(i):
        return across(to_far(i))

    rounds = [((to_far,), (far,))]
    if size == 4:
        rounds = [((to_far, to_near, across), (far, near, None))]
    elif size > 4:
        rounds = [((to_far, across, far_across), (far, None, None)), ((to_near,), (near,))]
        bit = 4
        while bit < half:
            rounds.append(((lambda i, bit=bit: i ^ bit,), (None,)))
            bit *= 2
    else:
        rounds.append(((), (near,)))
    faces = []
    load = values if following is None else jnp.concatenate([values, far])
    for n, (partners, riders) in enumerate(rounds):
        if not partners:
            faces.append(lax.ppermute(near, axis, [(i, to_near(i)) for i in range(size)]))
            continue
        heard, got = partner_loads(load, axis, partners, riders, count)
        faces += got
        rider = rounds[n + 1][1][0] if n + 1 < len(rounds) and rounds[n + 1][0] else following
        tail = jnp.zeros((8, values.shape[1]), jnp.float32) if rider is None else rider
        (load,) = call(
            functools.partial(add_loads, count), "add_loads", [(count + tail.shape[0], values.shape[1])],
            load, *heard, tail, meanwhile(),
        )
    if following is None:
        load = load[:count]
    return load, faces[1], faces[0]


def conjugate_coefficients(moments, centre, half):
    remaining, towards = list(moments), list(moments)
    one, zero = jnp.ones_like(moments[0]), jnp.zeros_like(moments[0])
    direction = [one] + [zero] * ITERS
    residual = list(direction)
    total = [zero] * ITERS
    for step in range(ITERS):
        count = len(towards) - 1
        image = []
        for level in range(count):
            side = (
                half * towards[1] if level == 0 else 0.5 * half * (towards[level + 1] + towards[level - 1])
            )
            image.append(centre * towards[level] + side)
        alpha = remaining[step] / image[step]
        total = [total[i] + alpha * direction[i] for i in range(ITERS)]
        if step == ITERS - 1:
            break
        applied = []
        for i in range(ITERS + 1):
            term = centre * direction[i]
            if i >= 1:
                term = term + (half if i == 1 else 0.5 * half) * direction[i - 1]
            if i < ITERS:
                term = term + 0.5 * half * direction[i + 1]
            applied.append(term)
        residual = [residual[i] - alpha * applied[i] for i in range(ITERS + 1)]
        following = [remaining[i] - alpha * image[i] for i in range(count)]
        beta = -alpha * (half if step == 0 else 0.5 * half) * following[step + 1] / remaining[step]
        towards = [following[i] + beta * towards[i] for i in range(count)]
        direction = [residual[i] + beta * direction[i] for i in range(ITERS + 1)]
        remaining = following
    return total


def on_device(old_fields, inverse_step, boundary):
    x, y, z = inverse_step.shape
    t = Tables(z)
    brick, four = (x, y, z), (4, x, y, z)
    faces = [(y, z)] * 2 + [(x, z)] * 2
    faces5 = [(5,) + f for f in faces]
    faces_back = [(y, z)] * 2 + [(x, z)] * 2

    place = [lax.axis_index(a) % 2 == 0 for a in ("gx", "gy")]
    even = jnp.stack([jnp.full((8, 128), p, jnp.float32) for p in place])

    old, step, x_near, x_far, y_near, y_far = call(
        load_faces, "right_faces", [four, brick] + faces5, old_fields, inverse_step, even, far_in=2, copies=5,
    )
    received = swap_all(x_near, x_far, y_near, y_far)
    (local,) = call(load_local, "right_local", [(5,) + brick], old, step, cost=busy(2 << 20))

    top = INTERVAL_SHARE * np.array([spectrum_top(c) for c in DIFFUSE])
    halves = [float(v) for v in 0.5 * top]
    scales = [float(v) for v in np.array(DIFFUSE) / (0.5 * top)]
    rates = [float(v) for v in 1.0 / (0.5 * top)]

    x_far, x_near, y_far, y_near = received
    relayed = [(6, x, z)] * 2
    x_faces, y_faces5 = [(5, y, z)] * 2, [(5, x, z)] * 2
    part, near, far = call(first_y, "first_y", [four] + relayed, local, boundary, y_far, y_near, even, cost=busy(2 << 20))
    right, y_near, y_far, x_near, x_far = call(
        first_x, "first_x", [four] + relayed + x_faces, part, near, far, boundary, x_far, x_near, even,
        aliases=[(0, 0), (1, 1), (2, 2)],
    )
    heard = [swap_all(x_near, x_far, y_near, y_far)]
    reaction, free, ahead = call(
        functools.partial(start_sums, scales, rates), "right_sums", [brick, brick, four],
        local, boundary, *received, even, right, t.summed, t.share, t.stiff_y, *t.stiff_z, cost=busy(8 << 20),
        scratch=[brick],
    )
    x_far, x_near, y_far, y_near = heard[0]
    part, right, reaction, near, far = call(
        functools.partial(second_y, scales, rates), "second_y", [four, four, brick] + y_faces5,
        ahead, free, *received, y_far, y_near, even, t.summed, *t.stiff_z, right, reaction,
        scratch=[(16, z)] * 2, aliases=[(12, 1), (13, 2)], cost=busy(3 << 20),
    )
    basis, sums = [right], []
    here = scales
    for k in range(1, ITERS - 1):
        field, y_near, y_far, x_near, x_far = call(
            functools.partial(grow_x, here), "basis_x", [four] + y_faces5 + x_faces,
            part, near, far, free, x_far, x_near, even, t.summed, aliases=[(0, 0), (1, 1), (2, 2)],
        )
        basis.append(field)
        heard.append(swap_all(x_near, x_far, y_near, y_far))
        x_far, x_near, y_far, y_near = heard[-1]
        outs = [four, (8, 128)] + ([(8, 128)] if k == 1 else [])
        ahead, *dots = call(
            functools.partial(basis_sums, scales, rates), "basis_sums", outs,
            basis[-1], basis[-2], reaction, free, t.summed, t.share, t.stiff_y, *t.stiff_z, cost=busy(8 << 20),
            scratch=[brick],
        )
        sums += dots[::-1]
        here = [2.0 * v for v in scales]
        if k < ITERS - 2:
            part, near, far = call(
                functools.partial(grow_y, here), "basis_y", [four] + y_faces5,
                ahead, free, y_far, y_near, even, t.summed, cost=busy(2 << 20),
            )
    part, near, far, products = call(
        functools.partial(last_y, scales, rates), "last_y", [four] + [(x, z)] * 2 + [(4, 3, 8, 128)],
        ahead, basis[-1], reaction, free, y_far, y_near, even, t.summed, t.share, t.stiff_y, *t.plain_z, t.local,
        scratch=[(8, y, z)], cost=busy(4 << 20),
    )
    field, y_near, y_far, sums, x_near, x_far = call(
        functools.partial(last_x, scales, rates), "last_x",
        [four] + [(x, z)] * 2 + [(ITERS, 8, 128)] + [(y, z)] * 2,
        part, near, far, products, basis[-1], reaction, free, x_far, x_near, even, t.summed, t.share, t.stiff_y,
        *t.plain_z, t.local, *sums, scratch=[(8, y, z)], aliases=[(0, 0), (1, 1), (2, 2)],
    )
    basis.append(field)
    heard[0] = call(mend_slopes, "slopes", faces_back, *received, *heard[0], free, even)
    sums = sums.reshape(ITERS * 8, z)
    sloped = []

    def meanwhile():
        if len(sloped) < ITERS:
            sloped.extend(
                call(
                    slope_sums, "slope_sums", [(3,) + brick] * 3,
                    *basis[len(sloped) : len(sloped) + 3], t.summed, t.slope_y, *t.slope_z, cost=busy(6 << 20),
                )
            )
        return sloped[-1]

    sums, x_near, x_far = all_sum(sums, "gx", x_near, x_far, y_far, meanwhile)
    sums, y_near, y_far = all_sum(sums, "gy", y_near, y_far, None, meanwhile)
    while len(sloped) < ITERS:
        meanwhile()
    sums = sums.reshape(ITERS, 8, z)
    slopes = (x_far, x_near, y_far, y_near)

    centre, half = chebyshev_bounds()
    factor = centre / half
    damping = 1.0 / factor
    weights, remainder, update, *sent = call(
        functools.partial(first_update, halves, 1.0 / centre), "first_update", [(ITERS, 8, 128), brick, brick] + faces,
        sums, *sloped, *[a for h in heard for a in h], *slopes, even, free, t.summed, t.inverse, scratch=faces_back,
    )
    pressure = update
    for step in range(1, CHEB):
        last = step == CHEB - 1
        received = swap_all(*sent)
        (raw,) = call(
            pressure_sums, "pressure_sums", [brick],
            update, t.summed, t.shift, t.stiff_y, *t.stiff_z, cost=busy(2 << 20), scratch=[brick],
        )
        if step == 1:
            (fields,) = call(combine_fields, "fields", [four], weights, *basis, cost=busy(4 << 20))
        following = 1.0 / (2.0 * factor - damping)
        keep, gain = following * damping, 2.0 * following / half
        damping = following
        kernel = functools.partial(pressure_step, last, keep, gain)
        args = [raw, free, *received, even, t.summed, t.inverse, remainder, update, pressure]
        if last:
            (pressure,) = call(
                kernel, "pressure_last", [brick], *args, scratch=[brick], far_out=1, copies=x // 8
            )
            break
        pressure, remainder, update, *sent = call(kernel, "pressure_step", [brick] * 3 + faces, *args)
    return (fields, pressure)


def solution(mesh):
    return jax.shard_map(
        on_device,
        mesh=mesh,
        in_specs=(P(None, "gx", "gy", None), P("gx", "gy", None), P("gx", "gy", None)),
        out_specs=(P(None, "gx", "gy", None), P("gx", "gy", None)),
        check_vma=False,
    )
```

```python
import functools

import jax
import jax.numpy as jnp
import ml_dtypes
import numpy as np
from jax import lax
from jax.experimental import pallas as pl
from jax.experimental.pallas import tpu as pltpu
from jax.sharding import PartitionSpec as P

ITERS = 6
CHEB = 6

SIGMA_SHIFT = 0.5
DIFFUSE = (1.0, 1.0, 1.0, 1.4)
COUPLING = 1.0
STRATIFY = 1.0
SPREAD = 20.0
STEP_MAX = 64.0
INTERVAL_SHARE = 0.82
HIGHEST_PRECISION = lax.Precision.HIGHEST
LOBATTO_POINTS = (
    -1.0,
    -0.8717401485096066,
    -0.5917001814331423,
    -0.2092992179024789,
    0.2092992179024789,
    0.5917001814331423,
    0.8717401485096066,
    1.0,
)


def legendre_value(points, degree):
    previous = points * 0.0 + 1.0
    current = points
    for order in range(1, degree):
        following = ((2 * order + 1) * points * current - order * previous) / (order + 1)
        previous = current
        current = following
    return current


def quadrature_tables():
    degree = 7
    points = np.array(LOBATTO_POINTS)
    values = legendre_value(points, degree)
    weights = 2.0 / (degree * (degree + 1) * values * values)
    derive = np.zeros((degree + 1, degree + 1))
    for row_index in range(degree + 1):
        for column_index in range(degree + 1):
            if row_index != column_index:
                derive[row_index, column_index] = values[row_index] / (
                    values[column_index] * (points[row_index] - points[column_index])
                )
    derive[0, 0] = -degree * (degree + 1) / 4.0
    derive[degree, degree] = degree * (degree + 1) / 4.0
    stiffness_table = derive.T @ (weights[:, None] * derive)
    return (weights, derive, stiffness_table)


WEIGHTS, DERIVE, STIFF = quadrature_tables()
SLOPE = WEIGHTS[:, None] * DERIVE
COPIES = np.where(np.arange(8) % 7 == 0, 2.0, 1.0)


def chebyshev_bounds():
    weight_matrix = np.eye(8) * WEIGHTS

    def kron3(a, b, c):
        return np.kron(np.kron(a, b), c)

    element_matrix = (
        kron3(STIFF, weight_matrix, weight_matrix)
        + kron3(weight_matrix, STIFF, weight_matrix)
        + kron3(weight_matrix, weight_matrix, STIFF)
        + SIGMA_SHIFT * kron3(weight_matrix, weight_matrix, weight_matrix)
    )
    bounds_ratio = np.sum(np.abs(element_matrix), axis=1) / np.diagonal(element_matrix)
    upper_bound = float(np.max(bounds_ratio))
    lower_bound = upper_bound / SPREAD
    return ((upper_bound + lower_bound) / 2.0, (upper_bound - lower_bound) / 2.0)


def spectrum_top(diffuse):
    root = np.sqrt(COPIES)
    stiff = root[:, None] * STIFF * root[None, :]
    weight = np.diag(WEIGHTS * COPIES)

    def kron3(a, b, c):
        return np.kron(np.kron(a, b), c)

    element = diffuse * (
        kron3(stiff, weight, weight) + kron3(weight, stiff, weight) + kron3(weight, weight, stiff)
    ) + STEP_MAX * kron3(weight, weight, weight)
    return float(np.linalg.eigvalsh(element)[-1])


def line_sums(table, length):
    matrix = np.kron(np.eye(length // 8), table)
    total = matrix.copy()
    for start in range(8, length, 8):
        total[start] += matrix[start - 1]
        total[start - 1] += matrix[start]
    return total


def depth_line(vector, length):
    line = np.tile(vector * COPIES, length // 8)
    line[0] = vector[0]
    line[-1] = vector[-1]
    return line


def f32(array):
    return np.ascontiguousarray(array, np.float32)


def rolled_rows(table):
    out = np.zeros((8, 8, 128))
    for shift in range(8):
        for row in range(8):
            out[shift, row] = table[row, (row - shift) % 8]
    return out


def block(a, b, c):
    return a[:, None, None] * b[:, None] * c


def parts_of(matrix):
    rest, parts = f32(matrix), []
    for _ in range(3):
        parts.append(rest.astype(ml_dtypes.bfloat16))
        rest = rest - parts[-1].astype(np.float32)
    hi, mid, lo = parts
    return np.block([[hi, mid], [hi, mid]]), np.concatenate([hi, lo])


def left_parts(table):
    rest, parts = f32(np.kron(np.eye(8), table)), []
    for _ in range(3):
        parts.append(rest.astype(ml_dtypes.bfloat16))
        rest = rest - parts[-1].astype(np.float32)
    hi, mid, lo = parts
    return np.block([[hi, hi], [mid, mid]]), np.concatenate([hi, lo], axis=1)


class Tables:
    def __init__(self, width, depth):
        self.left_y = left_parts(line_sums(STIFF, width))
        self.plain_y = left_parts(np.kron(np.eye(width // 8), STIFF))
        ones8, ones = np.ones(8), np.ones(depth)
        wide = WEIGHTS * COPIES
        deep = depth_line(WEIGHTS, depth)
        flat = np.tile(WEIGHTS, depth // 8)
        stiff = np.diagonal(STIFF)
        wide_s, deep_s = stiff * COPIES, depth_line(stiff, depth)
        share = 1.0 / COPIES
        share_z = np.tile(share, depth // 8)
        share_z[0] = share_z[-1] = 1.0
        self.summed = f32(
            np.stack([block(ones8, wide, deep), block(wide, ones8, deep), block(wide, wide, ones)])
        )
        self.local = f32(
            np.stack(
                [block(ones8, WEIGHTS, flat), block(WEIGHTS, ones8, flat), block(WEIGHTS, WEIGHTS, ones)]
            )
        )
        self.share = f32(block(share, share, share_z))
        diagonal = (
            block(wide_s, wide, deep)
            + block(wide, wide_s, deep)
            + block(wide, wide, deep_s)
            + SIGMA_SHIFT * block(wide, wide, deep)
        )
        self.inverse = f32(1.0 / diagonal)
        self.shift = f32(SIGMA_SHIFT * block(wide, wide, deep))
        self.stiff_y = f32(rolled_rows(STIFF))
        self.slope_y = f32(rolled_rows(SLOPE))
        self.stiff_z = parts_of(line_sums(STIFF, depth).T)
        self.plain_z = parts_of(np.kron(np.eye(depth // 8), STIFF).T)
        self.slope_z = parts_of(line_sums(SLOPE, depth).T)


def row_marks():
    row = lax.broadcasted_iota(jnp.int32, (8, 128), 0)
    return jnp.where(row == 0, 1.0, 0.0), jnp.where(row == 7, 1.0, 0.0)


def by_place(vector, place):
    out = jnp.full(place.shape, float(vector[0]), jnp.float32)
    for i in range(1, 8):
        out = jnp.where(place == i, float(vector[i]), out)
    return out


def along_x(rows, table):
    if np.allclose(table, table[::-1, ::-1]):
        even = 0.5 * (table[:4, :4] + table[:4, :3:-1])
        odd = 0.5 * (table[:4, :4] - table[:4, :3:-1])
        plus = [rows[i] + rows[7 - i] for i in range(4)]
        minus = [rows[i] - rows[7 - i] for i in range(4)]
        out = [None] * 8
        for a in range(4):
            p = sum(float(even[a, b]) * plus[b] for b in range(4))
            m = sum(float(odd[a, b]) * minus[b] for b in range(4))
            out[a], out[7 - a] = p + m, p - m
        return out
    return [sum(float(table[a, b]) * rows[b] for b in range(8)) for a in range(8)]


def along_y(tiles, factors):
    total = factors[0] * tiles
    for shift in range(1, 8):
        total = total + factors[shift] * pltpu.roll(tiles, shift, axis=1)
    return total


def along_z(tiles, matrix):
    wide, rest = matrix
    shape, depth = tiles.shape, tiles.shape[-1]
    flat = tiles.reshape(-1, depth)
    hi = flat.astype(jnp.bfloat16)
    flat = flat - hi.astype(jnp.float32)
    mid = flat.astype(jnp.bfloat16)
    lo = (flat - mid.astype(jnp.float32)).astype(jnp.bfloat16)
    first = jnp.dot(jnp.concatenate([hi, mid], axis=1), wide[...], preferred_element_type=jnp.float32)
    second = jnp.dot(jnp.concatenate([lo, hi], axis=1), rest[...], preferred_element_type=jnp.float32)
    return (first[:, :depth] + (first[:, depth:] + second)).reshape(shape)


def along_both(tiles, matrix, left):
    wide, rest = matrix
    tall, short = left
    shape, depth = tiles.shape, tiles.shape[-1]
    flat = tiles.reshape(-1, depth)
    lines = flat.shape[0]
    hi = flat.astype(jnp.bfloat16)
    flat = flat - hi.astype(jnp.float32)
    mid = flat.astype(jnp.bfloat16)
    lo = (flat - mid.astype(jnp.float32)).astype(jnp.bfloat16)

    def dot(a, b):
        return jnp.dot(a, b, preferred_element_type=jnp.float32)

    first = dot(jnp.concatenate([hi, mid], axis=1), wide[...])
    second = dot(jnp.concatenate([lo, hi], axis=1), rest[...])
    z_sums = first[:, :depth] + (first[:, depth:] + second)
    first = dot(tall[...], jnp.concatenate([hi, mid], axis=0))
    second = dot(short[...], jnp.concatenate([lo, hi], axis=0))
    y_sums = first[:lines] + (first[lines:] + second)
    return y_sums.reshape(shape), z_sums.reshape(shape)


def fill_z(out, field, matrix):
    for x in range(0, out.shape[0], 16):
        rows = pl.ds(x, min(16, out.shape[0] - x))
        out[rows] = along_z(field[rows], matrix)


def join_y(parts, low, high):
    out = list(parts)
    for e in range(1, len(parts)):
        out[e - 1] = out[e - 1] + high * pltpu.roll(parts[e], 7, axis=1)
        out[e] = out[e] + low * pltpu.roll(parts[e - 1], 1, axis=1)
    return out


def spread_rows(rows):
    return jnp.broadcast_to(rows[:, None, :], (rows.shape[0], 8, rows.shape[1]))


def column_sums(x_rows, y_parts, z_parts, summed, edges):
    y_parts = join_y(y_parts, edges[0], edges[1])
    return [
        jnp.stack(kx) * summed[0, 0] + ky * summed[1] + kz * summed[2]
        for kx, ky, kz in zip(x_rows, y_parts, z_parts)
    ]


def emit_column(ex, x_rows, y_parts, z_parts, summed, edges, out, state, finish):
    rows = pl.ds(8 * ex, 8)
    parts = column_sums(x_rows, y_parts, z_parts, summed, edges)
    for e, part in enumerate(parts):
        ys = pl.ds(8 * e, 8)
        out[rows, ys] = finish(e, part)
        if ex:
            for row, face in ((8 * ex, state[e]), (8 * ex - 1, x_rows[e][0])):
                out[row, ys] += face * summed[0, 0]
    return [r[7] for r in x_rows]


def end_rows(table):
    row = lax.broadcasted_iota(jnp.int32, (8, 128), 0)
    return (table[0], table[7]), (by_place(table[0], row), by_place(table[7], row))


def store_faces(ex, e, columns, count, tile, even, ends, faces, x=True, y=True):
    x_near, x_far, y_near, y_far = faces
    (x_low, x_high), (y_low, y_high) = ends
    rows, ys = pl.ds(8 * ex, 8), pl.ds(8 * e, 8)
    if x and ex == 0:
        low = sum(float(x_low[i]) * tile[i] for i in range(8))
        x_near[ys] = low
        x_far[ys] = low
    if x and ex == columns - 1:
        high = sum(float(x_high[i]) * tile[i] for i in range(8))
        x_near[ys] = jnp.where(even[0], high, x_near[ys])
        x_far[ys] = jnp.where(even[0], x_far[ys], high)
    if y and e == 0:
        low = jnp.sum(tile * y_low, axis=1)
        y_near[rows] = low
        y_far[rows] = low
    if y and e == count - 1:
        high = jnp.sum(tile * y_high, axis=1)
        y_near[rows] = jnp.where(even[1], high, y_near[rows])
        y_far[rows] = jnp.where(even[1], y_far[rows], high)


def parity(even_ref):
    return even_ref[0] > 0.5, even_ref[1] > 0.5


def even_rows(even_ref):
    return even_ref[0, 0:1] > 0.5, even_ref[1, 0:1] > 0.5


def before_of(even, near, far):
    return jnp.where(even, far, near)


def after_of(even, near, far):
    return jnp.where(even, near, far)


def with_faces(tile, ex, e, columns, count, received, even, edges, weight_x=None, weight_y=None, mask=None, x=True):
    x_far, x_near, y_far, y_near = received
    rows, ys = pl.ds(8 * ex, 8), pl.ds(8 * e, 8)

    def weighted(face, weight):
        return face if weight is None else face * weight

    if e == 0:
        face = before_of(even[1], y_near[rows], y_far[rows])
        face = spread_rows(face) * weighted(edges[0], weight_y)
        tile = tile + weighted(face, mask)
    if e == count - 1:
        face = after_of(even[1], y_near[rows], y_far[rows])
        face = spread_rows(face) * weighted(edges[1], weight_y)
        tile = tile + weighted(face, mask)
    if x and ex == 0:
        face = before_of(even[0], x_near[ys], x_far[ys])
        face = weighted(face, weight_x) if mask is None else weighted(face, weight_x) * mask[0]
        tile = jnp.concatenate([tile[0:1] + face[None], tile[1:]], axis=0)
    if x and ex == columns - 1:
        face = after_of(even[0], x_near[ys], x_far[ys])
        face = weighted(face, weight_x) if mask is None else weighted(face, weight_x) * mask[7]
        tile = jnp.concatenate([tile[:7], tile[7:8] + face[None]], axis=0)
    return tile


def split_rows(block_rows):
    return [block_rows[i] for i in range(8)]


def join_rows(parts, low, high):
    out = list(parts)
    for e in range(1, len(parts)):
        out[e - 1] = out[e - 1] + high * pltpu.roll(parts[e], 7, axis=0)
        out[e] = out[e] + low * pltpu.roll(parts[e - 1], 1, axis=0)
    return out


def depth_marks(depth):
    lane = lax.broadcasted_iota(jnp.int32, (8, depth), 1)
    place = lane & 7
    after = jnp.where((place == 0) & (lane > 0), 1.0, 0.0)
    before = jnp.where((place == 7) & (lane < depth - 1), 1.0, 0.0)
    return by_place(WEIGHTS, place), after, before


def join_depth(value, after, before):
    axis, depth = value.ndim - 1, value.shape[-1]
    return value + after * pltpu.roll(value, 1, axis=axis) + before * pltpu.roll(value, depth - 1, axis=axis)


def forced(field, old, step):
    if field == 4:
        return step
    value = step * old(field)
    if field == 2:
        value = value + COUPLING * old(3)
    if field == 3:
        value = value - STRATIFY * old(2)
    return value


def load_faces(old_far, step_far, even_ref, old, step, x_near, x_far, y_near, y_far, arrived):
    length, width, depth = step.shape
    columns, count = length // 8, width // 8
    copies = [pltpu.make_async_copy(step_far, step, arrived.at[4])]
    copies += [pltpu.make_async_copy(old_far.at[i], old.at[i], arrived.at[i]) for i in range(4)]
    for copy in copies:
        copy.start()
    even, (low, high) = parity(even_ref), row_marks()
    row = lax.broadcasted_iota(jnp.int32, (8, depth), 0)
    line, after, before = depth_marks(depth)
    mass = by_place(WEIGHTS, row) * line
    for field in (4, 0, 1, 2, 3):
        if field != 3:
            copies[0 if field == 4 else field + 1].wait()
        if field == 2:
            copies[4].wait()
        found = []
        for x in (0, length - 1):
            parts = []
            for e in range(count):
                ys = pl.ds(8 * e, 8)
                value = forced(field, lambda f: old[f, x, ys], step[x, ys])
                parts.append(join_depth(value * (float(WEIGHTS[x % 8]) * mass), after, before))
            found.append(join_rows(parts, low, high))
        for e in range(count):
            ys = pl.ds(8 * e, 8)
            x_near[field, ys] = jnp.where(even[0], found[1][e], found[0][e])
            x_far[field, ys] = jnp.where(even[0], found[0][e], found[1][e])
        found = []
        for y in (0, width - 1):
            parts = []
            for ex in range(columns):
                rows, ys = pl.ds(8 * ex, 8), pl.ds(y // 8 * 8, 8)
                value = forced(field, lambda f: old[f, rows, ys][:, y % 8], step[rows, ys][:, y % 8])
                parts.append(join_depth(value * (float(WEIGHTS[y % 8]) * mass), after, before))
            found.append(join_rows(parts, low, high))
        for ex in range(columns):
            rows = pl.ds(8 * ex, 8)
            y_near[field, rows] = jnp.where(even[1], found[1][ex], found[0][ex])
            y_far[field, rows] = jnp.where(even[1], found[0][ex], found[1][ex])


def load_local(old, step, out):
    columns, count, depth = out.shape[1] // 8, out.shape[2] // 8, out.shape[3]
    edges = row_marks()
    row = lax.broadcasted_iota(jnp.int32, (8, depth), 0)
    line, after, before = depth_marks(depth)
    plane = by_place(WEIGHTS, row) * line
    mass = jnp.stack([float(w) * plane for w in WEIGHTS])
    for field in range(5):
        state = [None] * count
        for ex in range(columns):
            rows = pl.ds(8 * ex, 8)
            parts = []
            for e in range(count):
                ys = pl.ds(8 * e, 8)
                value = forced(field, lambda f: old[f, rows, ys], step[rows, ys])
                parts.append(join_depth(value * mass, after, before))
            parts = join_y(parts, edges[0], edges[1])
            for e in range(count):
                ys = pl.ds(8 * e, 8)
                out[field, rows, ys] = parts[e]
                if ex:
                    out[field, 8 * ex, ys] += state[e]
                    out[field, 8 * ex - 1, ys] += parts[e][0]
                state[e] = parts[e][7]


def stiff_terms(ex, tiles, stiff_y, z_sums):
    x_rows = [along_x(split_rows(t), STIFF) for t in tiles]
    y_parts = [along_y(t, stiff_y) for t in tiles]
    z_parts = [z_sums[pl.ds(8 * ex, 8), pl.ds(8 * e, 8)] for e in range(len(tiles))]
    return x_rows, y_parts, z_parts


def square_sum(rows):
    total = 0.0
    for sign in (1.0, -1.0):
        form = 0.5 * (STIFF[:4, :4] + sign * STIFF[:4, :3:-1])
        part = [rows[i] + rows[7 - i] if sign > 0 else rows[i] - rows[7 - i] for i in range(4)]
        for i in range(4):
            pivot = form[i, i]
            if pivot < 1e-12:
                continue
            line = form[i] / np.sqrt(pivot)
            value = sum(float(line[b]) * part[b] for b in range(i, 4))
            total = total + value * value
            form = form - np.outer(line, line)
    return total


def join_x(c, out, x_far, x_near, even, even_row, ends, weight, mask, faces, slopes, slope_ends):
    columns, count = out.shape[0] // 8, out.shape[1] // 8
    for xi, side in enumerate((before_of, after_of)):
        row = (8 * columns - 1) * xi
        mended = [[0.0, 0.0], [0.0, 0.0]]
        for e in range(count):
            ys = pl.ds(8 * e, 8)
            change = side(even[0], x_near[c, ys], x_far[c, ys]) * weight * mask(row, ys)
            out[row, ys] += change
            for kind, (low, high) in enumerate((ends[1], slope_ends[1])):
                if e == 0:
                    mended[kind][0] = jnp.sum(change * low, axis=0, keepdims=True)
                if e == count - 1:
                    mended[kind][1] = jnp.sum(change * high, axis=0, keepdims=True)
        for kind, where in enumerate((faces, slopes if c == 1 else None)):
            if where is not None:
                low, high = mended[kind]
                where[2][row : row + 1] += jnp.where(even_row[1], high, low)
                where[3][row : row + 1] += jnp.where(even_row[1], low, high)
    for ex in sorted({0, columns - 1}):
        for e in range(count):
            tile = out[pl.ds(8 * ex, 8), pl.ds(8 * e, 8)]
            if faces is not None:
                store_faces(ex, e, columns, count, tile, even, ends, faces, True, False)
            if slopes is not None and c == 0:
                store_faces(ex, e, columns, count, tile, even, slope_ends, slopes, True, False)


def y_faces(c, ex, e, columns, count, tile, even, ends, slope_ends, y_near, y_far):
    store_faces(ex, e, columns, count, tile, even, ends, (None, None, y_near.at[c], y_far.at[c]), False, True)
    if c == 1:
        slopes = (None, None, y_near.at[4], y_far.at[4])
        store_faces(ex, e, columns, count, tile, even, slope_ends, slopes, False, True)


def first_y(local, boundary, y_far, y_near, even_ref, part, y_near_out, y_far_out):
    columns, count = part.shape[1] // 8, part.shape[2] // 8
    even, edges = parity(even_ref), row_marks()
    ends, slope_ends = end_rows(STIFF), end_rows(SLOPE)
    for c in range(4):
        for ex in range(columns):
            for e in range(count):
                rows, ys = pl.ds(8 * ex, 8), pl.ds(8 * e, 8)
                tile = with_faces(local[c, rows, ys], ex, e, columns, count, (None, None, y_far.at[c], y_near.at[c]),
                                  even, edges, x=False)
                tile = tile * boundary[rows, ys].astype(jnp.float32)
                part[c, rows, ys] = tile
                y_faces(c, ex, e, columns, count, tile, even, ends, slope_ends, y_near_out, y_far_out)


def first_x(part, y_near_in, y_far_in, boundary, x_far, x_near, even_ref, right, near, far, x_near_out, x_far_out):
    del part, y_near_in, y_far_in
    columns, count = right.shape[1] // 8, right.shape[2] // 8
    even, even_row = parity(even_ref), even_rows(even_ref)
    ends, slope_ends = end_rows(STIFF), end_rows(SLOPE)
    faces = (x_near_out, x_far_out, near, far)
    for c in range(4):
        join_x(c, right.at[c], x_far, x_near, even, even_row, ends, 1.0,
               lambda row, ys: boundary[row, ys].astype(jnp.float32),
               [f.at[c] for f in faces], [f.at[4] for f in faces], slope_ends)
    near[5] = jnp.zeros(near.shape[1:], jnp.float32)
    far[5] = jnp.zeros(far.shape[1:], jnp.float32)
    for xi, side in enumerate((before_of, after_of)):
        for field in range(5):
            low, high = [
                side(even_row[0], x_near[field, y : y + 1], x_far[field, y : y + 1]) for y in (0, 8 * count - 1)
            ]
            row = 8 * xi + field
            near[5, row : row + 1] = jnp.where(even_row[1], high, low)
            far[5, row : row + 1] = jnp.where(even_row[1], low, high)


def pick(c, values):
    out = jnp.float32(values[0])
    for i in range(1, 4):
        out = jnp.where(c == i, jnp.float32(values[i]), out)
    return out


def start_sums(scales, rates, local, boundary, x_far, x_near, y_far, y_near, even_ref, right, summed, share, tall_y,
               short_y, wide_z, rest_z, reaction, free, ahead):
    columns, count = ahead.shape[1] // 8, ahead.shape[2] // 8
    even, edges = parity(even_ref), row_marks()
    received = [r.at[4] for r in (x_far, x_near, y_far, y_near)]
    for ex in range(columns):
        for e in range(count):
            rows, ys = pl.ds(8 * ex, 8), pl.ds(8 * e, 8)
            reaction[rows, ys] = with_faces(local[4, rows, ys], ex, e, columns, count, received, even, edges)
            free[rows, ys] = boundary[rows, ys].astype(jnp.float32)
    basis_fill(scales, rates, right, None, reaction, free, summed, share, (tall_y, short_y), (wide_z, rest_z), ahead)


def basis_sums(scales, rates, newest, older, reaction, free, summed, share, tall_y, short_y, wide_z, rest_z, ahead, *dots):
    left, matrix = (tall_y, short_y), (wide_z, rest_z)
    basis_fill(scales, rates, newest, older, reaction, free, summed, share, left, matrix, ahead, *dots)


def basis_fill(scales, rates, newest, older, reaction, free, summed, share, left, matrix, ahead, dots=None, first=None):
    columns, count = ahead.shape[1] // 8, ahead.shape[2] // 8
    double = 1.0 if older is None else 2.0

    def component(c, carry):
        scale, rate = pick(c, [double * v for v in scales]), pick(c, [double * v for v in rates])
        same = jnp.zeros((8, 128), jnp.float32)
        cross = jnp.zeros((8, 128), jnp.float32)
        start = jnp.zeros((8, 128), jnp.float32)
        state = None
        for ex in range(columns):
            rows = pl.ds(8 * ex, 8)
            tiles = []
            for e in range(count):
                ys = pl.ds(8 * e, 8)
                tile = newest[c, rows, ys]
                if older is not None:
                    weighted = tile * share[...]
                    same = same + jnp.sum(weighted * tile, axis=0)
                    cross = cross + jnp.sum(weighted * older[c, rows, ys], axis=0)
                if first is not None:
                    start = start + jnp.sum(older[c, rows, ys] * older[c, rows, ys] * share[...], axis=0)
                tiles.append(tile)
            x_rows = [along_x(split_rows(t), STIFF) for t in tiles]
            y_all, z_all = along_both(newest[c, rows], matrix, left)
            following = [r[7] for r in x_rows]
            for e in range(count):
                ys = pl.ds(8 * e, 8)
                if ex:
                    x_rows[e][0] = x_rows[e][0] + state[e]
                if ex < columns - 1:
                    first_row = sum(float(STIFF[0, i]) * newest[c, 8 * ex + 8 + i, ys] for i in range(8))
                    x_rows[e][7] = x_rows[e][7] + first_row
                part = jnp.stack(x_rows[e]) * summed[0, 0]
                part = part + y_all[:, 8 * e : 8 * e + 8] * summed[1] + z_all[:, 8 * e : 8 * e + 8] * summed[2]
                value = scale * part + (rate * reaction[rows, ys] - double) * tiles[e]
                value = value * free[rows, ys]
                ahead[c, rows, ys] = value if older is None else value - older[c, rows, ys]
            state = following
        if older is not None:
            dots[pl.ds(c, 1)] = jnp.sum(same, axis=0, keepdims=True)
            dots[pl.ds(c + 4, 1)] = jnp.sum(cross, axis=0, keepdims=True)
        if first is not None:
            first[pl.ds(c, 1)] = jnp.sum(start, axis=0, keepdims=True)
            first[pl.ds(c + 4, 1)] = jnp.zeros((1, 128), jnp.float32)
        return carry

    lax.fori_loop(0, 4, component, 0)


def y_field(c, ex, e, ahead, free, y_far, y_near, scale, summed, edges, even, columns, count):
    rows, ys = pl.ds(8 * ex, 8), pl.ds(8 * e, 8)
    return with_faces(ahead[c, rows, ys], ex, e, columns, count, (None, None, y_far.at[c], y_near.at[c]), even, edges,
                      None, summed[1], scale * free[rows, ys], x=False)


def grow_y(scales, ahead, free, y_far, y_near, even_ref, summed, part, y_near_out, y_far_out):
    columns, count = part.shape[1] // 8, part.shape[2] // 8
    even, edges = parity(even_ref), row_marks()
    ends, slope_ends = end_rows(STIFF), end_rows(SLOPE)
    for c in range(4):
        for ex in range(columns):
            for e in range(count):
                tile = y_field(c, ex, e, ahead, free, y_far, y_near, scales[c], summed, edges, even, columns, count)
                part[c, pl.ds(8 * ex, 8), pl.ds(8 * e, 8)] = tile
                y_faces(c, ex, e, columns, count, tile, even, ends, slope_ends, y_near_out, y_far_out)


def grow_x(scales, part, y_near_in, y_far_in, free, x_far, x_near, even_ref, summed, out, y_near_out, y_far_out,
           x_near_out, x_far_out):
    del part, y_near_in, y_far_in
    even, even_row = parity(even_ref), even_rows(even_ref)
    ends, slope_ends = end_rows(STIFF), end_rows(SLOPE)
    faces = (x_near_out, x_far_out, y_near_out, y_far_out)
    for c in range(4):
        join_x(c, out.at[c], x_far, x_near, even, even_row, ends, scales[c] * summed[0, 0],
               lambda row, ys: free[row, ys], [f.at[c] for f in faces], [f.at[4] for f in faces], slope_ends)


def second_y(scales, rates, ahead, free, x_far0, x_near0, y_far0, y_near0, y_far, y_near, even_ref, summed, wide_z,
             rest_z, right_in, reaction_in, out, right, reaction, y_near_out, y_far_out, lines, depth_lines):
    columns, count = out.shape[1] // 8, out.shape[2] // 8
    even, edges, even_row = parity(even_ref), row_marks(), even_rows(even_ref)
    ends, slope_ends = end_rows(STIFF), end_rows(SLOPE)
    end_x, end_y = (0, 8 * columns - 1), (0, 8 * count - 1)
    sides = (before_of, after_of)
    corners = [(xi, yi) for xi in (0, 1) for yi in (0, 1)]

    def at(array, xi, yi):
        return array[end_x[xi], end_y[yi] : end_y[yi] + 1]

    def diagonal(field, xi, yi):
        row = 8 * xi + field
        return sides[yi](even_row[1], y_near[5, row : row + 1], y_far[5, row : row + 1])

    def beside(field, xi, yi):
        row = end_y[yi]
        return sides[xi](even_row[0], x_near0[field, row : row + 1], x_far0[field, row : row + 1])

    def beyond(field, xi, yi):
        row = end_x[xi]
        return sides[yi](even_row[1], y_near0[field, row : row + 1], y_far0[field, row : row + 1])

    for c in range(4):
        for n, (xi, yi) in enumerate(corners):
            lines[4 * c + n : 4 * c + n + 1] = diagonal(c, xi, yi) * at(free, xi, yi)
    depth_lines[...] = along_z(lines[...], (wide_z, rest_z))

    def missed(c, ex, e):
        found = []
        for n, (xi, yi) in enumerate(corners):
            cx, ce, sx, sy = (columns - 1) * xi, (count - 1) * yi, 7 * xi, 7 * yi
            line = lines[4 * c + n : 4 * c + n + 1]
            weight_x, weight_y = summed[0, 0, sy : sy + 1], summed[1, sx, 0:1]
            along = scales[c] * line * weight_x
            across = scales[c] * line * weight_y
            if ex == cx and e == ce:
                for i in range(8):
                    found.append((i, float(STIFF[i, sx]) * along * edges[yi]))
                found.append((sx, across * ends[1][yi]))
                side = beyond(c, xi, yi) * weight_x + beside(c, xi, yi) * weight_y
                side = float(STIFF[0, 0]) * side
                depth = depth_lines[4 * c + n : 4 * c + n + 1] * summed[2, sx, sy : sy + 1]
                gained = diagonal(4, xi, yi)
                node = scales[c] * (side + depth)
                node = node + (rates[c] * (at(reaction_in, xi, yi) + gained) - 1.0) * line
                node = node + rates[c] * gained * at(right_in.at[c], xi, yi)
                found.append((sx, node * edges[yi]))
            elif e == ce and ex == cx + 1 - 2 * xi:
                found.append((sx, float(STIFF[7 - sx, sx]) * along * edges[yi]))
            elif ex == cx and e == ce + 1 - 2 * yi:
                found.append((sx, float(STIFF[7 - sy, sy]) * across * edges[yi]))
        return found

    for c in range(4):
        for ex in range(columns):
            for e in range(count):
                rows, ys = pl.ds(8 * ex, 8), pl.ds(8 * e, 8)
                tile = y_field(c, ex, e, ahead, free, y_far, y_near, scales[c], summed, edges, even, columns, count)
                found = missed(c, ex, e)
                if found:
                    parts = []
                    for i in range(8):
                        extra = [t for row, t in found if row == i]
                        parts.append(tile[i] + sum(extra) * free[8 * ex + i, ys] if extra else tile[i])
                    tile = jnp.stack(parts)
                out[c, rows, ys] = tile
                y_faces(c, ex, e, columns, count, tile, even, ends, slope_ends, y_near_out, y_far_out)

    for n, (xi, yi) in enumerate(corners):
        x, y = end_x[xi], end_y[yi]
        reaction[x, y : y + 1] = at(reaction_in, xi, yi) + diagonal(4, xi, yi)
        for c in range(4):
            right[c, x, y : y + 1] = at(right_in.at[c], xi, yi) + lines[4 * c + n : 4 * c + n + 1]


def mend_slopes(x_far0, x_near0, y_far0, y_near0, x_far, x_near, y_far, y_near, free, even_ref,
                sx_far, sx_near, sy_far, sy_near):
    even_row = even_rows(even_ref)
    end_x, end_y = (0, free.shape[0] - 1), (0, free.shape[1] - 1)
    sides = (before_of, after_of)

    def at(array, xi, yi):
        return array[end_x[xi], end_y[yi] : end_y[yi] + 1]

    def beside(field, xi, yi):
        row = end_y[yi]
        return sides[xi](even_row[0], x_near0[field, row : row + 1], x_far0[field, row : row + 1])

    def beyond(field, xi, yi):
        row = end_x[xi]
        return sides[yi](even_row[1], y_near0[field, row : row + 1], y_far0[field, row : row + 1])

    sx_far[...], sx_near[...], sy_far[...], sy_near[...] = x_far[4], x_near[4], y_far[4], y_near[4]
    low, high = float(SLOPE[7, 7]), float(SLOPE[0, 0])
    for i in (0, 1):
        y, x = end_y[i], end_x[i]
        before = low * beyond(0, 0, i) * at(free, 0, i)
        after = high * beyond(0, 1, i) * at(free, 1, i)
        sx_near[y : y + 1] += jnp.where(even_row[0], after, before)
        sx_far[y : y + 1] += jnp.where(even_row[0], before, after)
        before = low * beside(1, i, 0) * at(free, i, 0)
        after = high * beside(1, i, 1) * at(free, i, 1)
        sy_near[x : x + 1] += jnp.where(even_row[1], after, before)
        sy_far[x : x + 1] += jnp.where(even_row[1], before, after)


def column_products(c, ex, out, newest, reaction, share, left, matrix, local, scale, rate):
    count = out.shape[2] // 8
    rows = pl.ds(8 * ex, 8)
    same = jnp.zeros((8, 128), jnp.float32)
    cross = jnp.zeros((8, 128), jnp.float32)
    work = jnp.zeros((8, 128), jnp.float32)
    y_sums, z_sums = along_both(out[c, rows], matrix, left)
    for e in range(count):
        ys = pl.ds(8 * e, 8)
        tile = out[c, rows, ys]
        weighted = tile * share[...]
        same = same + jnp.sum(weighted * tile, axis=0)
        cross = cross + jnp.sum(weighted * newest[c, rows, ys], axis=0)
        extra = (rate * reaction[rows, ys] - 1.0) * tile
        work = work + jnp.sum(weighted * extra, axis=0)
        work = work + scale * (square_sum(split_rows(tile)) * local[0, 0])
        term = y_sums[:, 8 * e : 8 * e + 8] * local[1] + z_sums[:, 8 * e : 8 * e + 8] * local[2]
        work = work + scale * jnp.sum(term * tile, axis=0)
    return same, cross, work


def last_y(scales, rates, ahead, newest, reaction, free, y_far, y_near, even_ref, summed, share, tall_y, short_y, wide_z,
           rest_z, local, part, sy_near, sy_far, products):
    columns, count = part.shape[1] // 8, part.shape[2] // 8
    even, edges = parity(even_ref), row_marks()
    slope_ends = end_rows(SLOPE)
    for c in range(4):
        total = [jnp.zeros((8, 128), jnp.float32)] * 3
        for ex in range(columns):
            for e in range(count):
                tile = y_field(c, ex, e, ahead, free, y_far, y_near, 2.0 * scales[c], summed, edges, even, columns, count)
                part[c, pl.ds(8 * ex, 8), pl.ds(8 * e, 8)] = tile
                if c == 1:
                    store_faces(ex, e, columns, count, tile, even, slope_ends, (None, None, sy_near, sy_far), False, True)
            if 0 < ex < columns - 1:
                found = column_products(c, ex, part, newest, reaction, share, (tall_y, short_y), (wide_z, rest_z), local,
                                        scales[c], rates[c])
                total = [a + b for a, b in zip(total, found)]
        for n in range(3):
            products[c, n] = total[n]


def last_x(scales, rates, part, sy_near_in, sy_far_in, products, newest, reaction, free, x_far, x_near, even_ref, summed,
           share, tall_y, short_y, wide_z, rest_z, local, d0, d1, d2, d3, d4, out, sy_near, sy_far, sums, sx_near, sx_far):
    del part, sy_near_in, sy_far_in
    dots = (d0, d1, d2, d3, d4)
    columns = out.shape[1] // 8
    even, even_row = parity(even_ref), even_rows(even_ref)
    ends, slope_ends = end_rows(STIFF), end_rows(SLOPE)
    for i in range(1, ITERS - 1):
        sums[i] = dots[i][...]
    for c in range(4):
        join_x(c, out.at[c], x_far, x_near, even, even_row, ends, 2.0 * scales[c] * summed[0, 0],
               lambda row, ys: free[row, ys], None, (sx_near, sx_far, sy_near, sy_far), slope_ends)
        total = [products[c, n] for n in range(3)]
        for ex in sorted({0, columns - 1}):
            found = column_products(c, ex, out, newest, reaction, share, (tall_y, short_y), (wide_z, rest_z), local,
                                    scales[c], rates[c])
            total = [a + b for a, b in zip(total, found)]
        same, cross, work = [jnp.sum(t, axis=0, keepdims=True) for t in total]
        sums[ITERS - 1, c : c + 1] = same
        sums[ITERS - 1, c + 4 : c + 5] = cross
        sums[0, c : c + 1] = dots[0][c : c + 1]
        sums[0, c + 4 : c + 5] = work


def slope_sums(*refs):
    fields, (summed, slope_y, wide_z, rest_z), outs = refs[:3], refs[3:7], refs[7:]
    columns, count = outs[0].shape[1] // 8, outs[0].shape[2] // 8
    edges = row_marks()
    for field, out in zip(fields, outs):
        fill_z(out.at[2], field.at[2], (wide_z, rest_z))
        state = None
        for ex in range(columns):
            rows, ends = pl.ds(8 * ex, 8), []
            y_parts = [along_y(field[1, rows, pl.ds(8 * e, 8)], slope_y) for e in range(count)]
            y_parts = join_y(y_parts, edges[0], edges[1])
            for e in range(count):
                ys = pl.ds(8 * e, 8)
                out[1, rows, ys] = y_parts[e] * summed[1]
                out[2, rows, ys] = out[2, rows, ys] * summed[2]
                x_rows = [r * summed[0, 0] for r in along_x(split_rows(field[0, rows, ys]), SLOPE)]
                out[0, rows, ys] = jnp.stack(x_rows)
                if ex:
                    out[0, 8 * ex, ys] += state[e]
                    out[0, 8 * ex - 1, ys] += x_rows[0]
                ends.append(x_rows[7])
            state = ends


def first_update(halves, gain, *refs):
    sums, *sloped = refs[: ITERS + 1]
    refs = refs[ITERS + 1 :]
    slopes = [refs[:4]]
    slopes += [[r.at[4] for r in refs[4 * k : 4 * k + 4]] for k in range(1, ITERS - 1)]
    refs = refs[4 * ITERS - 4 :]
    slopes.append(refs[:4])
    even_ref, free, summed, inverse = refs[4:8]
    weights, remainder, update, *faces = refs[8:15]
    joined = refs[15:]
    columns, count = update.shape[0] // 8, update.shape[1] // 8
    even, edges = parity(even_ref), row_marks()
    ends = end_rows(STIFF)
    total = [jnp.broadcast_to(jnp.sum(sums[i], axis=1, keepdims=True), (8, 128)) for i in range(ITERS)]
    other = [pltpu.roll(t, 4, axis=0) for t in total]
    row = lax.broadcasted_iota(jnp.int32, (8, 128), 0)
    half = jnp.full((8, 128), halves[0], jnp.float32)
    for i in range(1, 4):
        half = jnp.where(row == i, halves[i], half)
    moments = [total[0], other[1]]
    for level in range(2, 2 * ITERS - 1):
        inner = total[level // 2] if level % 2 == 0 else other[level // 2 + 1]
        moments.append(2.0 * inner - moments[level % 2])
    top = 2.0 * other[0] - other[5]
    moments.append(2.0 * top - moments[1])
    for i, value in enumerate(conjugate_coefficients(moments, half, half)):
        weights[i] = value
    for n in range(4):
        c = n // 2
        joined[n][...] = sum(slopes[i][n][...] * weights[i, c : c + 1] for i in range(ITERS))
    factor = [[weights[i, c : c + 1][None] for c in range(3)] for i in range(ITERS)]
    for ex in range(columns):
        for e in range(count):
            rows, ys = pl.ds(8 * ex, 8), pl.ds(8 * e, 8)
            tile = sum(sloped[i][c, rows, ys] * factor[i][c] for i in range(ITERS) for c in range(3))
            tile = with_faces(tile, ex, e, columns, count, joined, even, edges, summed[0, 0], summed[1])
            left = -tile * free[rows, ys]
            change = gain * inverse[...] * left
            remainder[rows, ys] = left
            update[rows, ys] = change
            store_faces(ex, e, columns, count, change, even, ends, faces)


def combine_fields(weights, *refs):
    *basis, fields = refs

    def combine(c, carry):
        factor = [weights[i, pl.ds(c, 1)] for i in range(ITERS)]
        for x in range(0, fields.shape[1], 8):
            rows = pl.ds(x, 8)
            value = basis[0][c, rows] * factor[0][None]
            for i in range(1, ITERS):
                value = value + basis[i][c, rows] * factor[i][None]
            fields[c, rows] = value
        return carry

    lax.fori_loop(0, 4, combine, 0)


def add_loads(count, *refs):
    *loads, rider, tick, out = refs
    del tick
    values = [load[:count] for load in loads]
    total = values[0] + values[1]
    if len(values) == 4:
        total = total + (values[2] + values[3])
    out[:count] = total
    out[count:] = rider[...]


def pressure_sums(update, summed, shift, stiff_y, wide_z, rest_z, raw, z_sums):
    columns, count = raw.shape[0] // 8, raw.shape[1] // 8
    edges = row_marks()
    state = None
    fill_z(z_sums, update, (wide_z, rest_z))
    for ex in range(columns):
        rows = pl.ds(8 * ex, 8)
        tiles = [update[rows, pl.ds(8 * e, 8)] for e in range(count)]
        x_rows, y_parts, z_parts = stiff_terms(ex, tiles, stiff_y, z_sums)
        state = emit_column(ex, x_rows, y_parts, z_parts, summed, edges, raw, state,
                            lambda e, part: part + shift[...] * tiles[e])


def pressure_step(last, keep, gain, *refs):
    raw, free, *received, even_ref, summed, inverse, remainder_in, update_in, pressure_in = refs[:12]
    if last:
        pressure_far, pressure, left_here = refs[12:]
    else:
        pressure, remainder, update, *faces = refs[12:]
    columns, count = raw.shape[0] // 8, raw.shape[1] // 8
    copies = []
    even, edges = parity(even_ref), row_marks()
    ends = end_rows(STIFF)
    for ex in range(columns):
        for e in range(count):
            rows, ys = pl.ds(8 * ex, 8), pl.ds(8 * e, 8)
            tile = with_faces(raw[rows, ys], ex, e, columns, count, received, even, edges,
                              summed[0, 0], summed[1])
            left = remainder_in[rows, ys] - tile * free[rows, ys]
            change = gain * inverse[...] * left + keep * update_in[rows, ys]
            pressure[rows, ys] = pressure_in[rows, ys] + change
            if not last:
                remainder[rows, ys] = left
                update[rows, ys] = change
                store_faces(ex, e, columns, count, change, even, ends, faces)
        if last:
            rows = pl.ds(8 * ex, 8)
            copies.append(pltpu.make_async_copy(pressure.at[rows], pressure_far.at[rows], left_here.at[ex]))
            copies[-1].start()
    for copy in copies:
        copy.wait()


VMEM_BYTES = 24 * 1024 * 1024


def call(kernel, name, outs, *args, scratch=(), cost=None, far_in=0, far_out=0, copies=0, aliases=()):
    held, far = pl.BlockSpec(memory_space=pltpu.VMEM), pl.BlockSpec(memory_space=pltpu.HBM)
    scratch_shapes = [pltpu.VMEM(s, jnp.float32) for s in scratch]
    if copies:
        scratch_shapes.append(pltpu.SemaphoreType.DMA((copies,)))
    return pl.pallas_call(
        kernel,
        name=name,
        out_shape=[jax.ShapeDtypeStruct(s, jnp.float32) for s in outs],
        in_specs=[far] * far_in + [held] * (len(args) - far_in),
        out_specs=[far] * far_out + [held] * (len(outs) - far_out),
        scratch_shapes=scratch_shapes,
        cost_estimate=cost,
        input_output_aliases=dict(aliases),
        compiler_params=pltpu.CompilerParams(vmem_limit_bytes=VMEM_BYTES),
    )(*[pltpu.with_memory_space_constraint(a, pltpu.HBM) for a in args[:far_in]], *args[far_in:])


def busy(bytes_accessed):
    return pl.CostEstimate(flops=0, bytes_accessed=bytes_accessed, transcendentals=0)


def swap_near(axis, face):
    return lax.ppermute(face, axis, [(i, i ^ 1) for i in range(lax.axis_size(axis))])


def swap_far(axis, face):
    size = lax.axis_size(axis)
    return lax.ppermute(face, axis, [(i, far_partner(i, size)) for i in range(size)])


def swap_all(x_near, x_far, y_near, y_far):
    y_far = swap_far("gy", y_far)
    x_far = swap_far("gx", x_far)
    x_near = swap_near("gx", x_near)
    y_near = swap_near("gy", y_near)
    return x_far, x_near, y_far, y_near


def far_partner(i, size):
    return (i + 1 if i % 2 else i - 1) % size


def partner_loads(load, axis, partners, riders, count):
    size, heard, faces = lax.axis_size(axis), [], []
    for n, (partner, rider) in enumerate(zip(partners, riders)):
        mine = load
        if n:
            mine = load[:count] if rider is None else jnp.concatenate([load[:count], rider])
        mine = lax.ppermute(mine, axis, [(i, partner(i)) for i in range(size)])
        heard.append(mine)
        if rider is not None:
            faces.append(mine[count:])
    return heard, faces


def all_sum(values, axis, near, far, following, meanwhile):
    size = lax.axis_size(axis)
    count = values.shape[0] - far.shape[0] if following is None else values.shape[0]
    half = size // 2

    def to_near(i):
        return i ^ 1

    def to_far(i):
        return far_partner(i, size)

    def across(i):
        return (i + half) % size

    def far_across(i):
        return across(to_far(i))

    rounds = [((to_far,), (far,))]
    if size == 4:
        rounds = [((to_far, to_near, across), (far, near, None))]
    elif size > 4:
        rounds = [((to_far, across, far_across), (far, None, None)), ((to_near,), (near,))]
        bit = 4
        while bit < half:
            rounds.append(((lambda i, bit=bit: i ^ bit,), (None,)))
            bit *= 2
    else:
        rounds.append(((), (near,)))
    faces = []
    load = values if following is None else jnp.concatenate([values, far])
    for n, (partners, riders) in enumerate(rounds):
        if not partners:
            faces.append(lax.ppermute(near, axis, [(i, to_near(i)) for i in range(size)]))
            continue
        heard, got = partner_loads(load, axis, partners, riders, count)
        faces += got
        rider = rounds[n + 1][1][0] if n + 1 < len(rounds) and rounds[n + 1][0] else following
        tail = jnp.zeros((8, values.shape[1]), jnp.float32) if rider is None else rider
        (load,) = call(
            functools.partial(add_loads, count), "add_loads", [(count + tail.shape[0], values.shape[1])],
            load, *heard, tail, meanwhile(),
        )
    if following is None:
        load = load[:count]
    return load, faces[1], faces[0]


def conjugate_coefficients(moments, centre, half):
    remaining, towards = list(moments), list(moments)
    one, zero = jnp.ones_like(moments[0]), jnp.zeros_like(moments[0])
    direction = [one] + [zero] * ITERS
    residual = list(direction)
    total = [zero] * ITERS
    for step in range(ITERS):
        count = len(towards) - 1
        image = []
        for level in range(count):
            side = (
                half * towards[1] if level == 0 else 0.5 * half * (towards[level + 1] + towards[level - 1])
            )
            image.append(centre * towards[level] + side)
        alpha = remaining[step] / image[step]
        total = [total[i] + alpha * direction[i] for i in range(ITERS)]
        if step == ITERS - 1:
            break
        applied = []
        for i in range(ITERS + 1):
            term = centre * direction[i]
            if i >= 1:
                term = term + (half if i == 1 else 0.5 * half) * direction[i - 1]
            if i < ITERS:
                term = term + 0.5 * half * direction[i + 1]
            applied.append(term)
        residual = [residual[i] - alpha * applied[i] for i in range(ITERS + 1)]
        following = [remaining[i] - alpha * image[i] for i in range(count)]
        beta = -alpha * (half if step == 0 else 0.5 * half) * following[step + 1] / remaining[step]
        towards = [following[i] + beta * towards[i] for i in range(count)]
        direction = [residual[i] + beta * direction[i] for i in range(ITERS + 1)]
        remaining = following
    return total


def on_device(old_fields, inverse_step, boundary):
    x, y, z = inverse_step.shape
    t = Tables(y, z)
    brick, four = (x, y, z), (4, x, y, z)
    faces = [(y, z)] * 2 + [(x, z)] * 2
    faces5 = [(5,) + f for f in faces]
    faces_back = [(y, z)] * 2 + [(x, z)] * 2

    place = [lax.axis_index(a) % 2 == 0 for a in ("gx", "gy")]
    even = jnp.stack([jnp.full((8, 128), p, jnp.float32) for p in place])

    old, step, x_near, x_far, y_near, y_far = call(
        load_faces, "right_faces", [four, brick] + faces5, old_fields, inverse_step, even, far_in=2, copies=5,
    )
    received = swap_all(x_near, x_far, y_near, y_far)
    (local,) = call(load_local, "right_local", [(5,) + brick], old, step, cost=busy(2 << 20))

    top = INTERVAL_SHARE * np.array([spectrum_top(c) for c in DIFFUSE])
    halves = [float(v) for v in 0.5 * top]
    scales = [float(v) for v in np.array(DIFFUSE) / (0.5 * top)]
    rates = [float(v) for v in 1.0 / (0.5 * top)]

    x_far, x_near, y_far, y_near = received
    relayed = [(6, x, z)] * 2
    x_faces, y_faces5 = [(5, y, z)] * 2, [(5, x, z)] * 2
    part, near, far = call(first_y, "first_y", [four] + relayed, local, boundary, y_far, y_near, even, cost=busy(2 << 20))
    right, y_near, y_far, x_near, x_far = call(
        first_x, "first_x", [four] + relayed + x_faces, part, near, far, boundary, x_far, x_near, even,
        aliases=[(0, 0), (1, 1), (2, 2)],
    )
    heard = [swap_all(x_near, x_far, y_near, y_far)]
    reaction, free, ahead = call(
        functools.partial(start_sums, scales, rates), "right_sums", [brick, brick, four],
        local, boundary, *received, even, right, t.summed, t.share, *t.left_y, *t.stiff_z, cost=busy(8 << 20),
    )
    x_far, x_near, y_far, y_near = heard[0]
    part, right, reaction, near, far = call(
        functools.partial(second_y, scales, rates), "second_y", [four, four, brick] + y_faces5,
        ahead, free, *received, y_far, y_near, even, t.summed, *t.stiff_z, right, reaction,
        scratch=[(16, z)] * 2, aliases=[(12, 1), (13, 2)], cost=busy(3 << 20),
    )
    basis, sums = [right], []
    here = scales
    for k in range(1, ITERS - 1):
        field, y_near, y_far, x_near, x_far = call(
            functools.partial(grow_x, here), "basis_x", [four] + y_faces5 + x_faces,
            part, near, far, free, x_far, x_near, even, t.summed, aliases=[(0, 0), (1, 1), (2, 2)],
        )
        basis.append(field)
        heard.append(swap_all(x_near, x_far, y_near, y_far))
        x_far, x_near, y_far, y_near = heard[-1]
        outs = [four, (8, 128)] + ([(8, 128)] if k == 1 else [])
        ahead, *dots = call(
            functools.partial(basis_sums, scales, rates), "basis_sums", outs,
            basis[-1], basis[-2], reaction, free, t.summed, t.share, *t.left_y, *t.stiff_z, cost=busy(8 << 20),
        )
        sums += dots[::-1]
        here = [2.0 * v for v in scales]
        if k < ITERS - 2:
            part, near, far = call(
                functools.partial(grow_y, here), "basis_y", [four] + y_faces5,
                ahead, free, y_far, y_near, even, t.summed, cost=busy(2 << 20),
            )
    part, near, far, products = call(
        functools.partial(last_y, scales, rates), "last_y", [four] + [(x, z)] * 2 + [(4, 3, 8, 128)],
        ahead, basis[-1], reaction, free, y_far, y_near, even, t.summed, t.share, *t.plain_y, *t.plain_z, t.local,
        cost=busy(4 << 20),
    )
    field, y_near, y_far, sums, x_near, x_far = call(
        functools.partial(last_x, scales, rates), "last_x",
        [four] + [(x, z)] * 2 + [(ITERS, 8, 128)] + [(y, z)] * 2,
        part, near, far, products, basis[-1], reaction, free, x_far, x_near, even, t.summed, t.share,
        *t.plain_y, *t.plain_z, t.local, *sums, aliases=[(0, 0), (1, 1), (2, 2)],
    )
    basis.append(field)
    heard[0] = call(mend_slopes, "slopes", faces_back, *received, *heard[0], free, even)
    sums = sums.reshape(ITERS * 8, z)
    sloped = []

    def meanwhile():
        if len(sloped) < ITERS:
            sloped.extend(
                call(
                    slope_sums, "slope_sums", [(3,) + brick] * 3,
                    *basis[len(sloped) : len(sloped) + 3], t.summed, t.slope_y, *t.slope_z, cost=busy(6 << 20),
                )
            )
        return sloped[-1]

    sums, x_near, x_far = all_sum(sums, "gx", x_near, x_far, y_far, meanwhile)
    sums, y_near, y_far = all_sum(sums, "gy", y_near, y_far, None, meanwhile)
    while len(sloped) < ITERS:
        meanwhile()
    sums = sums.reshape(ITERS, 8, z)
    slopes = (x_far, x_near, y_far, y_near)

    centre, half = chebyshev_bounds()
    factor = centre / half
    damping = 1.0 / factor
    weights, remainder, update, *sent = call(
        functools.partial(first_update, halves, 1.0 / centre), "first_update", [(ITERS, 8, 128), brick, brick] + faces,
        sums, *sloped, *[a for h in heard for a in h], *slopes, even, free, t.summed, t.inverse, scratch=faces_back,
    )
    pressure = update
    for step in range(1, CHEB):
        last = step == CHEB - 1
        received = swap_all(*sent)
        (raw,) = call(
            pressure_sums, "pressure_sums", [brick],
            update, t.summed, t.shift, t.stiff_y, *t.stiff_z, cost=busy(2 << 20), scratch=[brick],
        )
        if step == 1:
            (fields,) = call(combine_fields, "fields", [four], weights, *basis, cost=busy(4 << 20))
        following = 1.0 / (2.0 * factor - damping)
        keep, gain = following * damping, 2.0 * following / half
        damping = following
        kernel = functools.partial(pressure_step, last, keep, gain)
        args = [raw, free, *received, even, t.summed, t.inverse, remainder, update, pressure]
        if last:
            (pressure,) = call(
                kernel, "pressure_last", [brick], *args, scratch=[brick], far_out=1, copies=x // 8
            )
            break
        pressure, remainder, update, *sent = call(kernel, "pressure_step", [brick] * 3 + faces, *args)
    return (fields, pressure)


def solution(mesh):
    return jax.shard_map(
        on_device,
        mesh=mesh,
        in_specs=(P(None, "gx", "gy", None), P("gx", "gy", None), P("gx", "gy", None)),
        out_specs=(P(None, "gx", "gy", None), P("gx", "gy", None)),
        check_vma=False,
    )
```

```python
import functools

import jax
import jax.numpy as jnp
import ml_dtypes
import numpy as np
from jax import lax
from jax.experimental import pallas as pl
from jax.experimental.pallas import tpu as pltpu
from jax.sharding import PartitionSpec as P

ITERS = 6
CHEB = 6

SIGMA_SHIFT = 0.5
DIFFUSE = (1.0, 1.0, 1.0, 1.4)
COUPLING = 1.0
STRATIFY = 1.0
SPREAD = 20.0
STEP_MAX = 64.0
INTERVAL_SHARE = 0.82
HIGHEST_PRECISION = lax.Precision.HIGHEST
LOBATTO_POINTS = (
    -1.0,
    -0.8717401485096066,
    -0.5917001814331423,
    -0.2092992179024789,
    0.2092992179024789,
    0.5917001814331423,
    0.8717401485096066,
    1.0,
)


def legendre_value(points, degree):
    previous = points * 0.0 + 1.0
    current = points
    for order in range(1, degree):
        following = ((2 * order + 1) * points * current - order * previous) / (order + 1)
        previous = current
        current = following
    return current


def quadrature_tables():
    degree = 7
    points = np.array(LOBATTO_POINTS)
    values = legendre_value(points, degree)
    weights = 2.0 / (degree * (degree + 1) * values * values)
    derive = np.zeros((degree + 1, degree + 1))
    for row_index in range(degree + 1):
        for column_index in range(degree + 1):
            if row_index != column_index:
                derive[row_index, column_index] = values[row_index] / (
                    values[column_index] * (points[row_index] - points[column_index])
                )
    derive[0, 0] = -degree * (degree + 1) / 4.0
    derive[degree, degree] = degree * (degree + 1) / 4.0
    stiffness_table = derive.T @ (weights[:, None] * derive)
    return (weights, derive, stiffness_table)


WEIGHTS, DERIVE, STIFF = quadrature_tables()
SLOPE = WEIGHTS[:, None] * DERIVE
COPIES = np.where(np.arange(8) % 7 == 0, 2.0, 1.0)


def chebyshev_bounds():
    weight_matrix = np.eye(8) * WEIGHTS

    def kron3(a, b, c):
        return np.kron(np.kron(a, b), c)

    element_matrix = (
        kron3(STIFF, weight_matrix, weight_matrix)
        + kron3(weight_matrix, STIFF, weight_matrix)
        + kron3(weight_matrix, weight_matrix, STIFF)
        + SIGMA_SHIFT * kron3(weight_matrix, weight_matrix, weight_matrix)
    )
    bounds_ratio = np.sum(np.abs(element_matrix), axis=1) / np.diagonal(element_matrix)
    upper_bound = float(np.max(bounds_ratio))
    lower_bound = upper_bound / SPREAD
    return ((upper_bound + lower_bound) / 2.0, (upper_bound - lower_bound) / 2.0)


def spectrum_top(diffuse):
    root = np.sqrt(COPIES)
    stiff = root[:, None] * STIFF * root[None, :]
    weight = np.diag(WEIGHTS * COPIES)

    def kron3(a, b, c):
        return np.kron(np.kron(a, b), c)

    element = diffuse * (
        kron3(stiff, weight, weight) + kron3(weight, stiff, weight) + kron3(weight, weight, stiff)
    ) + STEP_MAX * kron3(weight, weight, weight)
    return float(np.linalg.eigvalsh(element)[-1])


def line_sums(table, length):
    matrix = np.kron(np.eye(length // 8), table)
    total = matrix.copy()
    for start in range(8, length, 8):
        total[start] += matrix[start - 1]
        total[start - 1] += matrix[start]
    return total


def depth_line(vector, length):
    line = np.tile(vector * COPIES, length // 8)
    line[0] = vector[0]
    line[-1] = vector[-1]
    return line


def f32(array):
    return np.ascontiguousarray(array, np.float32)


def rolled_rows(table):
    out = np.zeros((8, 8, 128))
    for shift in range(8):
        for row in range(8):
            out[shift, row] = table[row, (row - shift) % 8]
    return out


def block(a, b, c):
    return a[:, None, None] * b[:, None] * c


def parts_of(matrix):
    rest, parts = f32(matrix), []
    for _ in range(3):
        parts.append(rest.astype(ml_dtypes.bfloat16))
        rest = rest - parts[-1].astype(np.float32)
    hi, mid, lo = parts
    return np.block([[hi, mid], [hi, mid]]), np.concatenate([hi, lo])


def left_parts(table):
    rest, parts = f32(np.kron(np.eye(8), table)), []
    for _ in range(3):
        parts.append(rest.astype(ml_dtypes.bfloat16))
        rest = rest - parts[-1].astype(np.float32)
    hi, mid, lo = parts
    return np.block([[hi, hi], [mid, mid]]), np.concatenate([hi, lo], axis=1)


class Tables:
    def __init__(self, width, depth):
        self.left_y = left_parts(line_sums(STIFF, width))
        self.plain_y = left_parts(np.kron(np.eye(width // 8), STIFF))
        ones8, ones = np.ones(8), np.ones(depth)
        wide = WEIGHTS * COPIES
        deep = depth_line(WEIGHTS, depth)
        flat = np.tile(WEIGHTS, depth // 8)
        stiff = np.diagonal(STIFF)
        wide_s, deep_s = stiff * COPIES, depth_line(stiff, depth)
        share = 1.0 / COPIES
        share_z = np.tile(share, depth // 8)
        share_z[0] = share_z[-1] = 1.0
        self.summed = f32(
            np.stack([block(ones8, wide, deep), block(wide, ones8, deep), block(wide, wide, ones)])
        )
        self.local = f32(
            np.stack(
                [block(ones8, WEIGHTS, flat), block(WEIGHTS, ones8, flat), block(WEIGHTS, WEIGHTS, ones)]
            )
        )
        self.share = f32(block(share, share, share_z))
        diagonal = (
            block(wide_s, wide, deep)
            + block(wide, wide_s, deep)
            + block(wide, wide, deep_s)
            + SIGMA_SHIFT * block(wide, wide, deep)
        )
        self.inverse = f32(1.0 / diagonal)
        self.shift = f32(SIGMA_SHIFT * block(wide, wide, deep))
        self.stiff_y = f32(rolled_rows(STIFF))
        self.slope_y = f32(rolled_rows(SLOPE))
        self.stiff_z = parts_of(line_sums(STIFF, depth).T)
        self.plain_z = parts_of(np.kron(np.eye(depth // 8), STIFF).T)
        self.slope_z = parts_of(line_sums(SLOPE, depth).T)


def row_marks():
    row = lax.broadcasted_iota(jnp.int32, (8, 128), 0)
    return jnp.where(row == 0, 1.0, 0.0), jnp.where(row == 7, 1.0, 0.0)


def by_place(vector, place):
    out = jnp.full(place.shape, float(vector[0]), jnp.float32)
    for i in range(1, 8):
        out = jnp.where(place == i, float(vector[i]), out)
    return out


def along_x(rows, table):
    if np.allclose(table, table[::-1, ::-1]):
        even = 0.5 * (table[:4, :4] + table[:4, :3:-1])
        odd = 0.5 * (table[:4, :4] - table[:4, :3:-1])
        plus = [rows[i] + rows[7 - i] for i in range(4)]
        minus = [rows[i] - rows[7 - i] for i in range(4)]
        out = [None] * 8
        for a in range(4):
            p = sum(float(even[a, b]) * plus[b] for b in range(4))
            m = sum(float(odd[a, b]) * minus[b] for b in range(4))
            out[a], out[7 - a] = p + m, p - m
        return out
    return [sum(float(table[a, b]) * rows[b] for b in range(8)) for a in range(8)]


def along_y(tiles, factors):
    total = factors[0] * tiles
    for shift in range(1, 8):
        total = total + factors[shift] * pltpu.roll(tiles, shift, axis=1)
    return total


def along_z(tiles, matrix):
    wide, rest = matrix
    shape, depth = tiles.shape, tiles.shape[-1]
    flat = tiles.reshape(-1, depth)
    hi = flat.astype(jnp.bfloat16)
    flat = flat - hi.astype(jnp.float32)
    mid = flat.astype(jnp.bfloat16)
    lo = (flat - mid.astype(jnp.float32)).astype(jnp.bfloat16)
    first = jnp.dot(jnp.concatenate([hi, mid], axis=1), wide[...], preferred_element_type=jnp.float32)
    second = jnp.dot(jnp.concatenate([lo, hi], axis=1), rest[...], preferred_element_type=jnp.float32)
    return (first[:, :depth] + (first[:, depth:] + second)).reshape(shape)


def along_both(tiles, matrix, left):
    wide, rest = matrix
    tall, short = left
    shape, depth = tiles.shape, tiles.shape[-1]
    flat = tiles.reshape(-1, depth)
    lines = flat.shape[0]
    hi = flat.astype(jnp.bfloat16)
    flat = flat - hi.astype(jnp.float32)
    mid = flat.astype(jnp.bfloat16)
    lo = (flat - mid.astype(jnp.float32)).astype(jnp.bfloat16)

    def dot(a, b):
        return jnp.dot(a, b, preferred_element_type=jnp.float32)

    first = dot(jnp.concatenate([hi, mid], axis=1), wide[...])
    second = dot(jnp.concatenate([lo, hi], axis=1), rest[...])
    z_sums = first[:, :depth] + (first[:, depth:] + second)
    first = dot(tall[...], jnp.concatenate([hi, mid], axis=0))
    second = dot(short[...], jnp.concatenate([lo, hi], axis=0))
    y_sums = first[:lines] + (first[lines:] + second)
    return y_sums.reshape(shape), z_sums.reshape(shape)


def fill_z(out, field, matrix):
    for x in range(0, out.shape[0], 16):
        rows = pl.ds(x, min(16, out.shape[0] - x))
        out[rows] = along_z(field[rows], matrix)


def join_y(parts, low, high):
    out = list(parts)
    for e in range(1, len(parts)):
        out[e - 1] = out[e - 1] + high * pltpu.roll(parts[e], 7, axis=1)
        out[e] = out[e] + low * pltpu.roll(parts[e - 1], 1, axis=1)
    return out


def spread_rows(rows):
    return jnp.broadcast_to(rows[:, None, :], (rows.shape[0], 8, rows.shape[1]))


def column_sums(x_rows, y_parts, z_parts, summed, edges):
    y_parts = join_y(y_parts, edges[0], edges[1])
    return [
        jnp.stack(kx) * summed[0, 0] + ky * summed[1] + kz * summed[2]
        for kx, ky, kz in zip(x_rows, y_parts, z_parts)
    ]


def emit_column(ex, x_rows, y_parts, z_parts, summed, edges, out, state, finish):
    rows = pl.ds(8 * ex, 8)
    parts = column_sums(x_rows, y_parts, z_parts, summed, edges)
    for e, part in enumerate(parts):
        ys = pl.ds(8 * e, 8)
        out[rows, ys] = finish(e, part)
        if ex:
            for row, face in ((8 * ex, state[e]), (8 * ex - 1, x_rows[e][0])):
                out[row, ys] += face * summed[0, 0]
    return [r[7] for r in x_rows]


def end_rows(table):
    row = lax.broadcasted_iota(jnp.int32, (8, 128), 0)
    return (table[0], table[7]), (by_place(table[0], row), by_place(table[7], row))


def store_faces(ex, e, columns, count, tile, even, ends, faces, x=True, y=True):
    x_near, x_far, y_near, y_far = faces
    (x_low, x_high), (y_low, y_high) = ends
    rows, ys = pl.ds(8 * ex, 8), pl.ds(8 * e, 8)
    if x and ex == 0:
        low = sum(float(x_low[i]) * tile[i] for i in range(8))
        x_near[ys] = low
        x_far[ys] = low
    if x and ex == columns - 1:
        high = sum(float(x_high[i]) * tile[i] for i in range(8))
        x_near[ys] = jnp.where(even[0], high, x_near[ys])
        x_far[ys] = jnp.where(even[0], x_far[ys], high)
    if y and e == 0:
        low = jnp.sum(tile * y_low, axis=1)
        y_near[rows] = low
        y_far[rows] = low
    if y and e == count - 1:
        high = jnp.sum(tile * y_high, axis=1)
        y_near[rows] = jnp.where(even[1], high, y_near[rows])
        y_far[rows] = jnp.where(even[1], y_far[rows], high)


def parity(even_ref):
    return even_ref[0] > 0.5, even_ref[1] > 0.5


def even_rows(even_ref):
    return even_ref[0, 0:1] > 0.5, even_ref[1, 0:1] > 0.5


def before_of(even, near, far):
    return jnp.where(even, far, near)


def after_of(even, near, far):
    return jnp.where(even, near, far)


def with_faces(tile, ex, e, columns, count, received, even, edges, weight_x=None, weight_y=None, mask=None, x=True):
    x_far, x_near, y_far, y_near = received
    rows, ys = pl.ds(8 * ex, 8), pl.ds(8 * e, 8)

    def weighted(face, weight):
        return face if weight is None else face * weight

    if e == 0:
        face = before_of(even[1], y_near[rows], y_far[rows])
        face = spread_rows(face) * weighted(edges[0], weight_y)
        tile = tile + weighted(face, mask)
    if e == count - 1:
        face = after_of(even[1], y_near[rows], y_far[rows])
        face = spread_rows(face) * weighted(edges[1], weight_y)
        tile = tile + weighted(face, mask)
    if x and ex == 0:
        face = before_of(even[0], x_near[ys], x_far[ys])
        face = weighted(face, weight_x) if mask is None else weighted(face, weight_x) * mask[0]
        tile = jnp.concatenate([tile[0:1] + face[None], tile[1:]], axis=0)
    if x and ex == columns - 1:
        face = after_of(even[0], x_near[ys], x_far[ys])
        face = weighted(face, weight_x) if mask is None else weighted(face, weight_x) * mask[7]
        tile = jnp.concatenate([tile[:7], tile[7:8] + face[None]], axis=0)
    return tile


def split_rows(block_rows):
    return [block_rows[i] for i in range(8)]


def join_rows(parts, low, high):
    out = list(parts)
    for e in range(1, len(parts)):
        out[e - 1] = out[e - 1] + high * pltpu.roll(parts[e], 7, axis=0)
        out[e] = out[e] + low * pltpu.roll(parts[e - 1], 1, axis=0)
    return out


def depth_marks(depth):
    lane = lax.broadcasted_iota(jnp.int32, (8, depth), 1)
    place = lane & 7
    after = jnp.where((place == 0) & (lane > 0), 1.0, 0.0)
    before = jnp.where((place == 7) & (lane < depth - 1), 1.0, 0.0)
    return by_place(WEIGHTS, place), after, before


def join_depth(value, after, before):
    axis, depth = value.ndim - 1, value.shape[-1]
    return value + after * pltpu.roll(value, 1, axis=axis) + before * pltpu.roll(value, depth - 1, axis=axis)


def forced(field, old, step):
    if field == 4:
        return step
    value = step * old(field)
    if field == 2:
        value = value + COUPLING * old(3)
    if field == 3:
        value = value - STRATIFY * old(2)
    return value


def load_faces(old_far, step_far, even_ref, old, step, x_near, x_far, y_near, y_far, arrived):
    length, width, depth = step.shape
    columns, count = length // 8, width // 8
    copies = [pltpu.make_async_copy(step_far, step, arrived.at[4])]
    copies += [pltpu.make_async_copy(old_far.at[i], old.at[i], arrived.at[i]) for i in range(4)]
    for copy in copies:
        copy.start()
    even, (low, high) = parity(even_ref), row_marks()
    row = lax.broadcasted_iota(jnp.int32, (8, depth), 0)
    line, after, before = depth_marks(depth)
    mass = by_place(WEIGHTS, row) * line
    for field in (4, 0, 1, 2, 3):
        if field != 3:
            copies[0 if field == 4 else field + 1].wait()
        if field == 2:
            copies[4].wait()
        found = []
        for x in (0, length - 1):
            parts = []
            for e in range(count):
                ys = pl.ds(8 * e, 8)
                value = forced(field, lambda f: old[f, x, ys], step[x, ys])
                parts.append(join_depth(value * (float(WEIGHTS[x % 8]) * mass), after, before))
            found.append(join_rows(parts, low, high))
        for e in range(count):
            ys = pl.ds(8 * e, 8)
            x_near[field, ys] = jnp.where(even[0], found[1][e], found[0][e])
            x_far[field, ys] = jnp.where(even[0], found[0][e], found[1][e])
        found = []
        for y in (0, width - 1):
            parts = []
            for ex in range(columns):
                rows, ys = pl.ds(8 * ex, 8), pl.ds(y // 8 * 8, 8)
                value = forced(field, lambda f: old[f, rows, ys][:, y % 8], step[rows, ys][:, y % 8])
                parts.append(join_depth(value * (float(WEIGHTS[y % 8]) * mass), after, before))
            found.append(join_rows(parts, low, high))
        for ex in range(columns):
            rows = pl.ds(8 * ex, 8)
            y_near[field, rows] = jnp.where(even[1], found[1][ex], found[0][ex])
            y_far[field, rows] = jnp.where(even[1], found[0][ex], found[1][ex])


def load_local(old, step, out):
    columns, count, depth = out.shape[1] // 8, out.shape[2] // 8, out.shape[3]
    edges = row_marks()
    row = lax.broadcasted_iota(jnp.int32, (8, depth), 0)
    line, after, before = depth_marks(depth)
    plane = by_place(WEIGHTS, row) * line
    mass = jnp.stack([float(w) * plane for w in WEIGHTS])
    for field in range(5):
        state = [None] * count
        for ex in range(columns):
            rows = pl.ds(8 * ex, 8)
            parts = []
            for e in range(count):
                ys = pl.ds(8 * e, 8)
                value = forced(field, lambda f: old[f, rows, ys], step[rows, ys])
                parts.append(join_depth(value * mass, after, before))
            parts = join_y(parts, edges[0], edges[1])
            for e in range(count):
                ys = pl.ds(8 * e, 8)
                out[field, rows, ys] = parts[e]
                if ex:
                    out[field, 8 * ex, ys] += state[e]
                    out[field, 8 * ex - 1, ys] += parts[e][0]
                state[e] = parts[e][7]


def stiff_terms(ex, tiles, stiff_y, z_sums):
    x_rows = [along_x(split_rows(t), STIFF) for t in tiles]
    y_parts = [along_y(t, stiff_y) for t in tiles]
    z_parts = [z_sums[pl.ds(8 * ex, 8), pl.ds(8 * e, 8)] for e in range(len(tiles))]
    return x_rows, y_parts, z_parts


def square_sum(rows):
    total = 0.0
    for sign in (1.0, -1.0):
        form = 0.5 * (STIFF[:4, :4] + sign * STIFF[:4, :3:-1])
        part = [rows[i] + rows[7 - i] if sign > 0 else rows[i] - rows[7 - i] for i in range(4)]
        for i in range(4):
            pivot = form[i, i]
            if pivot < 1e-12:
                continue
            line = form[i] / np.sqrt(pivot)
            value = sum(float(line[b]) * part[b] for b in range(i, 4))
            total = total + value * value
            form = form - np.outer(line, line)
    return total


def join_x(c, out, x_far, x_near, even, even_row, ends, weight, mask, faces, slopes, slope_ends):
    columns, count = out.shape[0] // 8, out.shape[1] // 8
    for xi, side in enumerate((before_of, after_of)):
        row = (8 * columns - 1) * xi
        mended = [[0.0, 0.0], [0.0, 0.0]]
        for e in range(count):
            ys = pl.ds(8 * e, 8)
            change = side(even[0], x_near[c, ys], x_far[c, ys]) * weight * mask(row, ys)
            out[row, ys] += change
            for kind, (low, high) in enumerate((ends[1], slope_ends[1])):
                if e == 0:
                    mended[kind][0] = jnp.sum(change * low, axis=0, keepdims=True)
                if e == count - 1:
                    mended[kind][1] = jnp.sum(change * high, axis=0, keepdims=True)
        for kind, where in enumerate((faces, slopes if c == 1 else None)):
            if where is not None:
                low, high = mended[kind]
                where[2][row : row + 1] += jnp.where(even_row[1], high, low)
                where[3][row : row + 1] += jnp.where(even_row[1], low, high)
    for ex in sorted({0, columns - 1}):
        for e in range(count):
            tile = out[pl.ds(8 * ex, 8), pl.ds(8 * e, 8)]
            if faces is not None:
                store_faces(ex, e, columns, count, tile, even, ends, faces, True, False)
            if slopes is not None and c == 0:
                store_faces(ex, e, columns, count, tile, even, slope_ends, slopes, True, False)


def y_faces(c, ex, e, columns, count, tile, even, ends, slope_ends, y_near, y_far):
    store_faces(ex, e, columns, count, tile, even, ends, (None, None, y_near.at[c], y_far.at[c]), False, True)
    if c == 1:
        slopes = (None, None, y_near.at[4], y_far.at[4])
        store_faces(ex, e, columns, count, tile, even, slope_ends, slopes, False, True)


def first_y(local, boundary, y_far, y_near, even_ref, part, y_near_out, y_far_out):
    columns, count = part.shape[1] // 8, part.shape[2] // 8
    even, edges = parity(even_ref), row_marks()
    ends, slope_ends = end_rows(STIFF), end_rows(SLOPE)
    for c in range(4):
        for ex in range(columns):
            for e in range(count):
                rows, ys = pl.ds(8 * ex, 8), pl.ds(8 * e, 8)
                tile = with_faces(local[c, rows, ys], ex, e, columns, count, (None, None, y_far.at[c], y_near.at[c]),
                                  even, edges, x=False)
                tile = tile * boundary[rows, ys].astype(jnp.float32)
                part[c, rows, ys] = tile
                y_faces(c, ex, e, columns, count, tile, even, ends, slope_ends, y_near_out, y_far_out)


def first_x(part, y_near_in, y_far_in, boundary, x_far, x_near, even_ref, right, near, far, x_near_out, x_far_out):
    del part, y_near_in, y_far_in
    columns, count = right.shape[1] // 8, right.shape[2] // 8
    even, even_row = parity(even_ref), even_rows(even_ref)
    ends, slope_ends = end_rows(STIFF), end_rows(SLOPE)
    faces = (x_near_out, x_far_out, near, far)
    for c in range(4):
        join_x(c, right.at[c], x_far, x_near, even, even_row, ends, 1.0,
               lambda row, ys: boundary[row, ys].astype(jnp.float32),
               [f.at[c] for f in faces], [f.at[4] for f in faces], slope_ends)
    near[5] = jnp.zeros(near.shape[1:], jnp.float32)
    far[5] = jnp.zeros(far.shape[1:], jnp.float32)
    for xi, side in enumerate((before_of, after_of)):
        for field in range(5):
            low, high = [
                side(even_row[0], x_near[field, y : y + 1], x_far[field, y : y + 1]) for y in (0, 8 * count - 1)
            ]
            row = 8 * xi + field
            near[5, row : row + 1] = jnp.where(even_row[1], high, low)
            far[5, row : row + 1] = jnp.where(even_row[1], low, high)


def pick(c, values):
    out = jnp.float32(values[0])
    for i in range(1, 4):
        out = jnp.where(c == i, jnp.float32(values[i]), out)
    return out


def start_sums(scales, rates, local, boundary, x_far, x_near, y_far, y_near, even_ref, right, summed, share, tall_y,
               short_y, wide_z, rest_z, reaction, free, ahead):
    columns, count = ahead.shape[1] // 8, ahead.shape[2] // 8
    even, edges = parity(even_ref), row_marks()
    received = [r.at[4] for r in (x_far, x_near, y_far, y_near)]
    for ex in range(columns):
        for e in range(count):
            rows, ys = pl.ds(8 * ex, 8), pl.ds(8 * e, 8)
            reaction[rows, ys] = with_faces(local[4, rows, ys], ex, e, columns, count, received, even, edges)
            free[rows, ys] = boundary[rows, ys].astype(jnp.float32)
    basis_fill(scales, rates, right, None, reaction, free, summed, share, (tall_y, short_y), (wide_z, rest_z), ahead)


def basis_sums(scales, rates, newest, older, reaction, free, summed, share, tall_y, short_y, wide_z, rest_z, ahead, *dots):
    left, matrix = (tall_y, short_y), (wide_z, rest_z)
    basis_fill(scales, rates, newest, older, reaction, free, summed, share, left, matrix, ahead, *dots)


def basis_fill(scales, rates, newest, older, reaction, free, summed, share, left, matrix, ahead, dots=None, first=None):
    columns, count = ahead.shape[1] // 8, ahead.shape[2] // 8
    double = 1.0 if older is None else 2.0

    def component(c, carry):
        scale, rate = pick(c, [double * v for v in scales]), pick(c, [double * v for v in rates])
        same = jnp.zeros((8, 128), jnp.float32)
        cross = jnp.zeros((8, 128), jnp.float32)
        start = jnp.zeros((8, 128), jnp.float32)
        state = None
        for ex in range(columns):
            rows = pl.ds(8 * ex, 8)
            tiles = []
            for e in range(count):
                ys = pl.ds(8 * e, 8)
                tile = newest[c, rows, ys]
                if older is not None:
                    weighted = tile * share[...]
                    same = same + jnp.sum(weighted * tile, axis=0)
                    cross = cross + jnp.sum(weighted * older[c, rows, ys], axis=0)
                if first is not None:
                    start = start + jnp.sum(older[c, rows, ys] * older[c, rows, ys] * share[...], axis=0)
                tiles.append(tile)
            x_rows = [along_x(split_rows(t), STIFF) for t in tiles]
            y_all, z_all = along_both(newest[c, rows], matrix, left)
            following = [r[7] for r in x_rows]
            for e in range(count):
                ys = pl.ds(8 * e, 8)
                if ex:
                    x_rows[e][0] = x_rows[e][0] + state[e]
                if ex < columns - 1:
                    first_row = sum(float(STIFF[0, i]) * newest[c, 8 * ex + 8 + i, ys] for i in range(8))
                    x_rows[e][7] = x_rows[e][7] + first_row
                part = jnp.stack(x_rows[e]) * summed[0, 0]
                part = part + y_all[:, 8 * e : 8 * e + 8] * summed[1] + z_all[:, 8 * e : 8 * e + 8] * summed[2]
                value = scale * part + (rate * reaction[rows, ys] - double) * tiles[e]
                value = value * free[rows, ys]
                ahead[c, rows, ys] = value if older is None else value - older[c, rows, ys]
            state = following
        if older is not None:
            dots[pl.ds(c, 1)] = jnp.sum(same, axis=0, keepdims=True)
            dots[pl.ds(c + 4, 1)] = jnp.sum(cross, axis=0, keepdims=True)
        if first is not None:
            first[pl.ds(c, 1)] = jnp.sum(start, axis=0, keepdims=True)
            first[pl.ds(c + 4, 1)] = jnp.zeros((1, 128), jnp.float32)
        return carry

    lax.fori_loop(0, 4, component, 0)


def y_field(c, ex, e, ahead, free, y_far, y_near, scale, summed, edges, even, columns, count):
    rows, ys = pl.ds(8 * ex, 8), pl.ds(8 * e, 8)
    return with_faces(ahead[c, rows, ys], ex, e, columns, count, (None, None, y_far.at[c], y_near.at[c]), even, edges,
                      None, summed[1], scale * free[rows, ys], x=False)


def grow_y(scales, ahead, free, y_far, y_near, even_ref, summed, part, y_near_out, y_far_out):
    columns, count = part.shape[1] // 8, part.shape[2] // 8
    even, edges = parity(even_ref), row_marks()
    ends, slope_ends = end_rows(STIFF), end_rows(SLOPE)
    for c in range(4):
        for ex in range(columns):
            for e in range(count):
                tile = y_field(c, ex, e, ahead, free, y_far, y_near, scales[c], summed, edges, even, columns, count)
                part[c, pl.ds(8 * ex, 8), pl.ds(8 * e, 8)] = tile
                y_faces(c, ex, e, columns, count, tile, even, ends, slope_ends, y_near_out, y_far_out)


def grow_x(scales, part, y_near_in, y_far_in, free, x_far, x_near, even_ref, summed, out, y_near_out, y_far_out,
           x_near_out, x_far_out):
    del part, y_near_in, y_far_in
    even, even_row = parity(even_ref), even_rows(even_ref)
    ends, slope_ends = end_rows(STIFF), end_rows(SLOPE)
    faces = (x_near_out, x_far_out, y_near_out, y_far_out)
    for c in range(4):
        join_x(c, out.at[c], x_far, x_near, even, even_row, ends, scales[c] * summed[0, 0],
               lambda row, ys: free[row, ys], [f.at[c] for f in faces], [f.at[4] for f in faces], slope_ends)


def second_y(scales, rates, ahead, free, x_far0, x_near0, y_far0, y_near0, y_far, y_near, even_ref, summed, wide_z,
             rest_z, right_in, reaction_in, out, right, reaction, y_near_out, y_far_out, lines, depth_lines):
    columns, count = out.shape[1] // 8, out.shape[2] // 8
    even, edges, even_row = parity(even_ref), row_marks(), even_rows(even_ref)
    ends, slope_ends = end_rows(STIFF), end_rows(SLOPE)
    end_x, end_y = (0, 8 * columns - 1), (0, 8 * count - 1)
    sides = (before_of, after_of)
    corners = [(xi, yi) for xi in (0, 1) for yi in (0, 1)]

    def at(array, xi, yi):
        return array[end_x[xi], end_y[yi] : end_y[yi] + 1]

    def diagonal(field, xi, yi):
        row = 8 * xi + field
        return sides[yi](even_row[1], y_near[5, row : row + 1], y_far[5, row : row + 1])

    def beside(field, xi, yi):
        row = end_y[yi]
        return sides[xi](even_row[0], x_near0[field, row : row + 1], x_far0[field, row : row + 1])

    def beyond(field, xi, yi):
        row = end_x[xi]
        return sides[yi](even_row[1], y_near0[field, row : row + 1], y_far0[field, row : row + 1])

    for c in range(4):
        for n, (xi, yi) in enumerate(corners):
            lines[4 * c + n : 4 * c + n + 1] = diagonal(c, xi, yi) * at(free, xi, yi)
    depth_lines[...] = along_z(lines[...], (wide_z, rest_z))

    def missed(c, ex, e):
        found = []
        for n, (xi, yi) in enumerate(corners):
            cx, ce, sx, sy = (columns - 1) * xi, (count - 1) * yi, 7 * xi, 7 * yi
            line = lines[4 * c + n : 4 * c + n + 1]
            weight_x, weight_y = summed[0, 0, sy : sy + 1], summed[1, sx, 0:1]
            along = scales[c] * line * weight_x
            across = scales[c] * line * weight_y
            if ex == cx and e == ce:
                for i in range(8):
                    found.append((i, float(STIFF[i, sx]) * along * edges[yi]))
                found.append((sx, across * ends[1][yi]))
                side = beyond(c, xi, yi) * weight_x + beside(c, xi, yi) * weight_y
                side = float(STIFF[0, 0]) * side
                depth = depth_lines[4 * c + n : 4 * c + n + 1] * summed[2, sx, sy : sy + 1]
                gained = diagonal(4, xi, yi)
                node = scales[c] * (side + depth)
                node = node + (rates[c] * (at(reaction_in, xi, yi) + gained) - 1.0) * line
                node = node + rates[c] * gained * at(right_in.at[c], xi, yi)
                found.append((sx, node * edges[yi]))
            elif e == ce and ex == cx + 1 - 2 * xi:
                found.append((sx, float(STIFF[7 - sx, sx]) * along * edges[yi]))
            elif ex == cx and e == ce + 1 - 2 * yi:
                found.append((sx, float(STIFF[7 - sy, sy]) * across * edges[yi]))
        return found

    for c in range(4):
        for ex in range(columns):
            for e in range(count):
                rows, ys = pl.ds(8 * ex, 8), pl.ds(8 * e, 8)
                tile = y_field(c, ex, e, ahead, free, y_far, y_near, scales[c], summed, edges, even, columns, count)
                found = missed(c, ex, e)
                if found:
                    parts = []
                    for i in range(8):
                        extra = [t for row, t in found if row == i]
                        parts.append(tile[i] + sum(extra) * free[8 * ex + i, ys] if extra else tile[i])
                    tile = jnp.stack(parts)
                out[c, rows, ys] = tile
                y_faces(c, ex, e, columns, count, tile, even, ends, slope_ends, y_near_out, y_far_out)

    for n, (xi, yi) in enumerate(corners):
        x, y = end_x[xi], end_y[yi]
        reaction[x, y : y + 1] = at(reaction_in, xi, yi) + diagonal(4, xi, yi)
        for c in range(4):
            right[c, x, y : y + 1] = at(right_in.at[c], xi, yi) + lines[4 * c + n : 4 * c + n + 1]


def mend_slopes(x_far0, x_near0, y_far0, y_near0, x_far, x_near, y_far, y_near, free, even_ref,
                sx_far, sx_near, sy_far, sy_near):
    even_row = even_rows(even_ref)
    end_x, end_y = (0, free.shape[0] - 1), (0, free.shape[1] - 1)
    sides = (before_of, after_of)

    def at(array, xi, yi):
        return array[end_x[xi], end_y[yi] : end_y[yi] + 1]

    def beside(field, xi, yi):
        row = end_y[yi]
        return sides[xi](even_row[0], x_near0[field, row : row + 1], x_far0[field, row : row + 1])

    def beyond(field, xi, yi):
        row = end_x[xi]
        return sides[yi](even_row[1], y_near0[field, row : row + 1], y_far0[field, row : row + 1])

    sx_far[...], sx_near[...], sy_far[...], sy_near[...] = x_far[4], x_near[4], y_far[4], y_near[4]
    low, high = float(SLOPE[7, 7]), float(SLOPE[0, 0])
    for i in (0, 1):
        y, x = end_y[i], end_x[i]
        before = low * beyond(0, 0, i) * at(free, 0, i)
        after = high * beyond(0, 1, i) * at(free, 1, i)
        sx_near[y : y + 1] += jnp.where(even_row[0], after, before)
        sx_far[y : y + 1] += jnp.where(even_row[0], before, after)
        before = low * beside(1, i, 0) * at(free, i, 0)
        after = high * beside(1, i, 1) * at(free, i, 1)
        sy_near[x : x + 1] += jnp.where(even_row[1], after, before)
        sy_far[x : x + 1] += jnp.where(even_row[1], before, after)


def column_products(c, ex, out, newest, reaction, share, left, matrix, local, scale, rate):
    count = out.shape[2] // 8
    rows = pl.ds(8 * ex, 8)
    same = jnp.zeros((8, 128), jnp.float32)
    cross = jnp.zeros((8, 128), jnp.float32)
    work = jnp.zeros((8, 128), jnp.float32)
    y_sums, z_sums = along_both(out[c, rows], matrix, left)
    for e in range(count):
        ys = pl.ds(8 * e, 8)
        tile = out[c, rows, ys]
        weighted = tile * share[...]
        same = same + jnp.sum(weighted * tile, axis=0)
        cross = cross + jnp.sum(weighted * newest[c, rows, ys], axis=0)
        extra = (rate * reaction[rows, ys] - 1.0) * tile
        work = work + jnp.sum(weighted * extra, axis=0)
        work = work + scale * (square_sum(split_rows(tile)) * local[0, 0])
        term = y_sums[:, 8 * e : 8 * e + 8] * local[1] + z_sums[:, 8 * e : 8 * e + 8] * local[2]
        work = work + scale * jnp.sum(term * tile, axis=0)
    return same, cross, work


def last_y(scales, rates, ahead, newest, reaction, free, y_far, y_near, even_ref, summed, share, tall_y, short_y, wide_z,
           rest_z, local, part, sy_near, sy_far, products):
    columns, count = part.shape[1] // 8, part.shape[2] // 8
    even, edges = parity(even_ref), row_marks()
    slope_ends = end_rows(SLOPE)
    for c in range(4):
        total = [jnp.zeros((8, 128), jnp.float32)] * 3
        for ex in range(columns):
            for e in range(count):
                tile = y_field(c, ex, e, ahead, free, y_far, y_near, 2.0 * scales[c], summed, edges, even, columns, count)
                part[c, pl.ds(8 * ex, 8), pl.ds(8 * e, 8)] = tile
                if c == 1:
                    store_faces(ex, e, columns, count, tile, even, slope_ends, (None, None, sy_near, sy_far), False, True)
            if 0 < ex < columns - 1:
                found = column_products(c, ex, part, newest, reaction, share, (tall_y, short_y), (wide_z, rest_z), local,
                                        scales[c], rates[c])
                total = [a + b for a, b in zip(total, found)]
        for n in range(3):
            products[c, n] = total[n]


def last_x(scales, rates, part, sy_near_in, sy_far_in, products, newest, reaction, free, x_far, x_near, even_ref, summed,
           share, tall_y, short_y, wide_z, rest_z, local, d0, d1, d2, d3, d4, out, sy_near, sy_far, sums, sx_near, sx_far):
    del part, sy_near_in, sy_far_in
    dots = (d0, d1, d2, d3, d4)
    columns = out.shape[1] // 8
    even, even_row = parity(even_ref), even_rows(even_ref)
    ends, slope_ends = end_rows(STIFF), end_rows(SLOPE)
    for i in range(1, ITERS - 1):
        sums[i] = dots[i][...]
    for c in range(4):
        join_x(c, out.at[c], x_far, x_near, even, even_row, ends, 2.0 * scales[c] * summed[0, 0],
               lambda row, ys: free[row, ys], None, (sx_near, sx_far, sy_near, sy_far), slope_ends)
        total = [products[c, n] for n in range(3)]
        for ex in sorted({0, columns - 1}):
            found = column_products(c, ex, out, newest, reaction, share, (tall_y, short_y), (wide_z, rest_z), local,
                                    scales[c], rates[c])
            total = [a + b for a, b in zip(total, found)]
        same, cross, work = [jnp.sum(t, axis=0, keepdims=True) for t in total]
        sums[ITERS - 1, c : c + 1] = same
        sums[ITERS - 1, c + 4 : c + 5] = cross
        sums[0, c : c + 1] = dots[0][c : c + 1]
        sums[0, c + 4 : c + 5] = work


def slope_sums(*refs):
    fields, (summed, slope_y, wide_z, rest_z), outs = refs[:3], refs[3:7], refs[7:]
    columns, count = outs[0].shape[1] // 8, outs[0].shape[2] // 8
    edges = row_marks()
    for field, out in zip(fields, outs):
        fill_z(out.at[2], field.at[2], (wide_z, rest_z))
        state = None
        for ex in range(columns):
            rows, ends = pl.ds(8 * ex, 8), []
            y_parts = [along_y(field[1, rows, pl.ds(8 * e, 8)], slope_y) for e in range(count)]
            y_parts = join_y(y_parts, edges[0], edges[1])
            for e in range(count):
                ys = pl.ds(8 * e, 8)
                out[1, rows, ys] = y_parts[e] * summed[1]
                out[2, rows, ys] = out[2, rows, ys] * summed[2]
                x_rows = [r * summed[0, 0] for r in along_x(split_rows(field[0, rows, ys]), SLOPE)]
                out[0, rows, ys] = jnp.stack(x_rows)
                if ex:
                    out[0, 8 * ex, ys] += state[e]
                    out[0, 8 * ex - 1, ys] += x_rows[0]
                ends.append(x_rows[7])
            state = ends


def first_update(halves, gain, *refs):
    sums, *sloped = refs[: ITERS + 1]
    refs = refs[ITERS + 1 :]
    slopes = [refs[:4]]
    slopes += [[r.at[4] for r in refs[4 * k : 4 * k + 4]] for k in range(1, ITERS - 1)]
    refs = refs[4 * ITERS - 4 :]
    slopes.append(refs[:4])
    even_ref, free, summed, inverse = refs[4:8]
    weights, remainder, update, *faces = refs[8:15]
    joined = refs[15:]
    columns, count = update.shape[0] // 8, update.shape[1] // 8
    even, edges = parity(even_ref), row_marks()
    ends = end_rows(STIFF)
    total = [jnp.broadcast_to(jnp.sum(sums[i], axis=1, keepdims=True), (8, 128)) for i in range(ITERS)]
    other = [pltpu.roll(t, 4, axis=0) for t in total]
    row = lax.broadcasted_iota(jnp.int32, (8, 128), 0)
    half = jnp.full((8, 128), halves[0], jnp.float32)
    for i in range(1, 4):
        half = jnp.where(row == i, halves[i], half)
    moments = [total[0], other[1]]
    for level in range(2, 2 * ITERS - 1):
        inner = total[level // 2] if level % 2 == 0 else other[level // 2 + 1]
        moments.append(2.0 * inner - moments[level % 2])
    top = 2.0 * other[0] - other[5]
    moments.append(2.0 * top - moments[1])
    for i, value in enumerate(conjugate_coefficients(moments, half, half)):
        weights[i] = value
    for n in range(4):
        c = n // 2
        joined[n][...] = sum(slopes[i][n][...] * weights[i, c : c + 1] for i in range(ITERS))
    factor = [[weights[i, c : c + 1][None] for c in range(3)] for i in range(ITERS)]
    for ex in range(columns):
        for e in range(count):
            rows, ys = pl.ds(8 * ex, 8), pl.ds(8 * e, 8)
            tile = sum(sloped[i][c, rows, ys] * factor[i][c] for i in range(ITERS) for c in range(3))
            tile = with_faces(tile, ex, e, columns, count, joined, even, edges, summed[0, 0], summed[1])
            left = -tile * free[rows, ys]
            change = gain * inverse[...] * left
            remainder[rows, ys] = left
            update[rows, ys] = change
            store_faces(ex, e, columns, count, change, even, ends, faces)


def combine_fields(weights, *refs):
    *basis, fields, done = refs
    done[...] = weights[0]

    def combine(c, carry):
        factor = [weights[i, pl.ds(c, 1)] for i in range(ITERS)]
        for x in range(0, fields.shape[1], 8):
            rows = pl.ds(x, 8)
            value = basis[0][c, rows] * factor[0][None]
            for i in range(1, ITERS):
                value = value + basis[i][c, rows] * factor[i][None]
            fields[c, rows] = value
        return carry

    lax.fori_loop(0, 4, combine, 0)


def add_loads(count, *refs):
    *loads, rider, tick, out = refs
    del tick
    values = [load[:count] for load in loads]
    total = values[0] + values[1]
    if len(values) == 4:
        total = total + (values[2] + values[3])
    out[:count] = total
    out[count:] = rider[...]


def pressure_sums(update, tick, summed, shift, stiff_y, wide_z, rest_z, raw, z_sums):
    del tick
    columns, count = raw.shape[0] // 8, raw.shape[1] // 8
    edges = row_marks()
    state = None
    fill_z(z_sums, update, (wide_z, rest_z))
    for ex in range(columns):
        rows = pl.ds(8 * ex, 8)
        tiles = [update[rows, pl.ds(8 * e, 8)] for e in range(count)]
        x_rows, y_parts, z_parts = stiff_terms(ex, tiles, stiff_y, z_sums)
        state = emit_column(ex, x_rows, y_parts, z_parts, summed, edges, raw, state,
                            lambda e, part: part + shift[...] * tiles[e])


def pressure_part(ex, e, columns, count, keep, gain, raw, free, y_far, y_near, even, edges, summed, inverse, remainder,
                  update):
    rows, ys = pl.ds(8 * ex, 8), pl.ds(8 * e, 8)
    tile = with_faces(raw[rows, ys], ex, e, columns, count, (None, None, y_far, y_near), even, edges,
                      None, summed[1], x=False)
    left = remainder[rows, ys] - tile * free[rows, ys]
    return left, gain * inverse[...] * left + keep * update[rows, ys]


def pressure_y(keep, gain, raw, free, y_far, y_near, even_ref, summed, inverse, remainder_in, update_in, pressure_in,
               pressure, remainder, update, y_near_out, y_far_out):
    columns, count = raw.shape[0] // 8, raw.shape[1] // 8
    even, edges, ends = parity(even_ref), row_marks(), end_rows(STIFF)
    for ex in range(columns):
        for e in range(count):
            rows, ys = pl.ds(8 * ex, 8), pl.ds(8 * e, 8)
            left, change = pressure_part(ex, e, columns, count, keep, gain, raw, free, y_far, y_near, even, edges, summed,
                                         inverse, remainder_in, update_in)
            pressure[rows, ys] = pressure_in[rows, ys] + change
            remainder[rows, ys] = left
            update[rows, ys] = change
            store_faces(ex, e, columns, count, change, even, ends, (None, None, y_near_out, y_far_out), False, True)


def end_change(xi, e, gain, free_row, x_far, x_near, even, summed, inverse):
    side, ys = (before_of, after_of)[xi], pl.ds(8 * e, 8)
    face = side(even[0], x_near[ys], x_far[ys]) * summed[0, 0] * free_row[ys]
    return -face, -gain * inverse[7 * xi] * face


def pressure_x(gain, pressure_in, remainder_in, update_in, y_near_in, y_far_in, free, x_far, x_near, even_ref, summed,
               inverse, pressure, remainder, update, y_near, y_far, x_near_out, x_far_out):
    del pressure_in, remainder_in, update_in, y_near_in, y_far_in
    columns, count = update.shape[0] // 8, update.shape[1] // 8
    even, even_row, ends = parity(even_ref), even_rows(even_ref), end_rows(STIFF)
    for xi in (0, 1):
        row = (8 * columns - 1) * xi
        low = high = 0.0
        for e in range(count):
            ys = pl.ds(8 * e, 8)
            left, change = end_change(xi, e, gain, free.at[row], x_far, x_near, even, summed, inverse)
            remainder[row, ys] += left
            update[row, ys] += change
            pressure[row, ys] += change
            if e == 0:
                low = jnp.sum(change * ends[1][0], axis=0, keepdims=True)
            if e == count - 1:
                high = jnp.sum(change * ends[1][1], axis=0, keepdims=True)
        y_near[row : row + 1] += jnp.where(even_row[1], high, low)
        y_far[row : row + 1] += jnp.where(even_row[1], low, high)
    for ex in sorted({0, columns - 1}):
        for e in range(count):
            tile = update[pl.ds(8 * ex, 8), pl.ds(8 * e, 8)]
            store_faces(ex, e, columns, count, tile, even, ends, (x_near_out, x_far_out, None, None), True, False)


def last_pressure_y(keep, gain, raw, free, y_far, y_near, even_ref, summed, inverse, remainder, update, pressure_in,
                    far, end_part, pressure, gone):
    length = raw.shape[0]
    columns, count = length // 8, raw.shape[1] // 8
    even, edges = parity(even_ref), row_marks()
    for ex in range(columns):
        for e in range(count):
            rows, ys = pl.ds(8 * ex, 8), pl.ds(8 * e, 8)
            _, change = pressure_part(ex, e, columns, count, keep, gain, raw, free, y_far, y_near, even, edges, summed,
                                      inverse, remainder, update)
            pressure[rows, ys] = pressure_in[rows, ys] + change
    inner = pl.ds(1, length - 2)
    copy = pltpu.make_async_copy(pressure.at[inner], far.at[inner], gone.at[0])
    copy.start()
    end_part[0] = pressure[0]
    end_part[1] = pressure[length - 1]
    copy.wait()


def last_pressure_x(gain, far_in, end_part, free, x_far, x_near, even_ref, summed, inverse, far, rows, gone):
    del far_in
    last = free.shape[0] - 1
    even, copies = parity(even_ref), []
    for xi in (0, 1):
        for e in range(free.shape[1] // 8):
            ys = pl.ds(8 * e, 8)
            _, change = end_change(xi, e, gain, free.at[last * xi], x_far, x_near, even, summed, inverse)
            rows[xi, ys] = end_part[xi, ys] + change
        copies.append(pltpu.make_async_copy(rows.at[xi], far.at[last * xi], gone.at[xi]))
        copies[-1].start()
    for copy in copies:
        copy.wait()


VMEM_BYTES = 24 * 1024 * 1024


def call(kernel, name, outs, *args, scratch=(), cost=None, far_in=0, far_out=0, copies=0, aliases=()):
    held, far = pl.BlockSpec(memory_space=pltpu.VMEM), pl.BlockSpec(memory_space=pltpu.HBM)
    scratch_shapes = [pltpu.VMEM(s, jnp.float32) for s in scratch]
    if copies:
        scratch_shapes.append(pltpu.SemaphoreType.DMA((copies,)))
    return pl.pallas_call(
        kernel,
        name=name,
        out_shape=[jax.ShapeDtypeStruct(s, jnp.float32) for s in outs],
        in_specs=[far] * far_in + [held] * (len(args) - far_in),
        out_specs=[far] * far_out + [held] * (len(outs) - far_out),
        scratch_shapes=scratch_shapes,
        cost_estimate=cost,
        input_output_aliases=dict(aliases),
        compiler_params=pltpu.CompilerParams(vmem_limit_bytes=VMEM_BYTES),
    )(*[pltpu.with_memory_space_constraint(a, pltpu.HBM) for a in args[:far_in]], *args[far_in:])


def busy(bytes_accessed):
    return pl.CostEstimate(flops=0, bytes_accessed=bytes_accessed, transcendentals=0)


def swap_near(axis, face):
    return lax.ppermute(face, axis, [(i, i ^ 1) for i in range(lax.axis_size(axis))])


def swap_far(axis, face):
    size = lax.axis_size(axis)
    return lax.ppermute(face, axis, [(i, far_partner(i, size)) for i in range(size)])


def swap_all(x_near, x_far, y_near, y_far):
    y_far = swap_far("gy", y_far)
    x_far = swap_far("gx", x_far)
    x_near = swap_near("gx", x_near)
    y_near = swap_near("gy", y_near)
    return x_far, x_near, y_far, y_near


def far_partner(i, size):
    return (i + 1 if i % 2 else i - 1) % size


def partner_loads(load, axis, partners, riders, count):
    size, heard, faces = lax.axis_size(axis), [], []
    for n, (partner, rider) in enumerate(zip(partners, riders)):
        mine = load
        if n:
            mine = load[:count] if rider is None else jnp.concatenate([load[:count], rider])
        mine = lax.ppermute(mine, axis, [(i, partner(i)) for i in range(size)])
        heard.append(mine)
        if rider is not None:
            faces.append(mine[count:])
    return heard, faces


def all_sum(values, axis, near, far, following, meanwhile):
    size = lax.axis_size(axis)
    count = values.shape[0] - far.shape[0] if following is None else values.shape[0]
    half = size // 2

    def to_near(i):
        return i ^ 1

    def to_far(i):
        return far_partner(i, size)

    def across(i):
        return (i + half) % size

    def far_across(i):
        return across(to_far(i))

    rounds = [((to_far,), (far,))]
    if size == 4:
        rounds = [((to_far, to_near, across), (far, near, None))]
    elif size > 4:
        rounds = [((to_far, across, far_across), (far, None, None)), ((to_near,), (near,))]
        bit = 4
        while bit < half:
            rounds.append(((lambda i, bit=bit: i ^ bit,), (None,)))
            bit *= 2
    else:
        rounds.append(((), (near,)))
    faces = []
    load = values if following is None else jnp.concatenate([values, far])
    for n, (partners, riders) in enumerate(rounds):
        if not partners:
            faces.append(lax.ppermute(near, axis, [(i, to_near(i)) for i in range(size)]))
            continue
        heard, got = partner_loads(load, axis, partners, riders, count)
        faces += got
        rider = rounds[n + 1][1][0] if n + 1 < len(rounds) and rounds[n + 1][0] else following
        tail = jnp.zeros((8, values.shape[1]), jnp.float32) if rider is None else rider
        (load,) = call(
            functools.partial(add_loads, count), "add_loads", [(count + tail.shape[0], values.shape[1])],
            load, *heard, tail, meanwhile(),
        )
    if following is None:
        load = load[:count]
    return load, faces[1], faces[0]


def conjugate_coefficients(moments, centre, half):
    remaining, towards = list(moments), list(moments)
    one, zero = jnp.ones_like(moments[0]), jnp.zeros_like(moments[0])
    direction = [one] + [zero] * ITERS
    residual = list(direction)
    total = [zero] * ITERS
    for step in range(ITERS):
        count = len(towards) - 1
        image = []
        for level in range(count):
            side = (
                half * towards[1] if level == 0 else 0.5 * half * (towards[level + 1] + towards[level - 1])
            )
            image.append(centre * towards[level] + side)
        alpha = remaining[step] / image[step]
        total = [total[i] + alpha * direction[i] for i in range(ITERS)]
        if step == ITERS - 1:
            break
        applied = []
        for i in range(ITERS + 1):
            term = centre * direction[i]
            if i >= 1:
                term = term + (half if i == 1 else 0.5 * half) * direction[i - 1]
            if i < ITERS:
                term = term + 0.5 * half * direction[i + 1]
            applied.append(term)
        residual = [residual[i] - alpha * applied[i] for i in range(ITERS + 1)]
        following = [remaining[i] - alpha * image[i] for i in range(count)]
        beta = -alpha * (half if step == 0 else 0.5 * half) * following[step + 1] / remaining[step]
        towards = [following[i] + beta * towards[i] for i in range(count)]
        direction = [residual[i] + beta * direction[i] for i in range(ITERS + 1)]
        remaining = following
    return total


def on_device(old_fields, inverse_step, boundary):
    x, y, z = inverse_step.shape
    t = Tables(y, z)
    brick, four = (x, y, z), (4, x, y, z)
    faces = [(y, z)] * 2 + [(x, z)] * 2
    faces5 = [(5,) + f for f in faces]
    faces_back = [(y, z)] * 2 + [(x, z)] * 2

    place = [lax.axis_index(a) % 2 == 0 for a in ("gx", "gy")]
    even = jnp.stack([jnp.full((8, 128), p, jnp.float32) for p in place])

    old, step, x_near, x_far, y_near, y_far = call(
        load_faces, "right_faces", [four, brick] + faces5, old_fields, inverse_step, even, far_in=2, copies=5,
    )
    received = swap_all(x_near, x_far, y_near, y_far)
    (local,) = call(load_local, "right_local", [(5,) + brick], old, step, cost=busy(2 << 20))

    top = INTERVAL_SHARE * np.array([spectrum_top(c) for c in DIFFUSE])
    halves = [float(v) for v in 0.5 * top]
    scales = [float(v) for v in np.array(DIFFUSE) / (0.5 * top)]
    rates = [float(v) for v in 1.0 / (0.5 * top)]

    x_far, x_near, y_far, y_near = received
    relayed = [(6, x, z)] * 2
    x_faces, y_faces5 = [(5, y, z)] * 2, [(5, x, z)] * 2
    part, near, far = call(first_y, "first_y", [four] + relayed, local, boundary, y_far, y_near, even, cost=busy(2 << 20))
    right, y_near, y_far, x_near, x_far = call(
        first_x, "first_x", [four] + relayed + x_faces, part, near, far, boundary, x_far, x_near, even,
        aliases=[(0, 0), (1, 1), (2, 2)],
    )
    heard = [swap_all(x_near, x_far, y_near, y_far)]
    reaction, free, ahead = call(
        functools.partial(start_sums, scales, rates), "right_sums", [brick, brick, four],
        local, boundary, *received, even, right, t.summed, t.share, *t.left_y, *t.stiff_z, cost=busy(8 << 20),
    )
    x_far, x_near, y_far, y_near = heard[0]
    part, right, reaction, near, far = call(
        functools.partial(second_y, scales, rates), "second_y", [four, four, brick] + y_faces5,
        ahead, free, *received, y_far, y_near, even, t.summed, *t.stiff_z, right, reaction,
        scratch=[(16, z)] * 2, aliases=[(12, 1), (13, 2)], cost=busy(3 << 20),
    )
    basis, sums = [right], []
    here = scales
    for k in range(1, ITERS - 1):
        field, y_near, y_far, x_near, x_far = call(
            functools.partial(grow_x, here), "basis_x", [four] + y_faces5 + x_faces,
            part, near, far, free, x_far, x_near, even, t.summed, aliases=[(0, 0), (1, 1), (2, 2)],
        )
        basis.append(field)
        heard.append(swap_all(x_near, x_far, y_near, y_far))
        x_far, x_near, y_far, y_near = heard[-1]
        outs = [four, (8, 128)] + ([(8, 128)] if k == 1 else [])
        ahead, *dots = call(
            functools.partial(basis_sums, scales, rates), "basis_sums", outs,
            basis[-1], basis[-2], reaction, free, t.summed, t.share, *t.left_y, *t.stiff_z, cost=busy(8 << 20),
        )
        sums += dots[::-1]
        here = [2.0 * v for v in scales]
        if k < ITERS - 2:
            part, near, far = call(
                functools.partial(grow_y, here), "basis_y", [four] + y_faces5,
                ahead, free, y_far, y_near, even, t.summed, cost=busy(2 << 20),
            )
    part, near, far, products = call(
        functools.partial(last_y, scales, rates), "last_y", [four] + [(x, z)] * 2 + [(4, 3, 8, 128)],
        ahead, basis[-1], reaction, free, y_far, y_near, even, t.summed, t.share, *t.plain_y, *t.plain_z, t.local,
        cost=busy(4 << 20),
    )
    field, y_near, y_far, sums, x_near, x_far = call(
        functools.partial(last_x, scales, rates), "last_x",
        [four] + [(x, z)] * 2 + [(ITERS, 8, 128)] + [(y, z)] * 2,
        part, near, far, products, basis[-1], reaction, free, x_far, x_near, even, t.summed, t.share,
        *t.plain_y, *t.plain_z, t.local, *sums, aliases=[(0, 0), (1, 1), (2, 2)],
    )
    basis.append(field)
    heard[0] = call(mend_slopes, "slopes", faces_back, *received, *heard[0], free, even)
    sums = sums.reshape(ITERS * 8, z)
    sloped = []

    def meanwhile():
        if len(sloped) < ITERS:
            sloped.extend(
                call(
                    slope_sums, "slope_sums", [(3,) + brick] * 3,
                    *basis[len(sloped) : len(sloped) + 3], t.summed, t.slope_y, *t.slope_z, cost=busy(6 << 20),
                )
            )
        return sloped[-1]

    sums, x_near, x_far = all_sum(sums, "gx", x_near, x_far, y_far, meanwhile)
    sums, y_near, y_far = all_sum(sums, "gy", y_near, y_far, None, meanwhile)
    while len(sloped) < ITERS:
        meanwhile()
    sums = sums.reshape(ITERS, 8, z)
    slopes = (x_far, x_near, y_far, y_near)

    centre, half = chebyshev_bounds()
    factor = centre / half
    damping = 1.0 / factor
    weights, remainder, update, *sent = call(
        functools.partial(first_update, halves, 1.0 / centre), "first_update", [(ITERS, 8, 128), brick, brick] + faces,
        sums, *sloped, *[a for h in heard for a in h], *slopes, even, free, t.summed, t.inverse, scratch=faces_back,
    )
    pressure, tick = update, even
    for step in range(1, CHEB):
        last = step == CHEB - 1
        received = swap_all(*sent)
        (raw,) = call(
            pressure_sums, "pressure_sums", [brick],
            update, tick, t.summed, t.shift, t.stiff_y, *t.stiff_z, cost=busy(2 << 20), scratch=[brick],
        )
        if step == 1:
            fields, tick = call(combine_fields, "fields", [four, (8, z)], weights, *basis, cost=busy(4 << 20))
        following = 1.0 / (2.0 * factor - damping)
        keep, gain = following * damping, 2.0 * following / half
        damping = following
        x_far, x_near, y_far, y_near = received
        args = [raw, free, y_far, y_near, even, t.summed, t.inverse, remainder, update, pressure]
        if last:
            pressure, end_part = call(
                functools.partial(last_pressure_y, keep, gain), "last_pressure_y", [brick, (2, y, z)], *args,
                scratch=[brick], far_out=1, copies=1, cost=busy(1 << 20),
            )
            (pressure,) = call(
                functools.partial(last_pressure_x, gain), "last_pressure_x", [brick],
                pressure, end_part, free, x_far, x_near, even, t.summed, t.inverse,
                scratch=[(2, y, z)], far_in=1, far_out=1, copies=2, aliases=[(0, 0)],
            )
            break
        part = call(
            functools.partial(pressure_y, keep, gain), "pressure_y", [brick] * 3 + [(x, z)] * 2, *args, cost=busy(1 << 20)
        )
        pressure, remainder, update, y_near, y_far, x_near, x_far = call(
            functools.partial(pressure_x, gain), "pressure_x", [brick] * 3 + [(x, z)] * 2 + [(y, z)] * 2,
            *part, free, x_far, x_near, even, t.summed, t.inverse, aliases=[(i, i) for i in range(5)],
        )
        sent = x_near, x_far, y_near, y_far
    return (fields, pressure)


def solution(mesh):
    return jax.shard_map(
        on_device,
        mesh=mesh,
        in_specs=(P(None, "gx", "gy", None), P("gx", "gy", None), P("gx", "gy", None)),
        out_specs=(P(None, "gx", "gy", None), P("gx", "gy", None)),
        check_vma=False,
    )
```

```python
import functools

import jax
import jax.numpy as jnp
import ml_dtypes
import numpy as np
from jax import lax
from jax.experimental import pallas as pl
from jax.experimental.pallas import tpu as pltpu
from jax.sharding import PartitionSpec as P

ITERS = 6
CHEB = 6

SIGMA_SHIFT = 0.5
DIFFUSE = (1.0, 1.0, 1.0, 1.4)
COUPLING = 1.0
STRATIFY = 1.0
SPREAD = 20.0
STEP_MAX = 64.0
INTERVAL_SHARE = 0.82
HIGHEST_PRECISION = lax.Precision.HIGHEST
LOBATTO_POINTS = (
    -1.0,
    -0.8717401485096066,
    -0.5917001814331423,
    -0.2092992179024789,
    0.2092992179024789,
    0.5917001814331423,
    0.8717401485096066,
    1.0,
)


def legendre_value(points, degree):
    previous = points * 0.0 + 1.0
    current = points
    for order in range(1, degree):
        following = ((2 * order + 1) * points * current - order * previous) / (order + 1)
        previous = current
        current = following
    return current


def quadrature_tables():
    degree = 7
    points = np.array(LOBATTO_POINTS)
    values = legendre_value(points, degree)
    weights = 2.0 / (degree * (degree + 1) * values * values)
    derive = np.zeros((degree + 1, degree + 1))
    for row_index in range(degree + 1):
        for column_index in range(degree + 1):
            if row_index != column_index:
                derive[row_index, column_index] = values[row_index] / (
                    values[column_index] * (points[row_index] - points[column_index])
                )
    derive[0, 0] = -degree * (degree + 1) / 4.0
    derive[degree, degree] = degree * (degree + 1) / 4.0
    stiffness_table = derive.T @ (weights[:, None] * derive)
    return (weights, derive, stiffness_table)


WEIGHTS, DERIVE, STIFF = quadrature_tables()
SLOPE = WEIGHTS[:, None] * DERIVE
COPIES = np.where(np.arange(8) % 7 == 0, 2.0, 1.0)


def chebyshev_bounds():
    weight_matrix = np.eye(8) * WEIGHTS

    def kron3(a, b, c):
        return np.kron(np.kron(a, b), c)

    element_matrix = (
        kron3(STIFF, weight_matrix, weight_matrix)
        + kron3(weight_matrix, STIFF, weight_matrix)
        + kron3(weight_matrix, weight_matrix, STIFF)
        + SIGMA_SHIFT * kron3(weight_matrix, weight_matrix, weight_matrix)
    )
    bounds_ratio = np.sum(np.abs(element_matrix), axis=1) / np.diagonal(element_matrix)
    upper_bound = float(np.max(bounds_ratio))
    lower_bound = upper_bound / SPREAD
    return ((upper_bound + lower_bound) / 2.0, (upper_bound - lower_bound) / 2.0)


def spectrum_top(diffuse):
    root = np.sqrt(COPIES)
    stiff = root[:, None] * STIFF * root[None, :]
    weight = np.diag(WEIGHTS * COPIES)

    def kron3(a, b, c):
        return np.kron(np.kron(a, b), c)

    element = diffuse * (
        kron3(stiff, weight, weight) + kron3(weight, stiff, weight) + kron3(weight, weight, stiff)
    ) + STEP_MAX * kron3(weight, weight, weight)
    return float(np.linalg.eigvalsh(element)[-1])


def line_sums(table, length):
    matrix = np.kron(np.eye(length // 8), table)
    total = matrix.copy()
    for start in range(8, length, 8):
        total[start] += matrix[start - 1]
        total[start - 1] += matrix[start]
    return total


def depth_line(vector, length):
    line = np.tile(vector * COPIES, length // 8)
    line[0] = vector[0]
    line[-1] = vector[-1]
    return line


def f32(array):
    return np.ascontiguousarray(array, np.float32)


def rolled_rows(table):
    out = np.zeros((8, 8, 128))
    for shift in range(8):
        for row in range(8):
            out[shift, row] = table[row, (row - shift) % 8]
    return out


def block(a, b, c):
    return a[:, None, None] * b[:, None] * c


def parts_of(matrix):
    rest, parts = f32(matrix), []
    for _ in range(3):
        parts.append(rest.astype(ml_dtypes.bfloat16))
        rest = rest - parts[-1].astype(np.float32)
    hi, mid, lo = parts
    return np.block([[hi, mid], [hi, mid]]), np.concatenate([hi, lo])


def left_parts(table):
    rest, parts = f32(np.kron(np.eye(8), table)), []
    for _ in range(3):
        parts.append(rest.astype(ml_dtypes.bfloat16))
        rest = rest - parts[-1].astype(np.float32)
    hi, mid, lo = parts
    return np.block([[hi, hi], [mid, mid]]), np.concatenate([hi, lo], axis=1)


class Tables:
    def __init__(self, width, depth):
        self.left_y = left_parts(line_sums(STIFF, width))
        self.plain_y = left_parts(np.kron(np.eye(width // 8), STIFF))
        ones8, ones = np.ones(8), np.ones(depth)
        wide = WEIGHTS * COPIES
        deep = depth_line(WEIGHTS, depth)
        flat = np.tile(WEIGHTS, depth // 8)
        stiff = np.diagonal(STIFF)
        wide_s, deep_s = stiff * COPIES, depth_line(stiff, depth)
        share = 1.0 / COPIES
        share_z = np.tile(share, depth // 8)
        share_z[0] = share_z[-1] = 1.0
        self.summed = f32(
            np.stack([block(ones8, wide, deep), block(wide, ones8, deep), block(wide, wide, ones)])
        )
        self.local = f32(
            np.stack(
                [block(ones8, WEIGHTS, flat), block(WEIGHTS, ones8, flat), block(WEIGHTS, WEIGHTS, ones)]
            )
        )
        self.share = f32(block(share, share, share_z))
        diagonal = (
            block(wide_s, wide, deep)
            + block(wide, wide_s, deep)
            + block(wide, wide, deep_s)
            + SIGMA_SHIFT * block(wide, wide, deep)
        )
        self.inverse = f32(1.0 / diagonal)
        self.shift = f32(SIGMA_SHIFT * block(wide, wide, deep))
        self.stiff_y = f32(rolled_rows(STIFF))
        self.slope_y = f32(rolled_rows(SLOPE))
        self.stiff_z = parts_of(line_sums(STIFF, depth).T)
        self.plain_z = parts_of(np.kron(np.eye(depth // 8), STIFF).T)
        self.slope_z = parts_of(line_sums(SLOPE, depth).T)


def row_marks():
    row = lax.broadcasted_iota(jnp.int32, (8, 128), 0)
    return jnp.where(row == 0, 1.0, 0.0), jnp.where(row == 7, 1.0, 0.0)


def by_place(vector, place):
    out = jnp.full(place.shape, float(vector[0]), jnp.float32)
    for i in range(1, 8):
        out = jnp.where(place == i, float(vector[i]), out)
    return out


def along_x(rows, table):
    if np.allclose(table, table[::-1, ::-1]):
        even = 0.5 * (table[:4, :4] + table[:4, :3:-1])
        odd = 0.5 * (table[:4, :4] - table[:4, :3:-1])
        plus = [rows[i] + rows[7 - i] for i in range(4)]
        minus = [rows[i] - rows[7 - i] for i in range(4)]
        out = [None] * 8
        for a in range(4):
            p = sum(float(even[a, b]) * plus[b] for b in range(4))
            m = sum(float(odd[a, b]) * minus[b] for b in range(4))
            out[a], out[7 - a] = p + m, p - m
        return out
    return [sum(float(table[a, b]) * rows[b] for b in range(8)) for a in range(8)]


def along_y(tiles, factors):
    total = factors[0] * tiles
    for shift in range(1, 8):
        total = total + factors[shift] * pltpu.roll(tiles, shift, axis=1)
    return total


def along_z(tiles, matrix):
    wide, rest = matrix
    shape, depth = tiles.shape, tiles.shape[-1]
    flat = tiles.reshape(-1, depth)
    hi = flat.astype(jnp.bfloat16)
    flat = flat - hi.astype(jnp.float32)
    mid = flat.astype(jnp.bfloat16)
    lo = (flat - mid.astype(jnp.float32)).astype(jnp.bfloat16)
    first = jnp.dot(jnp.concatenate([hi, mid], axis=1), wide[...], preferred_element_type=jnp.float32)
    second = jnp.dot(jnp.concatenate([lo, hi], axis=1), rest[...], preferred_element_type=jnp.float32)
    return (first[:, :depth] + (first[:, depth:] + second)).reshape(shape)


def along_both(tiles, matrix, left):
    wide, rest = matrix
    tall, short = left
    shape, depth = tiles.shape, tiles.shape[-1]
    flat = tiles.reshape(-1, depth)
    lines = flat.shape[0]
    hi = flat.astype(jnp.bfloat16)
    flat = flat - hi.astype(jnp.float32)
    mid = flat.astype(jnp.bfloat16)
    lo = (flat - mid.astype(jnp.float32)).astype(jnp.bfloat16)

    def dot(a, b):
        return jnp.dot(a, b, preferred_element_type=jnp.float32)

    first = dot(jnp.concatenate([hi, mid], axis=1), wide[...])
    second = dot(jnp.concatenate([lo, hi], axis=1), rest[...])
    z_sums = first[:, :depth] + (first[:, depth:] + second)
    first = dot(tall[...], jnp.concatenate([hi, mid], axis=0))
    second = dot(short[...], jnp.concatenate([lo, hi], axis=0))
    y_sums = first[:lines] + (first[lines:] + second)
    return y_sums.reshape(shape), z_sums.reshape(shape)


def fill_z(out, field, matrix):
    for x in range(0, out.shape[0], 16):
        rows = pl.ds(x, min(16, out.shape[0] - x))
        out[rows] = along_z(field[rows], matrix)


def join_y(parts, low, high):
    out = list(parts)
    for e in range(1, len(parts)):
        out[e - 1] = out[e - 1] + high * pltpu.roll(parts[e], 7, axis=1)
        out[e] = out[e] + low * pltpu.roll(parts[e - 1], 1, axis=1)
    return out


def spread_rows(rows):
    return jnp.broadcast_to(rows[:, None, :], (rows.shape[0], 8, rows.shape[1]))


def column_sums(x_rows, y_parts, z_parts, summed, edges):
    y_parts = join_y(y_parts, edges[0], edges[1])
    return [
        jnp.stack(kx) * summed[0, 0] + ky * summed[1] + kz * summed[2]
        for kx, ky, kz in zip(x_rows, y_parts, z_parts)
    ]


def emit_column(ex, x_rows, y_parts, z_parts, summed, edges, out, state, finish):
    rows = pl.ds(8 * ex, 8)
    parts = column_sums(x_rows, y_parts, z_parts, summed, edges)
    for e, part in enumerate(parts):
        ys = pl.ds(8 * e, 8)
        out[rows, ys] = finish(e, part)
        if ex:
            for row, face in ((8 * ex, state[e]), (8 * ex - 1, x_rows[e][0])):
                out[row, ys] += face * summed[0, 0]
    return [r[7] for r in x_rows]


def end_rows(table):
    row = lax.broadcasted_iota(jnp.int32, (8, 128), 0)
    return (table[0], table[7]), (by_place(table[0], row), by_place(table[7], row))


def store_faces(ex, e, columns, count, tile, even, ends, faces, x=True, y=True):
    x_near, x_far, y_near, y_far = faces
    (x_low, x_high), (y_low, y_high) = ends
    rows, ys = pl.ds(8 * ex, 8), pl.ds(8 * e, 8)
    if x and ex == 0:
        low = sum(float(x_low[i]) * tile[i] for i in range(8))
        x_near[ys] = low
        x_far[ys] = low
    if x and ex == columns - 1:
        high = sum(float(x_high[i]) * tile[i] for i in range(8))
        x_near[ys] = jnp.where(even[0], high, x_near[ys])
        x_far[ys] = jnp.where(even[0], x_far[ys], high)
    if y and e == 0:
        low = jnp.sum(tile * y_low, axis=1)
        y_near[rows] = low
        y_far[rows] = low
    if y and e == count - 1:
        high = jnp.sum(tile * y_high, axis=1)
        y_near[rows] = jnp.where(even[1], high, y_near[rows])
        y_far[rows] = jnp.where(even[1], y_far[rows], high)


def parity(even_ref):
    return even_ref[0] > 0.5, even_ref[1] > 0.5


def even_rows(even_ref):
    return even_ref[0, 0:1] > 0.5, even_ref[1, 0:1] > 0.5


def before_of(even, near, far):
    return jnp.where(even, far, near)


def after_of(even, near, far):
    return jnp.where(even, near, far)


def with_faces(tile, ex, e, columns, count, received, even, edges, weight_x=None, weight_y=None, mask=None, x=True):
    x_far, x_near, y_far, y_near = received
    rows, ys = pl.ds(8 * ex, 8), pl.ds(8 * e, 8)

    def weighted(face, weight):
        return face if weight is None else face * weight

    if e == 0:
        face = before_of(even[1], y_near[rows], y_far[rows])
        face = spread_rows(face) * weighted(edges[0], weight_y)
        tile = tile + weighted(face, mask)
    if e == count - 1:
        face = after_of(even[1], y_near[rows], y_far[rows])
        face = spread_rows(face) * weighted(edges[1], weight_y)
        tile = tile + weighted(face, mask)
    if x and ex == 0:
        face = before_of(even[0], x_near[ys], x_far[ys])
        face = weighted(face, weight_x) if mask is None else weighted(face, weight_x) * mask[0]
        tile = jnp.concatenate([tile[0:1] + face[None], tile[1:]], axis=0)
    if x and ex == columns - 1:
        face = after_of(even[0], x_near[ys], x_far[ys])
        face = weighted(face, weight_x) if mask is None else weighted(face, weight_x) * mask[7]
        tile = jnp.concatenate([tile[:7], tile[7:8] + face[None]], axis=0)
    return tile


def split_rows(block_rows):
    return [block_rows[i] for i in range(8)]


def join_rows(parts, low, high):
    out = list(parts)
    for e in range(1, len(parts)):
        out[e - 1] = out[e - 1] + high * pltpu.roll(parts[e], 7, axis=0)
        out[e] = out[e] + low * pltpu.roll(parts[e - 1], 1, axis=0)
    return out


def depth_marks(depth):
    lane = lax.broadcasted_iota(jnp.int32, (8, depth), 1)
    place = lane & 7
    after = jnp.where((place == 0) & (lane > 0), 1.0, 0.0)
    before = jnp.where((place == 7) & (lane < depth - 1), 1.0, 0.0)
    return by_place(WEIGHTS, place), after, before


def join_depth(value, after, before):
    axis, depth = value.ndim - 1, value.shape[-1]
    return value + after * pltpu.roll(value, 1, axis=axis) + before * pltpu.roll(value, depth - 1, axis=axis)


def forced(field, old, step):
    if field == 4:
        return step
    value = step * old(field)
    if field == 2:
        value = value + COUPLING * old(3)
    if field == 3:
        value = value - STRATIFY * old(2)
    return value


def load_faces(old_far, step_far, even_ref, old, step, x_near, x_far, y_near, y_far, arrived):
    length, width, depth = step.shape
    columns, count = length // 8, width // 8
    copies = [pltpu.make_async_copy(step_far, step, arrived.at[4])]
    copies += [pltpu.make_async_copy(old_far.at[i], old.at[i], arrived.at[i]) for i in range(4)]
    for copy in copies:
        copy.start()
    even, (low, high) = parity(even_ref), row_marks()
    row = lax.broadcasted_iota(jnp.int32, (8, depth), 0)
    line, after, before = depth_marks(depth)
    mass = by_place(WEIGHTS, row) * line
    for field in (4, 0, 1, 2, 3):
        if field != 3:
            copies[0 if field == 4 else field + 1].wait()
        if field == 2:
            copies[4].wait()
        found = []
        for x in (0, length - 1):
            parts = []
            for e in range(count):
                ys = pl.ds(8 * e, 8)
                value = forced(field, lambda f: old[f, x, ys], step[x, ys])
                parts.append(join_depth(value * (float(WEIGHTS[x % 8]) * mass), after, before))
            found.append(join_rows(parts, low, high))
        for e in range(count):
            ys = pl.ds(8 * e, 8)
            x_near[field, ys] = jnp.where(even[0], found[1][e], found[0][e])
            x_far[field, ys] = jnp.where(even[0], found[0][e], found[1][e])
        found = []
        for y in (0, width - 1):
            parts = []
            for ex in range(columns):
                rows, ys = pl.ds(8 * ex, 8), pl.ds(y // 8 * 8, 8)
                value = forced(field, lambda f: old[f, rows, ys][:, y % 8], step[rows, ys][:, y % 8])
                parts.append(join_depth(value * (float(WEIGHTS[y % 8]) * mass), after, before))
            found.append(join_rows(parts, low, high))
        for ex in range(columns):
            rows = pl.ds(8 * ex, 8)
            y_near[field, rows] = jnp.where(even[1], found[1][ex], found[0][ex])
            y_far[field, rows] = jnp.where(even[1], found[0][ex], found[1][ex])


def load_local(old, step, out):
    columns, count, depth = out.shape[1] // 8, out.shape[2] // 8, out.shape[3]
    edges = row_marks()
    row = lax.broadcasted_iota(jnp.int32, (8, depth), 0)
    line, after, before = depth_marks(depth)
    plane = by_place(WEIGHTS, row) * line
    mass = jnp.stack([float(w) * plane for w in WEIGHTS])
    for field in range(5):
        state = [None] * count
        for ex in range(columns):
            rows = pl.ds(8 * ex, 8)
            parts = []
            for e in range(count):
                ys = pl.ds(8 * e, 8)
                value = forced(field, lambda f: old[f, rows, ys], step[rows, ys])
                parts.append(join_depth(value * mass, after, before))
            parts = join_y(parts, edges[0], edges[1])
            for e in range(count):
                ys = pl.ds(8 * e, 8)
                out[field, rows, ys] = parts[e]
                if ex:
                    out[field, 8 * ex, ys] += state[e]
                    out[field, 8 * ex - 1, ys] += parts[e][0]
                state[e] = parts[e][7]


def stiff_terms(ex, tiles, stiff_y, z_sums):
    x_rows = [along_x(split_rows(t), STIFF) for t in tiles]
    y_parts = [along_y(t, stiff_y) for t in tiles]
    z_parts = [z_sums[pl.ds(8 * ex, 8), pl.ds(8 * e, 8)] for e in range(len(tiles))]
    return x_rows, y_parts, z_parts


def square_sum(rows):
    total = 0.0
    for sign in (1.0, -1.0):
        form = 0.5 * (STIFF[:4, :4] + sign * STIFF[:4, :3:-1])
        part = [rows[i] + rows[7 - i] if sign > 0 else rows[i] - rows[7 - i] for i in range(4)]
        for i in range(4):
            pivot = form[i, i]
            if pivot < 1e-12:
                continue
            line = form[i] / np.sqrt(pivot)
            value = sum(float(line[b]) * part[b] for b in range(i, 4))
            total = total + value * value
            form = form - np.outer(line, line)
    return total


def join_x(c, out, x_far, x_near, even, even_row, ends, weight, mask, faces, slopes, slope_ends):
    columns, count = out.shape[0] // 8, out.shape[1] // 8
    for xi, side in enumerate((before_of, after_of)):
        row = (8 * columns - 1) * xi
        mended = [[0.0, 0.0], [0.0, 0.0]]
        for e in range(count):
            ys = pl.ds(8 * e, 8)
            change = side(even[0], x_near[c, ys], x_far[c, ys]) * weight * mask(row, ys)
            out[row, ys] += change
            for kind, (low, high) in enumerate((ends[1], slope_ends[1])):
                if e == 0:
                    mended[kind][0] = jnp.sum(change * low, axis=0, keepdims=True)
                if e == count - 1:
                    mended[kind][1] = jnp.sum(change * high, axis=0, keepdims=True)
        for kind, where in enumerate((faces, slopes if c == 1 else None)):
            if where is not None:
                low, high = mended[kind]
                where[2][row : row + 1] += jnp.where(even_row[1], high, low)
                where[3][row : row + 1] += jnp.where(even_row[1], low, high)
    for ex in sorted({0, columns - 1}):
        for e in range(count):
            tile = out[pl.ds(8 * ex, 8), pl.ds(8 * e, 8)]
            if faces is not None:
                store_faces(ex, e, columns, count, tile, even, ends, faces, True, False)
            if slopes is not None and c == 0:
                store_faces(ex, e, columns, count, tile, even, slope_ends, slopes, True, False)


def y_faces(c, ex, e, columns, count, tile, even, ends, slope_ends, y_near, y_far):
    store_faces(ex, e, columns, count, tile, even, ends, (None, None, y_near.at[c], y_far.at[c]), False, True)
    if c == 1:
        slopes = (None, None, y_near.at[4], y_far.at[4])
        store_faces(ex, e, columns, count, tile, even, slope_ends, slopes, False, True)


def first_y(local, boundary, y_far, y_near, even_ref, part, y_near_out, y_far_out):
    columns, count = part.shape[1] // 8, part.shape[2] // 8
    even, edges = parity(even_ref), row_marks()
    ends, slope_ends = end_rows(STIFF), end_rows(SLOPE)
    for c in range(4):
        for ex in range(columns):
            for e in range(count):
                rows, ys = pl.ds(8 * ex, 8), pl.ds(8 * e, 8)
                tile = with_faces(local[c, rows, ys], ex, e, columns, count, (None, None, y_far.at[c], y_near.at[c]),
                                  even, edges, x=False)
                tile = tile * boundary[rows, ys].astype(jnp.float32)
                part[c, rows, ys] = tile
                y_faces(c, ex, e, columns, count, tile, even, ends, slope_ends, y_near_out, y_far_out)


def first_x(part, y_near_in, y_far_in, boundary, x_far, x_near, even_ref, right, near, far, x_near_out, x_far_out):
    del part, y_near_in, y_far_in
    columns, count = right.shape[1] // 8, right.shape[2] // 8
    even, even_row = parity(even_ref), even_rows(even_ref)
    ends, slope_ends = end_rows(STIFF), end_rows(SLOPE)
    faces = (x_near_out, x_far_out, near, far)
    for c in range(4):
        join_x(c, right.at[c], x_far, x_near, even, even_row, ends, 1.0,
               lambda row, ys: boundary[row, ys].astype(jnp.float32),
               [f.at[c] for f in faces], [f.at[4] for f in faces], slope_ends)
    near[5] = jnp.zeros(near.shape[1:], jnp.float32)
    far[5] = jnp.zeros(far.shape[1:], jnp.float32)
    for xi, side in enumerate((before_of, after_of)):
        for field in range(5):
            low, high = [
                side(even_row[0], x_near[field, y : y + 1], x_far[field, y : y + 1]) for y in (0, 8 * count - 1)
            ]
            row = 8 * xi + field
            near[5, row : row + 1] = jnp.where(even_row[1], high, low)
            far[5, row : row + 1] = jnp.where(even_row[1], low, high)


def pick(c, values):
    out = jnp.float32(values[0])
    for i in range(1, 4):
        out = jnp.where(c == i, jnp.float32(values[i]), out)
    return out


def start_sums(scales, rates, local, boundary, x_far, x_near, y_far, y_near, even_ref, right, summed, share, tall_y,
               short_y, wide_z, rest_z, reaction, free, ahead):
    columns, count = ahead.shape[1] // 8, ahead.shape[2] // 8
    even, edges = parity(even_ref), row_marks()
    received = [r.at[4] for r in (x_far, x_near, y_far, y_near)]
    for ex in range(columns):
        for e in range(count):
            rows, ys = pl.ds(8 * ex, 8), pl.ds(8 * e, 8)
            reaction[rows, ys] = with_faces(local[4, rows, ys], ex, e, columns, count, received, even, edges)
            free[rows, ys] = boundary[rows, ys].astype(jnp.float32)
    basis_fill(scales, rates, right, None, reaction, free, summed, share, (tall_y, short_y), (wide_z, rest_z), ahead)


def basis_sums(scales, rates, newest, older, reaction, free, summed, share, tall_y, short_y, wide_z, rest_z, ahead, *dots):
    left, matrix = (tall_y, short_y), (wide_z, rest_z)
    basis_fill(scales, rates, newest, older, reaction, free, summed, share, left, matrix, ahead, *dots)


def basis_fill(scales, rates, newest, older, reaction, free, summed, share, left, matrix, ahead, dots=None, first=None):
    columns, count = ahead.shape[1] // 8, ahead.shape[2] // 8
    double = 1.0 if older is None else 2.0

    def component(c, carry):
        scale, rate = pick(c, [double * v for v in scales]), pick(c, [double * v for v in rates])
        same = jnp.zeros((8, 128), jnp.float32)
        cross = jnp.zeros((8, 128), jnp.float32)
        start = jnp.zeros((8, 128), jnp.float32)
        state = None
        for ex in range(columns):
            rows = pl.ds(8 * ex, 8)
            tiles = []
            for e in range(count):
                ys = pl.ds(8 * e, 8)
                tile = newest[c, rows, ys]
                if older is not None:
                    weighted = tile * share[...]
                    same = same + jnp.sum(weighted * tile, axis=0)
                    cross = cross + jnp.sum(weighted * older[c, rows, ys], axis=0)
                if first is not None:
                    start = start + jnp.sum(older[c, rows, ys] * older[c, rows, ys] * share[...], axis=0)
                tiles.append(tile)
            x_rows = [along_x(split_rows(t), STIFF) for t in tiles]
            y_all, z_all = along_both(newest[c, rows], matrix, left)
            following = [r[7] for r in x_rows]
            for e in range(count):
                ys = pl.ds(8 * e, 8)
                if ex:
                    x_rows[e][0] = x_rows[e][0] + state[e]
                if ex < columns - 1:
                    first_row = sum(float(STIFF[0, i]) * newest[c, 8 * ex + 8 + i, ys] for i in range(8))
                    x_rows[e][7] = x_rows[e][7] + first_row
                part = jnp.stack(x_rows[e]) * summed[0, 0]
                part = part + y_all[:, 8 * e : 8 * e + 8] * summed[1] + z_all[:, 8 * e : 8 * e + 8] * summed[2]
                value = scale * part + (rate * reaction[rows, ys] - double) * tiles[e]
                value = value * free[rows, ys]
                ahead[c, rows, ys] = value if older is None else value - older[c, rows, ys]
            state = following
        if older is not None:
            dots[pl.ds(c, 1)] = jnp.sum(same, axis=0, keepdims=True)
            dots[pl.ds(c + 4, 1)] = jnp.sum(cross, axis=0, keepdims=True)
        if first is not None:
            first[pl.ds(c, 1)] = jnp.sum(start, axis=0, keepdims=True)
            first[pl.ds(c + 4, 1)] = jnp.zeros((1, 128), jnp.float32)
        return carry

    lax.fori_loop(0, 4, component, 0)


def y_field(c, ex, e, ahead, free, y_far, y_near, scale, summed, edges, even, columns, count):
    rows, ys = pl.ds(8 * ex, 8), pl.ds(8 * e, 8)
    return with_faces(ahead[c, rows, ys], ex, e, columns, count, (None, None, y_far.at[c], y_near.at[c]), even, edges,
                      None, summed[1], scale * free[rows, ys], x=False)


def grow_y(scales, ahead, free, y_far, y_near, even_ref, summed, part, y_near_out, y_far_out):
    columns, count = part.shape[1] // 8, part.shape[2] // 8
    even, edges = parity(even_ref), row_marks()
    ends, slope_ends = end_rows(STIFF), end_rows(SLOPE)
    for c in range(4):
        for ex in range(columns):
            for e in range(count):
                tile = y_field(c, ex, e, ahead, free, y_far, y_near, scales[c], summed, edges, even, columns, count)
                part[c, pl.ds(8 * ex, 8), pl.ds(8 * e, 8)] = tile
                y_faces(c, ex, e, columns, count, tile, even, ends, slope_ends, y_near_out, y_far_out)


def grow_x(scales, part, y_near_in, y_far_in, free, x_far, x_near, even_ref, summed, out, y_near_out, y_far_out,
           x_near_out, x_far_out):
    del part, y_near_in, y_far_in
    even, even_row = parity(even_ref), even_rows(even_ref)
    ends, slope_ends = end_rows(STIFF), end_rows(SLOPE)
    faces = (x_near_out, x_far_out, y_near_out, y_far_out)
    for c in range(4):
        join_x(c, out.at[c], x_far, x_near, even, even_row, ends, scales[c] * summed[0, 0],
               lambda row, ys: free[row, ys], [f.at[c] for f in faces], [f.at[4] for f in faces], slope_ends)


def second_y(scales, rates, ahead, free, x_far0, x_near0, y_far0, y_near0, y_far, y_near, even_ref, summed, wide_z,
             rest_z, right_in, reaction_in, out, right, reaction, y_near_out, y_far_out, lines, depth_lines):
    columns, count = out.shape[1] // 8, out.shape[2] // 8
    even, edges, even_row = parity(even_ref), row_marks(), even_rows(even_ref)
    ends, slope_ends = end_rows(STIFF), end_rows(SLOPE)
    end_x, end_y = (0, 8 * columns - 1), (0, 8 * count - 1)
    sides = (before_of, after_of)
    corners = [(xi, yi) for xi in (0, 1) for yi in (0, 1)]

    def at(array, xi, yi):
        return array[end_x[xi], end_y[yi] : end_y[yi] + 1]

    def diagonal(field, xi, yi):
        row = 8 * xi + field
        return sides[yi](even_row[1], y_near[5, row : row + 1], y_far[5, row : row + 1])

    def beside(field, xi, yi):
        row = end_y[yi]
        return sides[xi](even_row[0], x_near0[field, row : row + 1], x_far0[field, row : row + 1])

    def beyond(field, xi, yi):
        row = end_x[xi]
        return sides[yi](even_row[1], y_near0[field, row : row + 1], y_far0[field, row : row + 1])

    for c in range(4):
        for n, (xi, yi) in enumerate(corners):
            lines[4 * c + n : 4 * c + n + 1] = diagonal(c, xi, yi) * at(free, xi, yi)
    depth_lines[...] = along_z(lines[...], (wide_z, rest_z))

    def missed(c, ex, e):
        found = []
        for n, (xi, yi) in enumerate(corners):
            cx, ce, sx, sy = (columns - 1) * xi, (count - 1) * yi, 7 * xi, 7 * yi
            line = lines[4 * c + n : 4 * c + n + 1]
            weight_x, weight_y = summed[0, 0, sy : sy + 1], summed[1, sx, 0:1]
            along = scales[c] * line * weight_x
            across = scales[c] * line * weight_y
            if ex == cx and e == ce:
                for i in range(8):
                    found.append((i, float(STIFF[i, sx]) * along * edges[yi]))
                found.append((sx, across * ends[1][yi]))
                side = beyond(c, xi, yi) * weight_x + beside(c, xi, yi) * weight_y
                side = float(STIFF[0, 0]) * side
                depth = depth_lines[4 * c + n : 4 * c + n + 1] * summed[2, sx, sy : sy + 1]
                gained = diagonal(4, xi, yi)
                node = scales[c] * (side + depth)
                node = node + (rates[c] * (at(reaction_in, xi, yi) + gained) - 1.0) * line
                node = node + rates[c] * gained * at(right_in.at[c], xi, yi)
                found.append((sx, node * edges[yi]))
            elif e == ce and ex == cx + 1 - 2 * xi:
                found.append((sx, float(STIFF[7 - sx, sx]) * along * edges[yi]))
            elif ex == cx and e == ce + 1 - 2 * yi:
                found.append((sx, float(STIFF[7 - sy, sy]) * across * edges[yi]))
        return found

    for c in range(4):
        for ex in range(columns):
            for e in range(count):
                rows, ys = pl.ds(8 * ex, 8), pl.ds(8 * e, 8)
                tile = y_field(c, ex, e, ahead, free, y_far, y_near, scales[c], summed, edges, even, columns, count)
                found = missed(c, ex, e)
                if found:
                    parts = []
                    for i in range(8):
                        extra = [t for row, t in found if row == i]
                        parts.append(tile[i] + sum(extra) * free[8 * ex + i, ys] if extra else tile[i])
                    tile = jnp.stack(parts)
                out[c, rows, ys] = tile
                y_faces(c, ex, e, columns, count, tile, even, ends, slope_ends, y_near_out, y_far_out)

    for n, (xi, yi) in enumerate(corners):
        x, y = end_x[xi], end_y[yi]
        reaction[x, y : y + 1] = at(reaction_in, xi, yi) + diagonal(4, xi, yi)
        for c in range(4):
            right[c, x, y : y + 1] = at(right_in.at[c], xi, yi) + lines[4 * c + n : 4 * c + n + 1]


def mend_slopes(x_far0, x_near0, y_far0, y_near0, x_far, x_near, y_far, y_near, free, even_ref,
                sx_far, sx_near, sy_far, sy_near):
    even_row = even_rows(even_ref)
    end_x, end_y = (0, free.shape[0] - 1), (0, free.shape[1] - 1)
    sides = (before_of, after_of)

    def at(array, xi, yi):
        return array[end_x[xi], end_y[yi] : end_y[yi] + 1]

    def beside(field, xi, yi):
        row = end_y[yi]
        return sides[xi](even_row[0], x_near0[field, row : row + 1], x_far0[field, row : row + 1])

    def beyond(field, xi, yi):
        row = end_x[xi]
        return sides[yi](even_row[1], y_near0[field, row : row + 1], y_far0[field, row : row + 1])

    sx_far[...], sx_near[...], sy_far[...], sy_near[...] = x_far[4], x_near[4], y_far[4], y_near[4]
    low, high = float(SLOPE[7, 7]), float(SLOPE[0, 0])
    for i in (0, 1):
        y, x = end_y[i], end_x[i]
        before = low * beyond(0, 0, i) * at(free, 0, i)
        after = high * beyond(0, 1, i) * at(free, 1, i)
        sx_near[y : y + 1] += jnp.where(even_row[0], after, before)
        sx_far[y : y + 1] += jnp.where(even_row[0], before, after)
        before = low * beside(1, i, 0) * at(free, i, 0)
        after = high * beside(1, i, 1) * at(free, i, 1)
        sy_near[x : x + 1] += jnp.where(even_row[1], after, before)
        sy_far[x : x + 1] += jnp.where(even_row[1], before, after)


def column_products(c, ex, out, newest, reaction, share, left, matrix, local, scale, rate):
    count = out.shape[2] // 8
    rows = pl.ds(8 * ex, 8)
    same = jnp.zeros((8, 128), jnp.float32)
    cross = jnp.zeros((8, 128), jnp.float32)
    work = jnp.zeros((8, 128), jnp.float32)
    y_sums, z_sums = along_both(out[c, rows], matrix, left)
    for e in range(count):
        ys = pl.ds(8 * e, 8)
        tile = out[c, rows, ys]
        weighted = tile * share[...]
        square = weighted * tile
        same = same + jnp.sum(square, axis=0)
        cross = cross + jnp.sum(weighted * newest[c, rows, ys], axis=0)
        work = work + jnp.sum((rate * reaction[rows, ys] - 1.0) * square, axis=0)
        work = work + scale * (square_sum(split_rows(tile)) * local[0, 0])
        term = y_sums[:, 8 * e : 8 * e + 8] * local[1] + z_sums[:, 8 * e : 8 * e + 8] * local[2]
        work = work + scale * jnp.sum(term * tile, axis=0)
    return same, cross, work


def last_y(scales, rates, ahead, newest, reaction, free, y_far, y_near, even_ref, summed, share, tall_y, short_y, wide_z,
           rest_z, local, part, sy_near, sy_far, products):
    columns, count = part.shape[1] // 8, part.shape[2] // 8
    even, edges = parity(even_ref), row_marks()
    slope_ends = end_rows(SLOPE)
    for c in range(4):
        total = [jnp.zeros((8, 128), jnp.float32)] * 3
        for ex in range(columns):
            for e in range(count):
                tile = y_field(c, ex, e, ahead, free, y_far, y_near, 2.0 * scales[c], summed, edges, even, columns, count)
                part[c, pl.ds(8 * ex, 8), pl.ds(8 * e, 8)] = tile
                if c == 1:
                    store_faces(ex, e, columns, count, tile, even, slope_ends, (None, None, sy_near, sy_far), False, True)
            if 0 < ex < columns - 1:
                found = column_products(c, ex, part, newest, reaction, share, (tall_y, short_y), (wide_z, rest_z), local,
                                        scales[c], rates[c])
                total = [a + b for a, b in zip(total, found)]
        for n in range(3):
            products[c, n] = total[n]


def last_x(scales, rates, part, sy_near_in, sy_far_in, products, newest, reaction, free, x_far, x_near, even_ref, summed,
           share, tall_y, short_y, wide_z, rest_z, local, d0, d1, d2, d3, d4, out, sy_near, sy_far, sums, sx_near, sx_far):
    del part, sy_near_in, sy_far_in
    dots = (d0, d1, d2, d3, d4)
    columns = out.shape[1] // 8
    even, even_row = parity(even_ref), even_rows(even_ref)
    ends, slope_ends = end_rows(STIFF), end_rows(SLOPE)
    for i in range(1, ITERS - 1):
        sums[i] = dots[i][...]
    for c in range(4):
        join_x(c, out.at[c], x_far, x_near, even, even_row, ends, 2.0 * scales[c] * summed[0, 0],
               lambda row, ys: free[row, ys], None, (sx_near, sx_far, sy_near, sy_far), slope_ends)
        total = [products[c, n] for n in range(3)]
        for ex in sorted({0, columns - 1}):
            found = column_products(c, ex, out, newest, reaction, share, (tall_y, short_y), (wide_z, rest_z), local,
                                    scales[c], rates[c])
            total = [a + b for a, b in zip(total, found)]
        same, cross, work = [jnp.sum(t, axis=0, keepdims=True) for t in total]
        sums[ITERS - 1, c : c + 1] = same
        sums[ITERS - 1, c + 4 : c + 5] = cross
        sums[0, c : c + 1] = dots[0][c : c + 1]
        sums[0, c + 4 : c + 5] = work


def slope_sums(*refs):
    fields, (summed, slope_y, wide_z, rest_z), outs = refs[:3], refs[3:7], refs[7:]
    columns, count = outs[0].shape[1] // 8, outs[0].shape[2] // 8
    edges = row_marks()
    for field, out in zip(fields, outs):
        fill_z(out.at[2], field.at[2], (wide_z, rest_z))
        state = None
        for ex in range(columns):
            rows, ends = pl.ds(8 * ex, 8), []
            y_parts = [along_y(field[1, rows, pl.ds(8 * e, 8)], slope_y) for e in range(count)]
            y_parts = join_y(y_parts, edges[0], edges[1])
            for e in range(count):
                ys = pl.ds(8 * e, 8)
                out[1, rows, ys] = y_parts[e] * summed[1]
                out[2, rows, ys] = out[2, rows, ys] * summed[2]
                x_rows = [r * summed[0, 0] for r in along_x(split_rows(field[0, rows, ys]), SLOPE)]
                out[0, rows, ys] = jnp.stack(x_rows)
                if ex:
                    out[0, 8 * ex, ys] += state[e]
                    out[0, 8 * ex - 1, ys] += x_rows[0]
                ends.append(x_rows[7])
            state = ends


def first_update(halves, gain, *refs):
    sums, *sloped = refs[: ITERS + 1]
    refs = refs[ITERS + 1 :]
    slopes = [refs[:4]]
    slopes += [[r.at[4] for r in refs[4 * k : 4 * k + 4]] for k in range(1, ITERS - 1)]
    refs = refs[4 * ITERS - 4 :]
    slopes.append(refs[:4])
    even_ref, free, summed, inverse = refs[4:8]
    weights, remainder, update, *faces = refs[8:15]
    joined = refs[15:]
    columns, count = update.shape[0] // 8, update.shape[1] // 8
    even, edges = parity(even_ref), row_marks()
    ends = end_rows(STIFF)
    total = [jnp.broadcast_to(jnp.sum(sums[i], axis=1, keepdims=True), (8, 128)) for i in range(ITERS)]
    other = [pltpu.roll(t, 4, axis=0) for t in total]
    row = lax.broadcasted_iota(jnp.int32, (8, 128), 0)
    half = jnp.full((8, 128), halves[0], jnp.float32)
    for i in range(1, 4):
        half = jnp.where(row == i, halves[i], half)
    moments = [total[0], other[1]]
    for level in range(2, 2 * ITERS - 1):
        inner = total[level // 2] if level % 2 == 0 else other[level // 2 + 1]
        moments.append(2.0 * inner - moments[level % 2])
    top = 2.0 * other[0] - other[5]
    moments.append(2.0 * top - moments[1])
    for i, value in enumerate(conjugate_coefficients(moments, half, half)):
        weights[i] = value
    for n in range(4):
        c = n // 2
        joined[n][...] = sum(slopes[i][n][...] * weights[i, c : c + 1] for i in range(ITERS))
    factor = [[weights[i, c : c + 1][None] for c in range(3)] for i in range(ITERS)]
    for ex in range(columns):
        for e in range(count):
            rows, ys = pl.ds(8 * ex, 8), pl.ds(8 * e, 8)
            tile = sum(sloped[i][c, rows, ys] * factor[i][c] for i in range(ITERS) for c in range(3))
            tile = with_faces(tile, ex, e, columns, count, joined, even, edges, summed[0, 0], summed[1])
            left = -tile * free[rows, ys]
            change = gain * inverse[...] * left
            remainder[rows, ys] = left
            update[rows, ys] = change
            store_faces(ex, e, columns, count, change, even, ends, faces)


def combine_fields(weights, *refs):
    *basis, fields, done = refs
    done[...] = weights[0]

    def combine(c, carry):
        factor = [weights[i, pl.ds(c, 1)] for i in range(ITERS)]
        for x in range(0, fields.shape[1], 8):
            rows = pl.ds(x, 8)
            value = basis[0][c, rows] * factor[0][None]
            for i in range(1, ITERS):
                value = value + basis[i][c, rows] * factor[i][None]
            fields[c, rows] = value
        return carry

    lax.fori_loop(0, 4, combine, 0)


def add_loads(count, *refs):
    *loads, rider, tick, out = refs
    del tick
    values = [load[:count] for load in loads]
    total = values[0] + values[1]
    if len(values) == 4:
        total = total + (values[2] + values[3])
    out[:count] = total
    out[count:] = rider[...]


def pressure_sums(update, tick, summed, shift, stiff_y, wide_z, rest_z, raw, z_sums):
    del tick
    columns, count = raw.shape[0] // 8, raw.shape[1] // 8
    edges = row_marks()
    state = None
    fill_z(z_sums, update, (wide_z, rest_z))
    for ex in range(columns):
        rows = pl.ds(8 * ex, 8)
        tiles = [update[rows, pl.ds(8 * e, 8)] for e in range(count)]
        x_rows, y_parts, z_parts = stiff_terms(ex, tiles, stiff_y, z_sums)
        state = emit_column(ex, x_rows, y_parts, z_parts, summed, edges, raw, state,
                            lambda e, part: part + shift[...] * tiles[e])


def pressure_part(ex, e, columns, count, keep, gain, raw, free, y_far, y_near, even, edges, summed, inverse, remainder,
                  update):
    rows, ys = pl.ds(8 * ex, 8), pl.ds(8 * e, 8)
    tile = with_faces(raw[rows, ys], ex, e, columns, count, (None, None, y_far, y_near), even, edges,
                      None, summed[1], x=False)
    left = remainder[rows, ys] - tile * free[rows, ys]
    return left, gain * inverse[...] * left + keep * update[rows, ys]


def pressure_y(keep, gain, raw, free, y_far, y_near, even_ref, summed, inverse, remainder_in, update_in, pressure_in,
               pressure, remainder, update, y_near_out, y_far_out):
    columns, count = raw.shape[0] // 8, raw.shape[1] // 8
    even, edges, ends = parity(even_ref), row_marks(), end_rows(STIFF)
    for ex in range(columns):
        for e in range(count):
            rows, ys = pl.ds(8 * ex, 8), pl.ds(8 * e, 8)
            left, change = pressure_part(ex, e, columns, count, keep, gain, raw, free, y_far, y_near, even, edges, summed,
                                         inverse, remainder_in, update_in)
            pressure[rows, ys] = pressure_in[rows, ys] + change
            remainder[rows, ys] = left
            update[rows, ys] = change
            store_faces(ex, e, columns, count, change, even, ends, (None, None, y_near_out, y_far_out), False, True)


def end_change(xi, e, gain, free_row, x_far, x_near, even, summed, inverse):
    side, ys = (before_of, after_of)[xi], pl.ds(8 * e, 8)
    face = side(even[0], x_near[ys], x_far[ys]) * summed[0, 0] * free_row[ys]
    return -face, -gain * inverse[7 * xi] * face


def pressure_x(gain, pressure_in, remainder_in, update_in, y_near_in, y_far_in, free, x_far, x_near, even_ref, summed,
               inverse, pressure, remainder, update, y_near, y_far, x_near_out, x_far_out):
    del pressure_in, remainder_in, update_in, y_near_in, y_far_in
    columns, count = update.shape[0] // 8, update.shape[1] // 8
    even, even_row, ends = parity(even_ref), even_rows(even_ref), end_rows(STIFF)
    for xi in (0, 1):
        row = (8 * columns - 1) * xi
        low = high = 0.0
        for e in range(count):
            ys = pl.ds(8 * e, 8)
            left, change = end_change(xi, e, gain, free.at[row], x_far, x_near, even, summed, inverse)
            remainder[row, ys] += left
            update[row, ys] += change
            pressure[row, ys] += change
            if e == 0:
                low = jnp.sum(change * ends[1][0], axis=0, keepdims=True)
            if e == count - 1:
                high = jnp.sum(change * ends[1][1], axis=0, keepdims=True)
        y_near[row : row + 1] += jnp.where(even_row[1], high, low)
        y_far[row : row + 1] += jnp.where(even_row[1], low, high)
    for ex in sorted({0, columns - 1}):
        for e in range(count):
            tile = update[pl.ds(8 * ex, 8), pl.ds(8 * e, 8)]
            store_faces(ex, e, columns, count, tile, even, ends, (x_near_out, x_far_out, None, None), True, False)


def last_pressure_y(keep, gain, raw, free, y_far, y_near, even_ref, summed, inverse, remainder, update, pressure_in,
                    far, end_part, pressure, gone):
    length = raw.shape[0]
    columns, count = length // 8, raw.shape[1] // 8
    even, edges = parity(even_ref), row_marks()
    for ex in range(columns):
        for e in range(count):
            rows, ys = pl.ds(8 * ex, 8), pl.ds(8 * e, 8)
            _, change = pressure_part(ex, e, columns, count, keep, gain, raw, free, y_far, y_near, even, edges, summed,
                                      inverse, remainder, update)
            pressure[rows, ys] = pressure_in[rows, ys] + change
    inner = pl.ds(1, length - 2)
    copy = pltpu.make_async_copy(pressure.at[inner], far.at[inner], gone.at[0])
    copy.start()
    end_part[0] = pressure[0]
    end_part[1] = pressure[length - 1]
    copy.wait()


def last_pressure_x(gain, far_in, end_part, free, x_far, x_near, even_ref, summed, inverse, far, rows, gone):
    del far_in
    last = free.shape[0] - 1
    even, copies = parity(even_ref), []
    for xi in (0, 1):
        for e in range(free.shape[1] // 8):
            ys = pl.ds(8 * e, 8)
            _, change = end_change(xi, e, gain, free.at[last * xi], x_far, x_near, even, summed, inverse)
            rows[xi, ys] = end_part[xi, ys] + change
        copies.append(pltpu.make_async_copy(rows.at[xi], far.at[last * xi], gone.at[xi]))
        copies[-1].start()
    for copy in copies:
        copy.wait()


VMEM_BYTES = 24 * 1024 * 1024


def call(kernel, name, outs, *args, scratch=(), cost=None, far_in=0, far_out=0, copies=0, aliases=()):
    held, far = pl.BlockSpec(memory_space=pltpu.VMEM), pl.BlockSpec(memory_space=pltpu.HBM)
    scratch_shapes = [pltpu.VMEM(s, jnp.float32) for s in scratch]
    if copies:
        scratch_shapes.append(pltpu.SemaphoreType.DMA((copies,)))
    return pl.pallas_call(
        kernel,
        name=name,
        out_shape=[jax.ShapeDtypeStruct(s, jnp.float32) for s in outs],
        in_specs=[far] * far_in + [held] * (len(args) - far_in),
        out_specs=[far] * far_out + [held] * (len(outs) - far_out),
        scratch_shapes=scratch_shapes,
        cost_estimate=cost,
        input_output_aliases=dict(aliases),
        compiler_params=pltpu.CompilerParams(vmem_limit_bytes=VMEM_BYTES),
    )(*[pltpu.with_memory_space_constraint(a, pltpu.HBM) for a in args[:far_in]], *args[far_in:])


def busy(bytes_accessed):
    return pl.CostEstimate(flops=0, bytes_accessed=bytes_accessed, transcendentals=0)


def swap_near(axis, face):
    return lax.ppermute(face, axis, [(i, i ^ 1) for i in range(lax.axis_size(axis))])


def swap_far(axis, face):
    size = lax.axis_size(axis)
    return lax.ppermute(face, axis, [(i, far_partner(i, size)) for i in range(size)])


def swap_all(x_near, x_far, y_near, y_far):
    y_far = swap_far("gy", y_far)
    x_far = swap_far("gx", x_far)
    x_near = swap_near("gx", x_near)
    y_near = swap_near("gy", y_near)
    return x_far, x_near, y_far, y_near


def far_partner(i, size):
    return (i + 1 if i % 2 else i - 1) % size


def partner_loads(load, axis, partners, riders, count):
    size, heard, faces = lax.axis_size(axis), [], []
    for n, (partner, rider) in enumerate(zip(partners, riders)):
        mine = load
        if n:
            mine = load[:count] if rider is None else jnp.concatenate([load[:count], rider])
        mine = lax.ppermute(mine, axis, [(i, partner(i)) for i in range(size)])
        heard.append(mine)
        if rider is not None:
            faces.append(mine[count:])
    return heard, faces


def all_sum(values, axis, near, far, following, meanwhile):
    size = lax.axis_size(axis)
    count = values.shape[0] - far.shape[0] if following is None else values.shape[0]
    half = size // 2

    def to_near(i):
        return i ^ 1

    def to_far(i):
        return far_partner(i, size)

    def across(i):
        return (i + half) % size

    def far_across(i):
        return across(to_far(i))

    rounds = [((to_far,), (far,))]
    if size == 4:
        rounds = [((to_far, to_near, across), (far, near, None))]
    elif size > 4:
        rounds = [((to_far, across, far_across), (far, None, None)), ((to_near,), (near,))]
        bit = 4
        while bit < half:
            rounds.append(((lambda i, bit=bit: i ^ bit,), (None,)))
            bit *= 2
    else:
        rounds.append(((), (near,)))
    faces = []
    load = values if following is None else jnp.concatenate([values, far])
    for n, (partners, riders) in enumerate(rounds):
        if not partners:
            faces.append(lax.ppermute(near, axis, [(i, to_near(i)) for i in range(size)]))
            continue
        heard, got = partner_loads(load, axis, partners, riders, count)
        faces += got
        rider = rounds[n + 1][1][0] if n + 1 < len(rounds) and rounds[n + 1][0] else following
        tail = jnp.zeros((8, values.shape[1]), jnp.float32) if rider is None else rider
        (load,) = call(
            functools.partial(add_loads, count), "add_loads", [(count + tail.shape[0], values.shape[1])],
            load, *heard, tail, meanwhile(),
        )
    if following is None:
        load = load[:count]
    return load, faces[1], faces[0]


def conjugate_coefficients(moments, centre, half):
    remaining, towards = list(moments), list(moments)
    one, zero = jnp.ones_like(moments[0]), jnp.zeros_like(moments[0])
    direction = [one] + [zero] * ITERS
    residual = list(direction)
    total = [zero] * ITERS
    for step in range(ITERS):
        count = len(towards) - 1
        image = []
        for level in range(count):
            side = (
                half * towards[1] if level == 0 else 0.5 * half * (towards[level + 1] + towards[level - 1])
            )
            image.append(centre * towards[level] + side)
        shrink = -(half if step == 0 else 0.5 * half) / remaining[step]
        alpha = remaining[step] / image[step]
        total = [total[i] + alpha * direction[i] for i in range(ITERS)]
        if step == ITERS - 1:
            break
        applied = []
        for i in range(ITERS + 1):
            term = centre * direction[i]
            if i >= 1:
                term = term + (half if i == 1 else 0.5 * half) * direction[i - 1]
            if i < ITERS:
                term = term + 0.5 * half * direction[i + 1]
            applied.append(term)
        residual = [residual[i] - alpha * applied[i] for i in range(ITERS + 1)]
        following = [remaining[i] - alpha * image[i] for i in range(count)]
        beta = (alpha * shrink) * following[step + 1]
        towards = [following[i] + beta * towards[i] for i in range(count)]
        direction = [residual[i] + beta * direction[i] for i in range(ITERS + 1)]
        remaining = following
    return total


def on_device(old_fields, inverse_step, boundary):
    x, y, z = inverse_step.shape
    t = Tables(y, z)
    brick, four = (x, y, z), (4, x, y, z)
    faces = [(y, z)] * 2 + [(x, z)] * 2
    faces5 = [(5,) + f for f in faces]
    faces_back = [(y, z)] * 2 + [(x, z)] * 2

    place = [lax.axis_index(a) % 2 == 0 for a in ("gx", "gy")]
    even = jnp.stack([jnp.full((8, 128), p, jnp.float32) for p in place])

    old, step, x_near, x_far, y_near, y_far = call(
        load_faces, "right_faces", [four, brick] + faces5, old_fields, inverse_step, even, far_in=2, copies=5,
    )
    received = swap_all(x_near, x_far, y_near, y_far)
    (local,) = call(load_local, "right_local", [(5,) + brick], old, step, cost=busy(2 << 20))

    top = INTERVAL_SHARE * np.array([spectrum_top(c) for c in DIFFUSE])
    halves = [float(v) for v in 0.5 * top]
    scales = [float(v) for v in np.array(DIFFUSE) / (0.5 * top)]
    rates = [float(v) for v in 1.0 / (0.5 * top)]

    x_far, x_near, y_far, y_near = received
    relayed = [(6, x, z)] * 2
    x_faces, y_faces5 = [(5, y, z)] * 2, [(5, x, z)] * 2
    part, near, far = call(first_y, "first_y", [four] + relayed, local, boundary, y_far, y_near, even, cost=busy(2 << 20))
    right, y_near, y_far, x_near, x_far = call(
        first_x, "first_x", [four] + relayed + x_faces, part, near, far, boundary, x_far, x_near, even,
        aliases=[(0, 0), (1, 1), (2, 2)],
    )
    heard = [swap_all(x_near, x_far, y_near, y_far)]
    reaction, free, ahead = call(
        functools.partial(start_sums, scales, rates), "right_sums", [brick, brick, four],
        local, boundary, *received, even, right, t.summed, t.share, *t.left_y, *t.stiff_z, cost=busy(8 << 20),
    )
    x_far, x_near, y_far, y_near = heard[0]
    part, right, reaction, near, far = call(
        functools.partial(second_y, scales, rates), "second_y", [four, four, brick] + y_faces5,
        ahead, free, *received, y_far, y_near, even, t.summed, *t.stiff_z, right, reaction,
        scratch=[(16, z)] * 2, aliases=[(12, 1), (13, 2)], cost=busy(3 << 20),
    )
    basis, sums = [right], []
    here = scales
    for k in range(1, ITERS - 1):
        field, y_near, y_far, x_near, x_far = call(
            functools.partial(grow_x, here), "basis_x", [four] + y_faces5 + x_faces,
            part, near, far, free, x_far, x_near, even, t.summed, aliases=[(0, 0), (1, 1), (2, 2)],
        )
        basis.append(field)
        heard.append(swap_all(x_near, x_far, y_near, y_far))
        x_far, x_near, y_far, y_near = heard[-1]
        outs = [four, (8, 128)] + ([(8, 128)] if k == 1 else [])
        ahead, *dots = call(
            functools.partial(basis_sums, scales, rates), "basis_sums", outs,
            basis[-1], basis[-2], reaction, free, t.summed, t.share, *t.left_y, *t.stiff_z, cost=busy(8 << 20),
        )
        sums += dots[::-1]
        here = [2.0 * v for v in scales]
        if k < ITERS - 2:
            part, near, far = call(
                functools.partial(grow_y, here), "basis_y", [four] + y_faces5,
                ahead, free, y_far, y_near, even, t.summed, cost=busy(2 << 20),
            )
    part, near, far, products = call(
        functools.partial(last_y, scales, rates), "last_y", [four] + [(x, z)] * 2 + [(4, 3, 8, 128)],
        ahead, basis[-1], reaction, free, y_far, y_near, even, t.summed, t.share, *t.plain_y, *t.plain_z, t.local,
        cost=busy(4 << 20),
    )
    field, y_near, y_far, sums, x_near, x_far = call(
        functools.partial(last_x, scales, rates), "last_x",
        [four] + [(x, z)] * 2 + [(ITERS, 8, 128)] + [(y, z)] * 2,
        part, near, far, products, basis[-1], reaction, free, x_far, x_near, even, t.summed, t.share,
        *t.plain_y, *t.plain_z, t.local, *sums, aliases=[(0, 0), (1, 1), (2, 2)],
    )
    basis.append(field)
    heard[0] = call(mend_slopes, "slopes", faces_back, *received, *heard[0], free, even)
    sums = sums.reshape(ITERS * 8, z)
    sloped = []

    def meanwhile():
        if len(sloped) < ITERS:
            sloped.extend(
                call(
                    slope_sums, "slope_sums", [(3,) + brick] * 3,
                    *basis[len(sloped) : len(sloped) + 3], t.summed, t.slope_y, *t.slope_z, cost=busy(6 << 20),
                )
            )
        return sloped[-1]

    sums, x_near, x_far = all_sum(sums, "gx", x_near, x_far, y_far, meanwhile)
    sums, y_near, y_far = all_sum(sums, "gy", y_near, y_far, None, meanwhile)
    while len(sloped) < ITERS:
        meanwhile()
    sums = sums.reshape(ITERS, 8, z)
    slopes = (x_far, x_near, y_far, y_near)

    centre, half = chebyshev_bounds()
    factor = centre / half
    damping = 1.0 / factor
    weights, remainder, update, *sent = call(
        functools.partial(first_update, halves, 1.0 / centre), "first_update", [(ITERS, 8, 128), brick, brick] + faces,
        sums, *sloped, *[a for h in heard for a in h], *slopes, even, free, t.summed, t.inverse, scratch=faces_back,
    )
    pressure, tick = update, even
    for step in range(1, CHEB):
        last = step == CHEB - 1
        received = swap_all(*sent)
        (raw,) = call(
            pressure_sums, "pressure_sums", [brick],
            update, tick, t.summed, t.shift, t.stiff_y, *t.stiff_z, cost=busy(2 << 20), scratch=[brick],
        )
        if step == 1:
            fields, tick = call(combine_fields, "fields", [four, (8, z)], weights, *basis, cost=busy(4 << 20))
        following = 1.0 / (2.0 * factor - damping)
        keep, gain = following * damping, 2.0 * following / half
        damping = following
        x_far, x_near, y_far, y_near = received
        args = [raw, free, y_far, y_near, even, t.summed, t.inverse, remainder, update, pressure]
        if last:
            pressure, end_part = call(
                functools.partial(last_pressure_y, keep, gain), "last_pressure_y", [brick, (2, y, z)], *args,
                scratch=[brick], far_out=1, copies=1, cost=busy(1 << 20),
            )
            (pressure,) = call(
                functools.partial(last_pressure_x, gain), "last_pressure_x", [brick],
                pressure, end_part, free, x_far, x_near, even, t.summed, t.inverse,
                scratch=[(2, y, z)], far_in=1, far_out=1, copies=2, aliases=[(0, 0)],
            )
            break
        part = call(
            functools.partial(pressure_y, keep, gain), "pressure_y", [brick] * 3 + [(x, z)] * 2, *args, cost=busy(1 << 20)
        )
        pressure, remainder, update, y_near, y_far, x_near, x_far = call(
            functools.partial(pressure_x, gain), "pressure_x", [brick] * 3 + [(x, z)] * 2 + [(y, z)] * 2,
            *part, free, x_far, x_near, even, t.summed, t.inverse, aliases=[(i, i) for i in range(5)],
        )
        sent = x_near, x_far, y_near, y_far
    return (fields, pressure)


def solution(mesh):
    return jax.shard_map(
        on_device,
        mesh=mesh,
        in_specs=(P(None, "gx", "gy", None), P("gx", "gy", None), P("gx", "gy", None)),
        out_specs=(P(None, "gx", "gy", None), P("gx", "gy", None)),
        check_vma=False,
    )
```

```python
import functools

import jax
import jax.numpy as jnp
import ml_dtypes
import numpy as np
from jax import lax
from jax.experimental import pallas as pl
from jax.experimental.pallas import tpu as pltpu
from jax.sharding import PartitionSpec as P

ITERS = 6
CHEB = 6

SIGMA_SHIFT = 0.5
DIFFUSE = (1.0, 1.0, 1.0, 1.4)
COUPLING = 1.0
STRATIFY = 1.0
SPREAD = 20.0
STEP_MAX = 64.0
INTERVAL_SHARE = 0.82
HIGHEST_PRECISION = lax.Precision.HIGHEST
LOBATTO_POINTS = (
    -1.0,
    -0.8717401485096066,
    -0.5917001814331423,
    -0.2092992179024789,
    0.2092992179024789,
    0.5917001814331423,
    0.8717401485096066,
    1.0,
)


def legendre_value(points, degree):
    previous = points * 0.0 + 1.0
    current = points
    for order in range(1, degree):
        following = ((2 * order + 1) * points * current - order * previous) / (order + 1)
        previous = current
        current = following
    return current


def quadrature_tables():
    degree = 7
    points = np.array(LOBATTO_POINTS)
    values = legendre_value(points, degree)
    weights = 2.0 / (degree * (degree + 1) * values * values)
    derive = np.zeros((degree + 1, degree + 1))
    for row_index in range(degree + 1):
        for column_index in range(degree + 1):
            if row_index != column_index:
                derive[row_index, column_index] = values[row_index] / (
                    values[column_index] * (points[row_index] - points[column_index])
                )
    derive[0, 0] = -degree * (degree + 1) / 4.0
    derive[degree, degree] = degree * (degree + 1) / 4.0
    stiffness_table = derive.T @ (weights[:, None] * derive)
    return (weights, derive, stiffness_table)


WEIGHTS, DERIVE, STIFF = quadrature_tables()
SLOPE = WEIGHTS[:, None] * DERIVE
COPIES = np.where(np.arange(8) % 7 == 0, 2.0, 1.0)


def chebyshev_bounds():
    weight_matrix = np.eye(8) * WEIGHTS

    def kron3(a, b, c):
        return np.kron(np.kron(a, b), c)

    element_matrix = (
        kron3(STIFF, weight_matrix, weight_matrix)
        + kron3(weight_matrix, STIFF, weight_matrix)
        + kron3(weight_matrix, weight_matrix, STIFF)
        + SIGMA_SHIFT * kron3(weight_matrix, weight_matrix, weight_matrix)
    )
    bounds_ratio = np.sum(np.abs(element_matrix), axis=1) / np.diagonal(element_matrix)
    upper_bound = float(np.max(bounds_ratio))
    lower_bound = upper_bound / SPREAD
    return ((upper_bound + lower_bound) / 2.0, (upper_bound - lower_bound) / 2.0)


def spectrum_top(diffuse):
    root = np.sqrt(COPIES)
    stiff = root[:, None] * STIFF * root[None, :]
    weight = np.diag(WEIGHTS * COPIES)

    def kron3(a, b, c):
        return np.kron(np.kron(a, b), c)

    element = diffuse * (
        kron3(stiff, weight, weight) + kron3(weight, stiff, weight) + kron3(weight, weight, stiff)
    ) + STEP_MAX * kron3(weight, weight, weight)
    return float(np.linalg.eigvalsh(element)[-1])


def line_sums(table, length):
    matrix = np.kron(np.eye(length // 8), table)
    total = matrix.copy()
    for start in range(8, length, 8):
        total[start] += matrix[start - 1]
        total[start - 1] += matrix[start]
    return total


def depth_line(vector, length):
    line = np.tile(vector * COPIES, length // 8)
    line[0] = vector[0]
    line[-1] = vector[-1]
    return line


def f32(array):
    return np.ascontiguousarray(array, np.float32)


def rolled_rows(table):
    out = np.zeros((8, 8, 128))
    for shift in range(8):
        for row in range(8):
            out[shift, row] = table[row, (row - shift) % 8]
    return out


def block(a, b, c):
    return a[:, None, None] * b[:, None] * c


def parts_of(matrix):
    rest, parts = f32(matrix), []
    for _ in range(3):
        parts.append(rest.astype(ml_dtypes.bfloat16))
        rest = rest - parts[-1].astype(np.float32)
    hi, mid, lo = parts
    return np.block([[hi, mid], [hi, mid]]), np.concatenate([hi, lo])


def left_parts(table):
    rest, parts = f32(np.kron(np.eye(8), table)), []
    for _ in range(3):
        parts.append(rest.astype(ml_dtypes.bfloat16))
        rest = rest - parts[-1].astype(np.float32)
    hi, mid, lo = parts
    return np.block([[hi, hi], [mid, mid]]), np.concatenate([hi, lo], axis=1)


class Tables:
    def __init__(self, width, depth):
        self.left_y = left_parts(line_sums(STIFF, width))
        self.plain_y = left_parts(np.kron(np.eye(width // 8), STIFF))
        ones8, ones = np.ones(8), np.ones(depth)
        wide = WEIGHTS * COPIES
        deep = depth_line(WEIGHTS, depth)
        flat = np.tile(WEIGHTS, depth // 8)
        stiff = np.diagonal(STIFF)
        wide_s, deep_s = stiff * COPIES, depth_line(stiff, depth)
        share = 1.0 / COPIES
        share_z = np.tile(share, depth // 8)
        share_z[0] = share_z[-1] = 1.0
        self.summed = f32(
            np.stack([block(ones8, wide, deep), block(wide, ones8, deep), block(wide, wide, ones)])
        )
        self.local = f32(
            np.stack(
                [block(ones8, WEIGHTS, flat), block(WEIGHTS, ones8, flat), block(WEIGHTS, WEIGHTS, ones)]
            )
        )
        self.share = f32(block(share, share, share_z))
        diagonal = (
            block(wide_s, wide, deep)
            + block(wide, wide_s, deep)
            + block(wide, wide, deep_s)
            + SIGMA_SHIFT * block(wide, wide, deep)
        )
        self.inverse = f32(1.0 / diagonal)
        self.shift = f32(SIGMA_SHIFT * block(wide, wide, deep))
        self.stiff_y = f32(rolled_rows(STIFF))
        self.slope_y = f32(rolled_rows(SLOPE))
        self.stiff_z = parts_of(line_sums(STIFF, depth).T)
        self.plain_z = parts_of(np.kron(np.eye(depth // 8), STIFF).T)
        self.slope_z = parts_of(line_sums(SLOPE, depth).T)


def row_marks():
    row = lax.broadcasted_iota(jnp.int32, (8, 128), 0)
    return jnp.where(row == 0, 1.0, 0.0), jnp.where(row == 7, 1.0, 0.0)


def by_place(vector, place):
    out = jnp.full(place.shape, float(vector[0]), jnp.float32)
    for i in range(1, 8):
        out = jnp.where(place == i, float(vector[i]), out)
    return out


def along_x(rows, table):
    if np.allclose(table, table[::-1, ::-1]):
        even = 0.5 * (table[:4, :4] + table[:4, :3:-1])
        odd = 0.5 * (table[:4, :4] - table[:4, :3:-1])
        plus = [rows[i] + rows[7 - i] for i in range(4)]
        minus = [rows[i] - rows[7 - i] for i in range(4)]
        out = [None] * 8
        for a in range(4):
            p = sum(float(even[a, b]) * plus[b] for b in range(4))
            m = sum(float(odd[a, b]) * minus[b] for b in range(4))
            out[a], out[7 - a] = p + m, p - m
        return out
    return [sum(float(table[a, b]) * rows[b] for b in range(8)) for a in range(8)]


def along_y(tiles, factors):
    total = factors[0] * tiles
    for shift in range(1, 8):
        total = total + factors[shift] * pltpu.roll(tiles, shift, axis=1)
    return total


def along_z(tiles, matrix):
    wide, rest = matrix
    shape, depth = tiles.shape, tiles.shape[-1]
    flat = tiles.reshape(-1, depth)
    hi = flat.astype(jnp.bfloat16)
    flat = flat - hi.astype(jnp.float32)
    mid = flat.astype(jnp.bfloat16)
    lo = (flat - mid.astype(jnp.float32)).astype(jnp.bfloat16)
    first = jnp.dot(jnp.concatenate([hi, mid], axis=1), wide[...], preferred_element_type=jnp.float32)
    second = jnp.dot(jnp.concatenate([lo, hi], axis=1), rest[...], preferred_element_type=jnp.float32)
    return (first[:, :depth] + (first[:, depth:] + second)).reshape(shape)


def along_both(tiles, matrix, left):
    wide, rest = matrix
    tall, short = left
    shape, depth = tiles.shape, tiles.shape[-1]
    flat = tiles.reshape(-1, depth)
    lines = flat.shape[0]
    hi = flat.astype(jnp.bfloat16)
    flat = flat - hi.astype(jnp.float32)
    mid = flat.astype(jnp.bfloat16)
    lo = (flat - mid.astype(jnp.float32)).astype(jnp.bfloat16)

    def dot(a, b):
        return jnp.dot(a, b, preferred_element_type=jnp.float32)

    first = dot(jnp.concatenate([hi, mid], axis=1), wide[...])
    second = dot(jnp.concatenate([lo, hi], axis=1), rest[...])
    z_sums = first[:, :depth] + (first[:, depth:] + second)
    first = dot(tall[...], jnp.concatenate([hi, mid], axis=0))
    second = dot(short[...], jnp.concatenate([lo, hi], axis=0))
    y_sums = first[:lines] + (first[lines:] + second)
    return y_sums.reshape(shape), z_sums.reshape(shape)


def fill_z(out, field, matrix):
    for x in range(0, out.shape[0], 16):
        rows = pl.ds(x, min(16, out.shape[0] - x))
        out[rows] = along_z(field[rows], matrix)


def join_y(parts, low, high):
    out = list(parts)
    for e in range(1, len(parts)):
        out[e - 1] = out[e - 1] + high * pltpu.roll(parts[e], 7, axis=1)
        out[e] = out[e] + low * pltpu.roll(parts[e - 1], 1, axis=1)
    return out


def spread_rows(rows):
    return jnp.broadcast_to(rows[:, None, :], (rows.shape[0], 8, rows.shape[1]))


def column_sums(x_rows, y_parts, z_parts, summed, edges):
    y_parts = join_y(y_parts, edges[0], edges[1])
    return [
        jnp.stack(kx) * summed[0, 0] + ky * summed[1] + kz * summed[2]
        for kx, ky, kz in zip(x_rows, y_parts, z_parts)
    ]


def emit_column(ex, x_rows, y_parts, z_parts, summed, edges, out, state, finish):
    rows = pl.ds(8 * ex, 8)
    parts = column_sums(x_rows, y_parts, z_parts, summed, edges)
    for e, part in enumerate(parts):
        ys = pl.ds(8 * e, 8)
        out[rows, ys] = finish(e, part)
        if ex:
            for row, face in ((8 * ex, state[e]), (8 * ex - 1, x_rows[e][0])):
                out[row, ys] += face * summed[0, 0]
    return [r[7] for r in x_rows]


def end_rows(table):
    row = lax.broadcasted_iota(jnp.int32, (8, 128), 0)
    return (table[0], table[7]), (by_place(table[0], row), by_place(table[7], row))


def store_faces(ex, e, columns, count, tile, even, ends, faces, x=True, y=True):
    x_near, x_far, y_near, y_far = faces
    (x_low, x_high), (y_low, y_high) = ends
    rows, ys = pl.ds(8 * ex, 8), pl.ds(8 * e, 8)
    if x and ex == 0:
        low = sum(float(x_low[i]) * tile[i] for i in range(8))
        x_near[ys] = low
        x_far[ys] = low
    if x and ex == columns - 1:
        high = sum(float(x_high[i]) * tile[i] for i in range(8))
        x_near[ys] = jnp.where(even[0], high, x_near[ys])
        x_far[ys] = jnp.where(even[0], x_far[ys], high)
    if y and e == 0:
        low = jnp.sum(tile * y_low, axis=1)
        y_near[rows] = low
        y_far[rows] = low
    if y and e == count - 1:
        high = jnp.sum(tile * y_high, axis=1)
        y_near[rows] = jnp.where(even[1], high, y_near[rows])
        y_far[rows] = jnp.where(even[1], y_far[rows], high)


def parity(even_ref):
    return even_ref[0] > 0.5, even_ref[1] > 0.5


def even_rows(even_ref):
    return even_ref[0, 0:1] > 0.5, even_ref[1, 0:1] > 0.5


def before_of(even, near, far):
    return jnp.where(even, far, near)


def after_of(even, near, far):
    return jnp.where(even, near, far)


def with_faces(tile, ex, e, columns, count, received, even, edges, weight_x=None, weight_y=None, mask=None, x=True):
    x_far, x_near, y_far, y_near = received
    rows, ys = pl.ds(8 * ex, 8), pl.ds(8 * e, 8)

    def weighted(face, weight):
        return face if weight is None else face * weight

    if e == 0:
        face = before_of(even[1], y_near[rows], y_far[rows])
        face = spread_rows(face) * weighted(edges[0], weight_y)
        tile = tile + weighted(face, mask)
    if e == count - 1:
        face = after_of(even[1], y_near[rows], y_far[rows])
        face = spread_rows(face) * weighted(edges[1], weight_y)
        tile = tile + weighted(face, mask)
    if x and ex == 0:
        face = before_of(even[0], x_near[ys], x_far[ys])
        face = weighted(face, weight_x) if mask is None else weighted(face, weight_x) * mask[0]
        tile = jnp.concatenate([tile[0:1] + face[None], tile[1:]], axis=0)
    if x and ex == columns - 1:
        face = after_of(even[0], x_near[ys], x_far[ys])
        face = weighted(face, weight_x) if mask is None else weighted(face, weight_x) * mask[7]
        tile = jnp.concatenate([tile[:7], tile[7:8] + face[None]], axis=0)
    return tile


def split_rows(block_rows):
    return [block_rows[i] for i in range(8)]


def join_rows(parts, low, high):
    out = list(parts)
    for e in range(1, len(parts)):
        out[e - 1] = out[e - 1] + high * pltpu.roll(parts[e], 7, axis=0)
        out[e] = out[e] + low * pltpu.roll(parts[e - 1], 1, axis=0)
    return out


def depth_marks(depth):
    lane = lax.broadcasted_iota(jnp.int32, (8, depth), 1)
    place = lane & 7
    after = jnp.where((place == 0) & (lane > 0), 1.0, 0.0)
    before = jnp.where((place == 7) & (lane < depth - 1), 1.0, 0.0)
    return by_place(WEIGHTS, place), after, before


def join_depth(value, after, before):
    axis, depth = value.ndim - 1, value.shape[-1]
    return value + after * pltpu.roll(value, 1, axis=axis) + before * pltpu.roll(value, depth - 1, axis=axis)


def forced(field, old, step):
    if field == 4:
        return step
    value = step * old(field)
    if field == 2:
        value = value + COUPLING * old(3)
    if field == 3:
        value = value - STRATIFY * old(2)
    return value


def load_faces(old_far, step_far, even_ref, old, step, x_near, x_far, y_near, y_far, arrived):
    length, width, depth = step.shape
    columns, count = length // 8, width // 8
    copies = [pltpu.make_async_copy(step_far, step, arrived.at[4])]
    copies += [pltpu.make_async_copy(old_far.at[i], old.at[i], arrived.at[i]) for i in range(4)]
    for copy in copies:
        copy.start()
    even, (low, high) = parity(even_ref), row_marks()
    row = lax.broadcasted_iota(jnp.int32, (8, depth), 0)
    line, after, before = depth_marks(depth)
    mass = by_place(WEIGHTS, row) * line
    for field in (4, 0, 1, 2, 3):
        if field != 3:
            copies[0 if field == 4 else field + 1].wait()
        if field == 2:
            copies[4].wait()
        found = []
        for x in (0, length - 1):
            parts = []
            for e in range(count):
                ys = pl.ds(8 * e, 8)
                value = forced(field, lambda f: old[f, x, ys], step[x, ys])
                parts.append(join_depth(value * (float(WEIGHTS[x % 8]) * mass), after, before))
            found.append(join_rows(parts, low, high))
        for e in range(count):
            ys = pl.ds(8 * e, 8)
            x_near[field, ys] = jnp.where(even[0], found[1][e], found[0][e])
            x_far[field, ys] = jnp.where(even[0], found[0][e], found[1][e])
        found = []
        for y in (0, width - 1):
            parts = []
            for ex in range(columns):
                rows, ys = pl.ds(8 * ex, 8), pl.ds(y // 8 * 8, 8)
                value = forced(field, lambda f: old[f, rows, ys][:, y % 8], step[rows, ys][:, y % 8])
                parts.append(join_depth(value * (float(WEIGHTS[y % 8]) * mass), after, before))
            found.append(join_rows(parts, low, high))
        for ex in range(columns):
            rows = pl.ds(8 * ex, 8)
            y_near[field, rows] = jnp.where(even[1], found[1][ex], found[0][ex])
            y_far[field, rows] = jnp.where(even[1], found[0][ex], found[1][ex])


def load_local(old, step, out):
    columns, count, depth = out.shape[1] // 8, out.shape[2] // 8, out.shape[3]
    edges = row_marks()
    row = lax.broadcasted_iota(jnp.int32, (8, depth), 0)
    line, after, before = depth_marks(depth)
    plane = by_place(WEIGHTS, row) * line
    mass = jnp.stack([float(w) * plane for w in WEIGHTS])
    for field in range(5):
        state = [None] * count
        for ex in range(columns):
            rows = pl.ds(8 * ex, 8)
            parts = []
            for e in range(count):
                ys = pl.ds(8 * e, 8)
                value = forced(field, lambda f: old[f, rows, ys], step[rows, ys])
                parts.append(join_depth(value * mass, after, before))
            parts = join_y(parts, edges[0], edges[1])
            for e in range(count):
                ys = pl.ds(8 * e, 8)
                out[field, rows, ys] = parts[e]
                if ex:
                    out[field, 8 * ex, ys] += state[e]
                    out[field, 8 * ex - 1, ys] += parts[e][0]
                state[e] = parts[e][7]


def stiff_terms(ex, tiles, stiff_y, z_sums):
    x_rows = [along_x(split_rows(t), STIFF) for t in tiles]
    y_parts = [along_y(t, stiff_y) for t in tiles]
    z_parts = [z_sums[pl.ds(8 * ex, 8), pl.ds(8 * e, 8)] for e in range(len(tiles))]
    return x_rows, y_parts, z_parts


def square_sum(rows):
    total = 0.0
    for sign in (1.0, -1.0):
        form = 0.5 * (STIFF[:4, :4] + sign * STIFF[:4, :3:-1])
        part = [rows[i] + rows[7 - i] if sign > 0 else rows[i] - rows[7 - i] for i in range(4)]
        for i in range(4):
            pivot = form[i, i]
            if pivot < 1e-12:
                continue
            line = form[i] / np.sqrt(pivot)
            value = sum(float(line[b]) * part[b] for b in range(i, 4))
            total = total + value * value
            form = form - np.outer(line, line)
    return total


def join_x(c, out, x_far, x_near, even, even_row, ends, weight, mask, faces, slopes, slope_ends):
    columns, count = out.shape[0] // 8, out.shape[1] // 8
    for xi, side in enumerate((before_of, after_of)):
        row = (8 * columns - 1) * xi
        mended = [[0.0, 0.0], [0.0, 0.0]]
        for e in range(count):
            ys = pl.ds(8 * e, 8)
            change = side(even[0], x_near[c, ys], x_far[c, ys]) * weight * mask(row, ys)
            out[row, ys] += change
            for kind, (low, high) in enumerate((ends[1], slope_ends[1])):
                if e == 0:
                    mended[kind][0] = jnp.sum(change * low, axis=0, keepdims=True)
                if e == count - 1:
                    mended[kind][1] = jnp.sum(change * high, axis=0, keepdims=True)
        for kind, where in enumerate((faces, slopes if c == 1 else None)):
            if where is not None:
                low, high = mended[kind]
                where[2][row : row + 1] += jnp.where(even_row[1], high, low)
                where[3][row : row + 1] += jnp.where(even_row[1], low, high)
    for ex in sorted({0, columns - 1}):
        for e in range(count):
            tile = out[pl.ds(8 * ex, 8), pl.ds(8 * e, 8)]
            if faces is not None:
                store_faces(ex, e, columns, count, tile, even, ends, faces, True, False)
            if slopes is not None and c == 0:
                store_faces(ex, e, columns, count, tile, even, slope_ends, slopes, True, False)


def y_faces(c, ex, e, columns, count, tile, even, ends, slope_ends, y_near, y_far):
    store_faces(ex, e, columns, count, tile, even, ends, (None, None, y_near.at[c], y_far.at[c]), False, True)
    if c == 1:
        slopes = (None, None, y_near.at[4], y_far.at[4])
        store_faces(ex, e, columns, count, tile, even, slope_ends, slopes, False, True)


def first_y(local, boundary, y_far, y_near, even_ref, part, y_near_out, y_far_out):
    columns, count = part.shape[1] // 8, part.shape[2] // 8
    even, edges = parity(even_ref), row_marks()
    ends, slope_ends = end_rows(STIFF), end_rows(SLOPE)
    for c in range(4):
        for ex in range(columns):
            for e in range(count):
                rows, ys = pl.ds(8 * ex, 8), pl.ds(8 * e, 8)
                tile = with_faces(local[c, rows, ys], ex, e, columns, count, (None, None, y_far.at[c], y_near.at[c]),
                                  even, edges, x=False)
                tile = tile * boundary[rows, ys].astype(jnp.float32)
                part[c, rows, ys] = tile
                y_faces(c, ex, e, columns, count, tile, even, ends, slope_ends, y_near_out, y_far_out)


def first_x(part, y_near_in, y_far_in, boundary, x_far, x_near, even_ref, right, near, far, x_near_out, x_far_out):
    del part, y_near_in, y_far_in
    columns, count = right.shape[1] // 8, right.shape[2] // 8
    even, even_row = parity(even_ref), even_rows(even_ref)
    ends, slope_ends = end_rows(STIFF), end_rows(SLOPE)
    faces = (x_near_out, x_far_out, near, far)
    for c in range(4):
        join_x(c, right.at[c], x_far, x_near, even, even_row, ends, 1.0,
               lambda row, ys: boundary[row, ys].astype(jnp.float32),
               [f.at[c] for f in faces], [f.at[4] for f in faces], slope_ends)
    near[5] = jnp.zeros(near.shape[1:], jnp.float32)
    far[5] = jnp.zeros(far.shape[1:], jnp.float32)
    for xi, side in enumerate((before_of, after_of)):
        for field in range(5):
            low, high = [
                side(even_row[0], x_near[field, y : y + 1], x_far[field, y : y + 1]) for y in (0, 8 * count - 1)
            ]
            row = 8 * xi + field
            near[5, row : row + 1] = jnp.where(even_row[1], high, low)
            far[5, row : row + 1] = jnp.where(even_row[1], low, high)


def pick(c, values):
    out = jnp.float32(values[0])
    for i in range(1, 4):
        out = jnp.where(c == i, jnp.float32(values[i]), out)
    return out


def start_sums(scales, rates, local, boundary, x_far, x_near, y_far, y_near, even_ref, right, summed, share, tall_y,
               short_y, wide_z, rest_z, reaction, free, ahead):
    columns, count = ahead.shape[1] // 8, ahead.shape[2] // 8
    even, edges = parity(even_ref), row_marks()
    received = [r.at[4] for r in (x_far, x_near, y_far, y_near)]
    for ex in range(columns):
        for e in range(count):
            rows, ys = pl.ds(8 * ex, 8), pl.ds(8 * e, 8)
            reaction[rows, ys] = with_faces(local[4, rows, ys], ex, e, columns, count, received, even, edges)
            free[rows, ys] = boundary[rows, ys].astype(jnp.float32)
    basis_fill(scales, rates, right, None, reaction, free, summed, share, (tall_y, short_y), (wide_z, rest_z), ahead)


def basis_sums(scales, rates, newest, older, reaction, free, summed, share, tall_y, short_y, wide_z, rest_z, ahead, *dots):
    left, matrix = (tall_y, short_y), (wide_z, rest_z)
    basis_fill(scales, rates, newest, older, reaction, free, summed, share, left, matrix, ahead, *dots)


def basis_fill(scales, rates, newest, older, reaction, free, summed, share, left, matrix, ahead, dots=None, first=None):
    columns, count = ahead.shape[1] // 8, ahead.shape[2] // 8
    double = 1.0 if older is None else 2.0

    def component(c, carry):
        rate = pick(c, [double * v for v in rates])
        same = jnp.zeros((8, 128), jnp.float32)
        cross = jnp.zeros((8, 128), jnp.float32)
        start = jnp.zeros((8, 128), jnp.float32)
        state = None
        for ex in range(columns):
            rows = pl.ds(8 * ex, 8)
            tiles = []
            for e in range(count):
                ys = pl.ds(8 * e, 8)
                tile = newest[c, rows, ys]
                if older is not None:
                    weighted = tile * share[...]
                    same = same + jnp.sum(weighted * tile, axis=0)
                    cross = cross + jnp.sum(weighted * older[c, rows, ys], axis=0)
                if first is not None:
                    start = start + jnp.sum(older[c, rows, ys] * older[c, rows, ys] * share[...], axis=0)
                tiles.append(tile)
            x_rows = [along_x(split_rows(t), STIFF) for t in tiles]
            y_all, z_all = along_both(newest[c, rows], matrix, left)
            following = [r[7] for r in x_rows]
            for e in range(count):
                ys = pl.ds(8 * e, 8)
                if ex:
                    x_rows[e][0] = x_rows[e][0] + state[e]
                if ex < columns - 1:
                    first_row = sum(float(STIFF[0, i]) * newest[c, 8 * ex + 8 + i, ys] for i in range(8))
                    x_rows[e][7] = x_rows[e][7] + first_row
                part = jnp.stack(x_rows[e]) * summed[c, 0, 0]
                part = part + y_all[:, 8 * e : 8 * e + 8] * summed[c, 1] + z_all[:, 8 * e : 8 * e + 8] * summed[c, 2]
                value = part + (rate * reaction[rows, ys] - double) * tiles[e]
                value = value * free[rows, ys]
                ahead[c, rows, ys] = value if older is None else value - older[c, rows, ys]
            state = following
        if older is not None:
            dots[pl.ds(c, 1)] = jnp.sum(same, axis=0, keepdims=True)
            dots[pl.ds(c + 4, 1)] = jnp.sum(cross, axis=0, keepdims=True)
        if first is not None:
            first[pl.ds(c, 1)] = jnp.sum(start, axis=0, keepdims=True)
            first[pl.ds(c + 4, 1)] = jnp.zeros((1, 128), jnp.float32)
        return carry

    lax.fori_loop(0, 4, component, 0)


def y_field(c, ex, e, ahead, free, y_far, y_near, scale, summed, edges, even, columns, count):
    rows, ys = pl.ds(8 * ex, 8), pl.ds(8 * e, 8)
    return with_faces(ahead[c, rows, ys], ex, e, columns, count, (None, None, y_far.at[c], y_near.at[c]), even, edges,
                      None, summed[1], scale * free[rows, ys], x=False)


def grow_y(scales, ahead, free, y_far, y_near, even_ref, summed, part, y_near_out, y_far_out):
    columns, count = part.shape[1] // 8, part.shape[2] // 8
    even, edges = parity(even_ref), row_marks()
    ends, slope_ends = end_rows(STIFF), end_rows(SLOPE)
    for c in range(4):
        for ex in range(columns):
            for e in range(count):
                tile = y_field(c, ex, e, ahead, free, y_far, y_near, scales[c], summed, edges, even, columns, count)
                part[c, pl.ds(8 * ex, 8), pl.ds(8 * e, 8)] = tile
                y_faces(c, ex, e, columns, count, tile, even, ends, slope_ends, y_near_out, y_far_out)


def grow_x(scales, part, y_near_in, y_far_in, free, x_far, x_near, even_ref, summed, out, y_near_out, y_far_out,
           x_near_out, x_far_out):
    del part, y_near_in, y_far_in
    even, even_row = parity(even_ref), even_rows(even_ref)
    ends, slope_ends = end_rows(STIFF), end_rows(SLOPE)
    faces = (x_near_out, x_far_out, y_near_out, y_far_out)
    for c in range(4):
        join_x(c, out.at[c], x_far, x_near, even, even_row, ends, scales[c] * summed[0, 0],
               lambda row, ys: free[row, ys], [f.at[c] for f in faces], [f.at[4] for f in faces], slope_ends)


def second_y(scales, rates, ahead, free, x_far0, x_near0, y_far0, y_near0, y_far, y_near, even_ref, summed, wide_z,
             rest_z, right_in, reaction_in, out, right, reaction, y_near_out, y_far_out, lines, depth_lines):
    columns, count = out.shape[1] // 8, out.shape[2] // 8
    even, edges, even_row = parity(even_ref), row_marks(), even_rows(even_ref)
    ends, slope_ends = end_rows(STIFF), end_rows(SLOPE)
    end_x, end_y = (0, 8 * columns - 1), (0, 8 * count - 1)
    sides = (before_of, after_of)
    corners = [(xi, yi) for xi in (0, 1) for yi in (0, 1)]

    def at(array, xi, yi):
        return array[end_x[xi], end_y[yi] : end_y[yi] + 1]

    def diagonal(field, xi, yi):
        row = 8 * xi + field
        return sides[yi](even_row[1], y_near[5, row : row + 1], y_far[5, row : row + 1])

    def beside(field, xi, yi):
        row = end_y[yi]
        return sides[xi](even_row[0], x_near0[field, row : row + 1], x_far0[field, row : row + 1])

    def beyond(field, xi, yi):
        row = end_x[xi]
        return sides[yi](even_row[1], y_near0[field, row : row + 1], y_far0[field, row : row + 1])

    for c in range(4):
        for n, (xi, yi) in enumerate(corners):
            lines[4 * c + n : 4 * c + n + 1] = diagonal(c, xi, yi) * at(free, xi, yi)
    depth_lines[...] = along_z(lines[...], (wide_z, rest_z))

    def missed(c, ex, e):
        found = []
        for n, (xi, yi) in enumerate(corners):
            cx, ce, sx, sy = (columns - 1) * xi, (count - 1) * yi, 7 * xi, 7 * yi
            line = lines[4 * c + n : 4 * c + n + 1]
            weight_x, weight_y = summed[0, 0, sy : sy + 1], summed[1, sx, 0:1]
            along = scales[c] * line * weight_x
            across = scales[c] * line * weight_y
            if ex == cx and e == ce:
                for i in range(8):
                    found.append((i, float(STIFF[i, sx]) * along * edges[yi]))
                found.append((sx, across * ends[1][yi]))
                side = beyond(c, xi, yi) * weight_x + beside(c, xi, yi) * weight_y
                side = float(STIFF[0, 0]) * side
                depth = depth_lines[4 * c + n : 4 * c + n + 1] * summed[2, sx, sy : sy + 1]
                gained = diagonal(4, xi, yi)
                node = scales[c] * (side + depth)
                node = node + (rates[c] * (at(reaction_in, xi, yi) + gained) - 1.0) * line
                node = node + rates[c] * gained * at(right_in.at[c], xi, yi)
                found.append((sx, node * edges[yi]))
            elif e == ce and ex == cx + 1 - 2 * xi:
                found.append((sx, float(STIFF[7 - sx, sx]) * along * edges[yi]))
            elif ex == cx and e == ce + 1 - 2 * yi:
                found.append((sx, float(STIFF[7 - sy, sy]) * across * edges[yi]))
        return found

    for c in range(4):
        for ex in range(columns):
            for e in range(count):
                rows, ys = pl.ds(8 * ex, 8), pl.ds(8 * e, 8)
                tile = y_field(c, ex, e, ahead, free, y_far, y_near, scales[c], summed, edges, even, columns, count)
                found = missed(c, ex, e)
                if found:
                    parts = []
                    for i in range(8):
                        extra = [t for row, t in found if row == i]
                        parts.append(tile[i] + sum(extra) * free[8 * ex + i, ys] if extra else tile[i])
                    tile = jnp.stack(parts)
                out[c, rows, ys] = tile
                y_faces(c, ex, e, columns, count, tile, even, ends, slope_ends, y_near_out, y_far_out)

    for n, (xi, yi) in enumerate(corners):
        x, y = end_x[xi], end_y[yi]
        reaction[x, y : y + 1] = at(reaction_in, xi, yi) + diagonal(4, xi, yi)
        for c in range(4):
            right[c, x, y : y + 1] = at(right_in.at[c], xi, yi) + lines[4 * c + n : 4 * c + n + 1]


def mend_slopes(x_far0, x_near0, y_far0, y_near0, x_far, x_near, y_far, y_near, free, even_ref,
                sx_far, sx_near, sy_far, sy_near):
    even_row = even_rows(even_ref)
    end_x, end_y = (0, free.shape[0] - 1), (0, free.shape[1] - 1)
    sides = (before_of, after_of)

    def at(array, xi, yi):
        return array[end_x[xi], end_y[yi] : end_y[yi] + 1]

    def beside(field, xi, yi):
        row = end_y[yi]
        return sides[xi](even_row[0], x_near0[field, row : row + 1], x_far0[field, row : row + 1])

    def beyond(field, xi, yi):
        row = end_x[xi]
        return sides[yi](even_row[1], y_near0[field, row : row + 1], y_far0[field, row : row + 1])

    sx_far[...], sx_near[...], sy_far[...], sy_near[...] = x_far[4], x_near[4], y_far[4], y_near[4]
    low, high = float(SLOPE[7, 7]), float(SLOPE[0, 0])
    for i in (0, 1):
        y, x = end_y[i], end_x[i]
        before = low * beyond(0, 0, i) * at(free, 0, i)
        after = high * beyond(0, 1, i) * at(free, 1, i)
        sx_near[y : y + 1] += jnp.where(even_row[0], after, before)
        sx_far[y : y + 1] += jnp.where(even_row[0], before, after)
        before = low * beside(1, i, 0) * at(free, i, 0)
        after = high * beside(1, i, 1) * at(free, i, 1)
        sy_near[x : x + 1] += jnp.where(even_row[1], after, before)
        sy_far[x : x + 1] += jnp.where(even_row[1], before, after)


def column_products(c, ex, out, newest, reaction, share, left, matrix, local, scale, rate):
    count = out.shape[2] // 8
    rows = pl.ds(8 * ex, 8)
    same = jnp.zeros((8, 128), jnp.float32)
    cross = jnp.zeros((8, 128), jnp.float32)
    work = jnp.zeros((8, 128), jnp.float32)
    y_sums, z_sums = along_both(out[c, rows], matrix, left)
    for e in range(count):
        ys = pl.ds(8 * e, 8)
        tile = out[c, rows, ys]
        weighted = tile * share[...]
        same = same + jnp.sum(weighted * tile, axis=0)
        cross = cross + jnp.sum(weighted * newest[c, rows, ys], axis=0)
        extra = (rate * reaction[rows, ys] - 1.0) * tile
        work = work + jnp.sum(weighted * extra, axis=0)
        work = work + scale * (square_sum(split_rows(tile)) * local[0, 0])
        term = y_sums[:, 8 * e : 8 * e + 8] * local[1] + z_sums[:, 8 * e : 8 * e + 8] * local[2]
        work = work + scale * jnp.sum(term * tile, axis=0)
    return same, cross, work


def last_y(scales, rates, ahead, newest, reaction, free, y_far, y_near, even_ref, summed, share, tall_y, short_y, wide_z,
           rest_z, local, part, sy_near, sy_far, products):
    columns, count = part.shape[1] // 8, part.shape[2] // 8
    even, edges = parity(even_ref), row_marks()
    slope_ends = end_rows(SLOPE)
    for c in range(4):
        total = [jnp.zeros((8, 128), jnp.float32)] * 3
        for ex in range(columns):
            for e in range(count):
                tile = y_field(c, ex, e, ahead, free, y_far, y_near, 2.0 * scales[c], summed, edges, even, columns, count)
                part[c, pl.ds(8 * ex, 8), pl.ds(8 * e, 8)] = tile
                if c == 1:
                    store_faces(ex, e, columns, count, tile, even, slope_ends, (None, None, sy_near, sy_far), False, True)
            if 0 < ex < columns - 1:
                found = column_products(c, ex, part, newest, reaction, share, (tall_y, short_y), (wide_z, rest_z), local,
                                        scales[c], rates[c])
                total = [a + b for a, b in zip(total, found)]
        for n in range(3):
            products[c, n] = total[n]


def last_x(scales, rates, part, sy_near_in, sy_far_in, products, newest, reaction, free, x_far, x_near, even_ref, summed,
           share, tall_y, short_y, wide_z, rest_z, local, d0, d1, d2, d3, d4, out, sy_near, sy_far, sums, sx_near, sx_far):
    del part, sy_near_in, sy_far_in
    dots = (d0, d1, d2, d3, d4)
    columns = out.shape[1] // 8
    even, even_row = parity(even_ref), even_rows(even_ref)
    ends, slope_ends = end_rows(STIFF), end_rows(SLOPE)
    for i in range(1, ITERS - 1):
        sums[i] = dots[i][...]
    for c in range(4):
        join_x(c, out.at[c], x_far, x_near, even, even_row, ends, 2.0 * scales[c] * summed[0, 0],
               lambda row, ys: free[row, ys], None, (sx_near, sx_far, sy_near, sy_far), slope_ends)
        total = [products[c, n] for n in range(3)]
        for ex in sorted({0, columns - 1}):
            found = column_products(c, ex, out, newest, reaction, share, (tall_y, short_y), (wide_z, rest_z), local,
                                    scales[c], rates[c])
            total = [a + b for a, b in zip(total, found)]
        same, cross, work = [jnp.sum(t, axis=0, keepdims=True) for t in total]
        sums[ITERS - 1, c : c + 1] = same
        sums[ITERS - 1, c + 4 : c + 5] = cross
        sums[0, c : c + 1] = dots[0][c : c + 1]
        sums[0, c + 4 : c + 5] = work


def slope_sums(*refs):
    fields, (summed, slope_y, wide_z, rest_z), outs = refs[:3], refs[3:7], refs[7:]
    columns, count = outs[0].shape[1] // 8, outs[0].shape[2] // 8
    edges = row_marks()
    for field, out in zip(fields, outs):
        fill_z(out.at[2], field.at[2], (wide_z, rest_z))
        state = None
        for ex in range(columns):
            rows, ends = pl.ds(8 * ex, 8), []
            y_parts = [along_y(field[1, rows, pl.ds(8 * e, 8)], slope_y) for e in range(count)]
            y_parts = join_y(y_parts, edges[0], edges[1])
            for e in range(count):
                ys = pl.ds(8 * e, 8)
                out[1, rows, ys] = y_parts[e] * summed[1]
                out[2, rows, ys] = out[2, rows, ys] * summed[2]
                x_rows = [r * summed[0, 0] for r in along_x(split_rows(field[0, rows, ys]), SLOPE)]
                out[0, rows, ys] = jnp.stack(x_rows)
                if ex:
                    out[0, 8 * ex, ys] += state[e]
                    out[0, 8 * ex - 1, ys] += x_rows[0]
                ends.append(x_rows[7])
            state = ends


def first_update(halves, gain, *refs):
    sums, *sloped = refs[: ITERS + 1]
    refs = refs[ITERS + 1 :]
    slopes = [refs[:4]]
    slopes += [[r.at[4] for r in refs[4 * k : 4 * k + 4]] for k in range(1, ITERS - 1)]
    refs = refs[4 * ITERS - 4 :]
    slopes.append(refs[:4])
    even_ref, free, summed, inverse = refs[4:8]
    weights, remainder, update, *faces = refs[8:15]
    joined = refs[15:]
    columns, count = update.shape[0] // 8, update.shape[1] // 8
    even, edges = parity(even_ref), row_marks()
    ends = end_rows(STIFF)
    total = [jnp.broadcast_to(jnp.sum(sums[i], axis=1, keepdims=True), (8, 128)) for i in range(ITERS)]
    other = [pltpu.roll(t, 4, axis=0) for t in total]
    row = lax.broadcasted_iota(jnp.int32, (8, 128), 0)
    half = jnp.full((8, 128), halves[0], jnp.float32)
    for i in range(1, 4):
        half = jnp.where(row == i, halves[i], half)
    moments = [total[0], other[1]]
    for level in range(2, 2 * ITERS - 1):
        inner = total[level // 2] if level % 2 == 0 else other[level // 2 + 1]
        moments.append(2.0 * inner - moments[level % 2])
    top = 2.0 * other[0] - other[5]
    moments.append(2.0 * top - moments[1])
    for i, value in enumerate(conjugate_coefficients(moments, half, half)):
        weights[i] = value
    for n in range(4):
        c = n // 2
        joined[n][...] = sum(slopes[i][n][...] * weights[i, c : c + 1] for i in range(ITERS))
    factor = [[weights[i, c : c + 1][None] for c in range(3)] for i in range(ITERS)]
    for ex in range(columns):
        for e in range(count):
            rows, ys = pl.ds(8 * ex, 8), pl.ds(8 * e, 8)
            tile = sum(sloped[i][c, rows, ys] * factor[i][c] for i in range(ITERS) for c in range(3))
            tile = with_faces(tile, ex, e, columns, count, joined, even, edges, summed[0, 0], summed[1])
            left = -tile * free[rows, ys]
            change = gain * inverse[...] * left
            remainder[rows, ys] = left
            update[rows, ys] = change
            store_faces(ex, e, columns, count, change, even, ends, faces)


def combine_fields(weights, *refs):
    *basis, fields, done = refs
    done[...] = weights[0]

    def combine(c, carry):
        factor = [weights[i, pl.ds(c, 1)] for i in range(ITERS)]
        for x in range(0, fields.shape[1], 8):
            rows = pl.ds(x, 8)
            value = basis[0][c, rows] * factor[0][None]
            for i in range(1, ITERS):
                value = value + basis[i][c, rows] * factor[i][None]
            fields[c, rows] = value
        return carry

    lax.fori_loop(0, 4, combine, 0)


def add_loads(count, *refs):
    *loads, rider, tick, out = refs
    del tick
    values = [load[:count] for load in loads]
    total = values[0] + values[1]
    if len(values) == 4:
        total = total + (values[2] + values[3])
    out[:count] = total
    out[count:] = rider[...]


def pressure_sums(update, tick, summed, shift, stiff_y, wide_z, rest_z, raw, z_sums):
    del tick
    columns, count = raw.shape[0] // 8, raw.shape[1] // 8
    edges = row_marks()
    state = None
    fill_z(z_sums, update, (wide_z, rest_z))
    for ex in range(columns):
        rows = pl.ds(8 * ex, 8)
        tiles = [update[rows, pl.ds(8 * e, 8)] for e in range(count)]
        x_rows, y_parts, z_parts = stiff_terms(ex, tiles, stiff_y, z_sums)
        state = emit_column(ex, x_rows, y_parts, z_parts, summed, edges, raw, state,
                            lambda e, part: part + shift[...] * tiles[e])


def pressure_part(ex, e, columns, count, keep, gain, raw, free, y_far, y_near, even, edges, summed, inverse, remainder,
                  update):
    rows, ys = pl.ds(8 * ex, 8), pl.ds(8 * e, 8)
    tile = with_faces(raw[rows, ys], ex, e, columns, count, (None, None, y_far, y_near), even, edges,
                      None, summed[1], x=False)
    left = remainder[rows, ys] - tile * free[rows, ys]
    return left, gain * inverse[...] * left + keep * update[rows, ys]


def pressure_y(keep, gain, raw, free, y_far, y_near, even_ref, summed, inverse, remainder_in, update_in, pressure_in,
               pressure, remainder, update, y_near_out, y_far_out):
    columns, count = raw.shape[0] // 8, raw.shape[1] // 8
    even, edges, ends = parity(even_ref), row_marks(), end_rows(STIFF)
    for ex in range(columns):
        for e in range(count):
            rows, ys = pl.ds(8 * ex, 8), pl.ds(8 * e, 8)
            left, change = pressure_part(ex, e, columns, count, keep, gain, raw, free, y_far, y_near, even, edges, summed,
                                         inverse, remainder_in, update_in)
            pressure[rows, ys] = pressure_in[rows, ys] + change
            remainder[rows, ys] = left
            update[rows, ys] = change
            store_faces(ex, e, columns, count, change, even, ends, (None, None, y_near_out, y_far_out), False, True)


def end_change(xi, e, gain, free_row, x_far, x_near, even, summed, inverse):
    side, ys = (before_of, after_of)[xi], pl.ds(8 * e, 8)
    face = side(even[0], x_near[ys], x_far[ys]) * summed[0, 0] * free_row[ys]
    return -face, -gain * inverse[7 * xi] * face


def pressure_x(gain, pressure_in, remainder_in, update_in, y_near_in, y_far_in, free, x_far, x_near, even_ref, summed,
               inverse, pressure, remainder, update, y_near, y_far, x_near_out, x_far_out):
    del pressure_in, remainder_in, update_in, y_near_in, y_far_in
    columns, count = update.shape[0] // 8, update.shape[1] // 8
    even, even_row, ends = parity(even_ref), even_rows(even_ref), end_rows(STIFF)
    for xi in (0, 1):
        row = (8 * columns - 1) * xi
        low = high = 0.0
        for e in range(count):
            ys = pl.ds(8 * e, 8)
            left, change = end_change(xi, e, gain, free.at[row], x_far, x_near, even, summed, inverse)
            remainder[row, ys] += left
            update[row, ys] += change
            pressure[row, ys] += change
            if e == 0:
                low = jnp.sum(change * ends[1][0], axis=0, keepdims=True)
            if e == count - 1:
                high = jnp.sum(change * ends[1][1], axis=0, keepdims=True)
        y_near[row : row + 1] += jnp.where(even_row[1], high, low)
        y_far[row : row + 1] += jnp.where(even_row[1], low, high)
    for ex in sorted({0, columns - 1}):
        for e in range(count):
            tile = update[pl.ds(8 * ex, 8), pl.ds(8 * e, 8)]
            store_faces(ex, e, columns, count, tile, even, ends, (x_near_out, x_far_out, None, None), True, False)


def last_pressure_y(keep, gain, raw, free, y_far, y_near, even_ref, summed, inverse, remainder, update, pressure_in,
                    far, end_part, pressure, gone):
    length = raw.shape[0]
    columns, count = length // 8, raw.shape[1] // 8
    even, edges = parity(even_ref), row_marks()
    for ex in range(columns):
        for e in range(count):
            rows, ys = pl.ds(8 * ex, 8), pl.ds(8 * e, 8)
            _, change = pressure_part(ex, e, columns, count, keep, gain, raw, free, y_far, y_near, even, edges, summed,
                                      inverse, remainder, update)
            pressure[rows, ys] = pressure_in[rows, ys] + change
    inner = pl.ds(1, length - 2)
    copy = pltpu.make_async_copy(pressure.at[inner], far.at[inner], gone.at[0])
    copy.start()
    end_part[0] = pressure[0]
    end_part[1] = pressure[length - 1]
    copy.wait()


def last_pressure_x(gain, far_in, end_part, free, x_far, x_near, even_ref, summed, inverse, far, rows, gone):
    del far_in
    last = free.shape[0] - 1
    even, copies = parity(even_ref), []
    for xi in (0, 1):
        for e in range(free.shape[1] // 8):
            ys = pl.ds(8 * e, 8)
            _, change = end_change(xi, e, gain, free.at[last * xi], x_far, x_near, even, summed, inverse)
            rows[xi, ys] = end_part[xi, ys] + change
        copies.append(pltpu.make_async_copy(rows.at[xi], far.at[last * xi], gone.at[xi]))
        copies[-1].start()
    for copy in copies:
        copy.wait()


VMEM_BYTES = 24 * 1024 * 1024


def call(kernel, name, outs, *args, scratch=(), cost=None, far_in=0, far_out=0, copies=0, aliases=()):
    held, far = pl.BlockSpec(memory_space=pltpu.VMEM), pl.BlockSpec(memory_space=pltpu.HBM)
    scratch_shapes = [pltpu.VMEM(s, jnp.float32) for s in scratch]
    if copies:
        scratch_shapes.append(pltpu.SemaphoreType.DMA((copies,)))
    return pl.pallas_call(
        kernel,
        name=name,
        out_shape=[jax.ShapeDtypeStruct(s, jnp.float32) for s in outs],
        in_specs=[far] * far_in + [held] * (len(args) - far_in),
        out_specs=[far] * far_out + [held] * (len(outs) - far_out),
        scratch_shapes=scratch_shapes,
        cost_estimate=cost,
        input_output_aliases=dict(aliases),
        compiler_params=pltpu.CompilerParams(vmem_limit_bytes=VMEM_BYTES),
    )(*[pltpu.with_memory_space_constraint(a, pltpu.HBM) for a in args[:far_in]], *args[far_in:])


def busy(bytes_accessed):
    return pl.CostEstimate(flops=0, bytes_accessed=bytes_accessed, transcendentals=0)


def swap_near(axis, face):
    return lax.ppermute(face, axis, [(i, i ^ 1) for i in range(lax.axis_size(axis))])


def swap_far(axis, face):
    size = lax.axis_size(axis)
    return lax.ppermute(face, axis, [(i, far_partner(i, size)) for i in range(size)])


def swap_all(x_near, x_far, y_near, y_far):
    y_far = swap_far("gy", y_far)
    x_far = swap_far("gx", x_far)
    x_near = swap_near("gx", x_near)
    y_near = swap_near("gy", y_near)
    return x_far, x_near, y_far, y_near


def far_partner(i, size):
    return (i + 1 if i % 2 else i - 1) % size


def partner_loads(load, axis, partners, riders, count):
    size, heard, faces = lax.axis_size(axis), [], []
    for n, (partner, rider) in enumerate(zip(partners, riders)):
        mine = load
        if n:
            mine = load[:count] if rider is None else jnp.concatenate([load[:count], rider])
        mine = lax.ppermute(mine, axis, [(i, partner(i)) for i in range(size)])
        heard.append(mine)
        if rider is not None:
            faces.append(mine[count:])
    return heard, faces


def all_sum(values, axis, near, far, following, meanwhile):
    size = lax.axis_size(axis)
    count = values.shape[0] - far.shape[0] if following is None else values.shape[0]
    half = size // 2

    def to_near(i):
        return i ^ 1

    def to_far(i):
        return far_partner(i, size)

    def across(i):
        return (i + half) % size

    def far_across(i):
        return across(to_far(i))

    rounds = [((to_far,), (far,))]
    if size == 4:
        rounds = [((to_far, to_near, across), (far, near, None))]
    elif size > 4:
        rounds = [((to_far, across, far_across), (far, None, None)), ((to_near,), (near,))]
        bit = 4
        while bit < half:
            rounds.append(((lambda i, bit=bit: i ^ bit,), (None,)))
            bit *= 2
    else:
        rounds.append(((), (near,)))
    faces = []
    load = values if following is None else jnp.concatenate([values, far])
    for n, (partners, riders) in enumerate(rounds):
        if not partners:
            faces.append(lax.ppermute(near, axis, [(i, to_near(i)) for i in range(size)]))
            continue
        heard, got = partner_loads(load, axis, partners, riders, count)
        faces += got
        rider = rounds[n + 1][1][0] if n + 1 < len(rounds) and rounds[n + 1][0] else following
        tail = jnp.zeros((8, values.shape[1]), jnp.float32) if rider is None else rider
        (load,) = call(
            functools.partial(add_loads, count), "add_loads", [(count + tail.shape[0], values.shape[1])],
            load, *heard, tail, meanwhile(),
        )
    if following is None:
        load = load[:count]
    return load, faces[1], faces[0]


def conjugate_coefficients(moments, centre, half):
    remaining, towards = list(moments), list(moments)
    one, zero = jnp.ones_like(moments[0]), jnp.zeros_like(moments[0])
    direction = [one] + [zero] * ITERS
    residual = list(direction)
    total = [zero] * ITERS
    for step in range(ITERS):
        count = len(towards) - 1
        image = []
        for level in range(count):
            side = (
                half * towards[1] if level == 0 else 0.5 * half * (towards[level + 1] + towards[level - 1])
            )
            image.append(centre * towards[level] + side)
        alpha = remaining[step] / image[step]
        total = [total[i] + alpha * direction[i] for i in range(ITERS)]
        if step == ITERS - 1:
            break
        applied = []
        for i in range(ITERS + 1):
            term = centre * direction[i]
            if i >= 1:
                term = term + (half if i == 1 else 0.5 * half) * direction[i - 1]
            if i < ITERS:
                term = term + 0.5 * half * direction[i + 1]
            applied.append(term)
        residual = [residual[i] - alpha * applied[i] for i in range(ITERS + 1)]
        following = [remaining[i] - alpha * image[i] for i in range(count)]
        beta = -alpha * (half if step == 0 else 0.5 * half) * following[step + 1] / remaining[step]
        towards = [following[i] + beta * towards[i] for i in range(count)]
        direction = [residual[i] + beta * direction[i] for i in range(ITERS + 1)]
        remaining = following
    return total


def on_device(old_fields, inverse_step, boundary):
    x, y, z = inverse_step.shape
    t = Tables(y, z)
    brick, four = (x, y, z), (4, x, y, z)
    faces = [(y, z)] * 2 + [(x, z)] * 2
    faces5 = [(5,) + f for f in faces]
    faces_back = [(y, z)] * 2 + [(x, z)] * 2

    place = [lax.axis_index(a) % 2 == 0 for a in ("gx", "gy")]
    even = jnp.stack([jnp.full((8, 128), p, jnp.float32) for p in place])

    old, step, x_near, x_far, y_near, y_far = call(
        load_faces, "right_faces", [four, brick] + faces5, old_fields, inverse_step, even, far_in=2, copies=5,
    )
    received = swap_all(x_near, x_far, y_near, y_far)
    (local,) = call(load_local, "right_local", [(5,) + brick], old, step, cost=busy(2 << 20))

    top = INTERVAL_SHARE * np.array([spectrum_top(c) for c in DIFFUSE])
    halves = [float(v) for v in 0.5 * top]
    scales = [float(v) for v in np.array(DIFFUSE) / (0.5 * top)]
    rates = [float(v) for v in 1.0 / (0.5 * top)]

    def scaled(factor):
        return f32(np.stack([factor * v * t.summed for v in scales]))


    x_far, x_near, y_far, y_near = received
    relayed = [(6, x, z)] * 2
    x_faces, y_faces5 = [(5, y, z)] * 2, [(5, x, z)] * 2
    part, near, far = call(first_y, "first_y", [four] + relayed, local, boundary, y_far, y_near, even, cost=busy(2 << 20))
    right, y_near, y_far, x_near, x_far = call(
        first_x, "first_x", [four] + relayed + x_faces, part, near, far, boundary, x_far, x_near, even,
        aliases=[(0, 0), (1, 1), (2, 2)],
    )
    heard = [swap_all(x_near, x_far, y_near, y_far)]
    reaction, free, ahead = call(
        functools.partial(start_sums, scales, rates), "right_sums", [brick, brick, four],
        local, boundary, *received, even, right, scaled(1.0), t.share, *t.left_y, *t.stiff_z, cost=busy(8 << 20),
    )
    x_far, x_near, y_far, y_near = heard[0]
    part, right, reaction, near, far = call(
        functools.partial(second_y, scales, rates), "second_y", [four, four, brick] + y_faces5,
        ahead, free, *received, y_far, y_near, even, t.summed, *t.stiff_z, right, reaction,
        scratch=[(16, z)] * 2, aliases=[(12, 1), (13, 2)], cost=busy(3 << 20),
    )
    basis, sums = [right], []
    here = scales
    for k in range(1, ITERS - 1):
        field, y_near, y_far, x_near, x_far = call(
            functools.partial(grow_x, here), "basis_x", [four] + y_faces5 + x_faces,
            part, near, far, free, x_far, x_near, even, t.summed, aliases=[(0, 0), (1, 1), (2, 2)],
        )
        basis.append(field)
        heard.append(swap_all(x_near, x_far, y_near, y_far))
        x_far, x_near, y_far, y_near = heard[-1]
        outs = [four, (8, 128)] + ([(8, 128)] if k == 1 else [])
        ahead, *dots = call(
            functools.partial(basis_sums, scales, rates), "basis_sums", outs,
            basis[-1], basis[-2], reaction, free, scaled(2.0), t.share, *t.left_y, *t.stiff_z, cost=busy(8 << 20),
        )
        sums += dots[::-1]
        here = [2.0 * v for v in scales]
        if k < ITERS - 2:
            part, near, far = call(
                functools.partial(grow_y, here), "basis_y", [four] + y_faces5,
                ahead, free, y_far, y_near, even, t.summed, cost=busy(2 << 20),
            )
    part, near, far, products = call(
        functools.partial(last_y, scales, rates), "last_y", [four] + [(x, z)] * 2 + [(4, 3, 8, 128)],
        ahead, basis[-1], reaction, free, y_far, y_near, even, t.summed, t.share, *t.plain_y, *t.plain_z, t.local,
        cost=busy(4 << 20),
    )
    field, y_near, y_far, sums, x_near, x_far = call(
        functools.partial(last_x, scales, rates), "last_x",
        [four] + [(x, z)] * 2 + [(ITERS, 8, 128)] + [(y, z)] * 2,
        part, near, far, products, basis[-1], reaction, free, x_far, x_near, even, t.summed, t.share,
        *t.plain_y, *t.plain_z, t.local, *sums, aliases=[(0, 0), (1, 1), (2, 2)],
    )
    basis.append(field)
    heard[0] = call(mend_slopes, "slopes", faces_back, *received, *heard[0], free, even)
    sums = sums.reshape(ITERS * 8, z)
    sloped = []

    def meanwhile():
        if len(sloped) < ITERS:
            sloped.extend(
                call(
                    slope_sums, "slope_sums", [(3,) + brick] * 3,
                    *basis[len(sloped) : len(sloped) + 3], t.summed, t.slope_y, *t.slope_z, cost=busy(6 << 20),
                )
            )
        return sloped[-1]

    sums, x_near, x_far = all_sum(sums, "gx", x_near, x_far, y_far, meanwhile)
    sums, y_near, y_far = all_sum(sums, "gy", y_near, y_far, None, meanwhile)
    while len(sloped) < ITERS:
        meanwhile()
    sums = sums.reshape(ITERS, 8, z)
    slopes = (x_far, x_near, y_far, y_near)

    centre, half = chebyshev_bounds()
    factor = centre / half
    damping = 1.0 / factor
    weights, remainder, update, *sent = call(
        functools.partial(first_update, halves, 1.0 / centre), "first_update", [(ITERS, 8, 128), brick, brick] + faces,
        sums, *sloped, *[a for h in heard for a in h], *slopes, even, free, t.summed, t.inverse, scratch=faces_back,
    )
    pressure, tick = update, even
    for step in range(1, CHEB):
        last = step == CHEB - 1
        received = swap_all(*sent)
        (raw,) = call(
            pressure_sums, "pressure_sums", [brick],
            update, tick, t.summed, t.shift, t.stiff_y, *t.stiff_z, cost=busy(2 << 20), scratch=[brick],
        )
        if step == 1:
            fields, tick = call(combine_fields, "fields", [four, (8, z)], weights, *basis, cost=busy(4 << 20))
        following = 1.0 / (2.0 * factor - damping)
        keep, gain = following * damping, 2.0 * following / half
        damping = following
        x_far, x_near, y_far, y_near = received
        args = [raw, free, y_far, y_near, even, t.summed, t.inverse, remainder, update, pressure]
        if last:
            pressure, end_part = call(
                functools.partial(last_pressure_y, keep, gain), "last_pressure_y", [brick, (2, y, z)], *args,
                scratch=[brick], far_out=1, copies=1, cost=busy(1 << 20),
            )
            (pressure,) = call(
                functools.partial(last_pressure_x, gain), "last_pressure_x", [brick],
                pressure, end_part, free, x_far, x_near, even, t.summed, t.inverse,
                scratch=[(2, y, z)], far_in=1, far_out=1, copies=2, aliases=[(0, 0)],
            )
            break
        part = call(
            functools.partial(pressure_y, keep, gain), "pressure_y", [brick] * 3 + [(x, z)] * 2, *args, cost=busy(1 << 20)
        )
        pressure, remainder, update, y_near, y_far, x_near, x_far = call(
            functools.partial(pressure_x, gain), "pressure_x", [brick] * 3 + [(x, z)] * 2 + [(y, z)] * 2,
            *part, free, x_far, x_near, even, t.summed, t.inverse, aliases=[(i, i) for i in range(5)],
        )
        sent = x_near, x_far, y_near, y_far
    return (fields, pressure)


def solution(mesh):
    return jax.shard_map(
        on_device,
        mesh=mesh,
        in_specs=(P(None, "gx", "gy", None), P("gx", "gy", None), P("gx", "gy", None)),
        out_specs=(P(None, "gx", "gy", None), P("gx", "gy", None)),
        check_vma=False,
    )
```
